32 devices in a mesh: wide: 8 (over z, y), narrow: 4 (over x, core).
Axes of the slice: x: 2, y: 2, z: 4, core: 2. Of those that a mesh axis runs over, the one named last changes fastest.
Arguments:
- weights: float32 [9060864], P('narrow')
- first_moment: float32 [4, 9060864], P('narrow', 'wide'), may hold values from -9.536743e-07 to 9.536743e-07
- second_moment: float32 [4, 9060864], P('narrow', 'wide'), may hold values from 4.458736e-15 to 1.787909e-14
- outer_momentum: float32 [9060864], P('narrow'), may hold values from -0.15625 to 0.15625
- noisy_input: bfloat16 [8, 128, 128, 128], P('wide', 'narrow'), may hold values from -6 to 6
- target: bfloat16 [8, 128, 128, 128], P('wide', 'narrow'), may hold values from -6 to 6
- text_tokens: bfloat16 [8, 128, 4096], P('wide', 'narrow'), may hold values from -6 to 6
- text_mask: int32 [8, 128], P('wide', 'narrow'), may hold values 0 or 1
- noise_level: int32 [8], P('wide'), may hold values from 0 to 999
- aug_level: int32 [8], P('wide'), may hold values from 0 to 23
- crop_size: int32 [8], P('wide'), may hold values from 32 to 128
Outputs:
- new_weights: float32 [9060864], P('narrow')
- momentum_out: float32 [9060864], P('narrow')
- moment_one: float32 [4, 9060864], P('narrow', 'wide')
- moment_two: float32 [4, 9060864], P('narrow', 'wide')
- loss_terms: float32 [1], replicated
- valid_count: float32 [1], replicated
The draws below stay inside these ranges and needn't reach their ends.
All inputs are finite; a program needn't handle non-finite values. No bound on the sum of `text_mask` on one device may be relied on, other than what follows from the above.
Results may differ from the reference program's by a relative error of at most 0.0061.
Values may be sent and summed in bfloat16 or wider, within the bound.
A program may use at most 256 MiB of HBM per device.

```python
import math
import jax
import jax.numpy as jnp
from jax import lax

C = 128
NORM_GROUPS = 32
HEADS = 8
HEAD = 128
TEXT_D = 4096
TXT = 128
H = 128
W = 128
NOISE_LEVELS = 1000
AUG_LEVELS = 24
GROUPS = 4
STEP = 8
ITEMS_DEV = 1
ITEMS = 8
LEVELS = 1024
PARAMS = 9060864
N_WIDE = 8
N_NARROW = 4


def draw_weights(key, part):
    key = jax.random.fold_in(key, 1)
    base = jax.random.normal(key, (PARAMS,), jnp.float32)
    base = jnp.clip(base, -6.0, 6.0)
    attn_width = HEADS * HEAD
    kv_total = TEXT_D * 2 * attn_width
    kv_part = (base[:kv_total] * TEXT_D ** (-0.5)).reshape(N_NARROW, -1)
    scale_parts = [jnp.full((9 * C * C,), (9.0 * C) ** (-0.5), jnp.float32), jnp.full((LEVELS * 2 * C,), 0.3, jnp.float32), jnp.full((4 * C,), 0.2, jnp.float32), jnp.full((C * attn_width,), C ** (-0.5), jnp.float32), jnp.full((attn_width * C,), (0.75 * TXT / attn_width) ** 0.5, jnp.float32)]
    gain_offset = jnp.concatenate([jnp.ones((C,), jnp.float32), jnp.zeros((C,), jnp.float32), jnp.ones((C,), jnp.float32), jnp.zeros((C,), jnp.float32)])
    offset_parts = [jnp.zeros((9 * C * C + LEVELS * 2 * C,), jnp.float32), gain_offset, jnp.zeros((C * attn_width + attn_width * C,), jnp.float32)]
    rest = jnp.concatenate(offset_parts) + jnp.concatenate(scale_parts) * base[kv_total:]
    rest_part = rest.reshape(N_NARROW, -1)
    return jnp.concatenate([kv_part, rest_part], axis=1).reshape(-1)


def set_ends(result, rng, smallest, top_value):
    extent = result.shape
    place = [jax.random.randint(jax.random.fold_in(rng, axis), (), 0, extent[axis]) for axis in range(len(extent))]
    result = result.at[tuple(place)].set(smallest)
    longest = extent.index(max(extent))
    place[longest] = (place[longest] + 1) % extent[longest]
    return result.at[tuple(place)].set(top_value)


def block_levels(rng, extent, cuts, smallest, high):
    def one(axis_at, parts):
        steps = jax.random.uniform(jax.random.fold_in(jax.random.fold_in(rng, 6), axis_at), (parts,), jnp.float32, smallest / len(cuts), high / len(cuts))
        return jnp.repeat(jnp.exp(steps), extent[axis_at] // parts).reshape((-1,) + (1,) * (len(extent) - axis_at - 1))

    gain = one(*cuts[0])
    for cut in cuts[1:]:
        gain = gain * one(*cut)
    return gain


def bell_draw(key, shape, width, reach, cuts=(), kind=jnp.bfloat16):
    entries = width * jax.random.normal(key, shape, jnp.float32)
    if cuts:
        entries = entries * block_levels(key, shape, cuts, -0.22, 0.18)
    return jnp.clip(entries, -reach, reach).astype(kind)


def setup_inputs(seed: int = 0) -> dict:
    key_of = jax.random.split(jax.random.key(seed), 12)
    return {
        "weights": draw_weights(jax.random.fold_in(key_of[11], 71), 0),
        "first_moment": bell_draw(key_of[1], (N_NARROW, GROUPS * PARAMS // N_NARROW), (0.000222 / PARAMS ** 0.5), 9.5367431640625e-07, ((0, 4), (1, 8)), jnp.float32),
        "second_moment": jnp.clip(jnp.exp(math.log(1.7879090135480835e-14) - 1.3887665 * jax.random.uniform(key_of[2], (N_NARROW, GROUPS * PARAMS // N_NARROW), jnp.float32) ** block_levels(key_of[2], (N_NARROW, GROUPS * PARAMS // N_NARROW), ((0, 4), (1, 8)), -0.2, 0.2)), 4.458736118083959e-15, 1.7879090135480835e-14),
        "outer_momentum": bell_draw(key_of[3], (PARAMS,), 0.01, 0.15625, ((0, 4),), jnp.float32),
        "noisy_input": bell_draw(key_of[4], (ITEMS, H, W, C), 1.0, 6.0, ((0, 8), (1, 4))),
        "target": bell_draw(key_of[5], (ITEMS, H, W, C), 1.0, 6.0, ((0, 8), (1, 4))),
        "text_tokens": bell_draw(key_of[6], (ITEMS, TXT, TEXT_D), 1.0, 6.0, ((0, 8), (1, 4))),
        "text_mask": set_ends((jax.random.randint(key_of[7], (ITEMS, TXT), 0, 4) < 3).astype(jnp.int32), jax.random.fold_in(key_of[7], 1), 0, 1),
        "noise_level": set_ends(jax.random.randint(key_of[8], (ITEMS,), 0, NOISE_LEVELS), jax.random.fold_in(key_of[8], 1), 0, NOISE_LEVELS - 1).astype(jnp.int32),
        "aug_level": set_ends(jax.random.randint(key_of[9], (ITEMS,), 0, AUG_LEVELS), jax.random.fold_in(key_of[9], 1), 0, AUG_LEVELS - 1).astype(jnp.int32),
        "crop_size": set_ends(jax.random.randint(key_of[10], (ITEMS,), H // 4, H + 1), jax.random.fold_in(key_of[10], 1), H // 4, H).astype(jnp.int32),
    }


EPS_NORM = 1e-05
CLIP_NORM = 0.002
BETA_ONE = 0.9
BETA_TWO = 0.99
INNER_RATE = 0.01
DECAY_RATE = 0.01
ADAM_EPS = 1e-08
OUTER_RATE = 0.7
OUTER_MOMENTUM = 0.9
HIGH = lax.Precision.HIGHEST

@jax.custom_vjp
def low(v):
    return lax.optimization_barrier(v.astype(jnp.bfloat16)).astype(jnp.float32)

@jax.custom_vjp
def low_back(v):
    return v

def low_keep(v):
    return (low(v), None)

def low_pass(kept, grad):
    return (grad,)

def back_keep(v):
    return (v, None)

def back_low(kept, grad):
    return (low(grad),)
low.defvjp(low_keep, low_pass)
low_back.defvjp(back_keep, back_low)

def unpack(packed):
    kv_width = 2 * HEADS * HEAD
    kv_block = kv_width // N_NARROW
    kv_len = TEXT_D * kv_block
    shard_rows = packed.reshape(N_NARROW, -1)
    keyval_w = shard_rows[:, :kv_len].reshape(N_NARROW, TEXT_D, kv_block).transpose(1, 0, 2).reshape(TEXT_D, kv_width)
    rest = shard_rows[:, kv_len:].reshape(-1)
    layouts = [(9 * C, C), (NOISE_LEVELS + AUG_LEVELS, 2 * C), (4, C), (C, HEADS * HEAD), (HEADS * HEAD, C)]
    pieces = []
    offset = 0
    for layout in layouts:
        number = layout[0] * layout[1]
        pieces.append(rest[offset:offset + number].reshape(layout))
        offset = offset + number
    return (pieces[0], pieces[1], pieces[2], pieces[3], keyval_w, pieces[4])

def film_norm(noisy_float, cond_table, norm_gains, noise_level, aug_level, group_sums, squares, element_count):
    num_items, height, columns, channels = noisy_float.shape
    levels = jnp.arange(NOISE_LEVELS + AUG_LEVELS, dtype=jnp.int32)
    level_hot = (levels[None, :] == noise_level[:, None]).astype(jnp.float32) + (levels[None, :] == (aug_level + NOISE_LEVELS)[:, None]).astype(jnp.float32)
    film_terms = jnp.dot(level_hot, cond_table, precision=HIGH)
    average = group_sums / element_count
    spread = lax.rsqrt(squares / element_count - average * average + EPS_NORM)
    grouped = noisy_float.reshape(num_items, height, columns, NORM_GROUPS, channels // NORM_GROUPS)
    normed = ((grouped - average[:, None, None, :, None]) * spread[:, None, None, :, None]).reshape(num_items, height, columns, channels)
    scaled = (normed * norm_gains[0] + norm_gains[1]) * (1.0 + film_terms[:, None, None, :channels]) + film_terms[:, None, None, channels:]
    return jax.nn.silu(scaled)

def convolve(padded, conv_w, height, columns):
    channels = conv_w.shape[1]
    padded = jnp.pad(padded, ((0, 0), (0, 0), (1, 1), (0, 0)))
    running = jnp.zeros((padded.shape[0], height, columns, channels), jnp.float32)
    for offset_y in range(3):
        for offset_x in range(3):
            tap_index = offset_y * 3 + offset_x
            window = padded[:, offset_y:offset_y + height, offset_x:offset_x + columns]
            running = running + jnp.einsum('ihwc,cd->ihwd', window, conv_w[tap_index * channels:(tap_index + 1) * channels], precision=HIGH)
    return running

def attend(convolved, norm_gains, query_w, out_w, keyval, valid_keys, lowered):
    num_items, height, columns, channels = convolved.shape
    centered = convolved - lax.optimization_barrier(jnp.mean(convolved, axis=-1, keepdims=True))
    layered = lowered(centered * lax.rsqrt(lax.optimization_barrier(jnp.mean(centered * centered, axis=-1, keepdims=True)) + EPS_NORM) * norm_gains[2] + norm_gains[3])
    queries = lowered(jnp.einsum('ihwc,cd->ihwd', layered, query_w, precision=HIGH)).reshape(num_items, height * columns, HEADS, HEAD)
    key_heads = keyval[..., :HEADS * HEAD].reshape(num_items, -1, HEADS, HEAD)
    value_heads = keyval[..., HEADS * HEAD:].reshape(num_items, -1, HEADS, HEAD)
    scores = jnp.einsum('iqhd,ikhd->ihqk', queries, key_heads, precision=HIGH) * (1.0 / math.sqrt(HEAD))
    scores = jnp.where(valid_keys[:, None, None, :], scores, -1e+30)
    maximum = lax.optimization_barrier(jnp.max(scores, axis=-1, keepdims=True))
    exponent = jnp.exp(scores - maximum)
    softmax_w = lowered(exponent / lax.optimization_barrier(jnp.sum(exponent, axis=-1, keepdims=True)))
    mixture = lowered(jnp.einsum('ihqk,ikhd->iqhd', softmax_w, value_heads, precision=HIGH)).reshape(num_items, height, columns, HEADS * HEAD)
    return convolved + jnp.einsum('ihwd,dc->ihwc', mixture, out_w, precision=HIGH)

def forward(packed, noisy_float, target_float, text_float, valid_keys, noise_level, aug_level, pixel_mask):
    conv_w, cond_table, norm_gains, query_w, keyval_w, out_w = unpack(low(packed))
    num_items, height, columns, channels = noisy_float.shape
    grouped = noisy_float.reshape(num_items, height * columns, NORM_GROUPS, channels // NORM_GROUPS)
    group_sums = lax.optimization_barrier(jnp.sum(grouped, axis=(1, 3)))
    squares = lax.optimization_barrier(jnp.sum(grouped * grouped, axis=(1, 3)))
    element_count = height * columns * channels // NORM_GROUPS
    active = low(film_norm(noisy_float, cond_table, norm_gains, noise_level, aug_level, group_sums, squares, element_count))
    padded = jnp.pad(active, ((0, 0), (1, 1), (0, 0), (0, 0)))
    convolved = noisy_float + convolve(padded, conv_w, height, columns)
    keyval = low(jnp.einsum('itc,cd->itd', text_float, keyval_w, precision=HIGH))
    output = attend(convolved, norm_gains, query_w, out_w, keyval, valid_keys, low)
    residual_err = output - target_float
    return jnp.sum(residual_err * residual_err * pixel_mask[..., None])

def reference(weights, first_moment, second_moment, outer_momentum, noisy_input, target, text_tokens, text_mask, noise_level, aug_level, crop_size):
    group_devs = N_WIDE // GROUPS
    shard_len = PARAMS // N_NARROW
    row_ids = jnp.arange(H, dtype=jnp.int32)
    col_ids = jnp.arange(W, dtype=jnp.int32)
    pixel_mask = ((row_ids[None, :, None] < crop_size[:, None, None]) & (col_ids[None, None, :] < crop_size[:, None, None])).astype(jnp.float32)
    token_ids = jnp.arange(TXT, dtype=jnp.int32)
    valid_keys = (text_mask > 0) | (token_ids[None, :] == 0)
    group_counts = lax.optimization_barrier(jnp.sum(pixel_mask.reshape(GROUPS, -1), axis=1))
    total_count = jnp.sum(group_counts)

    def shaped(array):
        return array.reshape((GROUPS, group_devs, ITEMS_DEV) + array.shape[1:])
    batches = (shaped(noisy_input), shaped(target), shaped(text_tokens), shaped(valid_keys), shaped(noise_level), shaped(aug_level), shaped(pixel_mask))

    def one_device(running_sum, device_batch):
        noisy_part, target_part, text_part, valid_part, noise_part, aug_part, mask_part = device_batch

        def loss_of(packed):
            return forward(packed, noisy_part.astype(jnp.float32), target_part.astype(jnp.float32), text_part.astype(jnp.float32), valid_part, noise_part, aug_part, mask_part)
        loss_value, pullback = jax.vjp(loss_of, weights)
        gradient, = pullback(jnp.ones((), jnp.float32))
        return ((running_sum[0] + loss_value, running_sum[1] + gradient), None)
    loss_total = jnp.zeros((), jnp.float32)
    gradients = []
    for group_id in range(GROUPS):
        initial = (jnp.zeros((), jnp.float32), jnp.zeros((PARAMS,), jnp.float32))
        outcome, unused = lax.scan(one_device, initial, tuple((member[group_id] for member in batches)))
        loss_total = loss_total + outcome[0]
        gradients.append(outcome[1] / total_count)
    gradients = jnp.stack(gradients)
    norms = jnp.sqrt(lax.optimization_barrier(jnp.sum(gradients * gradients, axis=1)))
    clipped = gradients * jnp.minimum(1.0, CLIP_NORM / norms)[:, None]

    def to_groups(state):
        return state.reshape(N_NARROW, GROUPS, shard_len).transpose(1, 0, 2).reshape(GROUPS, PARAMS)

    def from_groups(state):
        return state.reshape(GROUPS, N_NARROW, shard_len).transpose(1, 0, 2).reshape(N_NARROW, GROUPS * shard_len)
    moment_one = BETA_ONE * to_groups(first_moment) + (1.0 - BETA_ONE) * clipped
    moment_two = BETA_TWO * to_groups(second_moment) + (1.0 - BETA_TWO) * clipped * clipped
    corrected_one = moment_one / (1.0 - BETA_ONE ** STEP)
    corrected_two = moment_two / (1.0 - BETA_TWO ** STEP)
    inner = weights[None, :] - INNER_RATE * (corrected_one / (jnp.sqrt(corrected_two) + ADAM_EPS) + DECAY_RATE * weights[None, :])
    averaged = lax.optimization_barrier(jnp.sum(group_counts[:, None] * (weights[None, :] - inner), axis=0)) / total_count
    momentum_out = OUTER_MOMENTUM * outer_momentum + averaged
    new_weights = weights - OUTER_RATE * (averaged + OUTER_MOMENTUM * momentum_out)
    return (new_weights, momentum_out, from_groups(moment_one), from_groups(moment_two), jnp.stack([loss_total]), jnp.stack([total_count]))
```

```python
import functools
import math

import jax
import jax.numpy as jnp
from jax import lax
from jax.experimental import pallas as pl
from jax.experimental.pallas import tpu as pltpu
from jax.sharding import PartitionSpec as P

MESH = pl.DeviceIdType.MESH
C = 128
NORM_GROUPS = 32
HEADS = 8
HEAD = 128
TEXT_D = 4096
H = 128
W = 128
NOISE_LEVELS = 1000
AUG_LEVELS = 24
LEVELS = NOISE_LEVELS + AUG_LEVELS
GROUPS = 4
STEP = 8


EPS_NORM = 1e-05
CLIP_NORM = 0.002
BETA_ONE = 0.9
BETA_TWO = 0.99
INNER_RATE = 0.01
DECAY_RATE = 0.01
ADAM_EPS = 1e-08
OUTER_RATE = 0.7
OUTER_MOMENTUM = 0.9
F32 = jnp.float32
BF16 = jnp.bfloat16
LOG2E = 1.4426950408889634
LN2 = 0.6931471805599453
NT = (((1,), (1,)), ((), ()))
TILE = 2


def dot(a, b, dims=(((1,), (0,)), ((), ()))):
    return lax.dot_general(a, b, dims, preferred_element_type=F32)


def two_parts(value):
    top = value.astype(BF16)
    return top, (value - top.astype(F32)).astype(BF16)


def shifted(value, by, keep):
    return jnp.where(keep, pltpu.roll(value, by, 0), 0.0)


def main_kernel(
    band, columns, height, heads,
    info, noisy, target, vecs, conv_w, query_w, out_w, keyval, key_ok,
    dconv_w, y_t, z_t, sums,
    act3, diff3, m_cat, m_cat_t, n_cat, n_cat_t, conv_t, probs, dscore, wt3,
):
    tok = keyval.shape[0]
    width = heads * HEAD
    row0 = info[0]
    crop = info[1]
    pix = TILE * columns
    factor = LOG2E / math.sqrt(HEAD)
    for head in range(heads):
        cols = slice(head * HEAD, (head + 1) * HEAD)
        tcols = slice(head * tok, (head + 1) * tok)
        m_head = dot(query_w[:, cols], keyval[:, cols], NT) * factor
        top, rest = two_parts(m_head)
        m_cat[:C, tcols] = top
        m_cat[C:, tcols] = rest
        top, rest = two_parts(m_head.T)
        m_cat_t[tcols, :C] = top
        m_cat_t[tcols, C:] = rest
        n_head = dot(keyval[:, width + head * HEAD : width + (head + 1) * HEAD], out_w[cols, :])
        top, rest = two_parts(n_head)
        n_cat[tcols, :C] = top
        n_cat[tcols, C:] = rest
        top, rest = two_parts(n_head.T)
        n_cat_t[:C, tcols] = top
        n_cat_t[C:, tcols] = rest
    for tap in range(9):
        rows = slice(tap * C, (tap + 1) * C)
        wt3[rows, :] = conv_w[rows, :].astype(F32).T.astype(BF16)
    y_t[...] = jnp.zeros_like(y_t)
    z_t[...] = jnp.zeros_like(z_t)
    conv_t[...] = jnp.zeros_like(conv_t)
    sums[...] = jnp.zeros_like(sums)
    mean, spread = vecs[0:1, :], vecs[1:2, :]
    gain, offset = vecs[2:3, :], vecs[3:4, :]
    ln_gain, ln_offset = vecs[4:5, :], vecs[5:6, :]
    place = lax.broadcasted_iota(jnp.int32, (columns, C), 0)
    not_first, not_last = place > 0, place < columns - 1
    slope = spread * gain
    base = offset - mean * slope

    @pl.loop(0, band + 4)
    def _(r):
        scaled = noisy[r].astype(F32) * slope + base
        value = scaled * jax.nn.sigmoid(scaled)
        row = row0 + r - 2
        value = jnp.where(jnp.logical_and(row >= 0, row < height), value, 0.0)
        value = value.astype(BF16).astype(F32)
        act3[r, :, 0:C] = shifted(value, 1, not_first).astype(BF16)
        act3[r, :, C : 2 * C] = value.astype(BF16)
        act3[r, :, 2 * C : 3 * C] = shifted(value, columns - 1, not_last).astype(BF16)

    pix_row = lax.broadcasted_iota(jnp.int32, (pix, C), 0) // columns
    pix_col = lax.broadcasted_iota(jnp.int32, (pix, C), 0) % columns
    ok = key_ok[...] > 0.0

    @pl.loop(0, (band + 2) // TILE)
    def _(t):
        q = t * TILE
        conv = noisy[pl.ds(q + 1, TILE)].astype(F32).reshape(pix, C)
        for dy in range(3):
            window = act3[pl.ds(q + dy, TILE)].reshape(pix, 3 * C)
            conv = conv + dot(window, conv_w[dy * 3 * C : (dy + 1) * 3 * C, :])
        centered = conv - jnp.mean(conv, axis=1, keepdims=True)
        rs = lax.rsqrt(jnp.mean(centered * centered, axis=1, keepdims=True) + EPS_NORM)
        xhat = centered * rs
        layered = xhat * ln_gain + ln_offset
        low = layered.astype(BF16)
        low2 = jnp.concatenate([low, low], axis=1)
        for head in range(heads):
            tcols = slice(head * tok, (head + 1) * tok)
            score = dot(low2, m_cat[:, tcols])
            score = jnp.where(ok, score, -1e30)
            e = jnp.exp2(score - jnp.max(score, axis=1, keepdims=True))
            p = e * (1.0 / jnp.sum(e, axis=1, keepdims=True))
            probs[:, tcols] = p.astype(BF16)
        mixed = dot(probs[...], n_cat[...])
        output = conv + mixed[:, :C] + mixed[:, C:]
        row = row0 + q - 1 + pix_row
        valid = (row >= 0) & (row < crop) & (pix_col < crop)
        err = jnp.where(valid, output - target[pl.ds(q, TILE)].astype(F32).reshape(pix, C), 0.0)
        own_row = q + pix_row
        own = (own_row >= 1) & (own_row <= band)
        err_own = jnp.where(own, err, 0.0)
        sums[4:5, :] += jnp.sum(err_own * err_own, axis=0, keepdims=True)
        dout = 2.0 * err
        dout_low = dout.astype(BF16)
        dout2 = jnp.concatenate([dout_low, dout_low], axis=1)
        for head in range(heads):
            tcols = slice(head * tok, (head + 1) * tok)
            dprob = dot(dout2, n_cat_t[:, tcols])
            p = probs[:, tcols].astype(F32)
            pd = p * dprob
            ds = pd - p * jnp.sum(pd, axis=1, keepdims=True)
            dscore[:, tcols] = ds.astype(BF16)
        dlay2 = dot(dscore[...], m_cat_t[...])
        dlay = (dlay2[:, :C] + dlay2[:, C:]) * LN2
        dlay_own = jnp.where(own, dlay, 0.0)
        sums[2:3, :] += jnp.sum(dlay_own * xhat, axis=0, keepdims=True)
        sums[3:4, :] += jnp.sum(dlay_own, axis=0, keepdims=True)
        dxh = dlay * ln_gain
        dconv = dout + rs * (
            dxh
            - jnp.mean(dxh, axis=1, keepdims=True)
            - xhat * jnp.mean(dxh * xhat, axis=1, keepdims=True)
        )
        dout_t = (2.0 * err_own).T.astype(BF16)
        lay_t = jnp.where(own, layered, 0.0).T.astype(BF16)
        y_t[...] += dot(dout_t, probs[...])
        z_t[...] += dot(lay_t, dscore[...])
        dconv_t = jnp.where(own, dconv, 0.0).T.astype(BF16)
        for dy in range(3):
            window = act3[pl.ds(q + dy, TILE)].reshape(pix, 3 * C)
            conv_t[:, dy * 3 * C : (dy + 1) * 3 * C] += dot(dconv_t, window)
        for k in range(TILE):
            one = dconv[k * columns : (k + 1) * columns]
            diff3[q + k, :, 0:C] = shifted(one, columns - 1, not_last).astype(BF16)
            diff3[q + k, :, C : 2 * C] = one.astype(BF16)
            diff3[q + k, :, 2 * C : 3 * C] = shifted(one, 1, not_first).astype(BF16)

    @pl.loop(0, band // TILE)
    def _(t):
        r = t * TILE
        grad = jnp.zeros((pix, C), F32)
        for dy in range(3):
            window = diff3[pl.ds(r + 2 - dy, TILE)].reshape(pix, 3 * C)
            grad = grad + dot(window, wt3[dy * 3 * C : (dy + 1) * 3 * C, :])
        x = noisy[pl.ds(r + 2, TILE)].astype(F32).reshape(pix, C)
        scaled = x * slope + base
        sig = jax.nn.sigmoid(scaled)
        ds = grad * (sig * (1.0 + scaled * (1.0 - sig)))
        sums[0:1, :] += jnp.sum(ds, axis=0, keepdims=True)
        sums[1:2, :] += jnp.sum(ds * ((x - mean) * spread), axis=0, keepdims=True)

    for tap in range(9):
        cols = slice(tap * C, (tap + 1) * C)
        dconv_w[cols, :] = conv_t[:, cols].T


def run_main(info, noisy_ext, target_ext, vecs, conv_w, query_w, out_w, keyval, key_ok):
    band = target_ext.shape[0] - 2
    columns = target_ext.shape[1]
    tok = keyval.shape[0]
    vmem = pl.BlockSpec(memory_space=pltpu.VMEM)
    pix = TILE * columns
    return pl.pallas_call(
        functools.partial(main_kernel, band, columns, H, HEADS),
        out_shape=(
            jax.ShapeDtypeStruct((9 * C, C), F32),
            jax.ShapeDtypeStruct((C, HEADS * tok), F32),
            jax.ShapeDtypeStruct((C, HEADS * tok), F32),
            jax.ShapeDtypeStruct((8, C), F32),
        ),
        in_specs=[pl.BlockSpec(memory_space=pltpu.SMEM)] + [vmem] * 8,
        out_specs=(vmem,) * 4,
        scratch_shapes=[
            pltpu.VMEM((band + 4, columns, 3 * C), BF16),
            pltpu.VMEM((band + 2, columns, 3 * C), BF16),
            pltpu.VMEM((2 * C, HEADS * tok), BF16),
            pltpu.VMEM((HEADS * tok, 2 * C), BF16),
            pltpu.VMEM((HEADS * tok, 2 * C), BF16),
            pltpu.VMEM((2 * C, HEADS * tok), BF16),
            pltpu.VMEM((C, 9 * C), F32),
            pltpu.VMEM((pix, HEADS * tok), BF16),
            pltpu.VMEM((pix, HEADS * tok), BF16),
            pltpu.VMEM((9 * C, C), BF16),
        ],
        compiler_params=pltpu.CompilerParams(vmem_limit_bytes=40 * 2**20),
        name="main",
    )(info, noisy_ext, target_ext, vecs, conv_w, query_w, out_w, keyval, key_ok)


TROWS = 512
TN = (((0,), (0,)), ((), ()))


def adam_kernel(
    length, ints, scal, text_a, text_b, dkv, rest, first, second,
    first_out, second_out, step_out, gs, carry,
):
    i = pl.program_id(0)
    tokens = text_a.shape[0]
    lane0 = ints[0]

    @pl.when(i == 0)
    def _():
        carry[...] = jnp.zeros_like(carry)

    grad = dot(text_a[...], dkv[:tokens, :], TN) + dot(text_b[...], dkv[tokens:, :], TN)
    parts = TROWS // C
    for j in range(parts):
        gs[pl.ds(j, C, stride=parts), :] = grad[:, j * C : (j + 1) * C]
    g = (gs[...] + rest[...]) * scal[0]
    one = BETA_ONE * first.reshape(TROWS, C)[...] + (1.0 - BETA_ONE) * g
    two = BETA_TWO * second.reshape(TROWS, C)[...] + (1.0 - BETA_TWO) * g * g
    first_out.reshape(TROWS, C)[...] = one
    second_out.reshape(TROWS, C)[...] = two
    fixed_one = one * (1.0 / (1.0 - BETA_ONE**STEP))
    fixed_two = two * (1.0 / (1.0 - BETA_TWO**STEP))
    step = fixed_one / (jnp.sqrt(fixed_two) + ADAM_EPS) * scal[1]
    row = lax.broadcasted_iota(jnp.int32, (TROWS, C), 0)
    lane = lax.broadcasted_iota(jnp.int32, (TROWS, C), 1)
    step = jnp.where((i * TROWS + row) * C + lane < length, step, 0.0)
    turned = pltpu.roll(step, lane0, 1)
    above = pltpu.roll(turned, 1, 0)
    above = jnp.where(row == 0, carry[0:1, :], above)
    carry[0:1, :] = turned[TROWS - 1 : TROWS, :]
    step_out[...] = jnp.where(lane < lane0, above, turned).astype(BF16)


def run_adam(ints, scal, text_a, text_b, dkv, rest, first, second):
    length = first.shape[1]
    tiles = pl.cdiv(length + C, TROWS * C)
    tokens = text_a.shape[0]
    smem = pl.BlockSpec(memory_space=pltpu.SMEM)
    flat = pl.BlockSpec((1, TROWS * C), lambda i: (0, i))
    text_spec = pl.BlockSpec((tokens, C), lambda i: (0, i))
    square = pl.BlockSpec((TROWS, C), lambda i: (i, 0))
    return pl.pallas_call(
        functools.partial(adam_kernel, length),
        out_shape=(
            jax.ShapeDtypeStruct(first.shape, F32),
            jax.ShapeDtypeStruct(first.shape, F32),
            jax.ShapeDtypeStruct((tiles * TROWS, C), BF16),
        ),
        grid=(tiles,),
        in_specs=[
            smem, smem, text_spec, text_spec,
            pl.BlockSpec((2 * tokens, 4 * C), lambda i: (0, 0)),
            square, flat, flat,
        ],
        out_specs=(flat, flat, square),
        scratch_shapes=[pltpu.VMEM((TROWS, C), F32), pltpu.VMEM((8, C), F32)],
        compiler_params=pltpu.CompilerParams(vmem_limit_bytes=24 * 2**20),
        name="adam",
    )(ints, scal, text_a, text_b, dkv, rest, first, second)


def share_kernel(gd, rows, chunk, l1, l2, u_ref, out_ref, recv_a, recv_b, part,
                 s_u, s_fo, s_fi, s_y, r_a, r_b, r_f, r_y):
    wide = lax.axis_index("wide")
    g = wide // gd
    spot = wide % gd
    chunks = rows // chunk
    is_outer = jnp.logical_or(g == 0, g == GROUPS - 1)
    is_inner = jnp.logical_not(is_outer)
    low = g < GROUPS // 2
    outer_id = jnp.where(low, g - 1, g + 1) * gd + spot
    mate_id = jnp.where(low, g + 1, g - 1) * gd + spot
    barrier = pltpu.get_barrier_semaphore()
    for k in range(1, gd):
        other = g * gd + lax.rem(spot + k, gd)
        pl.semaphore_signal(barrier, inc=1, device_id={"wide": other}, device_id_type=MESH)
    pl.semaphore_signal(barrier, inc=1, device_id={"wide": mate_id}, device_id_type=MESH)
    @pl.when(is_inner)
    def _():
        pl.semaphore_signal(barrier, inc=1, device_id={"wide": outer_id}, device_id_type=MESH)
        pl.semaphore_wait(barrier, gd + 1)
    @pl.when(is_outer)
    def _():
        pl.semaphore_wait(barrier, gd)

    def sl(c):
        return pl.ds(pl.multiple_of(c * chunk, chunk), chunk)
    def copy(src, dst, ss, rs, dev):
        return pltpu.make_async_remote_copy(src_ref=src, dst_ref=dst, send_sem=ss, recv_sem=rs,
                                            device_id={"wide": dev}, device_id_type=MESH)
    def send_a(c):
        return copy(u_ref.at[sl(c)], recv_a.at[sl(c)], s_u.at[c], r_a.at[c], mate_id)
    def send_b(c):
        return copy(part.at[sl(c)], recv_b.at[sl(c)], s_u.at[c], r_b.at[c], mate_id)
    def send_fo(c):
        return copy(out_ref.at[spot, sl(c)], out_ref.at[spot, sl(c)], s_fo.at[c], r_f.at[c], outer_id)
    def send_fi(c):
        return copy(out_ref.at[spot, sl(c)], out_ref.at[spot, sl(c)], s_fi.at[c], r_f.at[c], mate_id)
    def send_y(c, k):
        return copy(out_ref.at[spot, sl(c)], out_ref.at[spot, sl(c)], s_y.at[k - 1, c], r_y.at[k - 1, c],
                    g * gd + lax.rem(spot + k, gd))
    def wait_y(c, k):
        src = lax.rem(spot + gd - k, gd)
        copy(out_ref.at[src, sl(c)], out_ref.at[src, sl(c)], s_y.at[k - 1, c], r_y.at[k - 1, c], wide).wait_recv()
    def spread(c):
        for k in range(1, gd):
            send_y(c, k).start()
    def is_root(c):
        return lax.rem(c + g, 2) == 1

    @pl.when(is_outer)
    def _():
        @pl.loop(0, chunks)
        def _(c):
            send_a(c).start()
        @pl.loop(0, chunks)
        def _(c):
            send_fo(c).wait_recv()
            spread(c)
    @pl.when(is_inner)
    def _():
        @pl.loop(0, chunks + l2)
        def _(c):
            @pl.when(jnp.logical_and(c < chunks, jnp.logical_not(is_root(c))))
            def _():
                send_a(c).wait_recv()
                part[sl(c)] = (u_ref[sl(c)].astype(jnp.float32) + recv_a[sl(c)].astype(jnp.float32)).astype(jnp.bfloat16)
                send_b(c).start()
            d = c - l1
            @pl.when(jnp.logical_and(jnp.logical_and(d >= 0, d < chunks), is_root(d)))
            def _():
                send_a(d).wait_recv()
                send_b(d).wait_recv()
                out_ref[spot, sl(d)] = (u_ref[sl(d)].astype(jnp.float32) + recv_a[sl(d)].astype(jnp.float32) + recv_b[sl(d)].astype(jnp.float32)).astype(jnp.bfloat16)
                send_fo(d).start()
                send_fi(d).start()
                spread(d)
            e = c - l2
            @pl.when(jnp.logical_and(e >= 0, jnp.logical_not(is_root(e))))
            def _():
                send_fi(e).wait_recv()
                send_fo(e).start()
                spread(e)
    @pl.loop(0, chunks)
    def _(c):
        for k in range(1, gd):
            wait_y(c, k)
            send_y(c, k).wait_send()
        @pl.when(is_outer)
        def _():
            send_a(c).wait_send()
        @pl.when(is_inner)
        def _():
            send_fo(c).wait_send()
            @pl.when(is_root(c))
            def _():
                send_fi(c).wait_send()
            @pl.when(jnp.logical_not(is_root(c)))
            def _():
                send_b(c).wait_send()

def share(u, gd, rows, chunk, l1, l2):
    n = rows // chunk
    D = pltpu.SemaphoreType.DMA
    return pl.pallas_call(
        functools.partial(share_kernel, gd, rows, chunk, l1, l2),
        out_shape=jax.ShapeDtypeStruct((gd, rows, 128), jnp.bfloat16),
        in_specs=[pl.BlockSpec(memory_space=pltpu.VMEM)],
        out_specs=pl.BlockSpec(memory_space=pltpu.VMEM),
        scratch_shapes=[pltpu.VMEM((rows, 128), jnp.bfloat16)] * 3 + [
            D((n,)), D((n,)), D((n,)), D((max(gd - 1, 1), n)), D((n,)), D((n,)), D((n,)), D((max(gd - 1, 1), n))],
        compiler_params=pltpu.CompilerParams(collective_id=9, has_side_effects=True, vmem_limit_bytes=24 * 2**20),
        name="share",
    )(u)


def ring_gather(value, axis, group):
    size = lax.axis_size(axis)
    found = [value]
    for k in range(1, group):
        pairs = [(s, s // group * group + (s % group + k) % group) for s in range(size)]
        found.append(lax.ppermute(value, axis, pairs))
    return found


def neighbour_rows(block, width):
    count = lax.axis_size("narrow")
    up = [(i, i + 1) for i in range(count - 1)]
    down = [(i + 1, i) for i in range(count - 1)]
    before = lax.ppermute(block[-width:], "narrow", up)
    after = lax.ppermute(block[:width], "narrow", down)
    return jnp.concatenate([before, block, after], axis=0)


def per_device(
    weights, first_moment, second_moment, outer_momentum, noisy_input, target,
    text_tokens, text_mask, noise_level, aug_level, crop_size,
):
    length = first_moment.shape[1]
    wide_count = lax.axis_size("wide")
    narrow_count = lax.axis_size("narrow")
    gd = wide_count // GROUPS
    wide_pos = lax.axis_index("wide")
    narrow_pos = lax.axis_index("narrow")
    spot = wide_pos % gd
    width = HEADS * HEAD
    kv_block = 2 * width // narrow_count
    kv_len = TEXT_D * kv_block
    shard_len = weights.shape[0]
    rest_len = shard_len - kv_len

    own_kv_w = weights[:kv_len].astype(BF16).reshape(TEXT_D, kv_block)
    rest_all = lax.all_gather(weights[kv_len:].astype(BF16), "narrow", axis=0, tiled=True)
    rest_all = rest_all.reshape(-1, C)
    n_table = LEVELS * 2
    conv_w = rest_all[: 9 * C]
    table = rest_all[9 * C : 9 * C + n_table].reshape(LEVELS, 2 * C)
    at = 9 * C + n_table
    gains = rest_all[at : at + 4].astype(F32)
    query_w = rest_all[at + 4 : at + 4 + width].reshape(C, width)
    out_w = rest_all[at + 4 + width :]

    noisy = noisy_input[0]
    band, columns, _ = noisy.shape
    x = noisy.astype(F32).reshape(-1, C)
    group_of = jnp.arange(C, dtype=jnp.int32) // (C // NORM_GROUPS)
    same = (group_of[:, None] == group_of[None, :]).astype(F32)
    stat = lax.psum(jnp.stack([jnp.sum(x, axis=0), jnp.sum(x * x, axis=0)]), "narrow")
    stat = jnp.dot(stat, same, precision=lax.Precision.HIGHEST)
    count = H * W * C // NORM_GROUPS
    mean = stat[0] / count
    spread = lax.rsqrt(stat[1] / count - mean * mean + EPS_NORM)
    film = (table[noise_level[0]].astype(F32) + table[NOISE_LEVELS + aug_level[0]].astype(F32))
    gain = gains[0] * (1.0 + film[:C])
    offset = gains[1] * (1.0 + film[:C]) + film[C:]
    zero = jnp.zeros((C,), F32)
    vecs = jnp.stack([mean, spread, gain, offset, gains[2], gains[3], zero, zero])
    noisy_ext = neighbour_rows(noisy, 2)
    target_ext = neighbour_rows(target[0], 1)

    text_all = lax.all_gather(text_tokens[0], "narrow", axis=0, tiled=True)
    mask_all = lax.all_gather(text_mask[0], "narrow", axis=0, tiled=True)
    tok = text_all.shape[0]
    own_cols = dot(text_all, own_kv_w).astype(BF16)
    keyval = lax.all_gather(own_cols, "narrow", axis=1, tiled=True)
    key_ok = ((mask_all > 0) | (jnp.arange(tok) == 0)).astype(F32)[None, :]
    crop = crop_size[0]
    info = jnp.stack([narrow_pos * band, crop]).astype(jnp.int32)

    dconv_w, y_t, z_t, sums = run_main(
        info, noisy_ext, target_ext, vecs, conv_w, query_w, out_w, keyval, key_ok
    )

    half = width // kv_block
    both = jnp.concatenate([z_t, y_t], axis=1).reshape(C, narrow_count, -1).transpose(1, 0, 2)
    own_x = lax.psum_scatter(both, "narrow", scatter_dimension=0, tiled=False)
    is_key = narrow_pos < half
    scale = jnp.where(is_key, 1.0 / math.sqrt(HEAD), 1.0)
    own_x = own_x * scale
    head_block = kv_block // HEAD
    col0 = (narrow_pos % half) * kv_block
    right = jnp.where(
        is_key,
        lax.dynamic_slice_in_dim(query_w, col0, kv_block, axis=1),
        lax.dynamic_slice_in_dim(out_w, col0, kv_block, axis=0).T,
    )
    dkv, dproj = [], []
    for h in range(head_block):
        xs = own_x[:, h * tok : (h + 1) * tok]
        cols = slice(h * HEAD, (h + 1) * HEAD)
        dkv.append(dot(xs.astype(BF16), right[:, cols], TN))
        dproj.append(dot(xs.astype(BF16), own_cols[:, cols]))
    dkv = jnp.concatenate(dkv, axis=1)
    dproj = jnp.concatenate(dproj, axis=1)
    text_group = jnp.concatenate(ring_gather(text_all, "wide", gd), axis=0)
    dkv_group = jnp.concatenate(ring_gather(dkv, "wide", gd), axis=0)

    def group_sum(value):
        return sum(ring_gather(value, "wide", gd))

    dproj = lax.all_gather(group_sum(dproj), "narrow", axis=0, tiled=False)
    grad_query = jnp.concatenate([dproj[n] for n in range(half)], axis=1)
    grad_out = jnp.concatenate([dproj[half + n].T for n in range(half)], axis=0)
    sums = lax.psum(sums, "narrow")
    a, b = sums[0], sums[1]
    g_rows = jnp.stack([(1.0 + film[:C]) * b, (1.0 + film[:C]) * a, sums[2], sums[3]])
    dfilm = jnp.concatenate([gains[0] * b + gains[1] * a, a])
    small = jnp.concatenate([g_rows, dfilm.reshape(2, C)], axis=0)
    levels = jnp.stack([noise_level[0], NOISE_LEVELS + aug_level[0]])
    smalls = ring_gather(small, "wide", gd)
    level_list = ring_gather(levels, "wide", gd)
    grad_gains = sum(s[:4] for s in smalls)
    grad_table = jnp.zeros((LEVELS, 2 * C), F32)
    ids = jnp.arange(LEVELS, dtype=jnp.int32)[:, None]
    for s, lv in zip(smalls, level_list):
        d = s[4:].reshape(1, 2 * C)
        grad_table = grad_table + jnp.where(ids == lv[0], d, 0.0) + jnp.where(ids == lv[1], d, 0.0)
    grad_conv = group_sum(lax.psum(dconv_w, "narrow"))
    rest_grad = jnp.concatenate(
        [grad_conv.reshape(-1), grad_table.reshape(-1), grad_gains.reshape(-1),
         grad_query.reshape(-1), grad_out.reshape(-1)]
    )
    rest_sq = jnp.sum(rest_grad * rest_grad)
    rest_shard = lax.dynamic_slice_in_dim(rest_grad, narrow_pos * rest_len, rest_len)

    gram = dot(text_group, text_group, (((1,), (1,)), ((), ())))
    kv_sq = jnp.sum(dkv_group * jnp.dot(gram, dkv_group, precision=lax.Precision.HIGHEST))
    kv_sq = lax.psum(kv_sq, "narrow")
    crops = lax.all_gather(crop, "wide")
    counts = (jnp.minimum(crops, H) * jnp.minimum(crops, columns)).astype(F32)
    total = jnp.sum(counts)
    own_group = jnp.arange(wide_count) // gd == wide_pos // gd
    group_count = jnp.sum(jnp.where(own_group, counts, 0.0))
    loss = lax.psum(jnp.sum(sums[4]), "wide")
    norm = jnp.sqrt(kv_sq + rest_sq) / total
    clip = jnp.minimum(1.0, CLIP_NORM / norm) / total

    start = spot * length
    i0, j0 = start // kv_block, start % kv_block
    tiles = pl.cdiv(length + C, TROWS * C)
    text_rows = tiles * C
    padded = jnp.pad(text_group, ((0, 0), (0, text_rows + 1)))
    text_a = lax.dynamic_slice_in_dim(padded, i0, text_rows, axis=1)
    text_b = lax.dynamic_slice_in_dim(padded, i0 + 1, text_rows, axis=1)
    rolled = jnp.roll(dkv_group, -j0, axis=1)
    wrapped = jnp.arange(kv_block)[None, :] >= kv_block - j0
    dkv_ab = jnp.concatenate(
        [jnp.where(wrapped, 0.0, rolled), jnp.where(wrapped, rolled, 0.0)], axis=0
    ).astype(BF16)
    full = tiles * TROWS * C
    rest_line = jnp.concatenate([jnp.zeros((length,), F32), rest_shard, jnp.zeros((full,), F32)])
    rest_piece = lax.dynamic_slice_in_dim(
        rest_line, jnp.maximum(start - kv_len + length, 0), full
    ).reshape(-1, C)
    moment_one, moment_two, step = run_adam(
        jnp.stack([start % C]).astype(jnp.int32),
        jnp.stack([clip, INNER_RATE * group_count / total]),
        text_a, text_b, dkv_ab, rest_piece, first_moment, second_moment,
    )
    chunk = 320
    rows = pl.cdiv(length // C + 2, chunk) * chunk
    spread_steps = share(step, gd, rows, chunk, 2, 4)
    all_rows = shard_len // C
    averaged = 0.0
    for p in range(gd):
        r0 = p * length // C
        use = min(rows, all_rows - r0)
        averaged = averaged + jnp.pad(
            spread_steps[p, :use].astype(F32), ((r0, all_rows - r0 - use), (0, 0))
        )
    weights2 = weights.reshape(-1, C)
    outer2 = outer_momentum.reshape(-1, C)
    averaged = averaged + INNER_RATE * DECAY_RATE * weights2
    momentum_out = OUTER_MOMENTUM * outer2 + averaged
    new_weights = weights2 - OUTER_RATE * (averaged + OUTER_MOMENTUM * momentum_out)
    return (
        new_weights.reshape(-1), momentum_out.reshape(-1), moment_one, moment_two,
        loss[None], total[None],
    )


def solution(mesh):
    placed = (
        P("narrow"),
        P("narrow", "wide"),
        P("narrow", "wide"),
        P("narrow"),
        P("wide", "narrow", None, None),
        P("wide", "narrow", None, None),
        P("wide", "narrow", None),
        P("wide", "narrow"),
        P("wide"),
        P("wide"),
        P("wide"),
    )
    return jax.shard_map(
        per_device,
        mesh=mesh,
        in_specs=placed,
        out_specs=(P("narrow"), P("narrow"), P("narrow", "wide"), P("narrow", "wide"), P(), P()),
        check_vma=False,
    )
```

```python
import functools
import math

import jax
import jax.numpy as jnp
from jax import lax
from jax.experimental import pallas as pl
from jax.experimental.pallas import tpu as pltpu
from jax.sharding import PartitionSpec as P

MESH = pl.DeviceIdType.MESH
C = 128
NORM_GROUPS = 32
HEADS = 8
HEAD = 128
TEXT_D = 4096
H = 128
W = 128
NOISE_LEVELS = 1000
AUG_LEVELS = 24
LEVELS = NOISE_LEVELS + AUG_LEVELS
GROUPS = 4
STEP = 8


EPS_NORM = 1e-05
CLIP_NORM = 0.002
BETA_ONE = 0.9
BETA_TWO = 0.99
INNER_RATE = 0.01
DECAY_RATE = 0.01
ADAM_EPS = 1e-08
OUTER_RATE = 0.7
OUTER_MOMENTUM = 0.9

TN = (((0,), (0,)), ((), ()))
F32 = jnp.float32
BF16 = jnp.bfloat16
LOG2E = 1.4426950408889634
LN2 = 0.6931471805599453
NT = (((1,), (1,)), ((), ()))
TILE = 2


def dot(a, b, dims=(((1,), (0,)), ((), ()))):
    return lax.dot_general(a, b, dims, preferred_element_type=F32)


def two_parts(value):
    top = value.astype(BF16)
    return top, (value - top.astype(F32)).astype(BF16)


def shifted(value, by, keep):
    return jnp.where(keep, pltpu.roll(value, by, 0), 0.0)


def main_kernel(
    band, columns, height, heads,
    rest_rows, info, noisy, target, small, rest, keyval,
    blocks, dconv_w, packet, right,
    act3, diff3, m_cat, m_cat_t, n_cat, n_cat_t, conv_t, probs, dscore, wt3, y_t, z_t, sums,
    stage, query, out_w,
):
    tok, kv_block = keyval.shape[1:]
    width = heads * HEAD
    per_block = kv_block // HEAD
    row0 = info[0]
    crop = info[1]
    pix = TILE * columns
    first_gain, first_query = 9 * C + 2 * LEVELS, 9 * C + 2 * LEVELS + 4
    first_out = first_query + C * heads

    def take(first, count, place):
        while count:
            owner, local = divmod(first, rest_rows)
            use = min(count, rest_rows - local)
            a = local // 16 * 16
            b = (local + use + 15) // 16 * 16
            stage[0 : b - a, :] = rest[owner, a:b, :].astype(F32)
            place(stage[local - a : local - a + use, :], use)
            first, count = first + use, count - use

    def filler(ref):
        at = [0]

        def place(value, use):
            ref[at[0] : at[0] + use, :] = value
            at[0] += use

        return place

    gains = []
    take(first_gain, 4, lambda value, use: gains.append(value))
    gains = gains[0] if len(gains) == 1 else jnp.concatenate(gains, axis=0)
    take(first_query, C * heads, filler(query))
    take(first_out, width, filler(out_w))
    conv_w = rest.at[0]
    total = small[0] + small[1] + small[2] + small[3]
    lane_group = lax.broadcasted_iota(jnp.int32, (C, C), 0) // (C // NORM_GROUPS)
    same = (lane_group == lax.broadcasted_iota(jnp.int32, (C, C), 1) // (C // NORM_GROUPS)).astype(F32)
    stats = jnp.dot(total, same, precision=lax.Precision.HIGHEST, preferred_element_type=F32)
    count = height * columns * C // NORM_GROUPS
    mean = stats[0:1] * (1.0 / count)
    spread = lax.rsqrt(stats[1:2] * (1.0 / count) - mean * mean + EPS_NORM)
    film_scale, film_shift = 1.0 + total[2:3], total[3:4]
    gain = gains[0:1] * film_scale
    offset = gains[1:2] * film_scale + film_shift
    ln_gain, ln_offset = gains[2:3], gains[3:4]
    quarter = tok // 4
    masks = [small[owner, 4:5, 0:quarter] for owner in range(4)]
    ok = (jnp.concatenate(masks, axis=1) > 0.0) | (lax.broadcasted_iota(jnp.int32, (1, tok), 1) == 0)
    factor = LOG2E / math.sqrt(HEAD)
    for head in range(heads):
        cols = slice(head * HEAD, (head + 1) * HEAD)
        tcols = slice(head * tok, (head + 1) * tok)
        block, at = head // per_block, head % per_block * HEAD
        query_head = query[pl.ds(head, C, stride=heads), :].astype(BF16)
        out_head = out_w[cols, :].astype(BF16)
        m_head = dot(query_head, keyval[block, :, at : at + HEAD], NT) * factor

        @pl.when(info[2] == block)
        def _():
            right[:, at : at + HEAD] = query_head

        @pl.when(info[2] == block + heads // per_block)
        def _():
            right[:, at : at + HEAD] = out_w[cols, :].T.astype(BF16)

        top, rest = two_parts(m_head)
        m_cat[:C, tcols] = top
        m_cat[C:, tcols] = rest
        top, rest = two_parts(m_head.T)
        m_cat_t[tcols, :C] = top
        m_cat_t[tcols, C:] = rest
        n_head = dot(keyval[block + heads // per_block, :, at : at + HEAD], out_head)
        top, rest = two_parts(n_head)
        n_cat[tcols, :C] = top
        n_cat[tcols, C:] = rest
        top, rest = two_parts(n_head.T)
        n_cat_t[:C, tcols] = top
        n_cat_t[C:, tcols] = rest
    for tap in range(9):
        rows = slice(tap * C, (tap + 1) * C)
        wt3[rows, :] = conv_w[rows, :].astype(F32).T.astype(BF16)
    y_t[...] = jnp.zeros_like(y_t)
    z_t[...] = jnp.zeros_like(z_t)
    conv_t[...] = jnp.zeros_like(conv_t)
    sums[...] = jnp.zeros_like(sums)
    place = lax.broadcasted_iota(jnp.int32, (columns, C), 0)
    not_first, not_last = place > 0, place < columns - 1
    slope = spread * gain
    base = offset - mean * slope

    @pl.loop(0, band + 4)
    def _(r):
        scaled = noisy[r].astype(F32) * slope + base
        value = scaled * jax.nn.sigmoid(scaled)
        row = row0 + r - 2
        value = jnp.where(jnp.logical_and(row >= 0, row < height), value, 0.0)
        value = value.astype(BF16).astype(F32)
        act3[r, :, 0:C] = shifted(value, 1, not_first).astype(BF16)
        act3[r, :, C : 2 * C] = value.astype(BF16)
        act3[r, :, 2 * C : 3 * C] = shifted(value, columns - 1, not_last).astype(BF16)

    pix_row = lax.broadcasted_iota(jnp.int32, (pix, C), 0) // columns
    pix_col = lax.broadcasted_iota(jnp.int32, (pix, C), 0) % columns
    @pl.loop(0, (band + 2) // TILE)
    def _(t):
        q = t * TILE
        conv = noisy[pl.ds(q + 1, TILE)].astype(F32).reshape(pix, C)
        for dy in range(3):
            window = act3[pl.ds(q + dy, TILE)].reshape(pix, 3 * C)
            conv = conv + dot(window, conv_w[dy * 3 * C : (dy + 1) * 3 * C, :])
        centered = conv - jnp.mean(conv, axis=1, keepdims=True)
        rs = lax.rsqrt(jnp.mean(centered * centered, axis=1, keepdims=True) + EPS_NORM)
        xhat = centered * rs
        layered = xhat * ln_gain + ln_offset
        low = layered.astype(BF16)
        low2 = jnp.concatenate([low, low], axis=1)
        for head in range(heads):
            tcols = slice(head * tok, (head + 1) * tok)
            score = dot(low2, m_cat[:, tcols])
            score = jnp.where(ok, score, -1e30)
            e = jnp.exp2(score - jnp.max(score, axis=1, keepdims=True))
            p = e * (1.0 / jnp.sum(e, axis=1, keepdims=True))
            probs[:, tcols] = p.astype(BF16)
        mixed = dot(probs[...], n_cat[...])
        output = conv + mixed[:, :C] + mixed[:, C:]
        row = row0 + q - 1 + pix_row
        valid = (row >= 0) & (row < crop) & (pix_col < crop)
        err = jnp.where(valid, output - target[pl.ds(q, TILE)].astype(F32).reshape(pix, C), 0.0)
        own_row = q + pix_row
        own = (own_row >= 1) & (own_row <= band)
        err_own = jnp.where(own, err, 0.0)
        sums[4:5, :] += jnp.sum(err_own * err_own, axis=0, keepdims=True)
        dout = 2.0 * err
        dout_low = dout.astype(BF16)
        dout2 = jnp.concatenate([dout_low, dout_low], axis=1)
        for head in range(heads):
            tcols = slice(head * tok, (head + 1) * tok)
            dprob = dot(dout2, n_cat_t[:, tcols])
            p = probs[:, tcols].astype(F32)
            pd = p * dprob
            ds = pd - p * jnp.sum(pd, axis=1, keepdims=True)
            dscore[:, tcols] = ds.astype(BF16)
        dlay2 = dot(dscore[...], m_cat_t[...])
        dlay = (dlay2[:, :C] + dlay2[:, C:]) * LN2
        dlay_own = jnp.where(own, dlay, 0.0)
        sums[2:3, :] += jnp.sum(dlay_own * xhat, axis=0, keepdims=True)
        sums[3:4, :] += jnp.sum(dlay_own, axis=0, keepdims=True)
        dxh = dlay * ln_gain
        dconv = dout + rs * (
            dxh
            - jnp.mean(dxh, axis=1, keepdims=True)
            - xhat * jnp.mean(dxh * xhat, axis=1, keepdims=True)
        )
        dout_t = (2.0 * err_own).T.astype(BF16)
        lay_t = jnp.where(own, layered, 0.0).T.astype(BF16)
        y_t[...] += dot(dout_t, probs[...])
        z_t[...] += dot(lay_t, dscore[...])
        dconv_t = jnp.where(own, dconv, 0.0).T.astype(BF16)
        for dy in range(3):
            window = act3[pl.ds(q + dy, TILE)].reshape(pix, 3 * C)
            conv_t[:, dy * 3 * C : (dy + 1) * 3 * C] += dot(dconv_t, window)
        for k in range(TILE):
            one = dconv[k * columns : (k + 1) * columns]
            diff3[q + k, :, 0:C] = shifted(one, columns - 1, not_last).astype(BF16)
            diff3[q + k, :, C : 2 * C] = one.astype(BF16)
            diff3[q + k, :, 2 * C : 3 * C] = shifted(one, 1, not_first).astype(BF16)

    @pl.loop(0, band // TILE)
    def _(t):
        r = t * TILE
        grad = jnp.zeros((pix, C), F32)
        for dy in range(3):
            window = diff3[pl.ds(r + 2 - dy, TILE)].reshape(pix, 3 * C)
            grad = grad + dot(window, wt3[dy * 3 * C : (dy + 1) * 3 * C, :])
        x = noisy[pl.ds(r + 2, TILE)].astype(F32).reshape(pix, C)
        scaled = x * slope + base
        sig = jax.nn.sigmoid(scaled)
        ds = grad * (sig * (1.0 + scaled * (1.0 - sig)))
        sums[0:1, :] += jnp.sum(ds, axis=0, keepdims=True)
        sums[1:2, :] += jnp.sum(ds * ((x - mean) * spread), axis=0, keepdims=True)

    share_rows = dconv_w.shape[1]
    full = conv_t[...].T
    for owner in range(4):
        dconv_w[owner] = full[owner * share_rows : (owner + 1) * share_rows].astype(BF16)
        part = z_t if owner < 2 else y_t
        at = owner % 2 * per_block * tok
        blocks[owner] = part[:, at : at + per_block * tok].astype(BF16)
    a, b = sums[0:1], sums[1:2]
    packet[0:1] = film_scale * b
    packet[1:2] = film_scale * a
    packet[2:4] = sums[2:4]
    packet[4:5] = gains[0:1] * b + gains[1:2] * a
    packet[5:6] = a
    packet[6:7] = sums[4:5]
    lane = lax.broadcasted_iota(jnp.int32, (1, C), 1)
    facts = jnp.zeros((1, C), F32)
    for k, fact in enumerate((info[3], info[4], crop)):
        facts = jnp.where(lane == k, fact.astype(F32), facts)
    packet[7:8] = jnp.where(row0 == 0, facts, 0.0)


def run_main(info, noisy_ext, target_ext, small, rest, keyval, rest_rows):
    band = target_ext.shape[0] - 2
    columns = target_ext.shape[1]
    tok, kv_block = keyval.shape[1:]
    vmem = pl.BlockSpec(memory_space=pltpu.VMEM)
    pix = TILE * columns
    assert 9 * C <= rest_rows and kv_block % HEAD == 0 and HEAD == C
    return pl.pallas_call(
        functools.partial(main_kernel, band, columns, H, HEADS, rest_rows),
        out_shape=(
            jax.ShapeDtypeStruct((4, C, kv_block // HEAD * tok), BF16),
            jax.ShapeDtypeStruct((4, 9 * C // 4, C), BF16),
            jax.ShapeDtypeStruct((8, C), F32),
            jax.ShapeDtypeStruct((C, kv_block), BF16),
        ),
        in_specs=[pl.BlockSpec(memory_space=pltpu.SMEM)] + [vmem] * 5,
        out_specs=(vmem,) * 4,
        scratch_shapes=[
            pltpu.VMEM((band + 4, columns, 3 * C), BF16),
            pltpu.VMEM((band + 2, columns, 3 * C), BF16),
            pltpu.VMEM((2 * C, HEADS * tok), BF16),
            pltpu.VMEM((HEADS * tok, 2 * C), BF16),
            pltpu.VMEM((HEADS * tok, 2 * C), BF16),
            pltpu.VMEM((2 * C, HEADS * tok), BF16),
            pltpu.VMEM((C, 9 * C), F32),
            pltpu.VMEM((pix, HEADS * tok), BF16),
            pltpu.VMEM((pix, HEADS * tok), BF16),
            pltpu.VMEM((9 * C, C), BF16),
            pltpu.VMEM((C, HEADS * tok), F32),
            pltpu.VMEM((C, HEADS * tok), F32),
            pltpu.VMEM((8, C), F32),
            pltpu.VMEM((rest.shape[1], C), F32),
            pltpu.VMEM((C * HEADS, C), F32),
            pltpu.VMEM((HEADS * HEAD, C), F32),
        ],
        compiler_params=pltpu.CompilerParams(vmem_limit_bytes=40 * 2**20),
        name="main",
    )(info, noisy_ext, target_ext, small, rest, keyval)


def cross_ids():
    n = lax.axis_index("narrow")
    mate = n + 1 - 2 * lax.rem(n, 2)
    across = lax.rem(n + 2, 4)
    corner = lax.rem(mate + 2, 4)
    return n, mate, across, corner


def to_narrow(src, dst, send_sem, recv_sem, device):
    return pltpu.make_async_remote_copy(
        src_ref=src, dst_ref=dst, send_sem=send_sem, recv_sem=recv_sem,
        device_id={"narrow": device}, device_id_type=MESH,
    )


class Gather:
    def __init__(self, view, sems, ids):
        self.view, self.sems = view, sems
        self.n, self.mate, self.across, self.corner = ids

    def _copy(self, block, slot, device):
        ref = self.view(block)
        return to_narrow(ref, ref, self.sems.at[0, slot], self.sems.at[1, slot], device)

    def start(self):
        self._copy(self.n, 1, self.across).start()
        self._copy(self.n, 0, self.mate).start()

    def relay(self):
        self._copy(self.across, 1, self.across).wait_recv()
        self._copy(self.across, 2, self.mate).start()

    def wait(self):
        self._copy(self.mate, 0, self.mate).wait_recv()
        self._copy(self.corner, 2, self.mate).wait_recv()

    def drain(self):
        self._copy(self.n, 1, self.across).wait_send()
        self._copy(self.n, 0, self.mate).wait_send()
        self._copy(self.across, 2, self.mate).wait_send()


def rest_needs(rest_rows):
    first, last = 9 * C, 9 * C + 2 * LEVELS
    needs = []
    for owner in range(4):
        lo, hi = owner * rest_rows, (owner + 1) * rest_rows
        keep = [r for r in ((lo, min(hi, first)), (max(lo, last), hi)) if r[0] < r[1]]
        assert len(keep) <= 1
        if keep:
            a, b = keep[0][0] - lo, keep[0][1] - lo
            needs.append((a // 16 * 16, (b + 15) // 16 * 16))
        else:
            needs.append(None)
    return needs


KPARTS = 4
WPARTS = 8


def front_kernel(
    kv_rows, rest_rows, noise_level, aug_level, weights, noisy, target, text, mask,
    noisy_ext, target_ext, text_all, rest_all, keyval, own_kv, small,
    wide_f32, wide_bf, rest_f32, acc,
    w_sem, in_sem, text_sem, rest_sem, kv_sem, small_sem, halo_sem,
):
    ids = cross_ids()
    n, mate, across, corner = ids
    barrier = pltpu.get_barrier_semaphore()
    for other in (mate, across, corner):
        pl.semaphore_signal(barrier, inc=1, device_id={"narrow": other}, device_id_type=MESH)
    band = noisy.shape[1]
    tokens, depth = text.shape[1:]
    in_text = pltpu.make_async_copy(text.at[0], text_all.at[n], in_sem.at[0])
    in_text.start()
    in_rest = pltpu.make_async_copy(
        weights.at[pl.ds(kv_rows, rest_rows)], rest_f32.at[pl.ds(0, rest_rows)], in_sem.at[1]
    )
    in_rest.start()
    in_noisy = pltpu.make_async_copy(noisy.at[0], noisy_ext.at[pl.ds(2, band)], in_sem.at[2])
    in_noisy.start()
    w_step = kv_rows // WPARTS
    in_w = [
        pltpu.make_async_copy(
            weights.at[pl.ds(k * w_step, w_step)], wide_f32.at[pl.ds(k * w_step, w_step)], w_sem.at[k]
        )
        for k in range(WPARTS)
    ]
    for copy in in_w:
        copy.start()
    in_target = pltpu.make_async_copy(target.at[0], target_ext.at[pl.ds(1, band)], in_sem.at[3])
    in_target.start()
    pl.semaphore_wait(barrier, 3)

    k_step = depth // KPARTS
    texts = [
        Gather(
            lambda b, k=k: text_all.at[b, :, pl.ds(k * k_step, k_step)], text_sem.at[k], ids
        )
        for k in range(KPARTS)
    ]
    in_text.wait()
    for part in texts:
        part.start()

    in_rest.wait()
    for k in range(2):
        row_sum = jnp.zeros((1, C), F32)
        for level in (noise_level[0], NOISE_LEVELS + aug_level[0]):
            row = 9 * C + 2 * level + k - n * rest_rows
            found = rest_f32[pl.ds(jnp.clip(row, 0, rest_rows - 1), 1), :]
            found = found.astype(BF16).astype(F32)
            row_sum = row_sum + jnp.where((row >= 0) & (row < rest_rows), found, 0.0)
        small[n, 2 + k : 3 + k, :] = row_sum
    small[n, 4:8, :] = jnp.zeros((4, C), F32)
    small[n, 4:5, 0:tokens] = mask[...].astype(F32)
    in_noisy.wait()

    def add_row(r, sums):
        x = noisy_ext[r + 2].astype(F32)
        return (
            sums[0] + jnp.sum(x.reshape(-1, 8, C), axis=0),
            sums[1] + jnp.sum((x * x).reshape(-1, 8, C), axis=0),
        )

    zero = jnp.zeros((8, C), F32)
    one, two = lax.fori_loop(0, band, add_row, (zero, zero))
    small[n, 0:1, :] = jnp.sum(one, axis=0, keepdims=True)
    small[n, 1:2, :] = jnp.sum(two, axis=0, keepdims=True)
    others = (mate, across, corner)

    def small_copy(slot, block):
        return to_narrow(
            small.at[block], small.at[block], small_sem.at[0, slot], small_sem.at[1, slot], others[slot]
        )

    for slot in range(3):
        small_copy(slot, n).start()

    in_target.wait()
    up = jnp.maximum(n - 1, 0)
    down = jnp.minimum(n + 1, 3)
    noisy_up = to_narrow(
        noisy_ext.at[pl.ds(2, 2)], noisy_ext.at[pl.ds(band + 2, 2)], halo_sem.at[0, 0], halo_sem.at[1, 0], up
    )
    noisy_down = to_narrow(
        noisy_ext.at[pl.ds(band, 2)], noisy_ext.at[pl.ds(0, 2)], halo_sem.at[0, 1], halo_sem.at[1, 1], down
    )
    target_up = to_narrow(
        target_ext.at[pl.ds(1, 1)], target_ext.at[pl.ds(band + 1, 1)], halo_sem.at[0, 2], halo_sem.at[1, 2], up
    )
    target_down = to_narrow(
        target_ext.at[pl.ds(band, 1)], target_ext.at[pl.ds(0, 1)], halo_sem.at[0, 3], halo_sem.at[1, 3], down
    )

    @pl.when(n > 0)
    def _():
        noisy_up.start()
        target_up.start()

    @pl.when(n < 3)
    def _():
        noisy_down.start()
        target_down.start()

    @pl.when(n == 0)
    def _():
        noisy_ext[0:2] = jnp.zeros((2,) + noisy_ext.shape[1:], BF16)
        target_ext[0:1] = jnp.zeros((1,) + target_ext.shape[1:], BF16)

    @pl.when(n == 3)
    def _():
        noisy_ext[band + 2 : band + 4] = jnp.zeros((2,) + noisy_ext.shape[1:], BF16)
        target_ext[band + 1 : band + 2] = jnp.zeros((1,) + target_ext.shape[1:], BF16)

    needs = rest_needs(rest_rows)
    rest_all[n] = rest_f32[...].astype(BF16)

    def rest_copy(owner, slot, device):
        a, b = needs[owner]
        ref = rest_all.at[owner, pl.ds(a, b - a)]
        return to_narrow(ref, ref, rest_sem.at[0, slot, owner], rest_sem.at[1, slot, owner], device)

    for owner in range(4):
        if needs[owner] is not None:
            @pl.when(n == owner)
            def _():
                rest_copy(owner, 1, across).start()
                rest_copy(owner, 0, mate).start()

    parts = wide_bf.shape[1] // C
    rows = 256
    for k in range(WPARTS):
        in_w[k].wait()

        @pl.loop(k * w_step // parts // rows, (k + 1) * w_step // parts // rows)
        def _(i):
            for j in range(parts):
                wide_bf[pl.ds(pl.multiple_of(i * rows, rows), rows), j * C : (j + 1) * C] = wide_f32[
                    pl.ds(i * rows * parts + j, rows, stride=parts), :
                ].astype(BF16)

    acc[...] = jnp.zeros_like(acc)
    for k in range(KPARTS):
        texts[k].relay()
    for k in range(KPARTS):
        texts[k].wait()

        @pl.loop(0, k_step // 512)
        def _(i):
            at = pl.ds(pl.multiple_of(k * k_step + i * 512, 512), 512)
            acc[...] += dot(text_all[:, :, at].reshape(4 * tokens, 512), wide_bf[at, :])

    keyval[n] = acc[...].astype(BF16)
    own_kv[...] = acc[...].astype(BF16)
    keys = Gather(lambda b: keyval.at[b], kv_sem, ids)
    keys.start()

    for owner in range(4):
        if needs[owner] is not None:
            @pl.when(across == owner)
            def _():
                rest_copy(owner, 1, across).wait_recv()
                rest_copy(owner, 2, mate).start()

    keys.relay()
    for slot, block in ((0, mate), (1, across), (2, corner)):
        small_copy(slot, block).wait_recv()
        small_copy(slot, n).wait_send()

    @pl.when(n > 0)
    def _():
        noisy_down.wait_recv()
        target_down.wait_recv()
        noisy_up.wait_send()
        target_up.wait_send()

    @pl.when(n < 3)
    def _():
        noisy_up.wait_recv()
        target_up.wait_recv()
        noisy_down.wait_send()
        target_down.wait_send()

    for owner in range(4):
        if needs[owner] is not None:
            @pl.when(mate == owner)
            def _():
                rest_copy(owner, 0, mate).wait_recv()

            @pl.when(corner == owner)
            def _():
                rest_copy(owner, 2, mate).wait_recv()

            @pl.when(n == owner)
            def _():
                rest_copy(owner, 1, across).wait_send()
                rest_copy(owner, 0, mate).wait_send()

            @pl.when(across == owner)
            def _():
                rest_copy(owner, 2, mate).wait_send()

    keys.wait()
    keys.drain()
    for part in texts:
        part.drain()


def run_front(noise_level, aug_level, weights2, noisy, target, text, mask):
    _, band, columns, _ = noisy.shape
    _, tokens, depth = text.shape
    kv_block = 2 * HEADS * HEAD // 4
    kv_rows = depth * kv_block // C
    rest_rows = weights2.shape[0] - kv_rows
    rest_pad = (rest_rows + 15) // 16 * 16
    vmem = pl.BlockSpec(memory_space=pltpu.VMEM)
    smem = pl.BlockSpec(memory_space=pltpu.SMEM)
    hbm = pl.BlockSpec(memory_space=pl.ANY)
    D = pltpu.SemaphoreType.DMA
    return pl.pallas_call(
        functools.partial(front_kernel, kv_rows, rest_rows),
        out_shape=(
            jax.ShapeDtypeStruct((band + 4, columns, C), BF16),
            jax.ShapeDtypeStruct((band + 2, columns, C), BF16),
            jax.ShapeDtypeStruct((4, tokens, depth), BF16),
            jax.ShapeDtypeStruct((4, rest_pad, C), BF16),
            jax.ShapeDtypeStruct((4, 4 * tokens, kv_block), BF16),
            jax.ShapeDtypeStruct((4 * tokens, kv_block), BF16),
            jax.ShapeDtypeStruct((4, 8, C), F32),
        ),
        in_specs=[smem, smem, hbm, hbm, hbm, hbm, vmem],
        out_specs=(vmem,) * 7,
        scratch_shapes=[
            pltpu.VMEM((kv_rows, C), F32),
            pltpu.VMEM((depth, kv_block), BF16),
            pltpu.VMEM((rest_pad, C), F32),
            pltpu.VMEM((4 * tokens, kv_block), F32),
            D((WPARTS,)), D((4,)), D((KPARTS, 2, 3)), D((2, 3, 4)), D((2, 3)), D((2, 3)), D((2, 4)),
        ],
        compiler_params=pltpu.CompilerParams(
            collective_id=1, has_side_effects=True, vmem_limit_bytes=36 * 2**20
        ),
        name="front",
    )(noise_level, aug_level, weights2, noisy, target, text, mask)


def mid_kernel(
    gd, height, columns, blocks, conv, packet, right, *refs,
):
    kvs, texts, refs = refs[:gd], refs[gd : 2 * gd], refs[2 * gd :]
    (
        dkv_all, conv_all, t_all, small_all, scal,
        near_b, near_c, sum_b, sum_c, far_b, far_c, own_b, own_c, group_b, group_c,
        packets, wides, t_own, t_send, c_send, gram, norms, conv_sum,
        near_sem, far_sem, group_sem, packet_sem, wide_sem, norm_sem, give_sem,
    ) = refs
    ids = cross_ids()
    n, mate, across, corner = ids
    others = (mate, across, corner)
    wide_count = wides.shape[0]
    wide = lax.axis_index("wide")
    group = wide // gd
    spot = lax.rem(wide, gd)
    tok, kv_block = kvs[0].shape
    heads = kv_block // HEAD
    barrier = pltpu.get_barrier_semaphore()
    for other in others:
        pl.semaphore_signal(barrier, inc=1, device_id={"narrow": other}, device_id_type=MESH)

    @pl.loop(1, wide_count)
    def _(k):
        pl.semaphore_signal(
            barrier, inc=1, device_id={"wide": lax.rem(wide + k, wide_count)}, device_id_type=MESH
        )

    packets[n] = packet[...]
    pl.semaphore_wait(barrier, 3 + wide_count - 1)

    def near(slot, which):
        owner = corner if slot == 0 else mate
        src, dst = ((blocks, near_b), (conv, near_c))[which]
        return to_narrow(
            src.at[owner], dst.at[slot], near_sem.at[0, slot, which], near_sem.at[1, slot, which], mate
        )

    for slot in range(2):
        for which in range(2):
            near(slot, which).start()

    def packet_copy(slot, block):
        return to_narrow(
            packets.at[block], packets.at[block],
            packet_sem.at[0, slot], packet_sem.at[1, slot], others[slot],
        )

    for slot in range(3):
        packet_copy(slot, n).start()

    def far(which):
        src, dst = ((sum_b, far_b), (sum_c, far_c))[which]
        return to_narrow(src, dst, far_sem.at[0, which], far_sem.at[1, which], across)

    near(0, 0).wait_recv()
    sum_b[...] = (blocks[across].astype(F32) + near_b[0].astype(F32)).astype(BF16)
    far(0).start()
    near(0, 1).wait_recv()
    sum_c[...] = (conv[across].astype(F32) + near_c[0].astype(F32)).astype(BF16)
    far(1).start()

    for slot, block in enumerate(others):
        packet_copy(slot, block).wait_recv()
    item = packets[0] + packets[1] + packets[2] + packets[3]
    wides[wide] = item

    def wide_copy(k, block):
        return pltpu.make_async_remote_copy(
            src_ref=wides.at[block], dst_ref=wides.at[block],
            send_sem=wide_sem.at[0, k - 1], recv_sem=wide_sem.at[1, k - 1],
            device_id={"wide": lax.rem(wide + k, wide_count)}, device_id_type=MESH,
        )

    @pl.loop(1, wide_count)
    def _(k):
        wide_copy(k, wide).start()

    depth = texts[0].shape[-1]
    gram[...] = jnp.zeros_like(gram)

    @pl.loop(0, depth // 1024)
    def _(i):
        at = pl.ds(pl.multiple_of(i * 1024, 1024), 1024)
        for a in range(gd):
            left = texts[a][:, :, at].reshape(tok, 1024)
            for b in range(a, gd):
                part = dot(left, texts[b][:, :, at].reshape(tok, 1024), NT)
                gram[a * tok : (a + 1) * tok, b * tok : (b + 1) * tok] += part

    near(1, 0).wait_recv()
    near(1, 1).wait_recv()
    far(0).wait_recv()
    own_b[...] = (
        blocks[n].astype(F32) + near_b[1].astype(F32) + far_b[...].astype(F32)
    ).astype(BF16)

    def group_copy(k, which):
        src, dst = ((own_b, group_b), (own_c, group_c))[which]
        return pltpu.make_async_remote_copy(
            src_ref=src, dst_ref=dst.at[k - 1],
            send_sem=group_sem.at[0, which, k - 1], recv_sem=group_sem.at[1, which, k - 1],
            device_id={"wide": group * gd + lax.rem(spot + k, gd)}, device_id_type=MESH,
        )

    for k in range(1, gd):
        group_copy(k, 0).start()
    far(1).wait_recv()
    conv_sum[...] = conv[n].astype(F32) + near_c[1].astype(F32) + far_c[...].astype(F32)
    own_c[...] = conv_sum[...].astype(BF16)
    for k in range(1, gd):
        group_copy(k, 1).start()

    scale = jnp.where(n < 2, 1.0 / math.sqrt(HEAD), 1.0)

    def project(k, value):
        for h in range(heads):
            cols = slice(h * HEAD, (h + 1) * HEAD)
            part = value[:, h * tok : (h + 1) * tok]
            dkv_all[k * tok : (k + 1) * tok, cols] = (dot(part, right[:, cols], TN) * scale).astype(BF16)
            term = dot(part, kvs[k][:, cols]) * scale
            t_own[:, cols] = term if k == 0 else t_own[:, cols] + term

    project(0, own_b[...])
    for k in range(1, gd):
        group_copy(k, 0).wait_recv()
        project(k, group_b[k - 1])
        group_copy(k, 1).wait_recv()
        conv_sum[...] += group_c[k - 1].astype(F32)
    t_send[...] = t_own[...].astype(BF16)
    c_send[...] = conv_sum[...].astype(BF16)

    q_rows = 96
    q_from = 80

    def give_conv(src_n):
        return to_narrow(c_send, conv_all.at[src_n], give_sem.at[0, 0], give_sem.at[1, src_n], 0)

    def give_head(src_n):
        at = pl.ds(0, q_rows)
        return to_narrow(t_send.at[at], t_all.at[src_n, at], give_sem.at[0, 1], give_sem.at[1, src_n], 2)

    def give_tail(src_n):
        at = pl.ds(q_from, C - q_from)
        return to_narrow(t_send.at[at], t_all.at[src_n, at], give_sem.at[0, 2], give_sem.at[1, src_n], 3)

    def give_values():
        return to_narrow(t_send, t_all.at[2], give_sem.at[0, 1], give_sem.at[1, 2], 3)

    for k in range(4):
        @pl.when(n == k)
        def _():
            if k < 2:
                give_head(k).start()
                give_tail(k).start()
            if k == 2:
                give_values().start()
            if k > 0:
                give_conv(k).start()
            else:
                conv_all[0] = c_send[...]
            if k == 3:
                t_all[3] = t_send[...]

    @pl.loop(1, wide_count)
    def _(k):
        wide_copy(k, lax.rem(wide + wide_count - k, wide_count)).wait_recv()

    sq = jnp.sum(t_own[...] * t_own[...]) + jnp.sum(conv_sum[...] * conv_sum[...])
    for a in range(gd):
        da = dkv_all[a * tok : (a + 1) * tok, :]
        for b in range(a, gd):
            db = dkv_all[b * tok : (b + 1) * tok, :]
            top, low = two_parts(gram[a * tok : (a + 1) * tok, b * tok : (b + 1) * tok])
            part = jnp.sum(da.astype(F32) * (dot(top, db) + dot(low, db)))
            sq = sq + (part if a == b else 2.0 * part)
    gains = jnp.zeros((4, C), F32)
    shared = jnp.zeros((1, C), F32)
    for a in range(gd):
        mine = wides[group * gd + a]
        small_all[a] = mine
        gains = gains + mine[0:4]
        for b in range(gd):
            his = wides[group * gd + b]
            same = (mine[7:8, 0:1] == his[7:8, 0:1]).astype(F32) + (mine[7:8, 1:2] == his[7:8, 1:2]).astype(F32)
            shared = shared + same * (mine[4:5] * his[4:5] + mine[5:6] * his[5:6])
    shared_sq = jnp.sum(gains * gains) + jnp.sum(shared)
    norms[n] = jnp.full((8, C), sq + jnp.where(n == 0, shared_sq, 0.0), F32)

    def norm_copy(slot, block):
        return to_narrow(
            norms.at[block], norms.at[block], norm_sem.at[0, slot], norm_sem.at[1, slot], others[slot]
        )

    for slot in range(3):
        norm_copy(slot, n).start()

    def tally(k, found):
        there = wides[k]
        crop = there[7:8, 2:3]
        pixels = jnp.minimum(crop, float(height)) * jnp.minimum(crop, float(columns))
        mine = jnp.where(k // gd == group, pixels, 0.0)
        return found[0] + pixels, found[1] + mine, found[2] + jnp.sum(there[6:7], axis=1, keepdims=True)

    none = jnp.zeros((1, 1), F32)
    total, own_count, loss = lax.fori_loop(0, wide_count, tally, (none, none, none))
    for slot, block in enumerate(others):
        norm_copy(slot, block).wait_recv()
    squares = norms[0, 0:1] + norms[1, 0:1] + norms[2, 0:1] + norms[3, 0:1]
    norm = jnp.sqrt(squares) / total
    scal[0:1] = jnp.minimum(1.0, CLIP_NORM / norm) / total
    scal[1:2] = jnp.broadcast_to(INNER_RATE * own_count / total, (1, C))
    scal[2:3] = jnp.broadcast_to(loss, (1, C))
    scal[3:4] = jnp.broadcast_to(total, (1, C))
    scal[4:8] = jnp.zeros((4, C), F32)

    for k in range(4):
        @pl.when(n == k)
        def _():
            if k < 2:
                give_head(k).wait_send()
                give_tail(k).wait_send()
            if k == 2:
                give_values().wait_send()
                give_head(0).wait_recv()
                give_head(1).wait_recv()
            if k == 3:
                give_tail(0).wait_recv()
                give_tail(1).wait_recv()
                give_values().wait_recv()
            if k > 0:
                give_conv(k).wait_send()
            else:
                for j in range(1, 4):
                    give_conv(j).wait_recv()
    for slot in range(2):
        for which in range(2):
            near(slot, which).wait_send()
    for which in range(2):
        far(which).wait_send()
        for k in range(1, gd):
            group_copy(k, which).wait_send()
    for slot in range(3):
        packet_copy(slot, n).wait_send()
        norm_copy(slot, n).wait_send()

    @pl.loop(1, wide_count)
    def _(k):
        wide_copy(k, wide).wait_send()


def run_mid(gd, wide_count, blocks, conv, packet, right, kvs, texts):
    tok, kv_block = kvs[0].shape
    vmem = pl.BlockSpec(memory_space=pltpu.VMEM)
    D = pltpu.SemaphoreType.DMA
    bshape, cshape = blocks.shape[1:], conv.shape[1:]
    V = pltpu.VMEM
    few = max(gd - 1, 1)
    return pl.pallas_call(
        functools.partial(mid_kernel, gd, H, W),
        out_shape=(
            jax.ShapeDtypeStruct((gd * tok, kv_block), BF16),
            jax.ShapeDtypeStruct((4,) + cshape, BF16),
            jax.ShapeDtypeStruct((4, C, kv_block), BF16),
            jax.ShapeDtypeStruct((gd, 8, C), F32),
            jax.ShapeDtypeStruct((8, C), F32),
        ),
        in_specs=[vmem] * (4 + 2 * gd),
        out_specs=(vmem,) * 5,
        scratch_shapes=[
            V((2,) + bshape, BF16), V((2,) + cshape, BF16), V(bshape, BF16), V(cshape, BF16),
            V(bshape, BF16), V(cshape, BF16), V(bshape, BF16), V(cshape, BF16),
            V((few,) + bshape, BF16), V((few,) + cshape, BF16),
            V((4, 8, C), F32), V((wide_count, 8, C), F32),
            V((C, kv_block), F32), V((C, kv_block), BF16), V(cshape, BF16),
            V((gd * tok, gd * tok), F32), V((4, 8, C), F32), V(cshape, F32),
            D((2, 2, 2)), D((2, 2)), D((2, 2, few)), D((2, 3)), D((2, wide_count)), D((2, 3)), D((2, 4)),
        ],
        compiler_params=pltpu.CompilerParams(
            collective_id=2, has_side_effects=True, vmem_limit_bytes=48 * 2**20
        ),
        name="mid",
    )(blocks, conv, packet, right, *kvs, *texts)


TROWS = 512


def adam_kernel(
    gd, length, kv_rows, rest_rows, where, *refs,
):
    firsts, texts, refs = refs[:gd], refs[gd : 2 * gd], refs[2 * gd :]
    (
        dkv, conv, t_all, small, scal, first, second, first_out, second_out, step_out,
        nat, rest, shift, carry,
    ) = refs
    s = pl.program_id(0)
    tiles = pl.num_programs(0) - 1
    tok = dkv.shape[0] // gd
    n, lane0, row_off, row_shift, block0 = (where[k] for k in range(5))
    kv_blocks = kv_rows // TROWS
    parts = TROWS // C

    def natural(text_refs, block):
        @pl.when(block < kv_blocks)
        def _():
            text = jnp.concatenate([ref[...].reshape(tok, C) for ref in text_refs], axis=0)
            grad = dot(text, dkv[...], TN)
            for j in range(parts):
                nat[pl.ds(TROWS + j, C, stride=parts), :] = grad[:, j * C : (j + 1) * C]

        @pl.when(block >= kv_blocks)
        def _():
            at = jnp.minimum(block - kv_blocks, rest.shape[0] // TROWS - 1) * TROWS
            nat[TROWS : 2 * TROWS, :] = rest[pl.ds(pl.multiple_of(at, TROWS), TROWS), :]

    @pl.when(s == 0)
    def _():
        rest[...] = jnp.zeros_like(rest)
        carry[...] = jnp.zeros_like(carry)
        shift[...] = jnp.zeros_like(shift)
        first_table, first_gain = 9 * C, 9 * C + 2 * LEVELS
        first_query = first_gain + 4
        first_out = first_query + C * HEADS
        quarter = conv.shape[1]
        width = dkv.shape[1]
        heads = width // HEAD
        for owner in range(4):
            lo, hi = owner * rest_rows, (owner + 1) * rest_rows

            @pl.when(n == owner)
            def _():
                for k in range(4):
                    a, b = max(lo, k * quarter), min(hi, (k + 1) * quarter)
                    if a < b:
                        assert (a, b) == (k * quarter, (k + 1) * quarter)
                        rest[a - lo : b - lo, :] = conv[k].astype(F32)
                a, b = max(lo, first_query), min(hi, first_out)
                if a < b:
                    for h in range(HEADS):
                        c0 = max(0, -(-(a - first_query - h) // HEADS))
                        c1 = min(C, -(-(b - first_query - h) // HEADS))
                        cols = slice(h % heads * HEAD, h % heads * HEAD + HEAD)
                        c_lo, c_hi = c0 // 16 * 16, (c1 + 15) // 16 * 16
                        value = t_all[h // heads, c_lo:c_hi, cols].astype(F32)
                        start = first_query + c0 * HEADS + h - lo
                        rest[pl.ds(start, c1 - c0, stride=HEADS), :] = value[c0 - c_lo : c1 - c_lo]
                for h in range(HEADS):
                    a, b = first_out + h * HEAD, first_out + (h + 1) * HEAD
                    if lo <= a and b <= hi:
                        cols = slice(h % heads * HEAD, h % heads * HEAD + HEAD)
                        rest[a - lo : b - lo, :] = t_all[2 + h // heads, :, cols].astype(F32).T
                    else:
                        assert b <= lo or hi <= a
                if lo <= first_gain and first_gain + 4 <= hi:
                    total = small[0, 0:4]
                    for k in range(1, gd):
                        total = total + small[k, 0:4]
                    rest[first_gain - lo : first_gain + 4 - lo, :] = total

        for k in range(2 * gd):
            for half in range(2):
                row = first_table + 2 * where[5 + k] + half - n * rest_rows

                @pl.when((row >= 0) & (row < rest_rows))
                def _():
                    rest[pl.ds(row, 1), :] += small[k // 2, 4 + half : 5 + half]

        natural(firsts, block0)

    nat[0:TROWS, :] = nat[TROWS : 2 * TROWS, :]
    natural(texts, block0 + s + 1)

    lane = lax.broadcasted_iota(jnp.int32, (TROWS, C), 1)
    row = lax.broadcasted_iota(jnp.int32, (TROWS, C), 0)
    same_row = nat[pl.ds(row_off, TROWS), :]
    next_row = nat[pl.ds(row_off + 1, TROWS), :]
    g = pltpu.roll(jnp.where(lane >= lane0, same_row, next_row), C - lane0, 1) * scal[0:1]
    one = BETA_ONE * first.reshape(TROWS, C)[...] + (1.0 - BETA_ONE) * g
    two = BETA_TWO * second.reshape(TROWS, C)[...] + (1.0 - BETA_TWO) * g * g
    first_out.reshape(TROWS, C)[...] = one
    second_out.reshape(TROWS, C)[...] = two
    fixed_one = one * (scal[1:2] * (1.0 / (1.0 - BETA_ONE**STEP)))
    fixed_two = two * (1.0 / (1.0 - BETA_TWO**STEP))
    step = fixed_one / (jnp.sqrt(fixed_two) + ADAM_EPS)
    step = jnp.where((s * TROWS + row) * C + lane < length, step, 0.0)
    turned = pltpu.roll(step, lane0, 1)
    above = pltpu.roll(turned, 1, 0)
    above = jnp.where(row == 0, carry[0:1, :], above)
    carry[0:1, :] = turned[TROWS - 1 : TROWS, :]
    shift[pl.ds(row_shift, TROWS), :] = jnp.where(lane < lane0, above, turned)
    step_out[...] = shift[0:TROWS, :].astype(BF16)
    shift[0:16, :] = shift[TROWS : TROWS + 16, :]


def run_adam(where, texts, dkv, conv, t_all, small, scal, first, second, kv_rows, rest_rows):
    gd = len(texts)
    length = first.shape[1]
    tiles = pl.cdiv(length + 17 * C, TROWS * C)
    last = kv_rows // TROWS - 1
    fixed = lambda shape: pl.BlockSpec(shape, lambda s, w: (0,) * len(shape))
    flat = pl.BlockSpec((1, TROWS * C), lambda s, w: (0, s))
    block = texts[0].shape[:2] + (C,)
    rest_pad = pl.cdiv(rest_rows, TROWS) * TROWS + TROWS
    return pl.pallas_call(
        functools.partial(adam_kernel, gd, length, kv_rows, rest_rows),
        out_shape=(
            jax.ShapeDtypeStruct(first.shape, F32),
            jax.ShapeDtypeStruct(first.shape, F32),
            jax.ShapeDtypeStruct((tiles * TROWS, C), BF16),
        ),
        grid_spec=pltpu.PrefetchScalarGridSpec(
            num_scalar_prefetch=1,
            grid=(tiles,),
            in_specs=[pl.BlockSpec(block, lambda s, w: (0, 0, jnp.minimum(w[4], last)))] * gd
            + [pl.BlockSpec(block, lambda s, w: (0, 0, jnp.minimum(w[4] + s + 1, last)))] * gd
            + [fixed(v.shape) for v in (dkv, conv, t_all, small, scal)]
            + [flat, flat],
            out_specs=[flat, flat, pl.BlockSpec((TROWS, C), lambda s, w: (s, 0))],
            scratch_shapes=[
                pltpu.VMEM((2 * TROWS + 8, C), F32),
                pltpu.VMEM((rest_pad, C), F32),
                pltpu.VMEM((TROWS + 16, C), F32),
                pltpu.VMEM((8, C), F32),
            ],
        ),
        compiler_params=pltpu.CompilerParams(vmem_limit_bytes=32 * 2**20),
        name="adam",
    )(where, *texts, *texts, dkv, conv, t_all, small, scal, first, second)


def final_kernel(bases, pad, weights, outer, pieces, new_weights, momentum):
    b = pl.program_id(0)
    total = pieces.shape[1]
    averaged = jnp.zeros((TROWS, C), F32)
    for p, base in enumerate(bases):
        at = jnp.clip(b * TROWS - base + pad, 0, total - TROWS)
        averaged = averaged + pieces[p, pl.ds(pl.multiple_of(at, 16), TROWS), :].astype(F32)
    w = weights[...]
    averaged = averaged + (INNER_RATE * DECAY_RATE) * w
    moved = OUTER_MOMENTUM * outer[...] + averaged
    momentum[...] = moved
    new_weights[...] = w - OUTER_RATE * (averaged + OUTER_MOMENTUM * moved)


def run_final(weights2, outer2, pieces, bases, pad):
    rows = weights2.shape[0]
    block = pl.BlockSpec((TROWS, C), lambda b: (b, 0))
    return pl.pallas_call(
        functools.partial(final_kernel, bases, pad),
        out_shape=(jax.ShapeDtypeStruct(weights2.shape, F32),) * 2,
        grid=(pl.cdiv(rows, TROWS),),
        in_specs=[block, block, pl.BlockSpec(pieces.shape, lambda b: (0, 0, 0))],
        out_specs=(block, block),
        compiler_params=pltpu.CompilerParams(vmem_limit_bytes=24 * 2**20),
        name="final",
    )(weights2, outer2, pieces)


def share_kernel(gd, rows, chunk, pad, l1, l2, u_ref, out_ref, recv_a, recv_b, part,
                 s_u, s_fo, s_fi, s_y, r_a, r_b, r_f, r_y):
    wide = lax.axis_index("wide")
    g = wide // gd
    spot = wide % gd
    chunks = rows // chunk
    is_outer = jnp.logical_or(g == 0, g == GROUPS - 1)
    is_inner = jnp.logical_not(is_outer)
    low = g < GROUPS // 2
    outer_id = jnp.where(low, g - 1, g + 1) * gd + spot
    mate_id = jnp.where(low, g + 1, g - 1) * gd + spot
    barrier = pltpu.get_barrier_semaphore()
    for k in range(1, gd):
        other = g * gd + lax.rem(spot + k, gd)
        pl.semaphore_signal(barrier, inc=1, device_id={"wide": other}, device_id_type=MESH)
    pl.semaphore_signal(barrier, inc=1, device_id={"wide": mate_id}, device_id_type=MESH)
    @pl.when(is_inner)
    def _():
        pl.semaphore_signal(barrier, inc=1, device_id={"wide": outer_id}, device_id_type=MESH)
        pl.semaphore_wait(barrier, gd + 1)
    @pl.when(is_outer)
    def _():
        pl.semaphore_wait(barrier, gd)

    def sl(c):
        return pl.ds(pl.multiple_of(c * chunk, chunk), chunk)
    def ol(c):
        return pl.ds(pl.multiple_of(pad + c * chunk, 16), chunk)
    def copy(src, dst, ss, rs, dev):
        return pltpu.make_async_remote_copy(src_ref=src, dst_ref=dst, send_sem=ss, recv_sem=rs,
                                            device_id={"wide": dev}, device_id_type=MESH)
    def send_a(c):
        return copy(u_ref.at[sl(c)], recv_a.at[sl(c)], s_u.at[c], r_a.at[c], mate_id)
    def send_b(c):
        return copy(part.at[sl(c)], recv_b.at[sl(c)], s_u.at[c], r_b.at[c], mate_id)
    def send_fo(c):
        return copy(out_ref.at[spot, ol(c)], out_ref.at[spot, ol(c)], s_fo.at[c], r_f.at[c], outer_id)
    def send_fi(c):
        return copy(out_ref.at[spot, ol(c)], out_ref.at[spot, ol(c)], s_fi.at[c], r_f.at[c], mate_id)
    def send_y(c, k):
        return copy(out_ref.at[spot, ol(c)], out_ref.at[spot, ol(c)], s_y.at[k - 1, c], r_y.at[k - 1, c],
                    g * gd + lax.rem(spot + k, gd))
    def wait_y(c, k):
        src = lax.rem(spot + gd - k, gd)
        copy(out_ref.at[src, ol(c)], out_ref.at[src, ol(c)], s_y.at[k - 1, c], r_y.at[k - 1, c], wide).wait_recv()
    def spread(c):
        for k in range(1, gd):
            send_y(c, k).start()
    def is_root(c):
        return lax.rem(c + g, 2) == 1

    @pl.when(is_outer)
    def _():
        @pl.loop(0, chunks)
        def _(c):
            send_a(c).start()
    for p in range(gd):
        out_ref[p, 0:pad] = jnp.zeros((pad, 128), jnp.bfloat16)
        out_ref[p, pad + rows : rows + 2 * pad] = jnp.zeros((pad, 128), jnp.bfloat16)

    @pl.when(is_outer)
    def _():
        @pl.loop(0, chunks)
        def _(c):
            send_fo(c).wait_recv()
            spread(c)
    @pl.when(is_inner)
    def _():
        @pl.loop(0, chunks + l2)
        def _(c):
            @pl.when(jnp.logical_and(c < chunks, jnp.logical_not(is_root(c))))
            def _():
                send_a(c).wait_recv()
                part[sl(c)] = (u_ref[sl(c)].astype(jnp.float32) + recv_a[sl(c)].astype(jnp.float32)).astype(jnp.bfloat16)
                send_b(c).start()
            d = c - l1
            @pl.when(jnp.logical_and(jnp.logical_and(d >= 0, d < chunks), is_root(d)))
            def _():
                send_a(d).wait_recv()
                send_b(d).wait_recv()
                out_ref[spot, ol(d)] = (u_ref[sl(d)].astype(jnp.float32) + recv_a[sl(d)].astype(jnp.float32) + recv_b[sl(d)].astype(jnp.float32)).astype(jnp.bfloat16)
                send_fo(d).start()
                send_fi(d).start()
                spread(d)
            e = c - l2
            @pl.when(jnp.logical_and(e >= 0, jnp.logical_not(is_root(e))))
            def _():
                send_fi(e).wait_recv()
                send_fo(e).start()
                spread(e)
    @pl.loop(0, chunks)
    def _(c):
        for k in range(1, gd):
            wait_y(c, k)
            send_y(c, k).wait_send()
        @pl.when(is_outer)
        def _():
            send_a(c).wait_send()
        @pl.when(is_inner)
        def _():
            send_fo(c).wait_send()
            @pl.when(is_root(c))
            def _():
                send_fi(c).wait_send()
            @pl.when(jnp.logical_not(is_root(c)))
            def _():
                send_b(c).wait_send()

def share(u, gd, rows, chunk, pad, l1, l2):
    n = rows // chunk
    D = pltpu.SemaphoreType.DMA
    return pl.pallas_call(
        functools.partial(share_kernel, gd, rows, chunk, pad, l1, l2),
        out_shape=jax.ShapeDtypeStruct((gd, rows + 2 * pad, 128), jnp.bfloat16),
        in_specs=[pl.BlockSpec(memory_space=pltpu.VMEM)],
        out_specs=pl.BlockSpec(memory_space=pltpu.VMEM),
        scratch_shapes=[pltpu.VMEM((rows, 128), jnp.bfloat16)] * 3 + [
            D((n,)), D((n,)), D((n,)), D((max(gd - 1, 1), n)), D((n,)), D((n,)), D((n,)), D((max(gd - 1, 1), n))],
        compiler_params=pltpu.CompilerParams(collective_id=9, has_side_effects=True, vmem_limit_bytes=24 * 2**20),
        name="share",
    )(u)


def ring_gather(value, axis, group):
    size = lax.axis_size(axis)
    found = [value]
    for k in range(1, group):
        pairs = [(s, s // group * group + (s % group + k) % group) for s in range(size)]
        found.append(lax.ppermute(value, axis, pairs))
    return found


def per_device(
    weights, first_moment, second_moment, outer_momentum, noisy_input, target,
    text_tokens, text_mask, noise_level, aug_level, crop_size,
):
    length = first_moment.shape[1]
    wide_count = lax.axis_size("wide")
    gd = wide_count // GROUPS
    wide_pos = lax.axis_index("wide")
    narrow_pos = lax.axis_index("narrow")
    spot = wide_pos % gd
    weights2 = weights.reshape(-1, C)
    outer2 = outer_momentum.reshape(-1, C)
    band = noisy_input.shape[1]

    noisy_ext, target_ext, text_all, rest_all, keyval, own_kv, small = run_front(
        noise_level, aug_level, weights2, noisy_input, target, text_tokens, text_mask
    )
    kv_rows = TEXT_D * keyval.shape[2] // C
    rest_rows = weights2.shape[0] - kv_rows
    texts = ring_gather(text_all, "wide", gd)
    kvs = ring_gather(own_kv, "wide", gd)
    info = jnp.stack(
        [narrow_pos * band, crop_size[0], narrow_pos, noise_level[0], aug_level[0]]
    ).astype(jnp.int32)
    blocks, conv, packet, right = run_main(
        info, noisy_ext, target_ext, small, rest_all, keyval, rest_rows
    )
    dkv, conv_all, t_all, small_all, scal = run_mid(
        gd, wide_count, blocks, conv, packet, right, kvs, texts
    )
    start = spot * length
    levels = small_all[:, 7, :2].astype(jnp.int32) + jnp.array([[0, NOISE_LEVELS]], jnp.int32)
    row0 = start // C
    where = jnp.concatenate(
        [
            jnp.stack([narrow_pos, start % C, row0 % TROWS, row0 % 16, row0 // TROWS]).astype(jnp.int32),
            levels.reshape(-1),
        ]
    )
    moment_one, moment_two, step = run_adam(
        where, texts, dkv, conv_all, t_all, small_all, scal, first_moment, second_moment, kv_rows, rest_rows
    )
    chunk = 320
    rows = pl.cdiv(length // C + 18, chunk) * chunk
    pieces = share(step, gd, rows, chunk, TROWS, 2, 4)
    bases = [p * length // C // 16 * 16 for p in range(gd)]
    new_weights, momentum_out = run_final(weights2, outer2, pieces, bases, TROWS)
    return (
        new_weights.reshape(-1), momentum_out.reshape(-1), moment_one, moment_two,
        scal[2, :1], scal[3, :1],
    )


def solution(mesh):
    placed = (
        P("narrow"),
        P("narrow", "wide"),
        P("narrow", "wide"),
        P("narrow"),
        P("wide", "narrow", None, None),
        P("wide", "narrow", None, None),
        P("wide", "narrow", None),
        P("wide", "narrow"),
        P("wide"),
        P("wide"),
        P("wide"),
    )
    return jax.shard_map(
        per_device,
        mesh=mesh,
        in_specs=placed,
        out_specs=(P("narrow"), P("narrow"), P("narrow", "wide"), P("narrow", "wide"), P(), P()),
        check_vma=False,
    )
```

```python
import functools
import math

import jax
import jax.numpy as jnp
from jax import lax
from jax.experimental import pallas as pl
from jax.experimental.pallas import tpu as pltpu
from jax.sharding import PartitionSpec as P

MESH = pl.DeviceIdType.MESH
C = 128
NORM_GROUPS = 32
HEADS = 8
HEAD = 128
TEXT_D = 4096
H = 128
W = 128
NOISE_LEVELS = 1000
AUG_LEVELS = 24
LEVELS = NOISE_LEVELS + AUG_LEVELS
GROUPS = 4
STEP = 8


EPS_NORM = 1e-05
CLIP_NORM = 0.002
BETA_ONE = 0.9
BETA_TWO = 0.99
INNER_RATE = 0.01
DECAY_RATE = 0.01
ADAM_EPS = 1e-08
OUTER_RATE = 0.7
OUTER_MOMENTUM = 0.9

TN = (((0,), (0,)), ((), ()))
F32 = jnp.float32
BF16 = jnp.bfloat16
LOG2E = 1.4426950408889634
LN2 = 0.6931471805599453
NT = (((1,), (1,)), ((), ()))
TILE = 7
TILE3 = 8


def dot(a, b, dims=(((1,), (0,)), ((), ()))):
    return lax.dot_general(a, b, dims, preferred_element_type=F32)


def two_parts(value):
    top = value.astype(BF16)
    return top, (value - top.astype(F32)).astype(BF16)


def shifted(value, by, keep):
    return jnp.where(keep, pltpu.roll(value, by, 0), 0.0)


def main_body(
    band, columns, height, heads,
    rest_rows, crop_size, noise_level, aug_level, noisy, target, small, rest, keyval,
    blocks, dconv_w, packet, right,
    act3, diff3, m_cat, m_cat_t, n_cat, n_cat_t, conv_t, probs, dscore, wt3, y_t, z_t, sums,
    stage, query, out_w,
):
    tok, kv_block = keyval.shape[1:]
    width = heads * HEAD
    per_block = kv_block // HEAD
    narrow = lax.axis_index("narrow")
    row0 = narrow * band
    crop = crop_size[0]
    pix = TILE * columns
    first_gain, first_query = 9 * C + 2 * LEVELS, 9 * C + 2 * LEVELS + 4
    first_out = first_query + C * heads

    def take(first, count, place):
        while count:
            owner, local = divmod(first, rest_rows)
            use = min(count, rest_rows - local)
            a = local // 16 * 16
            b = (local + use + 15) // 16 * 16
            stage[0 : b - a, :] = rest[owner, a:b, :].astype(F32)
            place(stage[local - a : local - a + use, :], use)
            first, count = first + use, count - use

    def filler(ref):
        at = [0]

        def place(value, use):
            ref[at[0] : at[0] + use, :] = value
            at[0] += use

        return place

    gains = []
    take(first_gain, 4, lambda value, use: gains.append(value))
    gains = gains[0] if len(gains) == 1 else jnp.concatenate(gains, axis=0)
    take(first_query, C * heads, filler(query))
    take(first_out, width, filler(out_w))
    conv_w = rest.at[0]
    total = small[0] + small[1] + small[2] + small[3]
    lane_group = lax.broadcasted_iota(jnp.int32, (C, C), 0) // (C // NORM_GROUPS)
    same = (lane_group == lax.broadcasted_iota(jnp.int32, (C, C), 1) // (C // NORM_GROUPS)).astype(F32)
    stats = jnp.dot(total, same, precision=lax.Precision.HIGHEST, preferred_element_type=F32)
    count = height * columns * C // NORM_GROUPS
    mean = stats[0:1] * (1.0 / count)
    spread = lax.rsqrt(stats[1:2] * (1.0 / count) - mean * mean + EPS_NORM)
    film_scale, film_shift = 1.0 + total[2:3], total[3:4]
    gain = gains[0:1] * film_scale
    offset = gains[1:2] * film_scale + film_shift
    ln_gain, ln_offset = gains[2:3], gains[3:4]
    quarter = tok // 4
    masks = [small[owner, 4:5, 0:quarter] for owner in range(4)]
    ok = (jnp.concatenate(masks, axis=1) > 0.0) | (lax.broadcasted_iota(jnp.int32, (1, tok), 1) == 0)
    factor = LOG2E / math.sqrt(HEAD)
    for head in range(heads):
        cols = slice(head * HEAD, (head + 1) * HEAD)
        tcols = slice(head * tok, (head + 1) * tok)
        block, at = head // per_block, head % per_block * HEAD
        query_head = query[pl.ds(head, C, stride=heads), :].astype(BF16)
        out_head = out_w[cols, :].astype(BF16)
        m_head = dot(query_head, keyval[block, :, at : at + HEAD], NT) * factor

        @pl.when(narrow == block)
        def _():
            right[:, at : at + HEAD] = query_head

        @pl.when(narrow == block + heads // per_block)
        def _():
            right[:, at : at + HEAD] = out_w[cols, :].T.astype(BF16)

        top, rest = two_parts(m_head)
        m_cat[:C, tcols] = top
        m_cat[C:, tcols] = rest
        top, rest = two_parts(m_head.T)
        m_cat_t[tcols, :C] = top
        m_cat_t[tcols, C:] = rest
        n_head = dot(keyval[block + heads // per_block, :, at : at + HEAD], out_head)
        top, rest = two_parts(n_head)
        n_cat[tcols, :C] = top
        n_cat[tcols, C:] = rest
        top, rest = two_parts(n_head.T)
        n_cat_t[:C, tcols] = top
        n_cat_t[C:, tcols] = rest
    for tap in range(9):
        rows = slice(tap * C, (tap + 1) * C)
        wt3[rows, :] = conv_w[rows, :].astype(F32).T.astype(BF16)
    y_t[...] = jnp.zeros_like(y_t)
    z_t[...] = jnp.zeros_like(z_t)
    conv_t[...] = jnp.zeros_like(conv_t)
    sums[...] = jnp.zeros_like(sums)
    place = lax.broadcasted_iota(jnp.int32, (columns, C), 0)
    not_first, not_last = place > 0, place < columns - 1
    slope = spread * gain
    base = offset - mean * slope

    @pl.loop(0, band + 4)
    def _(r):
        scaled = noisy[r].astype(F32) * slope + base
        value = scaled * jax.nn.sigmoid(scaled)
        row = row0 + r - 2
        value = jnp.where(jnp.logical_and(row >= 0, row < height), value, 0.0)
        value = value.astype(BF16).astype(F32)
        act3[r, :, 0:C] = shifted(value, 1, not_first).astype(BF16)
        act3[r, :, C : 2 * C] = value.astype(BF16)
        act3[r, :, 2 * C : 3 * C] = shifted(value, columns - 1, not_last).astype(BF16)

    pix_row = lax.broadcasted_iota(jnp.int32, (pix, C), 0) // columns
    pix_col = lax.broadcasted_iota(jnp.int32, (pix, C), 0) % columns
    @pl.loop(0, pl.cdiv(band + 2, TILE))
    def _(t):
        q = jnp.minimum(t * TILE, band + 2 - TILE)
        conv = noisy[pl.ds(q + 1, TILE)].astype(F32).reshape(pix, C)
        for dy in range(3):
            window = act3[pl.ds(q + dy, TILE)].reshape(pix, 3 * C)
            conv = conv + dot(window, conv_w[dy * 3 * C : (dy + 1) * 3 * C, :])
        centered = conv - jnp.mean(conv, axis=1, keepdims=True)
        rs = lax.rsqrt(jnp.mean(centered * centered, axis=1, keepdims=True) + EPS_NORM)
        xhat = centered * rs
        layered = xhat * ln_gain + ln_offset
        low = layered.astype(BF16)
        low2 = jnp.concatenate([low, low], axis=1)
        for head in range(heads):
            tcols = slice(head * tok, (head + 1) * tok)
            if head % 2 == 0:
                scores = dot(low2, m_cat[:, head * tok : (head + 2) * tok])
            score = scores[:, head % 2 * tok : (head % 2 + 1) * tok]
            score = jnp.where(ok, score, -1e30)
            e = jnp.exp2(score - jnp.max(score, axis=1, keepdims=True))
            p = e * (1.0 / jnp.sum(e, axis=1, keepdims=True))
            probs[:, tcols] = p.astype(BF16)
        mixed = dot(probs[...], n_cat[...])
        output = conv + mixed[:, :C] + mixed[:, C:]
        row = row0 + q - 1 + pix_row
        valid = (row >= 0) & (row < crop) & (pix_col < crop)
        err = jnp.where(valid, output - target[pl.ds(q, TILE)].astype(F32).reshape(pix, C), 0.0)
        own_row = q + pix_row
        own = (own_row >= jnp.maximum(t * TILE, 1)) & (own_row <= band)
        err_own = jnp.where(own, err, 0.0)
        sums[4:5, :] += jnp.sum(err_own * err_own, axis=0, keepdims=True)
        dout = 2.0 * err
        dout_low = dout.astype(BF16)
        dout2 = jnp.concatenate([dout_low, dout_low], axis=1)
        for head in range(heads):
            tcols = slice(head * tok, (head + 1) * tok)
            if head % 2 == 0:
                dprobs = dot(dout2, n_cat_t[:, head * tok : (head + 2) * tok])
            dprob = dprobs[:, head % 2 * tok : (head % 2 + 1) * tok]
            p = probs[:, tcols].astype(F32)
            pd = p * dprob
            ds = pd - p * jnp.sum(pd, axis=1, keepdims=True)
            dscore[:, tcols] = ds.astype(BF16)
        dlay2 = dot(dscore[...], m_cat_t[...])
        dlay = (dlay2[:, :C] + dlay2[:, C:]) * LN2
        dlay_own = jnp.where(own, dlay, 0.0)
        sums[2:3, :] += jnp.sum(dlay_own * xhat, axis=0, keepdims=True)
        sums[3:4, :] += jnp.sum(dlay_own, axis=0, keepdims=True)
        dxh = dlay * ln_gain
        dconv = dout + rs * (
            dxh
            - jnp.mean(dxh, axis=1, keepdims=True)
            - xhat * jnp.mean(dxh * xhat, axis=1, keepdims=True)
        )
        dout_t = (2.0 * err_own).T.astype(BF16)
        lay_t = jnp.where(own, layered, 0.0).T.astype(BF16)
        y_t[...] += dot(dout_t, probs[...])
        z_t[...] += dot(lay_t, dscore[...])
        dconv_t = jnp.where(own, dconv, 0.0).T.astype(BF16)
        for dy in range(3):
            window = act3[pl.ds(q + dy, TILE)].reshape(pix, 3 * C)
            conv_t[:, dy * 3 * C : (dy + 1) * 3 * C] += dot(dconv_t, window)
        for k in range(TILE):
            one = dconv[k * columns : (k + 1) * columns]
            diff3[q + k, :, 0:C] = shifted(one, columns - 1, not_last).astype(BF16)
            diff3[q + k, :, C : 2 * C] = one.astype(BF16)
            diff3[q + k, :, 2 * C : 3 * C] = shifted(one, 1, not_first).astype(BF16)

    @pl.loop(0, band // TILE3)
    def _(t):
        r = t * TILE3
        grad = jnp.zeros((TILE3 * columns, C), F32)
        for dy in range(3):
            window = diff3[pl.ds(r + 2 - dy, TILE3)].reshape(TILE3 * columns, 3 * C)
            grad = grad + dot(window, wt3[dy * 3 * C : (dy + 1) * 3 * C, :])
        x = noisy[pl.ds(r + 2, TILE3)].astype(F32).reshape(TILE3 * columns, C)
        scaled = x * slope + base
        sig = jax.nn.sigmoid(scaled)
        ds = grad * (sig * (1.0 + scaled * (1.0 - sig)))
        sums[0:1, :] += jnp.sum(ds, axis=0, keepdims=True)
        sums[1:2, :] += jnp.sum(ds * ((x - mean) * spread), axis=0, keepdims=True)

    share_rows = dconv_w.shape[1]
    full = conv_t[...].T
    for owner in range(4):
        dconv_w[owner] = full[owner * share_rows : (owner + 1) * share_rows].astype(BF16)
        part = z_t if owner < 2 else y_t
        at = owner % 2 * per_block * tok
        blocks[owner] = part[:, at : at + per_block * tok].astype(BF16)
    a, b = sums[0:1], sums[1:2]
    packet[0:1] = film_scale * b
    packet[1:2] = film_scale * a
    packet[2:4] = sums[2:4]
    packet[4:5] = gains[0:1] * b + gains[1:2] * a
    packet[5:6] = a
    packet[6:7] = sums[4:5]
    lane = lax.broadcasted_iota(jnp.int32, (1, C), 1)
    facts = jnp.zeros((1, C), F32)
    for k, fact in enumerate((noise_level[0], aug_level[0], crop)):
        facts = jnp.where(lane == k, fact.astype(F32), facts)
    packet[7:8] = jnp.where(row0 == 0, facts, 0.0)


def cross_ids():
    n = lax.axis_index("narrow")
    mate = n + 1 - 2 * lax.rem(n, 2)
    across = lax.rem(n + 2, 4)
    corner = lax.rem(mate + 2, 4)
    return n, mate, across, corner


def to_narrow(src, dst, send_sem, recv_sem, device):
    return pltpu.make_async_remote_copy(
        src_ref=src, dst_ref=dst, send_sem=send_sem, recv_sem=recv_sem,
        device_id={"narrow": device}, device_id_type=MESH,
    )


class Gather:
    def __init__(self, view, sems, ids):
        self.view, self.sems = view, sems
        self.n, self.mate, self.across, self.corner = ids

    def _copy(self, block, slot, device):
        ref = self.view(block)
        return to_narrow(ref, ref, self.sems.at[0, slot], self.sems.at[1, slot], device)

    def start(self):
        self._copy(self.n, 1, self.across).start()
        self._copy(self.n, 0, self.mate).start()

    def relay(self):
        self._copy(self.across, 1, self.across).wait_recv()
        self._copy(self.across, 2, self.mate).start()

    def wait(self):
        self._copy(self.mate, 0, self.mate).wait_recv()
        self._copy(self.corner, 2, self.mate).wait_recv()

    def drain(self):
        self._copy(self.n, 1, self.across).wait_send()
        self._copy(self.n, 0, self.mate).wait_send()
        self._copy(self.across, 2, self.mate).wait_send()


def rest_needs(rest_rows):
    first, last = 9 * C, 9 * C + 2 * LEVELS
    needs = []
    for owner in range(4):
        lo, hi = owner * rest_rows, (owner + 1) * rest_rows
        keep = [r for r in ((lo, min(hi, first)), (max(lo, last), hi)) if r[0] < r[1]]
        assert len(keep) <= 1
        if keep:
            a, b = keep[0][0] - lo, keep[0][1] - lo
            needs.append((a // 16 * 16, (b + 15) // 16 * 16))
        else:
            needs.append(None)
    return needs


KPARTS = 4
WPARTS = 8


def front_body(
    kv_rows, rest_rows, greet, to_group, noise_level, aug_level, weights, noisy, target, text, mask,
    noisy_ext, target_ext, text_all, rest_all, keyval, own_kv, small,
    wide_f32, wide_bf, rest_f32, acc,
    w_sem, in_sem, text_sem, rest_sem, kv_sem, small_sem, halo_sem,
):
    ids = cross_ids()
    n, mate, across, corner = ids
    band = noisy.shape[1]
    tokens, depth = text.shape[1:]
    in_text = pltpu.make_async_copy(text.at[0], text_all.at[n], in_sem.at[0])
    in_text.start()
    in_rest = pltpu.make_async_copy(
        weights.at[pl.ds(kv_rows, rest_rows)], rest_f32.at[pl.ds(0, rest_rows)], in_sem.at[1]
    )
    in_rest.start()
    in_noisy = pltpu.make_async_copy(noisy.at[0], noisy_ext.at[pl.ds(2, band)], in_sem.at[2])
    in_noisy.start()
    w_step = kv_rows // WPARTS
    in_w = [
        pltpu.make_async_copy(
            weights.at[pl.ds(k * w_step, w_step)], wide_f32.at[pl.ds(k * w_step, w_step)], w_sem.at[k]
        )
        for k in range(WPARTS)
    ]
    for copy in in_w:
        copy.start()
    in_target = pltpu.make_async_copy(target.at[0], target_ext.at[pl.ds(1, band)], in_sem.at[3])
    in_target.start()
    greet()

    k_step = depth // KPARTS
    texts = [
        Gather(
            lambda b, k=k: text_all.at[b, :, pl.ds(k * k_step, k_step)], text_sem.at[k], ids
        )
        for k in range(KPARTS)
    ]
    in_text.wait()
    for part in texts:
        part.start()

    in_rest.wait()
    rest_f32[rest_rows:] = jnp.zeros((rest_f32.shape[0] - rest_rows, C), F32)
    for k in range(2):
        row_sum = jnp.zeros((1, C), F32)
        for level in (noise_level[0], NOISE_LEVELS + aug_level[0]):
            row = 9 * C + 2 * level + k - n * rest_rows
            found = rest_f32[pl.ds(jnp.clip(row, 0, rest_rows - 1), 1), :]
            found = found.astype(BF16).astype(F32)
            row_sum = row_sum + jnp.where((row >= 0) & (row < rest_rows), found, 0.0)
        small[n, 2 + k : 3 + k, :] = row_sum
    small[n, 4:8, :] = jnp.zeros((4, C), F32)
    small[n, 4:5, 0:tokens] = mask[...].astype(F32)
    in_noisy.wait()

    def add_row(r, sums):
        x = noisy_ext[r + 2].astype(F32)
        return (
            sums[0] + jnp.sum(x.reshape(-1, 8, C), axis=0),
            sums[1] + jnp.sum((x * x).reshape(-1, 8, C), axis=0),
        )

    zero = jnp.zeros((8, C), F32)
    one, two = lax.fori_loop(0, band, add_row, (zero, zero))
    small[n, 0:1, :] = jnp.sum(one, axis=0, keepdims=True)
    small[n, 1:2, :] = jnp.sum(two, axis=0, keepdims=True)
    others = (mate, across, corner)

    def small_copy(slot, block):
        return to_narrow(
            small.at[block], small.at[block], small_sem.at[0, slot], small_sem.at[1, slot], others[slot]
        )

    for slot in range(3):
        small_copy(slot, n).start()

    in_target.wait()
    up = jnp.maximum(n - 1, 0)
    down = jnp.minimum(n + 1, 3)
    noisy_up = to_narrow(
        noisy_ext.at[pl.ds(2, 2)], noisy_ext.at[pl.ds(band + 2, 2)], halo_sem.at[0, 0], halo_sem.at[1, 0], up
    )
    noisy_down = to_narrow(
        noisy_ext.at[pl.ds(band, 2)], noisy_ext.at[pl.ds(0, 2)], halo_sem.at[0, 1], halo_sem.at[1, 1], down
    )
    target_up = to_narrow(
        target_ext.at[pl.ds(1, 1)], target_ext.at[pl.ds(band + 1, 1)], halo_sem.at[0, 2], halo_sem.at[1, 2], up
    )
    target_down = to_narrow(
        target_ext.at[pl.ds(band, 1)], target_ext.at[pl.ds(0, 1)], halo_sem.at[0, 3], halo_sem.at[1, 3], down
    )

    @pl.when(n > 0)
    def _():
        noisy_up.start()
        target_up.start()

    @pl.when(n < 3)
    def _():
        noisy_down.start()
        target_down.start()

    @pl.when(n == 0)
    def _():
        noisy_ext[0:2] = jnp.zeros((2,) + noisy_ext.shape[1:], BF16)
        target_ext[0:1] = jnp.zeros((1,) + target_ext.shape[1:], BF16)

    @pl.when(n == 3)
    def _():
        noisy_ext[band + 2 : band + 4] = jnp.zeros((2,) + noisy_ext.shape[1:], BF16)
        target_ext[band + 1 : band + 2] = jnp.zeros((1,) + target_ext.shape[1:], BF16)

    needs = rest_needs(rest_rows)
    rest_all[n] = rest_f32[...].astype(BF16)

    def rest_copy(owner, slot, device):
        a, b = needs[owner]
        ref = rest_all.at[owner, pl.ds(a, b - a)]
        return to_narrow(ref, ref, rest_sem.at[0, slot, owner], rest_sem.at[1, slot, owner], device)

    for owner in range(4):
        if needs[owner] is not None:
            @pl.when(n == owner)
            def _():
                rest_copy(owner, 1, across).start()
                rest_copy(owner, 0, mate).start()

    parts = wide_bf.shape[1] // C
    rows = 256
    for k in range(WPARTS):
        in_w[k].wait()

        @pl.loop(k * w_step // parts // rows, (k + 1) * w_step // parts // rows)
        def _(i):
            for j in range(parts):
                wide_bf[pl.ds(pl.multiple_of(i * rows, rows), rows), j * C : (j + 1) * C] = wide_f32[
                    pl.ds(i * rows * parts + j, rows, stride=parts), :
                ].astype(BF16)

    acc[...] = jnp.zeros_like(acc)
    for k in range(KPARTS):
        texts[k].relay()
    for k in range(KPARTS):
        texts[k].wait()

        @pl.loop(0, k_step // 512)
        def _(i):
            at = pl.ds(pl.multiple_of(k * k_step + i * 512, 512), 512)
            acc[...] += dot(text_all[:, :, at].reshape(4 * tokens, 512), wide_bf[at, :])

    keyval[n] = acc[...].astype(BF16)
    own_kv[...] = acc[...].astype(BF16)
    keys = Gather(lambda b: keyval.at[b], kv_sem, ids)
    keys.start()
    to_group()

    for owner in range(4):
        if needs[owner] is not None:
            @pl.when(across == owner)
            def _():
                rest_copy(owner, 1, across).wait_recv()
                rest_copy(owner, 2, mate).start()

    keys.relay()
    for slot, block in ((0, mate), (1, across), (2, corner)):
        small_copy(slot, block).wait_recv()
        small_copy(slot, n).wait_send()

    @pl.when(n > 0)
    def _():
        noisy_down.wait_recv()
        target_down.wait_recv()
        noisy_up.wait_send()
        target_up.wait_send()

    @pl.when(n < 3)
    def _():
        noisy_up.wait_recv()
        target_up.wait_recv()
        noisy_down.wait_send()
        target_down.wait_send()

    for owner in range(4):
        if needs[owner] is not None:
            @pl.when(mate == owner)
            def _():
                rest_copy(owner, 0, mate).wait_recv()

            @pl.when(corner == owner)
            def _():
                rest_copy(owner, 2, mate).wait_recv()

            @pl.when(n == owner)
            def _():
                rest_copy(owner, 1, across).wait_send()
                rest_copy(owner, 0, mate).wait_send()

            @pl.when(across == owner)
            def _():
                rest_copy(owner, 2, mate).wait_send()

    keys.wait()
    keys.drain()
    for part in texts:
        part.drain()


def mid_body(
    gd, height, columns, from_group, blocks, conv, packet, right, kvs, texts, *refs,
):
    (
        dkv_all, conv_all, t_all, small_all, scal,
        near_b, near_c, sum_b, sum_c, far_b, far_c, own_b, own_c, group_b, group_c,
        packets, wides, t_own, t_send, c_send, gram, norms, conv_sum,
        near_sem, far_sem, group_sem, packet_sem, wide_sem, norm_sem, give_sem,
    ) = refs
    ids = cross_ids()
    n, mate, across, corner = ids
    others = (mate, across, corner)
    wide_count = wides.shape[0]
    wide = lax.axis_index("wide")
    group = wide // gd
    spot = lax.rem(wide, gd)
    tok, kv_block = kvs.shape[1:]
    heads = kv_block // HEAD
    packets[n] = packet[...]

    def near(slot, which):
        owner = corner if slot == 0 else mate
        src, dst = ((blocks, near_b), (conv, near_c))[which]
        return to_narrow(
            src.at[owner], dst.at[slot], near_sem.at[0, slot, which], near_sem.at[1, slot, which], mate
        )

    for slot in range(2):
        for which in range(2):
            near(slot, which).start()

    def packet_copy(slot, block):
        return to_narrow(
            packets.at[block], packets.at[block],
            packet_sem.at[0, slot], packet_sem.at[1, slot], others[slot],
        )

    for slot in range(3):
        packet_copy(slot, n).start()

    def far(which):
        src, dst = ((sum_b, far_b), (sum_c, far_c))[which]
        return to_narrow(src, dst, far_sem.at[0, which], far_sem.at[1, which], across)

    near(0, 0).wait_recv()
    sum_b[...] = (blocks[across].astype(F32) + near_b[0].astype(F32)).astype(BF16)
    far(0).start()
    near(0, 1).wait_recv()
    sum_c[...] = (conv[across].astype(F32) + near_c[0].astype(F32)).astype(BF16)
    far(1).start()

    for slot, block in enumerate(others):
        packet_copy(slot, block).wait_recv()
    item = packets[0] + packets[1] + packets[2] + packets[3]
    wides[wide] = item

    def wide_copy(k, block):
        return pltpu.make_async_remote_copy(
            src_ref=wides.at[block], dst_ref=wides.at[block],
            send_sem=wide_sem.at[0, k - 1], recv_sem=wide_sem.at[1, k - 1],
            device_id={"wide": lax.rem(wide + k, wide_count)}, device_id_type=MESH,
        )

    @pl.loop(1, wide_count)
    def _(k):
        wide_copy(k, wide).start()

    depth = texts.shape[-1]
    from_group()
    gram[...] = jnp.zeros_like(gram)

    @pl.loop(0, depth // 1024)
    def _(i):
        at = pl.ds(pl.multiple_of(i * 1024, 1024), 1024)
        for a in range(gd):
            left = texts[a, :, :, at].reshape(tok, 1024)
            for b in range(a, gd):
                part = dot(left, texts[b, :, :, at].reshape(tok, 1024), NT)
                gram[a * tok : (a + 1) * tok, b * tok : (b + 1) * tok] += part

    near(1, 0).wait_recv()
    near(1, 1).wait_recv()
    far(0).wait_recv()
    own_b[...] = (
        blocks[n].astype(F32) + near_b[1].astype(F32) + far_b[...].astype(F32)
    ).astype(BF16)

    def group_copy(k, which):
        src, dst = ((own_b, group_b), (own_c, group_c))[which]
        return pltpu.make_async_remote_copy(
            src_ref=src, dst_ref=dst.at[k - 1],
            send_sem=group_sem.at[0, which, k - 1], recv_sem=group_sem.at[1, which, k - 1],
            device_id={"wide": group * gd + lax.rem(spot + k, gd)}, device_id_type=MESH,
        )

    for k in range(1, gd):
        group_copy(k, 0).start()
    far(1).wait_recv()
    conv_sum[...] = conv[n].astype(F32) + near_c[1].astype(F32) + far_c[...].astype(F32)
    own_c[...] = conv_sum[...].astype(BF16)
    for k in range(1, gd):
        group_copy(k, 1).start()

    scale = jnp.where(n < 2, 1.0 / math.sqrt(HEAD), 1.0)

    def project(k, value):
        for h in range(heads):
            cols = slice(h * HEAD, (h + 1) * HEAD)
            part = value[:, h * tok : (h + 1) * tok]
            dkv_all[k * tok : (k + 1) * tok, cols] = (dot(part, right[:, cols], TN) * scale).astype(BF16)
            term = dot(part, kvs[k, :, cols]) * scale
            t_own[:, cols] = term if k == 0 else t_own[:, cols] + term

    project(0, own_b[...])
    for k in range(1, gd):
        group_copy(k, 0).wait_recv()
        project(k, group_b[k - 1])
        group_copy(k, 1).wait_recv()
        conv_sum[...] += group_c[k - 1].astype(F32)
    t_send[...] = t_own[...].astype(BF16)
    c_send[...] = conv_sum[...].astype(BF16)

    q_rows = 96
    q_from = 80

    def give_conv(src_n):
        return to_narrow(c_send, conv_all.at[src_n], give_sem.at[0, 0], give_sem.at[1, src_n], 0)

    def give_head(src_n):
        at = pl.ds(0, q_rows)
        return to_narrow(t_send.at[at], t_all.at[src_n, at], give_sem.at[0, 1], give_sem.at[1, src_n], 2)

    def give_tail(src_n):
        at = pl.ds(q_from, C - q_from)
        return to_narrow(t_send.at[at], t_all.at[src_n, at], give_sem.at[0, 2], give_sem.at[1, src_n], 3)

    def give_values():
        return to_narrow(t_send, t_all.at[2], give_sem.at[0, 1], give_sem.at[1, 2], 3)

    for k in range(4):
        @pl.when(n == k)
        def _():
            if k < 2:
                give_head(k).start()
                give_tail(k).start()
            if k == 2:
                give_values().start()
            if k > 0:
                give_conv(k).start()
            else:
                conv_all[0] = c_send[...]
            if k == 3:
                t_all[3] = t_send[...]

    @pl.loop(1, wide_count)
    def _(k):
        wide_copy(k, lax.rem(wide + wide_count - k, wide_count)).wait_recv()

    sq = jnp.sum(t_own[...] * t_own[...]) + jnp.sum(conv_sum[...] * conv_sum[...])
    for a in range(gd):
        da = dkv_all[a * tok : (a + 1) * tok, :]
        for b in range(a, gd):
            db = dkv_all[b * tok : (b + 1) * tok, :]
            top, low = two_parts(gram[a * tok : (a + 1) * tok, b * tok : (b + 1) * tok])
            part = jnp.sum(da.astype(F32) * (dot(top, db) + dot(low, db)))
            sq = sq + (part if a == b else 2.0 * part)
    gains = jnp.zeros((4, C), F32)
    shared = jnp.zeros((1, C), F32)
    for a in range(gd):
        mine = wides[group * gd + a]
        small_all[a] = mine
        gains = gains + mine[0:4]
        for b in range(gd):
            his = wides[group * gd + b]
            same = (mine[7:8, 0:1] == his[7:8, 0:1]).astype(F32) + (mine[7:8, 1:2] == his[7:8, 1:2]).astype(F32)
            shared = shared + same * (mine[4:5] * his[4:5] + mine[5:6] * his[5:6])
    shared_sq = jnp.sum(gains * gains) + jnp.sum(shared)
    norms[n] = jnp.full((8, C), sq + jnp.where(n == 0, shared_sq, 0.0), F32)

    def norm_copy(slot, block):
        return to_narrow(
            norms.at[block], norms.at[block], norm_sem.at[0, slot], norm_sem.at[1, slot], others[slot]
        )

    for slot in range(3):
        norm_copy(slot, n).start()

    def tally(k, found):
        there = wides[k]
        crop = there[7:8, 2:3]
        pixels = jnp.minimum(crop, float(height)) * jnp.minimum(crop, float(columns))
        mine = jnp.where(k // gd == group, pixels, 0.0)
        return found[0] + pixels, found[1] + mine, found[2] + jnp.sum(there[6:7], axis=1, keepdims=True)

    none = jnp.zeros((1, 1), F32)
    total, own_count, loss = lax.fori_loop(0, wide_count, tally, (none, none, none))
    for slot, block in enumerate(others):
        norm_copy(slot, block).wait_recv()
    squares = norms[0, 0:1] + norms[1, 0:1] + norms[2, 0:1] + norms[3, 0:1]
    norm = jnp.sqrt(squares) / total
    scal[0:1] = jnp.minimum(1.0, CLIP_NORM / norm) / total
    scal[1:2] = jnp.broadcast_to(INNER_RATE * own_count / total, (1, C))
    scal[2:3] = jnp.broadcast_to(loss, (1, C))
    scal[3:4] = jnp.broadcast_to(total, (1, C))
    scal[4:8] = jnp.zeros((4, C), F32)

    for k in range(4):
        @pl.when(n == k)
        def _():
            if k < 2:
                give_head(k).wait_send()
                give_tail(k).wait_send()
            if k == 2:
                give_values().wait_send()
                give_head(0).wait_recv()
                give_head(1).wait_recv()
            if k == 3:
                give_tail(0).wait_recv()
                give_tail(1).wait_recv()
                give_values().wait_recv()
            if k > 0:
                give_conv(k).wait_send()
            else:
                for j in range(1, 4):
                    give_conv(j).wait_recv()
    for slot in range(2):
        for which in range(2):
            near(slot, which).wait_send()
    for which in range(2):
        far(which).wait_send()
        for k in range(1, gd):
            group_copy(k, which).wait_send()
    for slot in range(3):
        packet_copy(slot, n).wait_send()
        norm_copy(slot, n).wait_send()

    @pl.loop(1, wide_count)
    def _(k):
        wide_copy(k, wide).wait_send()


def step_kernel(gd, wide_count, kv_rows, rest_rows, band, columns, counts, *refs):
    refs = list(refs)
    noise_level, aug_level, crop_size, weights, noisy, target, text, first, second, mask = refs[:10]
    texts, dkv_all, conv_all, t_all, small_all, scal, first_near, second_near = refs[10:18]
    n_front, n_main, n_mid = counts
    at = 18
    (noisy_ext, target_ext, rest_all, keyval, kvs, small) = refs[at : at + 6]
    at += 6
    front_sems = refs[at : at + n_front]
    at += n_front
    (blocks, conv, packet, right) = refs[at : at + 4]
    at += 4
    mid_refs = refs[at : at + n_mid]
    at += n_mid
    group_text_sem, ahead_sem = refs[at], refs[at + 1]
    ahead = [
        pltpu.make_async_copy(far, near, ahead_sem.at[k])
        for k, (far, near) in enumerate(((first, first_near), (second, second_near)))
    ]
    n, mate, across, corner = cross_ids()
    wide = lax.axis_index("wide")
    group, spot = wide // gd, lax.rem(wide, gd)
    tok, kv_block = kvs.shape[1:]
    depth = text.shape[2]
    barrier = pltpu.get_barrier_semaphore()
    for other in (mate, across, corner):
        pl.semaphore_signal(barrier, inc=1, device_id={"narrow": other}, device_id_type=MESH)

    @pl.loop(1, wide_count)
    def _(k):
        pl.semaphore_signal(
            barrier, inc=1, device_id={"wide": lax.rem(wide + k, wide_count)}, device_id_type=MESH
        )

    def greet():
        pl.semaphore_wait(barrier, 3 + wide_count - 1)

    def group_send(k, which):
        buf = (texts, kvs)[which]
        return pltpu.make_async_remote_copy(
            src_ref=buf.at[0], dst_ref=buf.at[k],
            send_sem=group_text_sem.at[0, which, k - 1], recv_sem=group_text_sem.at[1, which, k - 1],
            device_id={"wide": group * gd + lax.rem(spot + k, gd)}, device_id_type=MESH,
        )

    def to_group():
        for which in (1, 0):
            for k in range(1, gd):
                group_send(k, which).start()

    def from_group():
        for which in (1, 0):
            for k in range(1, gd):
                group_send(k, which).wait_recv()
                group_send(k, which).wait_send()

    def front(wide_f32, wide_bf, rest_f32, acc):
        front_body(
            kv_rows, rest_rows, greet, to_group, noise_level, aug_level, weights, noisy, target, text, mask,
            noisy_ext, target_ext, texts.at[0], rest_all, keyval, kvs.at[0], small,
            wide_f32, wide_bf, rest_f32, acc, *front_sems,
        )

    V = pltpu.VMEM
    pl.run_scoped(
        front, V((kv_rows, C), F32), V((depth, kv_block), BF16), V((rest_all.shape[1], C), F32),
        V((tok, kv_block), F32),
    )
    for copy in ahead:
        copy.start()
    pix = TILE * columns

    def main(*scratch):
        main_body(
            band, columns, H, HEADS, rest_rows, crop_size, noise_level, aug_level,
            noisy_ext, target_ext, small, rest_all, keyval, blocks, conv, packet, right, *scratch,
        )

    pl.run_scoped(
        main,
        V((band + 4, columns, 3 * C), BF16),
        V((band + 2, columns, 3 * C), BF16),
        V((2 * C, HEADS * tok), BF16),
        V((HEADS * tok, 2 * C), BF16),
        V((HEADS * tok, 2 * C), BF16),
        V((2 * C, HEADS * tok), BF16),
        V((C, 9 * C), F32),
        V((pix, HEADS * tok), BF16),
        V((pix, HEADS * tok), BF16),
        V((9 * C, C), BF16),
        V((C, HEADS * tok), F32),
        V((C, HEADS * tok), F32),
        V((8, C), F32),
        V((rest_all.shape[1], C), F32),
        V((C * HEADS, C), F32),
        V((HEADS * HEAD, C), F32),
    )

    def middle(gram):
        mid_body(
            gd, H, W, from_group, blocks, conv, packet, right, kvs, texts,
            dkv_all, conv_all, t_all, small_all, scal, *mid_refs[:15], gram, *mid_refs[15:],
        )

    pl.run_scoped(middle, V((gd * tok, gd * tok), F32))
    for copy in ahead:
        copy.wait()


def near(gd):
    return pltpu.VMEM if gd <= 4 else jax.ShapeDtypeStruct


def hold(value, gd):
    return pltpu.with_memory_space_constraint(value, pltpu.VMEM) if gd <= 4 else value


def far(value):
    return pltpu.with_memory_space_constraint(value, pltpu.HBM)


def run_step(
    gd, wide_count, noise_level, aug_level, crop_size, weights2, noisy, target, text, first, second, mask
):
    _, band, columns, _ = noisy.shape
    _, tokens, depth = text.shape
    tok = 4 * tokens
    kv_block = 2 * HEADS * HEAD // 4
    kv_rows = depth * kv_block // C
    rest_rows = weights2.shape[0] - kv_rows
    rest_pad = (rest_rows + 15) // 16 * 16
    assert 9 * C <= rest_rows and kv_block % HEAD == 0 and HEAD == C
    vmem = pl.BlockSpec(memory_space=pltpu.VMEM)
    smem = pl.BlockSpec(memory_space=pltpu.SMEM)
    hbm = pl.BlockSpec(memory_space=pltpu.HBM)
    D, V = pltpu.SemaphoreType.DMA, pltpu.VMEM
    few = max(gd - 1, 1)
    bshape, cshape = (C, kv_block // HEAD * tok), (9 * C // 4, C)
    front_sems = [D((WPARTS,)), D((4,)), D((KPARTS, 2, 3)), D((2, 3, 4)), D((2, 3)), D((2, 3)), D((2, 4))]
    mid_refs = [
        V((2,) + bshape, BF16), V((2,) + cshape, BF16), V(bshape, BF16), V(cshape, BF16),
        V(bshape, BF16), V(cshape, BF16), V(bshape, BF16), V(cshape, BF16),
        V((few,) + bshape, BF16), V((few,) + cshape, BF16),
        V((4, 8, C), F32), V((wide_count, 8, C), F32),
        V((C, kv_block), F32), V((C, kv_block), BF16), V(cshape, BF16),
        V((4, 8, C), F32), V(cshape, F32),
        D((2, 2, 2)), D((2, 2)), D((2, 2, few)), D((2, 3)), D((2, wide_count)), D((2, 3)), D((2, 4)),
    ]
    return pl.pallas_call(
        functools.partial(
            step_kernel, gd, wide_count, kv_rows, rest_rows, band, columns,
            (len(front_sems), 0, len(mid_refs)),
        ),
        out_shape=tuple(
            near(gd)(shape, kind)
            for shape, kind in (
                ((gd, 4, tokens, depth), BF16),
                ((gd * tok, kv_block), BF16),
                ((4,) + cshape, BF16),
                ((4, C, kv_block), BF16),
                ((gd, 8, C), F32),
                ((8, C), F32),
                (first.shape, F32),
                (first.shape, F32),
            )
        ),
        in_specs=[smem] * 3 + [hbm] * 6 + [vmem],
        out_specs=(vmem,) * 8,
        scratch_shapes=[
            V((band + 4, columns, C), BF16), V((band + 2, columns, C), BF16), V((4, rest_pad, C), BF16),
            V((4, tok, kv_block), BF16), V((gd, tok, kv_block), BF16), V((4, 8, C), F32),
            *front_sems,
            V((4,) + bshape, BF16), V((4,) + cshape, BF16), V((8, C), F32), V((C, kv_block), BF16),
            *mid_refs,
            D((2, 2, few)),
            D((2,)),
        ],
        compiler_params=pltpu.CompilerParams(
            collective_id=1, has_side_effects=True, vmem_limit_bytes=(STEP_VMEM if gd <= 4 else 58) * 2**20
        ),
        name="step",
    )(noise_level, aug_level, crop_size, *map(far, (weights2, noisy, target, text, first, second)), mask)


STEP_VMEM = 48


AROWS = 1024


def adam_tiles(length):
    return pl.cdiv(length + 17 * C, AROWS * C)


def adam_kernel(
    gd, length, kv_rows, rest_rows, *refs,
):
    (
        texts, dkv, conv, t_all, small, scal, first, second, first_out, second_out, step_out,
        nat, rest, turned_dkv, edge, shift, carry,
    ) = refs
    s = pl.program_id(0)
    tok = dkv.shape[0] // gd
    n = lax.axis_index("narrow")
    start = lax.rem(lax.axis_index("wide"), gd) * length
    row0 = start // C
    lane0, row_off, row_shift, block0 = lax.rem(start, C), lax.rem(row0, AROWS), lax.rem(row0, 16), row0 // AROWS
    wrap = C - lane0
    kv_blocks = kv_rows // AROWS
    parts = dkv.shape[1] // C
    cols_tile = AROWS // parts

    def iotas(rows):
        shape = (rows, C)
        return lax.broadcasted_iota(jnp.int32, shape, 0), lax.broadcasted_iota(jnp.int32, shape, 1)

    def natural(tile):
        block = block0 + tile
        here = pl.multiple_of(tile * AROWS + 8, 8)

        @pl.when(block < kv_blocks)
        def _():
            at = pl.ds(pl.multiple_of(block * cols_tile, cols_tile), cols_tile)
            text = jnp.concatenate([texts[k, :, :, at].reshape(tok, cols_tile) for k in range(gd)], axis=0)
            grad = dot(text, turned_dkv[...], TN)
            for j in range(parts - 1):
                nat[pl.ds(here + j, cols_tile, stride=parts), :] = grad[:, j * C : (j + 1) * C]
            part = grad[:, (parts - 1) * C :]
            row, lane = iotas(cols_tile)
            before = jnp.where(row == 0, edge[0:1, :], pltpu.roll(part, 1, 0))
            nat[pl.ds(here - 1, cols_tile, stride=parts), :] = jnp.where(lane < wrap, before, part)
            edge[0:1, :] = part[cols_tile - 1 : cols_tile, :]

        @pl.when(block >= kv_blocks)
        def _():
            at = pl.multiple_of(jnp.minimum((block - kv_blocks) * AROWS, rest.shape[0] - 16 - AROWS), 8)
            row, lane = iotas(AROWS)
            both = jnp.where(lane >= lane0, rest[pl.ds(at + 8, AROWS), :], rest[pl.ds(at + 9, AROWS), :])
            nat[pl.ds(here, AROWS), :] = pltpu.roll(both, wrap, 1)

            @pl.when(block == kv_blocks)
            def _():
                row, lane = iotas(8)
                ahead = pltpu.roll(rest[8:16, :], wrap, 1)
                nat[pl.ds(here - 1, 1), :] = jnp.where(lane < wrap, edge[...], ahead)[0:1, :]

    def assemble():
        first_table, first_gain = 9 * C, 9 * C + 2 * LEVELS
        first_query = first_gain + 4
        first_out = first_query + C * HEADS
        quarter = conv.shape[1]
        width = dkv.shape[1]
        heads = width // HEAD
        for owner in range(4):
            lo, hi = owner * rest_rows, (owner + 1) * rest_rows

            @pl.when(n == owner)
            def _():
                for k in range(4):
                    a, b = max(lo, k * quarter), min(hi, (k + 1) * quarter)
                    if a < b:
                        assert (a, b) == (k * quarter, (k + 1) * quarter)
                        rest[8 + a - lo : 8 + b - lo, :] = conv[k].astype(F32)
                a, b = max(lo, first_query), min(hi, first_out)
                if a < b:
                    for h in range(HEADS):
                        c0 = max(0, -(-(a - first_query - h) // HEADS))
                        c1 = min(C, -(-(b - first_query - h) // HEADS))
                        cols = slice(h % heads * HEAD, h % heads * HEAD + HEAD)
                        c_lo, c_hi = c0 // 16 * 16, (c1 + 15) // 16 * 16
                        value = t_all[h // heads, c_lo:c_hi, cols].astype(F32)
                        start = first_query + c0 * HEADS + h - lo
                        rest[pl.ds(8 + start, c1 - c0, stride=HEADS), :] = value[c0 - c_lo : c1 - c_lo]
                for h in range(HEADS):
                    a, b = first_out + h * HEAD, first_out + (h + 1) * HEAD
                    if lo <= a and b <= hi:
                        cols = slice(h % heads * HEAD, h % heads * HEAD + HEAD)
                        rest[8 + a - lo : 8 + b - lo, :] = t_all[2 + h // heads, :, cols].astype(F32).T
                    else:
                        assert b <= lo or hi <= a
                if lo <= first_gain and first_gain + 4 <= hi:
                    total = small[0, 0:4]
                    for k in range(1, gd):
                        total = total + small[k, 0:4]
                    rest[8 + first_gain - lo : 8 + first_gain + 4 - lo, :] = total


        for k in range(gd):
            for level, shift_by in ((0, 0), (1, NOISE_LEVELS)):
                found = jnp.max(small[k, 7:8, level : level + 1]).astype(jnp.int32) + shift_by
                for half in range(2):
                    at_row = first_table + 2 * found + half - n * rest_rows

                    @pl.when((at_row >= 0) & (at_row < rest_rows))
                    def _():
                        rest[pl.ds(at_row + 8, 1), :] += small[k, 4 + half : 5 + half]

    @pl.when(s == 0)
    def _():
        edge[...] = jnp.zeros_like(edge)
        rest[...] = jnp.zeros_like(rest)
        carry[...] = jnp.zeros_like(carry)
        shift[...] = jnp.zeros_like(shift)
        row, lane = iotas(dkv.shape[0])
        moved = [
            pltpu.roll(dkv[:, j * C : (j + 1) * C].astype(F32), wrap, 1) for j in range(parts)
        ]
        for j in range(parts):
            turned_dkv[:, j * C : (j + 1) * C] = jnp.where(
                lane < wrap, moved[j], moved[(j + 1) % parts]
            ).astype(BF16)

        @pl.when(start + length > kv_rows * C)
        def _():
            assemble()

        natural(0)

    natural(s + 1)
    row, lane = iotas(AROWS)
    g = nat[pl.ds(s * AROWS + row_off + 8, AROWS), :] * scal[0:1]
    one = BETA_ONE * first.reshape(AROWS, C)[...] + (1.0 - BETA_ONE) * g
    two = BETA_TWO * second.reshape(AROWS, C)[...] + (1.0 - BETA_TWO) * g * g
    first_out.reshape(AROWS, C)[...] = one
    second_out.reshape(AROWS, C)[...] = two
    fixed_one = one * (scal[1:2] * (1.0 / (1.0 - BETA_ONE**STEP)))
    fixed_two = two * (1.0 / (1.0 - BETA_TWO**STEP))
    root = fixed_two * lax.rsqrt(fixed_two)
    step = fixed_one * pl.reciprocal(root + ADAM_EPS, approx=True)
    step = jnp.where((s * AROWS + row) * C + lane < length, step, 0.0)
    turned = pltpu.roll(step, lane0, 1)
    above = pltpu.roll(turned, 1, 0)
    above = jnp.where(row == 0, carry[0:1, :], above)
    carry[0:1, :] = turned[AROWS - 1 : AROWS, :]
    shift[pl.ds(row_shift, AROWS), :] = jnp.where(lane < lane0, above, turned)
    step_out[...] = shift[0:AROWS, :].astype(BF16)
    shift[0:16, :] = shift[AROWS : AROWS + 16, :]


def run_adam(texts, dkv, conv, t_all, small, scal, first, second, length, kv_rows, rest_rows):
    gd = texts.shape[0]
    tiles = adam_tiles(length)
    flat = pl.BlockSpec((1, AROWS * C), lambda s: (0, s))
    rest_pad = (pl.cdiv(rest_rows, AROWS) + 1) * AROWS + 16
    return pl.pallas_call(
        functools.partial(adam_kernel, gd, length, kv_rows, rest_rows),
        out_shape=(
            jax.ShapeDtypeStruct((1, length), F32),
            jax.ShapeDtypeStruct((1, length), F32),
            near(gd)((tiles * AROWS, C), BF16),
        ),
        grid=(tiles,),
        in_specs=[pl.BlockSpec(memory_space=pltpu.VMEM)] * 6 + [flat, flat],
        out_specs=[flat, flat, pl.BlockSpec((AROWS, C), lambda s: (s, 0))],
        scratch_shapes=[
            pltpu.VMEM(((tiles + 1) * AROWS + 16, C), F32),
            pltpu.VMEM((rest_pad, C), F32),
            pltpu.VMEM(dkv.shape, BF16),
            pltpu.VMEM((8, C), F32),
            pltpu.VMEM((AROWS + 16, C), F32),
            pltpu.VMEM((8, C), F32),
        ],
        compiler_params=pltpu.CompilerParams(vmem_limit_bytes=ADAM_VMEM),
        name="adam",
    )(*(hold(v, gd) for v in (texts, dkv, conv, t_all, small, scal, first, second)))


ADAM_VMEM = 24 * 2**20


def share_kernel(
    gd, rows, chunk, pad, l1, l2, u_ref, w_far, o_far, out_ref, w_near, o_near,
    recv_a, recv_b, part, in_sem, s_u, s_fo, s_fi, s_y, r_a, r_b, r_f, r_y,
):
    loads = [
        pltpu.make_async_copy(w_far, w_near.at[pl.ds(0, w_far.shape[0])], in_sem.at[1]),
        pltpu.make_async_copy(o_far, o_near.at[pl.ds(0, o_far.shape[0])], in_sem.at[2]),
    ]
    wide = lax.axis_index("wide")
    g = wide // gd
    spot = wide % gd
    chunks = rows // chunk
    is_outer = jnp.logical_or(g == 0, g == GROUPS - 1)
    is_inner = jnp.logical_not(is_outer)
    low = g < GROUPS // 2
    outer_id = jnp.where(low, g - 1, g + 1) * gd + spot
    mate_id = jnp.where(low, g + 1, g - 1) * gd + spot
    barrier = pltpu.get_barrier_semaphore()
    for k in range(1, gd):
        other = g * gd + lax.rem(spot + k, gd)
        pl.semaphore_signal(barrier, inc=1, device_id={"wide": other}, device_id_type=MESH)
    pl.semaphore_signal(barrier, inc=1, device_id={"wide": mate_id}, device_id_type=MESH)
    @pl.when(is_inner)
    def _():
        pl.semaphore_signal(barrier, inc=1, device_id={"wide": outer_id}, device_id_type=MESH)
        pl.semaphore_wait(barrier, gd + 1)
    @pl.when(is_outer)
    def _():
        pl.semaphore_wait(barrier, gd)

    def sl(c):
        return pl.ds(pl.multiple_of(c * chunk, chunk), chunk)
    def ol(c):
        return pl.ds(pl.multiple_of(pad + c * chunk, 16), chunk)
    def copy(src, dst, ss, rs, dev):
        return pltpu.make_async_remote_copy(src_ref=src, dst_ref=dst, send_sem=ss, recv_sem=rs,
                                            device_id={"wide": dev}, device_id_type=MESH)
    def send_a(c):
        return copy(u_ref.at[sl(c)], recv_a.at[sl(c)], s_u.at[c], r_a.at[c], mate_id)
    def send_b(c):
        return copy(part.at[sl(c)], recv_b.at[sl(c)], s_u.at[c], r_b.at[c], mate_id)
    def send_fo(c):
        return copy(out_ref.at[spot, ol(c)], out_ref.at[spot, ol(c)], s_fo.at[c], r_f.at[c], outer_id)
    def send_fi(c):
        return copy(out_ref.at[spot, ol(c)], out_ref.at[spot, ol(c)], s_fi.at[c], r_f.at[c], mate_id)
    def send_y(c, k):
        return copy(out_ref.at[spot, ol(c)], out_ref.at[spot, ol(c)], s_y.at[k - 1, c], r_y.at[k - 1, c],
                    g * gd + lax.rem(spot + k, gd))
    def wait_y(c, k):
        src = lax.rem(spot + gd - k, gd)
        copy(out_ref.at[src, ol(c)], out_ref.at[src, ol(c)], s_y.at[k - 1, c], r_y.at[k - 1, c], wide).wait_recv()
    def spread(c):
        for k in range(1, gd):
            send_y(c, k).start()
    def is_root(c):
        return lax.rem(c + g, 2) == 1

    @pl.when(is_outer)
    def _():
        @pl.loop(0, chunks)
        def _(c):
            send_a(c).start()
    for load in loads:
        load.start()
    for p in range(gd):
        out_ref[p, 0:pad] = jnp.zeros((pad, 128), jnp.bfloat16)
        out_ref[p, pad + rows : rows + 2 * pad] = jnp.zeros((pad, 128), jnp.bfloat16)

    @pl.when(is_outer)
    def _():
        @pl.loop(0, chunks)
        def _(c):
            send_fo(c).wait_recv()
            spread(c)
    @pl.when(is_inner)
    def _():
        @pl.loop(0, chunks + l2)
        def _(c):
            @pl.when(jnp.logical_and(c < chunks, jnp.logical_not(is_root(c))))
            def _():
                send_a(c).wait_recv()
                part[sl(c)] = (u_ref[sl(c)].astype(jnp.float32) + recv_a[sl(c)].astype(jnp.float32)).astype(jnp.bfloat16)
                send_b(c).start()
            d = c - l1
            @pl.when(jnp.logical_and(jnp.logical_and(d >= 0, d < chunks), is_root(d)))
            def _():
                send_a(d).wait_recv()
                send_b(d).wait_recv()
                out_ref[spot, ol(d)] = (u_ref[sl(d)].astype(jnp.float32) + recv_a[sl(d)].astype(jnp.float32) + recv_b[sl(d)].astype(jnp.float32)).astype(jnp.bfloat16)
                send_fo(d).start()
                send_fi(d).start()
                spread(d)
            e = c - l2
            @pl.when(jnp.logical_and(e >= 0, jnp.logical_not(is_root(e))))
            def _():
                send_fi(e).wait_recv()
                send_fo(e).start()
                spread(e)
    @pl.loop(0, chunks)
    def _(c):
        for k in range(1, gd):
            wait_y(c, k)
            send_y(c, k).wait_send()
        @pl.when(is_outer)
        def _():
            send_a(c).wait_send()
        @pl.when(is_inner)
        def _():
            send_fo(c).wait_send()
            @pl.when(is_root(c))
            def _():
                send_fi(c).wait_send()
            @pl.when(jnp.logical_not(is_root(c)))
            def _():
                send_b(c).wait_send()
    for load in loads:
        load.wait()


def share(u, weights2, outer2, gd, rows, chunk, pad, l1, l2):
    n = rows // chunk
    D = pltpu.SemaphoreType.DMA
    few = max(gd - 1, 1)
    held = pl.cdiv(weights2.shape[0], 256) * 256
    vmem, hbm = pl.BlockSpec(memory_space=pltpu.VMEM), pl.BlockSpec(memory_space=pltpu.HBM)
    return pl.pallas_call(
        functools.partial(share_kernel, gd, rows, chunk, pad, l1, l2),
        out_shape=(near(gd)((gd, rows + 2 * pad, C), BF16),) + (near(gd)((held, C), F32),) * 2,
        in_specs=[vmem, hbm, hbm],
        out_specs=(vmem,) * 3,
        scratch_shapes=[pltpu.VMEM((rows, C), BF16)] * 3
        + [
            D((3,)), D((n,)), D((n,)), D((n,)), D((few, n)),
            D((n,)), D((n,)), D((n,)), D((few, n)),
        ],
        compiler_params=pltpu.CompilerParams(
            collective_id=9, has_side_effects=True, vmem_limit_bytes=SHARE_VMEM
        ),
        name="share",
    )(hold(u, gd), far(weights2), far(outer2))


SHARE_VMEM = 32 * 2**20


def final_kernel(bases, pad, block, weights, outer, pieces, scal, new_weights, momentum, loss, count, held, sem):
    rows = new_weights.shape[0]
    total = pieces.shape[1]
    steps = pl.cdiv(rows, block)

    def writes(b, slot, size):
        here = pl.ds(b * block, size)
        return [
            pltpu.make_async_copy(held.at[slot, k, pl.ds(0, size)], out.at[here], sem.at[slot, k])
            for k, out in enumerate((new_weights, momentum))
        ]

    for b in range(steps):
        slot = b % 3
        size = min(block, rows - b * block)
        if b >= 3:
            for copy in writes(b - 3, slot, block):
                copy.wait()
        averaged = jnp.zeros((block, C), F32)
        for p, base in enumerate(bases):
            at = min(max(b * block - base + pad, 0), total - block)
            averaged = averaged + pieces[p, at : at + block, :].astype(F32)
        w = weights[b * block : (b + 1) * block, :]
        averaged = averaged + (INNER_RATE * DECAY_RATE) * w
        moved = OUTER_MOMENTUM * outer[b * block : (b + 1) * block, :] + averaged
        held[slot, 1] = moved
        held[slot, 0] = w - OUTER_RATE * (averaged + OUTER_MOMENTUM * moved)
        for copy in writes(b, slot, size):
            copy.start()
    loss[0] = jnp.max(scal[2:3])
    count[0] = jnp.max(scal[3:4])
    for b in range(max(steps - 3, 0), steps):
        for copy in writes(b, b % 3, min(block, rows - b * block)):
            copy.wait()


def run_final(rows, weights2, outer2, pieces, scal, bases, pad):
    hbm, smem = pl.BlockSpec(memory_space=pltpu.HBM), pl.BlockSpec(memory_space=pltpu.SMEM)
    block = weights2.shape[0] // 16
    assert block % 16 == 0 and block <= pad
    return pl.pallas_call(
        functools.partial(final_kernel, bases, pad, block),
        out_shape=(jax.ShapeDtypeStruct((rows, C), F32),) * 2 + (jax.ShapeDtypeStruct((1,), F32),) * 2,
        in_specs=[pl.BlockSpec(memory_space=pltpu.VMEM)] * 4,
        out_specs=(hbm, hbm, smem, smem),
        scratch_shapes=[pltpu.VMEM((3, 2, block, C), F32), pltpu.SemaphoreType.DMA((3, 2))],
        compiler_params=pltpu.CompilerParams(vmem_limit_bytes=12 * 2**20),
        name="final",
    )(*(hold(v, len(bases)) for v in (weights2, outer2, pieces, scal)))


def per_device(
    weights, first_moment, second_moment, outer_momentum, noisy_input, target,
    text_tokens, text_mask, noise_level, aug_level, crop_size,
):
    length = first_moment.shape[1]
    wide_count = lax.axis_size("wide")
    gd = wide_count // GROUPS
    weights2 = weights.reshape(-1, C)
    outer2 = outer_momentum.reshape(-1, C)

    texts, dkv, conv_all, t_all, small_all, scal, first, second = run_step(
        gd, wide_count, noise_level, aug_level, crop_size, weights2, noisy_input, target, text_tokens,
        first_moment, second_moment, text_mask,
    )
    kv_rows = TEXT_D * dkv.shape[1] // C
    rest_rows = weights2.shape[0] - kv_rows
    moment_one, moment_two, step = run_adam(
        texts, dkv, conv_all, t_all, small_all, scal, first, second, length, kv_rows, rest_rows
    )
    chunk = 320
    rows = pl.cdiv(length // C + 18, chunk) * chunk
    pad = 1120
    pieces, w_near, o_near = share(step, weights2, outer2, gd, rows, chunk, pad, 2, 4)
    bases = [p * length // C // 16 * 16 for p in range(gd)]
    new_weights, momentum_out, loss, count = run_final(
        weights2.shape[0], w_near, o_near, pieces, scal, bases, pad
    )
    return (
        new_weights.reshape(-1), momentum_out.reshape(-1), moment_one, moment_two,
        loss, count,
    )


def solution(mesh):
    placed = (
        P("narrow"),
        P("narrow", "wide"),
        P("narrow", "wide"),
        P("narrow"),
        P("wide", "narrow", None, None),
        P("wide", "narrow", None, None),
        P("wide", "narrow", None),
        P("wide", "narrow"),
        P("wide"),
        P("wide"),
        P("wide"),
    )
    return jax.shard_map(
        per_device,
        mesh=mesh,
        in_specs=placed,
        out_specs=(P("narrow"), P("narrow"), P("narrow", "wide"), P("narrow", "wide"), P(), P()),
        check_vma=False,
    )
```

```python
import functools
import math

import jax
import jax.numpy as jnp
from jax import lax
from jax.experimental import pallas as pl
from jax.experimental.pallas import tpu as pltpu
from jax.sharding import PartitionSpec as P

MESH = pl.DeviceIdType.MESH
C = 128
NORM_GROUPS = 32
HEADS = 8
HEAD = 128
TEXT_D = 4096
H = 128
W = 128
NOISE_LEVELS = 1000
AUG_LEVELS = 24
LEVELS = NOISE_LEVELS + AUG_LEVELS
GROUPS = 4
STEP = 8


EPS_NORM = 1e-05
CLIP_NORM = 0.002
BETA_ONE = 0.9
BETA_TWO = 0.99
INNER_RATE = 0.01
DECAY_RATE = 0.01
ADAM_EPS = 1e-08
OUTER_RATE = 0.7
OUTER_MOMENTUM = 0.9

TN = (((0,), (0,)), ((), ()))
F32 = jnp.float32
BF16 = jnp.bfloat16
LOG2E = 1.4426950408889634
LN2 = 0.6931471805599453
NT = (((1,), (1,)), ((), ()))
TILE = 7
TILE3 = 8


def dot(a, b, dims=(((1,), (0,)), ((), ()))):
    return lax.dot_general(a, b, dims, preferred_element_type=F32)


def two_parts(value):
    top = value.astype(BF16)
    return top, (value - top.astype(F32)).astype(BF16)


def shifted(value, by, keep):
    return jnp.where(keep, pltpu.roll(value, by, 0), 0.0)


CTILE = 7


def vectors(small, height, columns):
    total = small[0] + small[1] + small[2] + small[3]
    lane_group = lax.broadcasted_iota(jnp.int32, (C, C), 0) // (C // NORM_GROUPS)
    same = (lane_group == lax.broadcasted_iota(jnp.int32, (C, C), 1) // (C // NORM_GROUPS)).astype(F32)
    stats = jnp.dot(total[0:8], same, precision=lax.Precision.HIGHEST, preferred_element_type=F32)
    count = height * columns * C // NORM_GROUPS
    mean = stats[0:1] * (1.0 / count)
    spread = lax.rsqrt(stats[1:2] * (1.0 / count) - mean * mean + EPS_NORM)
    film_scale, film_shift = 1.0 + total[2:3], total[3:4]
    gains = total[8:12]
    gain = gains[0:1] * film_scale
    offset = gains[1:2] * film_scale + film_shift
    slope = spread * gain
    return mean, spread, slope, offset - mean * slope, film_scale, gains


def edges(columns):
    place = lax.broadcasted_iota(jnp.int32, (columns, C), 0)
    return place > 0, place < columns - 1


def activate(band, columns, height, noisy, small, conv_w, act3, wt3):
    row0 = lax.axis_index("narrow") * band
    mean, spread, slope, base, film_scale, gains = vectors(small, height, columns)
    not_first, not_last = edges(columns)

    @pl.loop(0, band + 4)
    def _(r):
        scaled = noisy[r].astype(F32) * slope + base
        value = scaled * jax.nn.sigmoid(scaled)
        row = row0 + r - 2
        value = jnp.where(jnp.logical_and(row >= 0, row < height), value, 0.0)
        value = value.astype(BF16).astype(F32)
        act3[r, :, 0:C] = shifted(value, 1, not_first).astype(BF16)
        act3[r, :, C : 2 * C] = value.astype(BF16)
        act3[r, :, 2 * C : 3 * C] = shifted(value, columns - 1, not_last).astype(BF16)

    for tap in range(9):
        rows = slice(tap * C, (tap + 1) * C)
        wt3[rows, :] = conv_w[rows, :].astype(F32).T.astype(BF16)


def convolve_tiles(first, last, band, columns, height, noisy, small, conv_w, act3, conv_s, xhat_s, rs_s, low_s):
    gains = vectors(small, height, columns)[5]
    pix = CTILE * columns

    @pl.loop(first, last)
    def _(t):
        q = jnp.minimum(t * CTILE, band + 2 - CTILE)
        conv = noisy[pl.ds(q + 1, CTILE)].astype(F32).reshape(pix, C)
        for dy in range(3):
            window = act3[pl.ds(q + dy, CTILE)].reshape(pix, 3 * C)
            conv = conv + dot(window, conv_w[dy * 3 * C : (dy + 1) * 3 * C, :])
        centered = conv - jnp.mean(conv, axis=1, keepdims=True)
        rs = lax.rsqrt(jnp.mean(centered * centered, axis=1, keepdims=True) + EPS_NORM)
        xhat = centered * rs
        here = pl.ds(q, CTILE)
        conv_s[here] = conv.reshape(CTILE, columns, C)
        xhat_s[here] = xhat.reshape(CTILE, columns, C)
        rs_s[here] = jnp.broadcast_to(rs, (pix, C)).reshape(CTILE, columns, C)
        low_s[here] = (xhat * gains[2:3] + gains[3:4]).astype(BF16).reshape(CTILE, columns, C)


def main_body(
    start_near, start_far, band, columns, height, heads,
    rest_rows, crop_size, noise_level, aug_level, noisy, target, small, rest, keyval,
    blocks, dconv_w, packet, right,
    act3, wt3, conv_s, xhat_s, rs_s, low_s,
    diff3, m_cat, m_cat_t, n_cat, n_cat_t, conv_t, probs, dscore, y_t, z_t, sums,
    stage, query, out_w,
):
    tok, kv_block = keyval.shape[1:]
    width = heads * HEAD
    per_block = kv_block // HEAD
    narrow = lax.axis_index("narrow")
    row0 = narrow * band
    crop = crop_size[0]
    pix = TILE * columns
    first_query = 9 * C + 2 * LEVELS + 4
    first_out = first_query + C * heads

    def take(first, count, place):
        while count:
            owner, local = divmod(first, rest_rows)
            use = min(count, rest_rows - local)
            a = local // 16 * 16
            b = (local + use + 15) // 16 * 16
            stage[0 : b - a, :] = rest[owner, a:b, :].astype(F32)
            place(stage[local - a : local - a + use, :], use)
            first, count = first + use, count - use

    def filler(ref):
        at = [0]

        def place(value, use):
            ref[at[0] : at[0] + use, :] = value
            at[0] += use

        return place

    take(first_query, C * heads, filler(query))
    take(first_out, width, filler(out_w))
    mean, spread, slope, base, film_scale, gains = vectors(small, height, columns)
    ln_gain = gains[2:3]
    quarter = tok // 4
    masks = [small[owner, 4:5, 0:quarter] for owner in range(4)]
    ok = (jnp.concatenate(masks, axis=1) > 0.0) | (lax.broadcasted_iota(jnp.int32, (1, tok), 1) == 0)
    factor = LOG2E / math.sqrt(HEAD)
    for head in range(heads):
        cols = slice(head * HEAD, (head + 1) * HEAD)
        tcols = slice(head * tok, (head + 1) * tok)
        block, at = head // per_block, head % per_block * HEAD
        query_head = query[pl.ds(head, C, stride=heads), :].astype(BF16)
        out_head = out_w[cols, :].astype(BF16)
        m_head = dot(query_head, keyval[block, :, at : at + HEAD], NT) * factor

        @pl.when(narrow == block)
        def _():
            right[:, at : at + HEAD] = query_head

        @pl.when(narrow == block + heads // per_block)
        def _():
            right[:, at : at + HEAD] = out_w[cols, :].T.astype(BF16)

        top, rest = two_parts(m_head)
        m_cat[:C, tcols] = top
        m_cat[C:, tcols] = rest
        top, rest = two_parts(m_head.T)
        m_cat_t[tcols, :C] = top
        m_cat_t[tcols, C:] = rest
        n_head = dot(keyval[block + heads // per_block, :, at : at + HEAD], out_head)
        top, rest = two_parts(n_head)
        n_cat[tcols, :C] = top
        n_cat[tcols, C:] = rest
        top, rest = two_parts(n_head.T)
        n_cat_t[:C, tcols] = top
        n_cat_t[C:, tcols] = rest
    y_t[...] = jnp.zeros_like(y_t)
    z_t[...] = jnp.zeros_like(z_t)
    conv_t[...] = jnp.zeros_like(conv_t)
    sums[...] = jnp.zeros_like(sums)
    not_first, not_last = edges(columns)
    pix_row = lax.broadcasted_iota(jnp.int32, (pix, C), 0) // columns
    pix_col = lax.broadcasted_iota(jnp.int32, (pix, C), 0) % columns
    @pl.loop(0, pl.cdiv(band + 2, TILE))
    def _(t):
        q = jnp.minimum(t * TILE, band + 2 - TILE)
        here = pl.ds(q, TILE)
        conv = conv_s[here].reshape(pix, C)
        low = low_s[here].reshape(pix, C)
        low2 = jnp.concatenate([low, low], axis=1)
        for head in range(heads):
            tcols = slice(head * tok, (head + 1) * tok)
            if head % 2 == 0:
                scores = dot(low2, m_cat[:, head * tok : (head + 2) * tok])
            score = scores[:, head % 2 * tok : (head % 2 + 1) * tok]
            score = jnp.where(ok, score, -1e30)
            e = jnp.exp2(score - jnp.max(score, axis=1, keepdims=True))
            p = e * (1.0 / jnp.sum(e, axis=1, keepdims=True))
            probs[:, tcols] = p.astype(BF16)
        mixed = dot(probs[...], n_cat[...])
        output = conv + mixed[:, :C] + mixed[:, C:]
        row = row0 + q - 1 + pix_row
        valid = (row >= 0) & (row < crop) & (pix_col < crop)
        err = jnp.where(valid, output - target[pl.ds(q, TILE)].astype(F32).reshape(pix, C), 0.0)
        own_row = q + pix_row
        own = (own_row >= jnp.maximum(t * TILE, 1)) & (own_row <= band)
        err_own = jnp.where(own, err, 0.0)
        sums[4:5, :] += jnp.sum(err_own * err_own, axis=0, keepdims=True)
        dout = 2.0 * err
        dout_low = dout.astype(BF16)
        dout2 = jnp.concatenate([dout_low, dout_low], axis=1)
        for head in range(heads):
            tcols = slice(head * tok, (head + 1) * tok)
            if head % 2 == 0:
                dprobs = dot(dout2, n_cat_t[:, head * tok : (head + 2) * tok])
            dprob = dprobs[:, head % 2 * tok : (head % 2 + 1) * tok]
            p = probs[:, tcols].astype(F32)
            pd = p * dprob
            ds = pd - p * jnp.sum(pd, axis=1, keepdims=True)
            dscore[:, tcols] = ds.astype(BF16)
        dlay2 = dot(dscore[...], m_cat_t[...])
        dlay = (dlay2[:, :C] + dlay2[:, C:]) * LN2
        dlay_own = jnp.where(own, dlay, 0.0)
        xhat = xhat_s[here].reshape(pix, C)
        rs = rs_s[here].reshape(pix, C)
        sums[2:3, :] += jnp.sum(dlay_own * xhat, axis=0, keepdims=True)
        sums[3:4, :] += jnp.sum(dlay_own, axis=0, keepdims=True)
        dxh = dlay * ln_gain
        dconv = dout + rs * (
            dxh
            - jnp.mean(dxh, axis=1, keepdims=True)
            - xhat * jnp.mean(dxh * xhat, axis=1, keepdims=True)
        )
        dout_t = (2.0 * err_own).T.astype(BF16)
        lay_t = jnp.where(own, low.astype(F32), 0.0).T.astype(BF16)
        y_t[...] += dot(dout_t, probs[...])
        z_t[...] += dot(lay_t, dscore[...])
        dconv_t = jnp.where(own, dconv, 0.0).T.astype(BF16)
        for dy in range(3):
            window = act3[pl.ds(q + dy, TILE)].reshape(pix, 3 * C)
            conv_t[:, dy * 3 * C : (dy + 1) * 3 * C] += dot(dconv_t, window)
        for k in range(TILE):
            one = dconv[k * columns : (k + 1) * columns]
            diff3[q + k, :, 0:C] = shifted(one, columns - 1, not_last).astype(BF16)
            diff3[q + k, :, C : 2 * C] = one.astype(BF16)
            diff3[q + k, :, 2 * C : 3 * C] = shifted(one, 1, not_first).astype(BF16)

    def back(t):
        r = t * TILE3
        grad = jnp.zeros((TILE3 * columns, C), F32)
        for dy in range(3):
            window = diff3[pl.ds(r + 2 - dy, TILE3)].reshape(TILE3 * columns, 3 * C)
            grad = grad + dot(window, wt3[dy * 3 * C : (dy + 1) * 3 * C, :])
        x = noisy[pl.ds(r + 2, TILE3)].astype(F32).reshape(TILE3 * columns, C)
        scaled = x * slope + base
        sig = jax.nn.sigmoid(scaled)
        ds = grad * (sig * (1.0 + scaled * (1.0 - sig)))
        sums[0:1, :] += jnp.sum(ds, axis=0, keepdims=True)
        sums[1:2, :] += jnp.sum(ds * ((x - mean) * spread), axis=0, keepdims=True)

    share_rows = dconv_w.shape[1]
    full = conv_t[...].T
    for owner in range(4):
        dconv_w[owner] = full[owner * share_rows : (owner + 1) * share_rows].astype(BF16)
        part = z_t if owner < 2 else y_t
        at = owner % 2 * per_block * tok
        blocks[owner] = part[:, at : at + per_block * tok].astype(BF16)
    start_near()
    halves = band // TILE3 // 2
    pl.loop(0, halves)(back)
    start_far()
    pl.loop(halves, band // TILE3)(back)
    a, b = sums[0:1], sums[1:2]
    packet[0:1] = film_scale * b
    packet[1:2] = film_scale * a
    packet[2:4] = sums[2:4]
    packet[4:5] = gains[0:1] * b + gains[1:2] * a
    packet[5:6] = a
    packet[6:7] = sums[4:5]
    lane = lax.broadcasted_iota(jnp.int32, (1, C), 1)
    facts = jnp.zeros((1, C), F32)
    for k, fact in enumerate((noise_level[0], aug_level[0], crop)):
        facts = jnp.where(lane == k, fact.astype(F32), facts)
    packet[7:8] = jnp.where(row0 == 0, facts, 0.0)


def cross_ids():
    n = lax.axis_index("narrow")
    mate = n + 1 - 2 * lax.rem(n, 2)
    across = lax.rem(n + 2, 4)
    corner = lax.rem(mate + 2, 4)
    return n, mate, across, corner


def to_narrow(src, dst, send_sem, recv_sem, device):
    return pltpu.make_async_remote_copy(
        src_ref=src, dst_ref=dst, send_sem=send_sem, recv_sem=recv_sem,
        device_id={"narrow": device}, device_id_type=MESH,
    )


class Gather:
    def __init__(self, view, sems, ids):
        self.view, self.sems = view, sems
        self.n, self.mate, self.across, self.corner = ids

    def _copy(self, block, slot, device):
        ref = self.view(block)
        return to_narrow(ref, ref, self.sems.at[0, slot], self.sems.at[1, slot], device)

    def start(self):
        self._copy(self.n, 1, self.across).start()
        self._copy(self.n, 0, self.mate).start()

    def relay(self):
        self._copy(self.across, 1, self.across).wait_recv()
        self._copy(self.across, 2, self.mate).start()

    def wait(self):
        self._copy(self.mate, 0, self.mate).wait_recv()
        self._copy(self.corner, 2, self.mate).wait_recv()

    def drain(self):
        self._copy(self.n, 1, self.across).wait_send()
        self._copy(self.n, 0, self.mate).wait_send()
        self._copy(self.across, 2, self.mate).wait_send()


def rest_needs(rest_rows):
    first, last = 9 * C, 9 * C + 2 * LEVELS
    needs = []
    for owner in range(4):
        lo, hi = owner * rest_rows, (owner + 1) * rest_rows
        keep = [r for r in ((lo, min(hi, first)), (max(lo, last), hi)) if r[0] < r[1]]
        assert len(keep) <= 1
        if keep:
            a, b = keep[0][0] - lo, keep[0][1] - lo
            needs.append((a // 16 * 16, (b + 15) // 16 * 16))
        else:
            needs.append(None)
    return needs


KPARTS = 4
WPARTS = 8


def front_body(
    kv_rows, rest_rows, greet, to_group, early, noise_level, aug_level, weights, noisy, target, text, mask,
    noisy_ext, target_ext, text_all, rest_all, keyval, own_kv, small,
    wide_f32, wide_bf, rest_f32, acc,
    w_sem, in_sem, text_sem, rest_sem, kv_sem, small_sem, halo_sem,
):
    ids = cross_ids()
    n, mate, across, corner = ids
    band = noisy.shape[1]
    tokens, depth = text.shape[1:]
    in_text = pltpu.make_async_copy(text.at[0], text_all.at[n], in_sem.at[0])
    in_text.start()
    in_rest = pltpu.make_async_copy(
        weights.at[pl.ds(kv_rows, rest_rows)], rest_f32.at[pl.ds(0, rest_rows)], in_sem.at[1]
    )
    in_rest.start()
    in_noisy = pltpu.make_async_copy(noisy.at[0], noisy_ext.at[pl.ds(2, band)], in_sem.at[2])
    in_noisy.start()
    w_step = kv_rows // WPARTS
    in_w = [
        pltpu.make_async_copy(
            weights.at[pl.ds(k * w_step, w_step)], wide_f32.at[pl.ds(k * w_step, w_step)], w_sem.at[k]
        )
        for k in range(WPARTS)
    ]
    for copy in in_w:
        copy.start()
    in_target = pltpu.make_async_copy(target.at[0], target_ext.at[pl.ds(1, band)], in_sem.at[3])
    in_target.start()
    greet()

    k_step = depth // KPARTS
    texts = [
        Gather(
            lambda b, k=k: text_all.at[b, :, pl.ds(k * k_step, k_step)], text_sem.at[k], ids
        )
        for k in range(KPARTS)
    ]
    in_text.wait()
    for part in texts:
        part.start()

    in_rest.wait()
    rest_f32[rest_rows:] = jnp.zeros((rest_f32.shape[0] - rest_rows, C), F32)
    for k in range(2):
        row_sum = jnp.zeros((1, C), F32)
        for level in (noise_level[0], NOISE_LEVELS + aug_level[0]):
            row = 9 * C + 2 * level + k - n * rest_rows
            found = rest_f32[pl.ds(jnp.clip(row, 0, rest_rows - 1), 1), :]
            found = found.astype(BF16).astype(F32)
            row_sum = row_sum + jnp.where((row >= 0) & (row < rest_rows), found, 0.0)
        small[n, 2 + k : 3 + k, :] = row_sum
    small[n, 4:16, :] = jnp.zeros((12, C), F32)
    for owner in range(4):
        for k in range(4):
            row = 9 * C + 2 * LEVELS + k - owner * rest_rows
            if 0 <= row < rest_rows:
                @pl.when(n == owner)
                def _():
                    small[n, 8 + k : 9 + k, :] = rest_f32[row : row + 1, :].astype(BF16).astype(F32)
    small[n, 4:5, 0:tokens] = mask[...].astype(F32)
    in_noisy.wait()

    def add_row(r, sums):
        x = noisy_ext[r + 2].astype(F32)
        return (
            sums[0] + jnp.sum(x.reshape(-1, 8, C), axis=0),
            sums[1] + jnp.sum((x * x).reshape(-1, 8, C), axis=0),
        )

    zero = jnp.zeros((8, C), F32)
    one, two = lax.fori_loop(0, band, add_row, (zero, zero))
    small[n, 0:1, :] = jnp.sum(one, axis=0, keepdims=True)
    small[n, 1:2, :] = jnp.sum(two, axis=0, keepdims=True)
    others = (mate, across, corner)

    def small_copy(slot, block):
        return to_narrow(
            small.at[block], small.at[block], small_sem.at[0, slot], small_sem.at[1, slot], others[slot]
        )

    for slot in range(3):
        small_copy(slot, n).start()

    in_target.wait()
    up = jnp.maximum(n - 1, 0)
    down = jnp.minimum(n + 1, 3)
    noisy_up = to_narrow(
        noisy_ext.at[pl.ds(2, 2)], noisy_ext.at[pl.ds(band + 2, 2)], halo_sem.at[0, 0], halo_sem.at[1, 0], up
    )
    noisy_down = to_narrow(
        noisy_ext.at[pl.ds(band, 2)], noisy_ext.at[pl.ds(0, 2)], halo_sem.at[0, 1], halo_sem.at[1, 1], down
    )
    target_up = to_narrow(
        target_ext.at[pl.ds(1, 1)], target_ext.at[pl.ds(band + 1, 1)], halo_sem.at[0, 2], halo_sem.at[1, 2], up
    )
    target_down = to_narrow(
        target_ext.at[pl.ds(band, 1)], target_ext.at[pl.ds(0, 1)], halo_sem.at[0, 3], halo_sem.at[1, 3], down
    )

    @pl.when(n > 0)
    def _():
        noisy_up.start()
        target_up.start()

    @pl.when(n < 3)
    def _():
        noisy_down.start()
        target_down.start()

    @pl.when(n == 0)
    def _():
        noisy_ext[0:2] = jnp.zeros((2,) + noisy_ext.shape[1:], BF16)
        target_ext[0:1] = jnp.zeros((1,) + target_ext.shape[1:], BF16)

    @pl.when(n == 3)
    def _():
        noisy_ext[band + 2 : band + 4] = jnp.zeros((2,) + noisy_ext.shape[1:], BF16)
        target_ext[band + 1 : band + 2] = jnp.zeros((1,) + target_ext.shape[1:], BF16)

    needs = rest_needs(rest_rows)
    rest_all[n] = rest_f32[...].astype(BF16)

    def rest_copy(owner, slot, device):
        a, b = needs[owner]
        ref = rest_all.at[owner, pl.ds(a, b - a)]
        return to_narrow(ref, ref, rest_sem.at[0, slot, owner], rest_sem.at[1, slot, owner], device)

    for owner in range(4):
        if needs[owner] is not None:
            @pl.when(n == owner)
            def _():
                rest_copy(owner, 1, across).start()
                rest_copy(owner, 0, mate).start()

    parts = wide_bf.shape[1] // C
    rows = 256
    for k in range(WPARTS):
        in_w[k].wait()

        @pl.loop(k * w_step // parts // rows, (k + 1) * w_step // parts // rows)
        def _(i):
            for j in range(parts):
                wide_bf[pl.ds(pl.multiple_of(i * rows, rows), rows), j * C : (j + 1) * C] = wide_f32[
                    pl.ds(i * rows * parts + j, rows, stride=parts), :
                ].astype(BF16)

    acc[...] = jnp.zeros_like(acc)
    for k in range(KPARTS):
        texts[k].relay()
    for k in range(KPARTS):
        texts[k].wait()

        @pl.loop(0, k_step // 512)
        def _(i):
            at = pl.ds(pl.multiple_of(k * k_step + i * 512, 512), 512)
            acc[...] += dot(text_all[:, :, at].reshape(4 * tokens, 512), wide_bf[at, :])

    keyval[n] = acc[...].astype(BF16)
    own_kv[...] = acc[...].astype(BF16)
    keys = Gather(lambda b: keyval.at[b], kv_sem, ids)
    keys.start()
    to_group()


    def relay_rest(owner):
        if needs[owner] is not None:
            @pl.when(across == owner)
            def _():
                rest_copy(owner, 1, across).wait_recv()
                rest_copy(owner, 2, mate).start()

    def settle_rest(owner):
        if needs[owner] is not None:
            @pl.when(mate == owner)
            def _():
                rest_copy(owner, 0, mate).wait_recv()

            @pl.when(corner == owner)
            def _():
                rest_copy(owner, 2, mate).wait_recv()

            @pl.when(n == owner)
            def _():
                rest_copy(owner, 1, across).wait_send()
                rest_copy(owner, 0, mate).wait_send()

            @pl.when(across == owner)
            def _():
                rest_copy(owner, 2, mate).wait_send()

    relay_rest(0)
    for slot, block in ((0, mate), (1, across), (2, corner)):
        small_copy(slot, block).wait_recv()
        small_copy(slot, n).wait_send()

    @pl.when(n > 0)
    def _():
        noisy_down.wait_recv()
        target_down.wait_recv()
        noisy_up.wait_send()
        target_up.wait_send()

    @pl.when(n < 3)
    def _():
        noisy_up.wait_recv()
        target_up.wait_recv()
        noisy_down.wait_send()
        target_down.wait_send()

    settle_rest(0)
    early(0)
    for owner in range(1, 4):
        relay_rest(owner)
    keys.relay()
    early(1)
    for owner in range(1, 4):
        settle_rest(owner)
    keys.wait()
    keys.drain()
    for part in texts:
        part.drain()


def mid_stages(gd, height, columns, from_group, blocks, conv, packet, right, kvs, texts, *refs):
    (
        dkv_all, conv_all, t_all, small_all, scal,
        near_b, near_c, sum_b, sum_c, far_b, far_c, own_b, own_c, group_b, group_c,
        packets, wides, t_own, t_send, c_send, norms, conv_sum,
        near_sem, far_sem, group_sem, packet_sem, wide_sem, norm_sem, give_sem,
    ) = refs
    ids = cross_ids()
    n, mate, across, corner = ids
    others = (mate, across, corner)
    wide_count = wides.shape[0]
    wide = lax.axis_index("wide")
    group = wide // gd
    spot = lax.rem(wide, gd)
    tok, kv_block = kvs.shape[1:]
    heads = kv_block // HEAD
    depth = texts.shape[-1]
    scale = jnp.where(n < 2, 1.0 / math.sqrt(HEAD), 1.0)

    def lanes(h):
        return pl.ds(h * tok, tok)

    def near(slot, which):
        owner = corner if slot == 0 else mate
        src, dst = ((blocks, near_b), (conv, near_c))[which]
        return to_narrow(
            src.at[owner], dst.at[slot], near_sem.at[0, slot, which], near_sem.at[1, slot, which], mate
        )

    def far(h):
        if h < heads:
            src, dst = sum_b.at[:, lanes(h)], far_b.at[:, lanes(h)]
        else:
            src, dst = sum_c, far_c
        return to_narrow(src, dst, far_sem.at[0, h], far_sem.at[1, h], across)

    def group_copy(k, h):
        if h < heads:
            src, dst = own_b.at[:, lanes(h)], group_b.at[k - 1, :, lanes(h)]
        else:
            src, dst = own_c, group_c.at[k - 1]
        return pltpu.make_async_remote_copy(
            src_ref=src, dst_ref=dst,
            send_sem=group_sem.at[0, h, k - 1], recv_sem=group_sem.at[1, h, k - 1],
            device_id={"wide": group * gd + lax.rem(spot + k, gd)}, device_id_type=MESH,
        )

    def packet_copy(slot, block):
        return to_narrow(
            packets.at[block], packets.at[block],
            packet_sem.at[0, slot], packet_sem.at[1, slot], others[slot],
        )

    def wide_copy(k, block):
        return pltpu.make_async_remote_copy(
            src_ref=wides.at[block], dst_ref=wides.at[block],
            send_sem=wide_sem.at[0, k - 1], recv_sem=wide_sem.at[1, k - 1],
            device_id={"wide": lax.rem(wide + k, wide_count)}, device_id_type=MESH,
        )

    def start_near():
        for slot in range(2):
            for which in range(2):
                near(slot, which).start()

    def start_far():
        near(0, 0).wait_recv()
        sum_b[...] = (blocks[across].astype(F32) + near_b[0].astype(F32)).astype(BF16)
        for h in range(heads):
            far(h).start()
        near(0, 1).wait_recv()
        sum_c[...] = (conv[across].astype(F32) + near_c[0].astype(F32)).astype(BF16)
        far(heads).start()

    q_rows, q_from = 96, 80

    def give_head(src_n, h):
        src, dst = t_send.at[pl.ds(0, q_rows), lanes(h)], t_all.at[src_n, pl.ds(0, q_rows), lanes(h)]
        return to_narrow(src, dst, give_sem.at[0, 0, h], give_sem.at[1, src_n, h], 2)

    def give_tail(src_n, h):
        rows = pl.ds(q_from, C - q_from)
        src, dst = t_send.at[rows, lanes(h)], t_all.at[src_n, rows, lanes(h)]
        return to_narrow(src, dst, give_sem.at[0, 1, h], give_sem.at[1, src_n, h], 3)

    def give_values(h):
        src, dst = t_send.at[:, lanes(h)], t_all.at[2, :, lanes(h)]
        return to_narrow(src, dst, give_sem.at[0, 1, h], give_sem.at[1, 2, h], 3)

    def give_conv(src_n):
        return to_narrow(
            c_send, conv_all.at[src_n], give_sem.at[0, 2, 0], give_sem.at[1, src_n, heads], 0
        )

    def project(k, h, value):
        cols = slice(h * HEAD, (h + 1) * HEAD)
        dkv_all[k * tok : (k + 1) * tok, cols] = (dot(value, right[:, cols], TN) * scale).astype(BF16)
        term = dot(value, kvs[k, :, cols]) * scale
        t_own[:, cols] = term if k == 0 else t_own[:, cols] + term

    def finish(gram):
        packets[n] = packet[...]
        for slot in range(3):
            packet_copy(slot, n).start()
        near(1, 0).wait_recv()
        near(1, 1).wait_recv()
        for h in range(heads):
            far(h).wait_recv()
            at = slice(h * tok, (h + 1) * tok)
            own_b[:, at] = (
                blocks[n, :, at].astype(F32) + near_b[1, :, at].astype(F32) + far_b[:, at].astype(F32)
            ).astype(BF16)
            for k in range(1, gd):
                group_copy(k, h).start()
        for slot, block in enumerate(others):
            packet_copy(slot, block).wait_recv()
        wides[wide] = packets[0] + packets[1] + packets[2] + packets[3]

        @pl.loop(1, wide_count)
        def _(k):
            wide_copy(k, wide).start()

        far(heads).wait_recv()
        conv_sum[...] = conv[n].astype(F32) + near_c[1].astype(F32) + far_c[...].astype(F32)
        own_c[...] = conv_sum[...].astype(BF16)
        for k in range(1, gd):
            group_copy(k, heads).start()
        for h in range(heads):
            project(0, h, own_b[:, h * tok : (h + 1) * tok])
        from_group()
        def text_products(a, firsts):
            rows = slice(a * tok, (a + 1) * tok) if gd <= 4 else slice(0, tok)
            gram[rows, :] = jnp.zeros((tok, gd * tok), F32)

            @pl.loop(0, depth // 1024)
            def _(i):
                at = pl.ds(pl.multiple_of(i * 1024, 1024), 1024)
                left = texts[a, :, :, at].reshape(tok, 1024)
                for b in range(firsts, gd):
                    part = dot(left, texts[b, :, :, at].reshape(tok, 1024), NT)
                    gram[rows, b * tok : (b + 1) * tok] += part

        if gd <= 4:
            for a in range(gd):
                text_products(a, a)
        for h in range(heads):
            for k in range(1, gd):
                group_copy(k, h).wait_recv()
                project(k, h, group_b[k - 1, :, h * tok : (h + 1) * tok])
            at = slice(h * HEAD, (h + 1) * HEAD)
            t_send[:, at] = t_own[:, at].astype(BF16)
            for k in range(4):
                @pl.when(n == k)
                def _():
                    if k < 2:
                        give_head(k, h).start()
                        give_tail(k, h).start()
                    elif k == 2:
                        give_values(h).start()
                    else:
                        t_all[3, :, at] = t_send[:, at]
        for k in range(1, gd):
            group_copy(k, heads).wait_recv()
            conv_sum[...] += group_c[k - 1].astype(F32)
        c_send[...] = conv_sum[...].astype(BF16)
        for k in range(4):
            @pl.when(n == k)
            def _():
                if k > 0:
                    give_conv(k).start()
                else:
                    conv_all[0] = c_send[...]

        @pl.loop(1, wide_count)
        def _(k):
            wide_copy(k, lax.rem(wide + wide_count - k, wide_count)).wait_recv()

        sq = jnp.sum(t_own[...] * t_own[...]) + jnp.sum(conv_sum[...] * conv_sum[...])
        for a in range(gd):
            da = dkv_all[a * tok : (a + 1) * tok, :]
            if gd > 4:
                text_products(a, a)
            rows = slice(a * tok, (a + 1) * tok) if gd <= 4 else slice(0, tok)
            for b in range(a, gd):
                db = dkv_all[b * tok : (b + 1) * tok, :]
                top, low = two_parts(gram[rows, b * tok : (b + 1) * tok])
                part = jnp.sum(da.astype(F32) * (dot(top, db) + dot(low, db)))
                sq = sq + (part if a == b else 2.0 * part)
        gains = jnp.zeros((4, C), F32)
        shared = jnp.zeros((1, C), F32)
        for a in range(gd):
            mine = wides[group * gd + a]
            small_all[a] = mine
            gains = gains + mine[0:4]
            for b in range(gd):
                his = wides[group * gd + b]
                same = (mine[7:8, 0:1] == his[7:8, 0:1]).astype(F32) + (mine[7:8, 1:2] == his[7:8, 1:2]).astype(F32)
                shared = shared + same * (mine[4:5] * his[4:5] + mine[5:6] * his[5:6])
        shared_sq = jnp.sum(gains * gains) + jnp.sum(shared)
        norms[n] = jnp.full((8, C), sq + jnp.where(n == 0, shared_sq, 0.0), F32)

        def norm_copy(slot, block):
            return to_narrow(
                norms.at[block], norms.at[block], norm_sem.at[0, slot], norm_sem.at[1, slot], others[slot]
            )

        for slot in range(3):
            norm_copy(slot, n).start()

        def tally(k, found):
            there = wides[k]
            crop = there[7:8, 2:3]
            pixels = jnp.minimum(crop, float(height)) * jnp.minimum(crop, float(columns))
            mine = jnp.where(k // gd == group, pixels, 0.0)
            return found[0] + pixels, found[1] + mine, found[2] + jnp.sum(there[6:7], axis=1, keepdims=True)

        none = jnp.zeros((1, 1), F32)
        total, own_count, loss = lax.fori_loop(0, wide_count, tally, (none, none, none))
        for slot, block in enumerate(others):
            norm_copy(slot, block).wait_recv()
        squares = norms[0, 0:1] + norms[1, 0:1] + norms[2, 0:1] + norms[3, 0:1]
        norm = jnp.sqrt(squares) / total
        scal[0:1] = jnp.minimum(1.0, CLIP_NORM / norm) / total
        scal[1:2] = jnp.broadcast_to(INNER_RATE * own_count / total, (1, C))
        scal[2:3] = jnp.broadcast_to(loss, (1, C))
        scal[3:4] = jnp.broadcast_to(total, (1, C))
        scal[4:8] = jnp.zeros((4, C), F32)

        for k in range(4):
            @pl.when(n == k)
            def _():
                for h in range(heads):
                    if k < 2:
                        give_head(k, h).wait_send()
                        give_tail(k, h).wait_send()
                    if k == 2:
                        give_values(h).wait_send()
                        give_head(0, h).wait_recv()
                        give_head(1, h).wait_recv()
                    if k == 3:
                        give_tail(0, h).wait_recv()
                        give_tail(1, h).wait_recv()
                        give_values(h).wait_recv()
                if k > 0:
                    give_conv(k).wait_send()
                else:
                    for j in range(1, 4):
                        give_conv(j).wait_recv()
        for slot in range(2):
            for which in range(2):
                near(slot, which).wait_send()
        for h in range(heads + 1):
            far(h).wait_send()
            for k in range(1, gd):
                group_copy(k, h).wait_send()
        for slot in range(3):
            packet_copy(slot, n).wait_send()
            norm_copy(slot, n).wait_send()

        @pl.loop(1, wide_count)
        def _(k):
            wide_copy(k, wide).wait_send()

    return start_near, start_far, finish


def step_kernel(gd, wide_count, kv_rows, rest_rows, band, columns, counts, *refs):
    refs = list(refs)
    noise_level, aug_level, crop_size, weights, noisy, target, text, first, second, mask = refs[:10]
    texts, dkv_all, conv_all, t_all, small_all, scal, first_near, second_near = refs[10:18]
    n_front, n_main, n_mid = counts
    at = 18
    (noisy_ext, target_ext, rest_all, keyval, kvs, small) = refs[at : at + 6]
    act3, wt3, conv_s, xhat_s, rs_s, low_s = refs[at + 6 : at + 12]
    at += 12
    front_sems = refs[at : at + n_front]
    at += n_front
    (blocks, conv, packet, right) = refs[at : at + 4]
    at += 4
    mid_refs = refs[at : at + n_mid]
    at += n_mid
    group_text_sem, ahead_sem = refs[at], refs[at + 1]
    ahead = [
        pltpu.make_async_copy(far, near, ahead_sem.at[k])
        for k, (far, near) in enumerate(((first, first_near), (second, second_near)))
    ]
    n, mate, across, corner = cross_ids()
    wide = lax.axis_index("wide")
    group, spot = wide // gd, lax.rem(wide, gd)
    tok, kv_block = kvs.shape[1:]
    depth = text.shape[2]
    barrier = pltpu.get_barrier_semaphore()
    for other in (mate, across, corner):
        pl.semaphore_signal(barrier, inc=1, device_id={"narrow": other}, device_id_type=MESH)

    @pl.loop(1, wide_count)
    def _(k):
        pl.semaphore_signal(
            barrier, inc=1, device_id={"wide": lax.rem(wide + k, wide_count)}, device_id_type=MESH
        )

    def greet():
        pl.semaphore_wait(barrier, 3 + wide_count - 1)

    def group_send(k, which):
        buf = (texts, kvs)[which]
        return pltpu.make_async_remote_copy(
            src_ref=buf.at[0], dst_ref=buf.at[k],
            send_sem=group_text_sem.at[0, which, k - 1], recv_sem=group_text_sem.at[1, which, k - 1],
            device_id={"wide": group * gd + lax.rem(spot + k, gd)}, device_id_type=MESH,
        )

    def to_group():
        for which in (1, 0):
            for k in range(1, gd):
                group_send(k, which).start()

    def from_group():
        for which in (1, 0):
            for k in range(1, gd):
                group_send(k, which).wait_recv()
                group_send(k, which).wait_send()

    def early(part):
        common = (band, columns, H, noisy_ext, small, rest_all.at[0], act3)
        tiles = pl.cdiv(band + 2, CTILE)
        if part == 0:
            activate(*common, wt3)
        bounds = (0, 2) if part == 0 else (2, tiles)
        convolve_tiles(*bounds, *common, conv_s, xhat_s, rs_s, low_s)

    def front(wide_f32, wide_bf, rest_f32, acc):
        front_body(
            kv_rows, rest_rows, greet, to_group, early, noise_level, aug_level, weights, noisy, target, text, mask,
            noisy_ext, target_ext, texts.at[0], rest_all, keyval, kvs.at[0], small,
            wide_f32, wide_bf, rest_f32, acc, *front_sems,
        )

    V = pltpu.VMEM
    pl.run_scoped(
        front, V((kv_rows, C), F32), V((depth, kv_block), BF16), V((rest_all.shape[1], C), F32),
        V((tok, kv_block), F32),
    )
    for copy in ahead:
        copy.start()
    pix = TILE * columns

    start_near, start_far, finish = mid_stages(
        gd, H, W, from_group, blocks, conv, packet, right, kvs, texts,
        dkv_all, conv_all, t_all, small_all, scal, *mid_refs,
    )

    def main(*scratch):
        main_body(
            start_near, start_far, band, columns, H, HEADS, rest_rows, crop_size, noise_level, aug_level,
            noisy_ext, target_ext, small, rest_all, keyval, blocks, conv, packet, right,
            act3, wt3, conv_s, xhat_s, rs_s, low_s, *scratch,
        )

    pl.run_scoped(
        main,
        V((band + 2, columns, 3 * C), BF16),
        V((2 * C, HEADS * tok), BF16),
        V((HEADS * tok, 2 * C), BF16),
        V((HEADS * tok, 2 * C), BF16),
        V((2 * C, HEADS * tok), BF16),
        V((C, 9 * C), F32),
        V((pix, HEADS * tok), BF16),
        V((pix, HEADS * tok), BF16),
        V((C, HEADS * tok), F32),
        V((C, HEADS * tok), F32),
        V((8, C), F32),
        V((rest_all.shape[1], C), F32),
        V((C * HEADS, C), F32),
        V((HEADS * HEAD, C), F32),
    )

    pl.run_scoped(finish, V((gd * tok if gd <= 4 else tok, gd * tok), F32))
    for copy in ahead:
        copy.wait()


def near(gd):
    return pltpu.VMEM if gd <= 4 else jax.ShapeDtypeStruct


def hold(value, gd):
    return pltpu.with_memory_space_constraint(value, pltpu.VMEM) if gd <= 4 else value


def far(value):
    return pltpu.with_memory_space_constraint(value, pltpu.HBM)


def run_step(
    gd, wide_count, noise_level, aug_level, crop_size, weights2, noisy, target, text, first, second, mask
):
    _, band, columns, _ = noisy.shape
    _, tokens, depth = text.shape
    tok = 4 * tokens
    kv_block = 2 * HEADS * HEAD // 4
    kv_rows = depth * kv_block // C
    rest_rows = weights2.shape[0] - kv_rows
    rest_pad = (rest_rows + 15) // 16 * 16
    assert 9 * C <= rest_rows and kv_block % HEAD == 0 and HEAD == C
    vmem = pl.BlockSpec(memory_space=pltpu.VMEM)
    smem = pl.BlockSpec(memory_space=pltpu.SMEM)
    hbm = pl.BlockSpec(memory_space=pltpu.HBM)
    D, V = pltpu.SemaphoreType.DMA, pltpu.VMEM
    few = max(gd - 1, 1)
    heads = kv_block // HEAD
    bshape, cshape = (C, kv_block // HEAD * tok), (9 * C // 4, C)
    front_sems = [D((WPARTS,)), D((4,)), D((KPARTS, 2, 3)), D((2, 3, 4)), D((2, 3)), D((2, 3)), D((2, 4))]
    mid_refs = [
        V((2,) + bshape, BF16), V((2,) + cshape, BF16), V(bshape, BF16), V(cshape, BF16),
        V(bshape, BF16), V(cshape, BF16), V(bshape, BF16), V(cshape, BF16),
        V((few,) + bshape, BF16), V((few,) + cshape, BF16),
        V((4, 8, C), F32), V((wide_count, 8, C), F32),
        V((C, kv_block), F32), V((C, kv_block), BF16), V(cshape, BF16),
        V((4, 8, C), F32), V(cshape, F32),
        D((2, 2, 2)), D((2, heads + 1)), D((2, heads + 1, few)), D((2, 3)), D((2, wide_count)), D((2, 3)),
        D((2, 4, heads + 1)),
    ]
    return pl.pallas_call(
        functools.partial(
            step_kernel, gd, wide_count, kv_rows, rest_rows, band, columns,
            (len(front_sems), 0, len(mid_refs)),
        ),
        out_shape=tuple(
            near(gd)(shape, kind)
            for shape, kind in (
                ((gd, 4, tokens, depth), BF16),
                ((gd * tok, kv_block), BF16),
                ((4,) + cshape, BF16),
                ((4, C, kv_block), BF16),
                ((gd, 8, C), F32),
                ((8, C), F32),
                (first.shape, F32),
                (first.shape, F32),
            )
        ),
        in_specs=[smem] * 3 + [hbm] * 6 + [vmem],
        out_specs=(vmem,) * 8,
        scratch_shapes=[
            V((band + 4, columns, C), BF16), V((band + 2, columns, C), BF16), V((4, rest_pad, C), BF16),
            V((4, tok, kv_block), BF16), V((gd, tok, kv_block), BF16), V((4, 16, C), F32),
            V((band + 4, columns, 3 * C), BF16), V((9 * C, C), BF16),
            *[V((band + 2, columns, C), F32)] * 3, V((band + 2, columns, C), BF16),
            *front_sems,
            V((4,) + bshape, BF16), V((4,) + cshape, BF16), V((8, C), F32), V((C, kv_block), BF16),
            *mid_refs,
            D((2, 2, few)),
            D((2,)),
        ],
        compiler_params=pltpu.CompilerParams(
            collective_id=1, has_side_effects=True, vmem_limit_bytes=(STEP_VMEM if gd <= 4 else 58) * 2**20
        ),
        name="step",
    )(noise_level, aug_level, crop_size, *map(far, (weights2, noisy, target, text, first, second)), mask)


STEP_VMEM = 48


AROWS = 1024


def adam_tiles(length):
    return pl.cdiv(length + 17 * C, AROWS * C)


def adam_kernel(
    gd, length, kv_rows, rest_rows, *refs,
):
    (
        texts, dkv, conv, t_all, small, scal, first, second, first_out, second_out, step_out,
        nat, rest, turned_dkv, edge, shift, carry,
    ) = refs
    s = pl.program_id(0)
    tok = dkv.shape[0] // gd
    n = lax.axis_index("narrow")
    start = lax.rem(lax.axis_index("wide"), gd) * length
    row0 = start // C
    lane0, row_off, row_shift, block0 = lax.rem(start, C), lax.rem(row0, AROWS), lax.rem(row0, 16), row0 // AROWS
    wrap = C - lane0
    kv_blocks = kv_rows // AROWS
    parts = dkv.shape[1] // C
    cols_tile = AROWS // parts

    def iotas(rows):
        shape = (rows, C)
        return lax.broadcasted_iota(jnp.int32, shape, 0), lax.broadcasted_iota(jnp.int32, shape, 1)

    def natural(tile):
        block = block0 + tile
        here = pl.multiple_of(tile * AROWS + 8, 8)

        @pl.when(block < kv_blocks)
        def _():
            at = pl.ds(pl.multiple_of(block * cols_tile, cols_tile), cols_tile)
            text = jnp.concatenate([texts[k, :, :, at].reshape(tok, cols_tile) for k in range(gd)], axis=0)
            grad = dot(text, turned_dkv[...], TN)
            for j in range(parts - 1):
                nat[pl.ds(here + j, cols_tile, stride=parts), :] = grad[:, j * C : (j + 1) * C]
            part = grad[:, (parts - 1) * C :]
            row, lane = iotas(cols_tile)
            before = jnp.where(row == 0, edge[0:1, :], pltpu.roll(part, 1, 0))
            nat[pl.ds(here - 1, cols_tile, stride=parts), :] = jnp.where(lane < wrap, before, part)
            edge[0:1, :] = part[cols_tile - 1 : cols_tile, :]

        @pl.when(block >= kv_blocks)
        def _():
            at = pl.multiple_of(jnp.minimum((block - kv_blocks) * AROWS, rest.shape[0] - 16 - AROWS), 8)
            row, lane = iotas(AROWS)
            both = jnp.where(lane >= lane0, rest[pl.ds(at + 8, AROWS), :], rest[pl.ds(at + 9, AROWS), :])
            nat[pl.ds(here, AROWS), :] = pltpu.roll(both, wrap, 1)

            @pl.when(block == kv_blocks)
            def _():
                row, lane = iotas(8)
                ahead = pltpu.roll(rest[8:16, :], wrap, 1)
                nat[pl.ds(here - 1, 1), :] = jnp.where(lane < wrap, edge[...], ahead)[0:1, :]

    def assemble():
        first_table, first_gain = 9 * C, 9 * C + 2 * LEVELS
        first_query = first_gain + 4
        first_out = first_query + C * HEADS
        quarter = conv.shape[1]
        width = dkv.shape[1]
        heads = width // HEAD
        for owner in range(4):
            lo, hi = owner * rest_rows, (owner + 1) * rest_rows

            @pl.when(n == owner)
            def _():
                for k in range(4):
                    a, b = max(lo, k * quarter), min(hi, (k + 1) * quarter)
                    if a < b:
                        assert (a, b) == (k * quarter, (k + 1) * quarter)
                        rest[8 + a - lo : 8 + b - lo, :] = conv[k].astype(F32)
                a, b = max(lo, first_query), min(hi, first_out)
                if a < b:
                    for h in range(HEADS):
                        c0 = max(0, -(-(a - first_query - h) // HEADS))
                        c1 = min(C, -(-(b - first_query - h) // HEADS))
                        cols = slice(h % heads * HEAD, h % heads * HEAD + HEAD)
                        c_lo, c_hi = c0 // 16 * 16, (c1 + 15) // 16 * 16
                        value = t_all[h // heads, c_lo:c_hi, cols].astype(F32)
                        start = first_query + c0 * HEADS + h - lo
                        rest[pl.ds(8 + start, c1 - c0, stride=HEADS), :] = value[c0 - c_lo : c1 - c_lo]
                for h in range(HEADS):
                    a, b = first_out + h * HEAD, first_out + (h + 1) * HEAD
                    if lo <= a and b <= hi:
                        cols = slice(h % heads * HEAD, h % heads * HEAD + HEAD)
                        rest[8 + a - lo : 8 + b - lo, :] = t_all[2 + h // heads, :, cols].astype(F32).T
                    else:
                        assert b <= lo or hi <= a
                if lo <= first_gain and first_gain + 4 <= hi:
                    total = small[0, 0:4]
                    for k in range(1, gd):
                        total = total + small[k, 0:4]
                    rest[8 + first_gain - lo : 8 + first_gain + 4 - lo, :] = total


        for k in range(gd):
            for level, shift_by in ((0, 0), (1, NOISE_LEVELS)):
                found = jnp.max(small[k, 7:8, level : level + 1]).astype(jnp.int32) + shift_by
                for half in range(2):
                    at_row = first_table + 2 * found + half - n * rest_rows

                    @pl.when((at_row >= 0) & (at_row < rest_rows))
                    def _():
                        rest[pl.ds(at_row + 8, 1), :] += small[k, 4 + half : 5 + half]

    @pl.when(s == 0)
    def _():
        edge[...] = jnp.zeros_like(edge)
        rest[...] = jnp.zeros_like(rest)
        carry[...] = jnp.zeros_like(carry)
        shift[...] = jnp.zeros_like(shift)
        row, lane = iotas(dkv.shape[0])
        moved = [
            pltpu.roll(dkv[:, j * C : (j + 1) * C].astype(F32), wrap, 1) for j in range(parts)
        ]
        for j in range(parts):
            turned_dkv[:, j * C : (j + 1) * C] = jnp.where(
                lane < wrap, moved[j], moved[(j + 1) % parts]
            ).astype(BF16)

        @pl.when(start + length > kv_rows * C)
        def _():
            assemble()

        natural(0)

    natural(s + 1)
    row, lane = iotas(AROWS)
    g = nat[pl.ds(s * AROWS + row_off + 8, AROWS), :] * scal[0:1]
    one = BETA_ONE * first.reshape(AROWS, C)[...] + (1.0 - BETA_ONE) * g
    two = BETA_TWO * second.reshape(AROWS, C)[...] + (1.0 - BETA_TWO) * g * g
    first_out.reshape(AROWS, C)[...] = one
    second_out.reshape(AROWS, C)[...] = two
    fixed_one = one * (scal[1:2] * (1.0 / (1.0 - BETA_ONE**STEP)))
    fixed_two = two * (1.0 / (1.0 - BETA_TWO**STEP))
    root = fixed_two * lax.rsqrt(fixed_two)
    step = fixed_one * pl.reciprocal(root + ADAM_EPS, approx=True)
    step = jnp.where((s * AROWS + row) * C + lane < length, step, 0.0)
    turned = pltpu.roll(step, lane0, 1)
    above = pltpu.roll(turned, 1, 0)
    above = jnp.where(row == 0, carry[0:1, :], above)
    carry[0:1, :] = turned[AROWS - 1 : AROWS, :]
    shift[pl.ds(row_shift, AROWS), :] = jnp.where(lane < lane0, above, turned)
    step_out[...] = shift[0:AROWS, :].astype(BF16)
    shift[0:16, :] = shift[AROWS : AROWS + 16, :]


def run_adam(texts, dkv, conv, t_all, small, scal, first, second, length, kv_rows, rest_rows):
    gd = texts.shape[0]
    tiles = adam_tiles(length)
    flat = pl.BlockSpec((1, AROWS * C), lambda s: (0, s))
    rest_pad = (pl.cdiv(rest_rows, AROWS) + 1) * AROWS + 16
    return pl.pallas_call(
        functools.partial(adam_kernel, gd, length, kv_rows, rest_rows),
        out_shape=(
            jax.ShapeDtypeStruct((1, length), F32),
            jax.ShapeDtypeStruct((1, length), F32),
            near(gd)((tiles * AROWS, C), BF16),
        ),
        grid=(tiles,),
        in_specs=[pl.BlockSpec(memory_space=pltpu.VMEM)] * 6 + [flat, flat],
        out_specs=[flat, flat, pl.BlockSpec((AROWS, C), lambda s: (s, 0))],
        scratch_shapes=[
            pltpu.VMEM(((tiles + 1) * AROWS + 16, C), F32),
            pltpu.VMEM((rest_pad, C), F32),
            pltpu.VMEM(dkv.shape, BF16),
            pltpu.VMEM((8, C), F32),
            pltpu.VMEM((AROWS + 16, C), F32),
            pltpu.VMEM((8, C), F32),
        ],
        compiler_params=pltpu.CompilerParams(vmem_limit_bytes=ADAM_VMEM),
        name="adam",
    )(*(hold(v, gd) for v in (texts, dkv, conv, t_all, small, scal, first, second)))


ADAM_VMEM = 24 * 2**20


def share_kernel(
    gd, rows, chunk, pad, l1, l2, u_ref, w_far, o_far, out_ref, w_near, o_near,
    recv_a, recv_b, part, in_sem, s_u, s_fo, s_fi, s_y, r_a, r_b, r_f, r_y,
):
    loads = [
        pltpu.make_async_copy(w_far, w_near.at[pl.ds(0, w_far.shape[0])], in_sem.at[1]),
        pltpu.make_async_copy(o_far, o_near.at[pl.ds(0, o_far.shape[0])], in_sem.at[2]),
    ]
    wide = lax.axis_index("wide")
    g = wide // gd
    spot = wide % gd
    chunks = rows // chunk
    is_outer = jnp.logical_or(g == 0, g == GROUPS - 1)
    is_inner = jnp.logical_not(is_outer)
    low = g < GROUPS // 2
    outer_id = jnp.where(low, g - 1, g + 1) * gd + spot
    mate_id = jnp.where(low, g + 1, g - 1) * gd + spot
    barrier = pltpu.get_barrier_semaphore()
    for k in range(1, gd):
        other = g * gd + lax.rem(spot + k, gd)
        pl.semaphore_signal(barrier, inc=1, device_id={"wide": other}, device_id_type=MESH)
    pl.semaphore_signal(barrier, inc=1, device_id={"wide": mate_id}, device_id_type=MESH)
    @pl.when(is_inner)
    def _():
        pl.semaphore_signal(barrier, inc=1, device_id={"wide": outer_id}, device_id_type=MESH)
        pl.semaphore_wait(barrier, gd + 1)
    @pl.when(is_outer)
    def _():
        pl.semaphore_wait(barrier, gd)

    def sl(c):
        return pl.ds(pl.multiple_of(c * chunk, chunk), chunk)
    def ol(c):
        return pl.ds(pl.multiple_of(pad + c * chunk, 16), chunk)
    def copy(src, dst, ss, rs, dev):
        return pltpu.make_async_remote_copy(src_ref=src, dst_ref=dst, send_sem=ss, recv_sem=rs,
                                            device_id={"wide": dev}, device_id_type=MESH)
    def send_a(c):
        return copy(u_ref.at[sl(c)], recv_a.at[sl(c)], s_u.at[c], r_a.at[c], mate_id)
    def send_b(c):
        return copy(part.at[sl(c)], recv_b.at[sl(c)], s_u.at[c], r_b.at[c], mate_id)
    def send_fo(c):
        return copy(out_ref.at[spot, ol(c)], out_ref.at[spot, ol(c)], s_fo.at[c], r_f.at[c], outer_id)
    def send_fi(c):
        return copy(out_ref.at[spot, ol(c)], out_ref.at[spot, ol(c)], s_fi.at[c], r_f.at[c], mate_id)
    def send_y(c, k):
        return copy(out_ref.at[spot, ol(c)], out_ref.at[spot, ol(c)], s_y.at[k - 1, c], r_y.at[k - 1, c],
                    g * gd + lax.rem(spot + k, gd))
    def wait_y(c, k):
        src = lax.rem(spot + gd - k, gd)
        copy(out_ref.at[src, ol(c)], out_ref.at[src, ol(c)], s_y.at[k - 1, c], r_y.at[k - 1, c], wide).wait_recv()
    def spread(c):
        for k in range(1, gd):
            send_y(c, k).start()
    def is_root(c):
        return lax.rem(c + g, 2) == 1

    @pl.when(is_outer)
    def _():
        @pl.loop(0, chunks)
        def _(c):
            send_a(c).start()
    for load in loads:
        load.start()
    for p in range(gd):
        out_ref[p, 0:pad] = jnp.zeros((pad, 128), jnp.bfloat16)
        out_ref[p, pad + rows : rows + 2 * pad] = jnp.zeros((pad, 128), jnp.bfloat16)

    @pl.when(is_outer)
    def _():
        @pl.loop(0, chunks)
        def _(c):
            send_fo(c).wait_recv()
            spread(c)
    @pl.when(is_inner)
    def _():
        @pl.loop(0, chunks + l2)
        def _(c):
            @pl.when(jnp.logical_and(c < chunks, jnp.logical_not(is_root(c))))
            def _():
                send_a(c).wait_recv()
                part[sl(c)] = (u_ref[sl(c)].astype(jnp.float32) + recv_a[sl(c)].astype(jnp.float32)).astype(jnp.bfloat16)
                send_b(c).start()
            d = c - l1
            @pl.when(jnp.logical_and(jnp.logical_and(d >= 0, d < chunks), is_root(d)))
            def _():
                send_a(d).wait_recv()
                send_b(d).wait_recv()
                out_ref[spot, ol(d)] = (u_ref[sl(d)].astype(jnp.float32) + recv_a[sl(d)].astype(jnp.float32) + recv_b[sl(d)].astype(jnp.float32)).astype(jnp.bfloat16)
                send_fo(d).start()
                send_fi(d).start()
                spread(d)
            e = c - l2
            @pl.when(jnp.logical_and(e >= 0, jnp.logical_not(is_root(e))))
            def _():
                send_fi(e).wait_recv()
                send_fo(e).start()
                spread(e)
    @pl.loop(0, chunks)
    def _(c):
        for k in range(1, gd):
            wait_y(c, k)
            send_y(c, k).wait_send()
        @pl.when(is_outer)
        def _():
            send_a(c).wait_send()
        @pl.when(is_inner)
        def _():
            send_fo(c).wait_send()
            @pl.when(is_root(c))
            def _():
                send_fi(c).wait_send()
            @pl.when(jnp.logical_not(is_root(c)))
            def _():
                send_b(c).wait_send()
    for load in loads:
        load.wait()


def share(u, weights2, outer2, gd, rows, chunk, pad, l1, l2):
    n = rows // chunk
    D = pltpu.SemaphoreType.DMA
    few = max(gd - 1, 1)
    held = pl.cdiv(weights2.shape[0], 256) * 256
    vmem, hbm = pl.BlockSpec(memory_space=pltpu.VMEM), pl.BlockSpec(memory_space=pltpu.HBM)
    return pl.pallas_call(
        functools.partial(share_kernel, gd, rows, chunk, pad, l1, l2),
        out_shape=(near(gd)((gd, rows + 2 * pad, C), BF16),) + (near(gd)((held, C), F32),) * 2,
        in_specs=[vmem, hbm, hbm],
        out_specs=(vmem,) * 3,
        scratch_shapes=[pltpu.VMEM((rows, C), BF16)] * 3
        + [
            D((3,)), D((n,)), D((n,)), D((n,)), D((few, n)),
            D((n,)), D((n,)), D((n,)), D((few, n)),
        ],
        compiler_params=pltpu.CompilerParams(
            collective_id=9, has_side_effects=True, vmem_limit_bytes=SHARE_VMEM
        ),
        name="share",
    )(hold(u, gd), far(weights2), far(outer2))


SHARE_VMEM = 32 * 2**20


def final_kernel(bases, pad, block, weights, outer, pieces, scal, new_weights, momentum, loss, count, held, sem):
    rows = new_weights.shape[0]
    total = pieces.shape[1]
    steps = pl.cdiv(rows, block)

    def writes(b, slot, size):
        here = pl.ds(b * block, size)
        return [
            pltpu.make_async_copy(held.at[slot, k, pl.ds(0, size)], out.at[here], sem.at[slot, k])
            for k, out in enumerate((new_weights, momentum))
        ]

    for b in range(steps):
        slot = b % 3
        size = min(block, rows - b * block)
        if b >= 3:
            for copy in writes(b - 3, slot, block):
                copy.wait()
        averaged = jnp.zeros((block, C), F32)
        for p, base in enumerate(bases):
            at = min(max(b * block - base + pad, 0), total - block)
            averaged = averaged + pieces[p, at : at + block, :].astype(F32)
        w = weights[b * block : (b + 1) * block, :]
        averaged = averaged + (INNER_RATE * DECAY_RATE) * w
        moved = OUTER_MOMENTUM * outer[b * block : (b + 1) * block, :] + averaged
        held[slot, 1] = moved
        held[slot, 0] = w - OUTER_RATE * (averaged + OUTER_MOMENTUM * moved)
        for copy in writes(b, slot, size):
            copy.start()
    loss[0] = jnp.max(scal[2:3])
    count[0] = jnp.max(scal[3:4])
    for b in range(max(steps - 3, 0), steps):
        for copy in writes(b, b % 3, min(block, rows - b * block)):
            copy.wait()


def run_final(rows, weights2, outer2, pieces, scal, bases, pad):
    hbm, smem = pl.BlockSpec(memory_space=pltpu.HBM), pl.BlockSpec(memory_space=pltpu.SMEM)
    block = weights2.shape[0] // 16
    assert block % 16 == 0 and block <= pad
    return pl.pallas_call(
        functools.partial(final_kernel, bases, pad, block),
        out_shape=(jax.ShapeDtypeStruct((rows, C), F32),) * 2 + (jax.ShapeDtypeStruct((1,), F32),) * 2,
        in_specs=[pl.BlockSpec(memory_space=pltpu.VMEM)] * 4,
        out_specs=(hbm, hbm, smem, smem),
        scratch_shapes=[pltpu.VMEM((3, 2, block, C), F32), pltpu.SemaphoreType.DMA((3, 2))],
        compiler_params=pltpu.CompilerParams(vmem_limit_bytes=12 * 2**20),
        name="final",
    )(*(hold(v, len(bases)) for v in (weights2, outer2, pieces, scal)))


def per_device(
    weights, first_moment, second_moment, outer_momentum, noisy_input, target,
    text_tokens, text_mask, noise_level, aug_level, crop_size,
):
    length = first_moment.shape[1]
    wide_count = lax.axis_size("wide")
    gd = wide_count // GROUPS
    weights2 = weights.reshape(-1, C)
    outer2 = outer_momentum.reshape(-1, C)

    texts, dkv, conv_all, t_all, small_all, scal, first, second = run_step(
        gd, wide_count, noise_level, aug_level, crop_size, weights2, noisy_input, target, text_tokens,
        first_moment, second_moment, text_mask,
    )
    kv_rows = TEXT_D * dkv.shape[1] // C
    rest_rows = weights2.shape[0] - kv_rows
    moment_one, moment_two, step = run_adam(
        texts, dkv, conv_all, t_all, small_all, scal, first, second, length, kv_rows, rest_rows
    )
    chunk = 160
    rows = pl.cdiv(length // C + 18, chunk) * chunk
    pad = 1120
    pieces, w_near, o_near = share(step, weights2, outer2, gd, rows, chunk, pad, 3, 6)
    bases = [p * length // C // 16 * 16 for p in range(gd)]
    new_weights, momentum_out, loss, count = run_final(
        weights2.shape[0], w_near, o_near, pieces, scal, bases, pad
    )
    return (
        new_weights.reshape(-1), momentum_out.reshape(-1), moment_one, moment_two,
        loss, count,
    )


def solution(mesh):
    placed = (
        P("narrow"),
        P("narrow", "wide"),
        P("narrow", "wide"),
        P("narrow"),
        P("wide", "narrow", None, None),
        P("wide", "narrow", None, None),
        P("wide", "narrow", None),
        P("wide", "narrow"),
        P("wide"),
        P("wide"),
        P("wide"),
    )
    return jax.shard_map(
        per_device,
        mesh=mesh,
        in_specs=placed,
        out_specs=(P("narrow"), P("narrow"), P("narrow", "wide"), P("narrow", "wide"), P(), P()),
        check_vma=False,
    )
```

```python
import functools
import math

import jax
import jax.numpy as jnp
from jax import lax
from jax.experimental import pallas as pl
from jax.experimental.pallas import tpu as pltpu
from jax.sharding import PartitionSpec as P

MESH = pl.DeviceIdType.MESH
C = 128
NORM_GROUPS = 32
HEADS = 8
HEAD = 128
TEXT_D = 4096
H = 128
W = 128
NOISE_LEVELS = 1000
AUG_LEVELS = 24
LEVELS = NOISE_LEVELS + AUG_LEVELS
GROUPS = 4
STEP = 8


EPS_NORM = 1e-05
CLIP_NORM = 0.002
BETA_ONE = 0.9
BETA_TWO = 0.99
INNER_RATE = 0.01
DECAY_RATE = 0.01
ADAM_EPS = 1e-08
OUTER_RATE = 0.7
OUTER_MOMENTUM = 0.9

TN = (((0,), (0,)), ((), ()))
F32 = jnp.float32
BF16 = jnp.bfloat16
LOG2E = 1.4426950408889634
LN2 = 0.6931471805599453
NT = (((1,), (1,)), ((), ()))
TILE = 8
TILE3 = 8


def dot(a, b, dims=(((1,), (0,)), ((), ()))):
    return lax.dot_general(a, b, dims, preferred_element_type=F32)


def two_parts(value):
    top = value.astype(BF16)
    return top, (value - top.astype(F32)).astype(BF16)


def shifted(value, by, keep):
    return jnp.where(keep, pltpu.roll(value, by, 0), 0.0)


CTILE = 16


def vectors(small, height, columns):
    total = small[0] + small[1] + small[2] + small[3]
    lane_group = lax.broadcasted_iota(jnp.int32, (C, C), 0) // (C // NORM_GROUPS)
    same = (lane_group == lax.broadcasted_iota(jnp.int32, (C, C), 1) // (C // NORM_GROUPS)).astype(F32)
    stats = jnp.dot(total[0:8], same, precision=lax.Precision.HIGHEST, preferred_element_type=F32)
    count = height * columns * C // NORM_GROUPS
    mean = stats[0:1] * (1.0 / count)
    spread = lax.rsqrt(stats[1:2] * (1.0 / count) - mean * mean + EPS_NORM)
    film_scale, film_shift = 1.0 + total[2:3], total[3:4]
    gains = total[8:12]
    gain = gains[0:1] * film_scale
    offset = gains[1:2] * film_scale + film_shift
    slope = spread * gain
    return mean, spread, slope, offset - mean * slope, film_scale, gains


def edges(columns):
    place = lax.broadcasted_iota(jnp.int32, (columns, C), 0)
    return place > 0, place < columns - 1


def activate(band, columns, height, noisy, small, conv_w, act3, wt3):
    row0 = lax.axis_index("narrow") * band
    mean, spread, slope, base, film_scale, gains = vectors(small, height, columns)
    not_first, not_last = edges(columns)

    @pl.loop(0, band + 4)
    def _(r):
        scaled = noisy[r].astype(F32) * slope + base
        value = scaled * jax.nn.sigmoid(scaled)
        row = row0 + r - 2
        value = jnp.where(jnp.logical_and(row >= 0, row < height), value, 0.0)
        value = value.astype(BF16).astype(F32)
        act3[r, :, 0:C] = shifted(value, 1, not_first).astype(BF16)
        act3[r, :, C : 2 * C] = value.astype(BF16)
        act3[r, :, 2 * C : 3 * C] = shifted(value, columns - 1, not_last).astype(BF16)

    for tap in range(9):
        rows = slice(tap * C, (tap + 1) * C)
        wt3[rows, :] = conv_w[rows, :].astype(F32).T.astype(BF16)


def convolve_tiles(first, last, band, columns, height, noisy, small, conv_w, act3, conv_s, xhat_s, rs_s, low_s):
    gains = vectors(small, height, columns)[5]
    pix = CTILE * columns

    @pl.loop(first, last)
    def _(t):
        q = t * CTILE
        conv = noisy[pl.ds(q + 2, CTILE)].astype(F32).reshape(pix, C)
        for dy in range(3):
            window = act3[pl.ds(q + 1 + dy, CTILE)].reshape(pix, 3 * C)
            conv = conv + dot(window, conv_w[dy * 3 * C : (dy + 1) * 3 * C, :])
        centered = conv - jnp.mean(conv, axis=1, keepdims=True)
        rs = lax.rsqrt(jnp.mean(centered * centered, axis=1, keepdims=True) + EPS_NORM)
        xhat = centered * rs
        here = pl.ds(q, CTILE)
        conv_s[here] = conv.reshape(CTILE, columns, C)
        xhat_s[here] = xhat.reshape(CTILE, columns, C)
        rs_s[here] = jnp.broadcast_to(rs, (pix, C)).reshape(CTILE, columns, C)
        low_s[here] = (xhat * gains[2:3] + gains[3:4]).astype(BF16).reshape(CTILE, columns, C)


def main_body(
    start_near, start_far, edge_send, edge_wait, band, columns, height, heads,
    rest_rows, crop_size, noise_level, aug_level, noisy, target, small, rest, keyval,
    blocks, dconv_w, packet, right,
    act3, wt3, conv_s, xhat_s, rs_s, low_s, diff3,
    m_cat, m_cat_t, n_cat, n_cat_t, conv_t, probs, dscore, y_t, z_t, sums,
    stage, query, out_w,
):
    tok, kv_block = keyval.shape[1:]
    width = heads * HEAD
    per_block = kv_block // HEAD
    narrow = lax.axis_index("narrow")
    row0 = narrow * band
    crop = crop_size[0]
    pix = TILE * columns
    first_query = 9 * C + 2 * LEVELS + 4
    first_out = first_query + C * heads

    def take(first, count, place):
        while count:
            owner, local = divmod(first, rest_rows)
            use = min(count, rest_rows - local)
            a = local // 16 * 16
            b = (local + use + 15) // 16 * 16
            stage[0 : b - a, :] = rest[owner, a:b, :].astype(F32)
            place(stage[local - a : local - a + use, :], use)
            first, count = first + use, count - use

    def filler(ref):
        at = [0]

        def place(value, use):
            ref[at[0] : at[0] + use, :] = value
            at[0] += use

        return place

    take(first_query, C * heads, filler(query))
    take(first_out, width, filler(out_w))
    mean, spread, slope, base, film_scale, gains = vectors(small, height, columns)
    ln_gain = gains[2:3]
    quarter = tok // 4
    masks = [small[owner, 4:5, 0:quarter] for owner in range(4)]
    ok = (jnp.concatenate(masks, axis=1) > 0.0) | (lax.broadcasted_iota(jnp.int32, (1, tok), 1) == 0)
    factor = LOG2E / math.sqrt(HEAD)
    for head in range(heads):
        cols = slice(head * HEAD, (head + 1) * HEAD)
        tcols = slice(head * tok, (head + 1) * tok)
        block, at = head // per_block, head % per_block * HEAD
        query_head = query[pl.ds(head, C, stride=heads), :].astype(BF16)
        out_head = out_w[cols, :].astype(BF16)
        m_head = dot(query_head, keyval[block, :, at : at + HEAD], NT) * factor

        @pl.when(narrow == block)
        def _():
            right[:, at : at + HEAD] = query_head

        @pl.when(narrow == block + heads // per_block)
        def _():
            right[:, at : at + HEAD] = out_w[cols, :].T.astype(BF16)

        top, rest = two_parts(m_head)
        m_cat[:C, tcols] = top
        m_cat[C:, tcols] = rest
        top, rest = two_parts(m_head.T)
        m_cat_t[tcols, :C] = top
        m_cat_t[tcols, C:] = rest
        n_head = dot(keyval[block + heads // per_block, :, at : at + HEAD], out_head)
        top, rest = two_parts(n_head)
        n_cat[tcols, :C] = top
        n_cat[tcols, C:] = rest
        top, rest = two_parts(n_head.T)
        n_cat_t[:C, tcols] = top
        n_cat_t[C:, tcols] = rest
    y_t[...] = jnp.zeros_like(y_t)
    z_t[...] = jnp.zeros_like(z_t)
    conv_t[...] = jnp.zeros_like(conv_t)
    sums[...] = jnp.zeros_like(sums)
    not_first, not_last = edges(columns)
    pix_row = lax.broadcasted_iota(jnp.int32, (pix, C), 0) // columns
    pix_col = lax.broadcasted_iota(jnp.int32, (pix, C), 0) % columns
    tiles = band // TILE

    @pl.loop(0, tiles)
    def _(t):
        q = jnp.where(t == 0, 0, jnp.where(t == 1, tiles - 1, t - 1)) * TILE
        here = pl.ds(q, TILE)
        conv = conv_s[here].reshape(pix, C)
        low = low_s[here].reshape(pix, C)
        low2 = jnp.concatenate([low, low], axis=1)
        for head in range(heads):
            tcols = slice(head * tok, (head + 1) * tok)
            if head % 2 == 0:
                scores = dot(low2, m_cat[:, head * tok : (head + 2) * tok])
            score = scores[:, head % 2 * tok : (head % 2 + 1) * tok]
            score = jnp.where(ok, score, -1e30)
            e = jnp.exp2(score - jnp.max(score, axis=1, keepdims=True))
            p = e * (1.0 / jnp.sum(e, axis=1, keepdims=True))
            probs[:, tcols] = p.astype(BF16)
        mixed = dot(probs[...], n_cat[...])
        output = conv + mixed[:, :C] + mixed[:, C:]
        valid = (row0 + q + pix_row < crop) & (pix_col < crop)
        err = jnp.where(valid, output - target[pl.ds(q + 1, TILE)].astype(F32).reshape(pix, C), 0.0)
        sums[4:5, :] += jnp.sum(err * err, axis=0, keepdims=True)
        dout = 2.0 * err
        dout_low = dout.astype(BF16)
        dout2 = jnp.concatenate([dout_low, dout_low], axis=1)
        for head in range(heads):
            tcols = slice(head * tok, (head + 1) * tok)
            if head % 2 == 0:
                dprobs = dot(dout2, n_cat_t[:, head * tok : (head + 2) * tok])
            dprob = dprobs[:, head % 2 * tok : (head % 2 + 1) * tok]
            p = probs[:, tcols].astype(F32)
            pd = p * dprob
            ds = pd - p * jnp.sum(pd, axis=1, keepdims=True)
            dscore[:, tcols] = ds.astype(BF16)
        dlay2 = dot(dscore[...], m_cat_t[...])
        dlay = (dlay2[:, :C] + dlay2[:, C:]) * LN2
        xhat = xhat_s[here].reshape(pix, C)
        rs = rs_s[here].reshape(pix, C)
        sums[2:3, :] += jnp.sum(dlay * xhat, axis=0, keepdims=True)
        sums[3:4, :] += jnp.sum(dlay, axis=0, keepdims=True)
        dxh = dlay * ln_gain
        dconv = dout + rs * (
            dxh
            - jnp.mean(dxh, axis=1, keepdims=True)
            - xhat * jnp.mean(dxh * xhat, axis=1, keepdims=True)
        )
        dout_t = dout.T.astype(BF16)
        lay_t = low.astype(F32).T.astype(BF16)
        y_t[...] += dot(dout_t, probs[...])
        z_t[...] += dot(lay_t, dscore[...])
        dconv_t = dconv.T.astype(BF16)
        for dy in range(3):
            window = act3[pl.ds(q + 1 + dy, TILE)].reshape(pix, 3 * C)
            conv_t[:, dy * 3 * C : (dy + 1) * 3 * C] += dot(dconv_t, window)
        for k in range(TILE):
            one = dconv[k * columns : (k + 1) * columns]
            diff3[q + 1 + k, :, 0:C] = shifted(one, columns - 1, not_last).astype(BF16)
            diff3[q + 1 + k, :, C : 2 * C] = one.astype(BF16)
            diff3[q + 1 + k, :, 2 * C : 3 * C] = shifted(one, 1, not_first).astype(BF16)

        for order in range(2):
            @pl.when(t == order)
            def _():
                edge_send(order)

    def back(t):
        r = t * TILE3
        grad = jnp.zeros((TILE3 * columns, C), F32)
        for dy in range(3):
            window = diff3[pl.ds(r + 2 - dy, TILE3)].reshape(TILE3 * columns, 3 * C)
            grad = grad + dot(window, wt3[dy * 3 * C : (dy + 1) * 3 * C, :])
        x = noisy[pl.ds(r + 2, TILE3)].astype(F32).reshape(TILE3 * columns, C)
        scaled = x * slope + base
        sig = jax.nn.sigmoid(scaled)
        ds = grad * (sig * (1.0 + scaled * (1.0 - sig)))
        sums[0:1, :] += jnp.sum(ds, axis=0, keepdims=True)
        sums[1:2, :] += jnp.sum(ds * ((x - mean) * spread), axis=0, keepdims=True)

    share_rows = dconv_w.shape[1]
    full = conv_t[...].T
    for owner in range(4):
        dconv_w[owner] = full[owner * share_rows : (owner + 1) * share_rows].astype(BF16)
        part = z_t if owner < 2 else y_t
        at = owner % 2 * per_block * tok
        blocks[owner] = part[:, at : at + per_block * tok].astype(BF16)
    start_near()
    edge_wait()
    halves = band // TILE3 // 2
    pl.loop(0, halves)(back)
    start_far()
    pl.loop(halves, band // TILE3)(back)
    a, b = sums[0:1], sums[1:2]
    packet[0:1] = film_scale * b
    packet[1:2] = film_scale * a
    packet[2:4] = sums[2:4]
    packet[4:5] = gains[0:1] * b + gains[1:2] * a
    packet[5:6] = a
    packet[6:7] = sums[4:5]
    lane = lax.broadcasted_iota(jnp.int32, (1, C), 1)
    facts = jnp.zeros((1, C), F32)
    for k, fact in enumerate((noise_level[0], aug_level[0], crop)):
        facts = jnp.where(lane == k, fact.astype(F32), facts)
    packet[7:8] = jnp.where(row0 == 0, facts, 0.0)


def cross_ids():
    n = lax.axis_index("narrow")
    mate = n + 1 - 2 * lax.rem(n, 2)
    across = lax.rem(n + 2, 4)
    corner = lax.rem(mate + 2, 4)
    return n, mate, across, corner


def to_narrow(src, dst, send_sem, recv_sem, device):
    return pltpu.make_async_remote_copy(
        src_ref=src, dst_ref=dst, send_sem=send_sem, recv_sem=recv_sem,
        device_id={"narrow": device}, device_id_type=MESH,
    )


class Gather:
    def __init__(self, view, sems, ids):
        self.view, self.sems = view, sems
        self.n, self.mate, self.across, self.corner = ids

    def _copy(self, block, slot, device):
        ref = self.view(block)
        return to_narrow(ref, ref, self.sems.at[0, slot], self.sems.at[1, slot], device)

    def start(self):
        self._copy(self.n, 1, self.across).start()
        self._copy(self.n, 0, self.mate).start()

    def relay(self):
        self._copy(self.across, 1, self.across).wait_recv()
        self._copy(self.across, 2, self.mate).start()

    def wait(self):
        self._copy(self.mate, 0, self.mate).wait_recv()
        self._copy(self.corner, 2, self.mate).wait_recv()

    def drain(self):
        self._copy(self.n, 1, self.across).wait_send()
        self._copy(self.n, 0, self.mate).wait_send()
        self._copy(self.across, 2, self.mate).wait_send()


def rest_needs(rest_rows):
    first, last = 9 * C, 9 * C + 2 * LEVELS
    needs = []
    for owner in range(4):
        lo, hi = owner * rest_rows, (owner + 1) * rest_rows
        keep = [r for r in ((lo, min(hi, first)), (max(lo, last), hi)) if r[0] < r[1]]
        assert len(keep) <= 1
        if keep:
            a, b = keep[0][0] - lo, keep[0][1] - lo
            needs.append((a // 16 * 16, (b + 15) // 16 * 16))
        else:
            needs.append(None)
    return needs


KPARTS = 4
WPARTS = 8


def front_body(
    kv_rows, rest_rows, greet, to_group, early, noise_level, aug_level, weights, noisy, target, text, mask,
    noisy_ext, target_ext, text_all, rest_all, keyval, own_kv, small,
    wide_f32, wide_bf, rest_f32, acc,
    w_sem, in_sem, text_sem, rest_sem, kv_sem, small_sem, halo_sem,
):
    ids = cross_ids()
    n, mate, across, corner = ids
    band = noisy.shape[1]
    tokens, depth = text.shape[1:]
    in_text = pltpu.make_async_copy(text.at[0], text_all.at[n], in_sem.at[0])
    in_text.start()
    in_rest = pltpu.make_async_copy(
        weights.at[pl.ds(kv_rows, rest_rows)], rest_f32.at[pl.ds(0, rest_rows)], in_sem.at[1]
    )
    in_rest.start()
    in_noisy = pltpu.make_async_copy(noisy.at[0], noisy_ext.at[pl.ds(2, band)], in_sem.at[2])
    in_noisy.start()
    w_step = kv_rows // WPARTS
    in_w = [
        pltpu.make_async_copy(
            weights.at[pl.ds(k * w_step, w_step)], wide_f32.at[pl.ds(k * w_step, w_step)], w_sem.at[k]
        )
        for k in range(WPARTS)
    ]
    for copy in in_w:
        copy.start()
    in_target = pltpu.make_async_copy(target.at[0], target_ext.at[pl.ds(1, band)], in_sem.at[3])
    in_target.start()
    greet()

    k_step = depth // KPARTS
    texts = [
        Gather(
            lambda b, k=k: text_all.at[b, :, pl.ds(k * k_step, k_step)], text_sem.at[k], ids
        )
        for k in range(KPARTS)
    ]
    in_text.wait()
    for part in texts:
        part.start()

    in_rest.wait()
    rest_f32[rest_rows:] = jnp.zeros((rest_f32.shape[0] - rest_rows, C), F32)
    for k in range(2):
        row_sum = jnp.zeros((1, C), F32)
        for level in (noise_level[0], NOISE_LEVELS + aug_level[0]):
            row = 9 * C + 2 * level + k - n * rest_rows
            found = rest_f32[pl.ds(jnp.clip(row, 0, rest_rows - 1), 1), :]
            found = found.astype(BF16).astype(F32)
            row_sum = row_sum + jnp.where((row >= 0) & (row < rest_rows), found, 0.0)
        small[n, 2 + k : 3 + k, :] = row_sum
    small[n, 4:16, :] = jnp.zeros((12, C), F32)
    for owner in range(4):
        for k in range(4):
            row = 9 * C + 2 * LEVELS + k - owner * rest_rows
            if 0 <= row < rest_rows:
                @pl.when(n == owner)
                def _():
                    small[n, 8 + k : 9 + k, :] = rest_f32[row : row + 1, :].astype(BF16).astype(F32)
    small[n, 4:5, 0:tokens] = mask[...].astype(F32)
    in_noisy.wait()

    def add_row(r, sums):
        x = noisy_ext[r + 2].astype(F32)
        return (
            sums[0] + jnp.sum(x.reshape(-1, 8, C), axis=0),
            sums[1] + jnp.sum((x * x).reshape(-1, 8, C), axis=0),
        )

    zero = jnp.zeros((8, C), F32)
    one, two = lax.fori_loop(0, band, add_row, (zero, zero))
    small[n, 0:1, :] = jnp.sum(one, axis=0, keepdims=True)
    small[n, 1:2, :] = jnp.sum(two, axis=0, keepdims=True)
    others = (mate, across, corner)

    def small_copy(slot, block):
        return to_narrow(
            small.at[block], small.at[block], small_sem.at[0, slot], small_sem.at[1, slot], others[slot]
        )

    for slot in range(3):
        small_copy(slot, n).start()

    in_target.wait()
    up = jnp.maximum(n - 1, 0)
    down = jnp.minimum(n + 1, 3)
    noisy_up = to_narrow(
        noisy_ext.at[pl.ds(2, 2)], noisy_ext.at[pl.ds(band + 2, 2)], halo_sem.at[0, 0], halo_sem.at[1, 0], up
    )
    noisy_down = to_narrow(
        noisy_ext.at[pl.ds(band, 2)], noisy_ext.at[pl.ds(0, 2)], halo_sem.at[0, 1], halo_sem.at[1, 1], down
    )
    @pl.when(n > 0)
    def _():
        noisy_up.start()

    @pl.when(n < 3)
    def _():
        noisy_down.start()

    @pl.when(n == 0)
    def _():
        noisy_ext[0:2] = jnp.zeros((2,) + noisy_ext.shape[1:], BF16)

    @pl.when(n == 3)
    def _():
        noisy_ext[band + 2 : band + 4] = jnp.zeros((2,) + noisy_ext.shape[1:], BF16)

    needs = rest_needs(rest_rows)
    rest_all[n] = rest_f32[...].astype(BF16)

    def rest_copy(owner, slot, device):
        a, b = needs[owner]
        ref = rest_all.at[owner, pl.ds(a, b - a)]
        return to_narrow(ref, ref, rest_sem.at[0, slot, owner], rest_sem.at[1, slot, owner], device)

    for owner in range(4):
        if needs[owner] is not None:
            @pl.when(n == owner)
            def _():
                rest_copy(owner, 1, across).start()
                rest_copy(owner, 0, mate).start()

    parts = wide_bf.shape[1] // C
    rows = 256
    for k in range(WPARTS):
        in_w[k].wait()

        @pl.loop(k * w_step // parts // rows, (k + 1) * w_step // parts // rows)
        def _(i):
            for j in range(parts):
                wide_bf[pl.ds(pl.multiple_of(i * rows, rows), rows), j * C : (j + 1) * C] = wide_f32[
                    pl.ds(i * rows * parts + j, rows, stride=parts), :
                ].astype(BF16)

    acc[...] = jnp.zeros_like(acc)
    for k in range(KPARTS):
        texts[k].relay()
    for k in range(KPARTS):
        texts[k].wait()

        @pl.loop(0, k_step // 512)
        def _(i):
            at = pl.ds(pl.multiple_of(k * k_step + i * 512, 512), 512)
            acc[...] += dot(text_all[:, :, at].reshape(4 * tokens, 512), wide_bf[at, :])

    keyval[n] = acc[...].astype(BF16)
    own_kv[...] = acc[...].astype(BF16)
    keys = Gather(lambda b: keyval.at[b], kv_sem, ids)
    keys.start()
    to_group()


    def relay_rest(owner):
        if needs[owner] is not None:
            @pl.when(across == owner)
            def _():
                rest_copy(owner, 1, across).wait_recv()
                rest_copy(owner, 2, mate).start()

    def settle_rest(owner):
        if needs[owner] is not None:
            @pl.when(mate == owner)
            def _():
                rest_copy(owner, 0, mate).wait_recv()

            @pl.when(corner == owner)
            def _():
                rest_copy(owner, 2, mate).wait_recv()

            @pl.when(n == owner)
            def _():
                rest_copy(owner, 1, across).wait_send()
                rest_copy(owner, 0, mate).wait_send()

            @pl.when(across == owner)
            def _():
                rest_copy(owner, 2, mate).wait_send()

    relay_rest(0)
    for slot, block in ((0, mate), (1, across), (2, corner)):
        small_copy(slot, block).wait_recv()
        small_copy(slot, n).wait_send()

    @pl.when(n > 0)
    def _():
        noisy_down.wait_recv()
        noisy_up.wait_send()

    @pl.when(n < 3)
    def _():
        noisy_up.wait_recv()
        noisy_down.wait_send()

    settle_rest(0)
    early(0)
    for owner in range(1, 4):
        relay_rest(owner)
    keys.relay()
    early(1)
    for owner in range(1, 4):
        settle_rest(owner)
    keys.wait()
    keys.drain()
    for part in texts:
        part.drain()


def mid_stages(gd, height, columns, from_group, blocks, conv, packet, right, kvs, texts, *refs):
    (
        dkv_all, conv_all, t_all, small_all, scal,
        near_b, near_c, sum_b, sum_c, far_b, far_c, own_b, own_c, group_b, group_c,
        packets, wides, t_own, t_send, c_send, norms, conv_sum,
        near_sem, far_sem, group_sem, packet_sem, wide_sem, norm_sem, give_sem,
    ) = refs
    ids = cross_ids()
    n, mate, across, corner = ids
    others = (mate, across, corner)
    wide_count = wides.shape[0]
    wide = lax.axis_index("wide")
    group = wide // gd
    spot = lax.rem(wide, gd)
    tok, kv_block = kvs.shape[1:]
    heads = kv_block // HEAD
    depth = texts.shape[-1]
    scale = jnp.where(n < 2, 1.0 / math.sqrt(HEAD), 1.0)

    def lanes(h):
        return pl.ds(h * tok, tok)

    def near(slot, which):
        owner = corner if slot == 0 else mate
        src, dst = ((blocks, near_b), (conv, near_c))[which]
        return to_narrow(
            src.at[owner], dst.at[slot], near_sem.at[0, slot, which], near_sem.at[1, slot, which], mate
        )

    def far(h):
        if h < heads:
            src, dst = sum_b.at[:, lanes(h)], far_b.at[:, lanes(h)]
        else:
            src, dst = sum_c, far_c
        return to_narrow(src, dst, far_sem.at[0, h], far_sem.at[1, h], across)

    def group_copy(k, h):
        if h < heads:
            src, dst = own_b.at[:, lanes(h)], group_b.at[k - 1, :, lanes(h)]
        else:
            src, dst = own_c, group_c.at[k - 1]
        return pltpu.make_async_remote_copy(
            src_ref=src, dst_ref=dst,
            send_sem=group_sem.at[0, h, k - 1], recv_sem=group_sem.at[1, h, k - 1],
            device_id={"wide": group * gd + lax.rem(spot + k, gd)}, device_id_type=MESH,
        )

    def packet_copy(slot, block):
        return to_narrow(
            packets.at[block], packets.at[block],
            packet_sem.at[0, slot], packet_sem.at[1, slot], others[slot],
        )

    def wide_copy(k, block):
        return pltpu.make_async_remote_copy(
            src_ref=wides.at[block], dst_ref=wides.at[block],
            send_sem=wide_sem.at[0, k - 1], recv_sem=wide_sem.at[1, k - 1],
            device_id={"wide": lax.rem(wide + k, wide_count)}, device_id_type=MESH,
        )

    def start_near():
        for slot in range(2):
            for which in range(2):
                near(slot, which).start()

    def start_far():
        near(0, 0).wait_recv()
        sum_b[...] = (blocks[across].astype(F32) + near_b[0].astype(F32)).astype(BF16)
        for h in range(heads):
            far(h).start()
        near(0, 1).wait_recv()
        sum_c[...] = (conv[across].astype(F32) + near_c[0].astype(F32)).astype(BF16)
        far(heads).start()

    q_rows, q_from = 96, 80

    def give_head(src_n, h):
        src, dst = t_send.at[pl.ds(0, q_rows), lanes(h)], t_all.at[src_n, pl.ds(0, q_rows), lanes(h)]
        return to_narrow(src, dst, give_sem.at[0, 0, h], give_sem.at[1, src_n, h], 2)

    def give_tail(src_n, h):
        rows = pl.ds(q_from, C - q_from)
        src, dst = t_send.at[rows, lanes(h)], t_all.at[src_n, rows, lanes(h)]
        return to_narrow(src, dst, give_sem.at[0, 1, h], give_sem.at[1, src_n, h], 3)

    def give_values(h):
        src, dst = t_send.at[:, lanes(h)], t_all.at[2, :, lanes(h)]
        return to_narrow(src, dst, give_sem.at[0, 1, h], give_sem.at[1, 2, h], 3)

    def give_conv(src_n):
        return to_narrow(
            c_send, conv_all.at[src_n], give_sem.at[0, 2, 0], give_sem.at[1, src_n, heads], 0
        )

    def project(k, h, value):
        cols = slice(h * HEAD, (h + 1) * HEAD)
        dkv_all[k * tok : (k + 1) * tok, cols] = (dot(value, right[:, cols], TN) * scale).astype(BF16)
        term = dot(value, kvs[k, :, cols]) * scale
        t_own[:, cols] = term if k == 0 else t_own[:, cols] + term

    def finish(gram):
        packets[n] = packet[...]
        for slot in range(3):
            packet_copy(slot, n).start()
        near(1, 0).wait_recv()
        near(1, 1).wait_recv()
        for h in range(heads):
            far(h).wait_recv()
            at = slice(h * tok, (h + 1) * tok)
            own_b[:, at] = (
                blocks[n, :, at].astype(F32) + near_b[1, :, at].astype(F32) + far_b[:, at].astype(F32)
            ).astype(BF16)
            for k in range(1, gd):
                group_copy(k, h).start()
        for slot, block in enumerate(others):
            packet_copy(slot, block).wait_recv()
        wides[wide] = packets[0] + packets[1] + packets[2] + packets[3]

        @pl.loop(1, wide_count)
        def _(k):
            wide_copy(k, wide).start()

        far(heads).wait_recv()
        conv_sum[...] = conv[n].astype(F32) + near_c[1].astype(F32) + far_c[...].astype(F32)
        own_c[...] = conv_sum[...].astype(BF16)
        for k in range(1, gd):
            group_copy(k, heads).start()
        for h in range(heads):
            project(0, h, own_b[:, h * tok : (h + 1) * tok])
        from_group()
        def text_products(a, firsts):
            rows = slice(a * tok, (a + 1) * tok) if gd <= 4 else slice(0, tok)
            gram[rows, :] = jnp.zeros((tok, gd * tok), F32)

            @pl.loop(0, depth // 1024)
            def _(i):
                at = pl.ds(pl.multiple_of(i * 1024, 1024), 1024)
                left = texts[a, :, :, at].reshape(tok, 1024)
                for b in range(firsts, gd):
                    part = dot(left, texts[b, :, :, at].reshape(tok, 1024), NT)
                    gram[rows, b * tok : (b + 1) * tok] += part

        if gd <= 4:
            for a in range(gd):
                text_products(a, a)
        for h in range(heads):
            for k in range(1, gd):
                group_copy(k, h).wait_recv()
                project(k, h, group_b[k - 1, :, h * tok : (h + 1) * tok])
            at = slice(h * HEAD, (h + 1) * HEAD)
            t_send[:, at] = t_own[:, at].astype(BF16)
            for k in range(4):
                @pl.when(n == k)
                def _():
                    if k < 2:
                        give_head(k, h).start()
                        give_tail(k, h).start()
                    elif k == 2:
                        give_values(h).start()
                    else:
                        t_all[3, :, at] = t_send[:, at]
        for k in range(1, gd):
            group_copy(k, heads).wait_recv()
            conv_sum[...] += group_c[k - 1].astype(F32)
        c_send[...] = conv_sum[...].astype(BF16)
        for k in range(4):
            @pl.when(n == k)
            def _():
                if k > 0:
                    give_conv(k).start()
                else:
                    conv_all[0] = c_send[...]

        @pl.loop(1, wide_count)
        def _(k):
            wide_copy(k, lax.rem(wide + wide_count - k, wide_count)).wait_recv()

        sq = jnp.sum(t_own[...] * t_own[...]) + jnp.sum(conv_sum[...] * conv_sum[...])
        for a in range(gd):
            da = dkv_all[a * tok : (a + 1) * tok, :]
            if gd > 4:
                text_products(a, a)
            rows = slice(a * tok, (a + 1) * tok) if gd <= 4 else slice(0, tok)
            for b in range(a, gd):
                db = dkv_all[b * tok : (b + 1) * tok, :]
                top, low = two_parts(gram[rows, b * tok : (b + 1) * tok])
                part = jnp.sum(da.astype(F32) * (dot(top, db) + dot(low, db)))
                sq = sq + (part if a == b else 2.0 * part)
        gains = jnp.zeros((4, C), F32)
        shared = jnp.zeros((1, C), F32)
        for a in range(gd):
            mine = wides[group * gd + a]
            small_all[a] = mine
            gains = gains + mine[0:4]
            for b in range(gd):
                his = wides[group * gd + b]
                same = (mine[7:8, 0:1] == his[7:8, 0:1]).astype(F32) + (mine[7:8, 1:2] == his[7:8, 1:2]).astype(F32)
                shared = shared + same * (mine[4:5] * his[4:5] + mine[5:6] * his[5:6])
        shared_sq = jnp.sum(gains * gains) + jnp.sum(shared)
        norms[n] = jnp.full((8, C), sq + jnp.where(n == 0, shared_sq, 0.0), F32)

        def norm_copy(slot, block):
            return to_narrow(
                norms.at[block], norms.at[block], norm_sem.at[0, slot], norm_sem.at[1, slot], others[slot]
            )

        for slot in range(3):
            norm_copy(slot, n).start()

        def tally(k, found):
            there = wides[k]
            crop = there[7:8, 2:3]
            pixels = jnp.minimum(crop, float(height)) * jnp.minimum(crop, float(columns))
            mine = jnp.where(k // gd == group, pixels, 0.0)
            return found[0] + pixels, found[1] + mine, found[2] + jnp.sum(there[6:7], axis=1, keepdims=True)

        none = jnp.zeros((1, 1), F32)
        total, own_count, loss = lax.fori_loop(0, wide_count, tally, (none, none, none))
        for slot, block in enumerate(others):
            norm_copy(slot, block).wait_recv()
        squares = norms[0, 0:1] + norms[1, 0:1] + norms[2, 0:1] + norms[3, 0:1]
        norm = jnp.sqrt(squares) / total
        scal[0:1] = jnp.minimum(1.0, CLIP_NORM / norm) / total
        scal[1:2] = jnp.broadcast_to(INNER_RATE * own_count / total, (1, C))
        scal[2:3] = jnp.broadcast_to(loss, (1, C))
        scal[3:4] = jnp.broadcast_to(total, (1, C))
        scal[4:8] = jnp.zeros((4, C), F32)

        for k in range(4):
            @pl.when(n == k)
            def _():
                for h in range(heads):
                    if k < 2:
                        give_head(k, h).wait_send()
                        give_tail(k, h).wait_send()
                    if k == 2:
                        give_values(h).wait_send()
                        give_head(0, h).wait_recv()
                        give_head(1, h).wait_recv()
                    if k == 3:
                        give_tail(0, h).wait_recv()
                        give_tail(1, h).wait_recv()
                        give_values(h).wait_recv()
                if k > 0:
                    give_conv(k).wait_send()
                else:
                    for j in range(1, 4):
                        give_conv(j).wait_recv()
        for slot in range(2):
            for which in range(2):
                near(slot, which).wait_send()
        for h in range(heads + 1):
            far(h).wait_send()
            for k in range(1, gd):
                group_copy(k, h).wait_send()
        for slot in range(3):
            packet_copy(slot, n).wait_send()
            norm_copy(slot, n).wait_send()

        @pl.loop(1, wide_count)
        def _(k):
            wide_copy(k, wide).wait_send()

    return start_near, start_far, finish


def step_kernel(gd, wide_count, kv_rows, rest_rows, band, columns, counts, *refs):
    refs = list(refs)
    noise_level, aug_level, crop_size, weights, noisy, target, text, first, second, mask = refs[:10]
    texts, dkv_all, conv_all, t_all, small_all, scal, first_near, second_near = refs[10:18]
    n_front, n_main, n_mid = counts
    at = 18
    (noisy_ext, target_ext, rest_all, keyval, kvs, small) = refs[at : at + 6]
    act3, wt3, conv_s, xhat_s, rs_s, low_s, diff3 = refs[at + 6 : at + 13]
    at += 13
    front_sems = refs[at : at + n_front]
    at += n_front
    (blocks, conv, packet, right) = refs[at : at + 4]
    at += 4
    mid_refs = refs[at : at + n_mid]
    at += n_mid
    group_text_sem, ahead_sem, edge_sem = refs[at : at + 3]
    ahead = [
        pltpu.make_async_copy(far, near, ahead_sem.at[k])
        for k, (far, near) in enumerate(((first, first_near), (second, second_near)))
    ]
    n, mate, across, corner = cross_ids()
    wide = lax.axis_index("wide")
    group, spot = wide // gd, lax.rem(wide, gd)
    tok, kv_block = kvs.shape[1:]
    depth = text.shape[2]
    barrier = pltpu.get_barrier_semaphore()
    for other in (mate, across, corner):
        pl.semaphore_signal(barrier, inc=1, device_id={"narrow": other}, device_id_type=MESH)

    @pl.loop(1, wide_count)
    def _(k):
        pl.semaphore_signal(
            barrier, inc=1, device_id={"wide": lax.rem(wide + k, wide_count)}, device_id_type=MESH
        )

    def greet():
        pl.semaphore_wait(barrier, 3 + wide_count - 1)

    def group_send(k, which):
        buf = (texts, kvs)[which]
        return pltpu.make_async_remote_copy(
            src_ref=buf.at[0], dst_ref=buf.at[k],
            send_sem=group_text_sem.at[0, which, k - 1], recv_sem=group_text_sem.at[1, which, k - 1],
            device_id={"wide": group * gd + lax.rem(spot + k, gd)}, device_id_type=MESH,
        )

    def to_group():
        for which in (1, 0):
            for k in range(1, gd):
                group_send(k, which).start()

    def from_group():
        for which in (1, 0):
            for k in range(1, gd):
                group_send(k, which).wait_recv()
                group_send(k, which).wait_send()

    def early(part):
        common = (band, columns, H, noisy_ext, small, rest_all.at[0], act3)
        tiles = band // CTILE
        if part == 0:
            activate(*common, wt3)
        bounds = (0, tiles // 2) if part == 0 else (tiles // 2, tiles)
        convolve_tiles(*bounds, *common, conv_s, xhat_s, rs_s, low_s)

    def front(wide_f32, wide_bf, rest_f32, acc):
        front_body(
            kv_rows, rest_rows, greet, to_group, early, noise_level, aug_level, weights, noisy, target, text, mask,
            noisy_ext, target_ext, texts.at[0], rest_all, keyval, kvs.at[0], small,
            wide_f32, wide_bf, rest_f32, acc, *front_sems,
        )

    V = pltpu.VMEM
    pl.run_scoped(
        front, V((kv_rows, C), F32), V((depth, kv_block), BF16), V((rest_all.shape[1], C), F32),
        V((tok, kv_block), F32),
    )
    for copy in ahead:
        copy.start()
    pix = TILE * columns

    start_near, start_far, finish = mid_stages(
        gd, H, W, from_group, blocks, conv, packet, right, kvs, texts,
        dkv_all, conv_all, t_all, small_all, scal, *mid_refs,
    )

    def edge(order):
        src, dst = (1, band + 1) if order == 0 else (band, 0)
        other = jnp.maximum(n - 1, 0) if order == 0 else jnp.minimum(n + 1, 3)
        return to_narrow(diff3.at[src], diff3.at[dst], edge_sem.at[0, order], edge_sem.at[1, order], other)

    def edge_send(order):
        @pl.when(n > 0 if order == 0 else n < 3)
        def _():
            edge(order).start()

    def edge_wait():
        @pl.when(n > 0)
        def _():
            edge(1).wait_recv()
            edge(0).wait_send()

        @pl.when(n < 3)
        def _():
            edge(0).wait_recv()
            edge(1).wait_send()

        @pl.when(n == 0)
        def _():
            diff3[0] = jnp.zeros(diff3.shape[1:], BF16)

        @pl.when(n == 3)
        def _():
            diff3[band + 1] = jnp.zeros(diff3.shape[1:], BF16)

    def main(*scratch):
        main_body(
            start_near, start_far, edge_send, edge_wait, band, columns, H, HEADS, rest_rows, crop_size, noise_level, aug_level,
            noisy_ext, target_ext, small, rest_all, keyval, blocks, conv, packet, right,
            act3, wt3, conv_s, xhat_s, rs_s, low_s, diff3, *scratch,
        )

    pl.run_scoped(
        main,
        V((2 * C, HEADS * tok), BF16),
        V((HEADS * tok, 2 * C), BF16),
        V((HEADS * tok, 2 * C), BF16),
        V((2 * C, HEADS * tok), BF16),
        V((C, 9 * C), F32),
        V((pix, HEADS * tok), BF16),
        V((pix, HEADS * tok), BF16),
        V((C, HEADS * tok), F32),
        V((C, HEADS * tok), F32),
        V((8, C), F32),
        V((rest_all.shape[1], C), F32),
        V((C * HEADS, C), F32),
        V((HEADS * HEAD, C), F32),
    )

    pl.run_scoped(finish, V((gd * tok if gd <= 4 else tok, gd * tok), F32))
    for copy in ahead:
        copy.wait()


def near(gd):
    return pltpu.VMEM if gd <= 4 else jax.ShapeDtypeStruct


def hold(value, gd):
    return pltpu.with_memory_space_constraint(value, pltpu.VMEM) if gd <= 4 else value


def far(value):
    return pltpu.with_memory_space_constraint(value, pltpu.HBM)


def run_step(
    gd, wide_count, noise_level, aug_level, crop_size, weights2, noisy, target, text, first, second, mask
):
    _, band, columns, _ = noisy.shape
    _, tokens, depth = text.shape
    tok = 4 * tokens
    kv_block = 2 * HEADS * HEAD // 4
    kv_rows = depth * kv_block // C
    rest_rows = weights2.shape[0] - kv_rows
    rest_pad = (rest_rows + 15) // 16 * 16
    assert 9 * C <= rest_rows and kv_block % HEAD == 0 and HEAD == C
    vmem = pl.BlockSpec(memory_space=pltpu.VMEM)
    smem = pl.BlockSpec(memory_space=pltpu.SMEM)
    hbm = pl.BlockSpec(memory_space=pltpu.HBM)
    D, V = pltpu.SemaphoreType.DMA, pltpu.VMEM
    few = max(gd - 1, 1)
    heads = kv_block // HEAD
    bshape, cshape = (C, kv_block // HEAD * tok), (9 * C // 4, C)
    front_sems = [D((WPARTS,)), D((4,)), D((KPARTS, 2, 3)), D((2, 3, 4)), D((2, 3)), D((2, 3)), D((2, 4))]
    mid_refs = [
        V((2,) + bshape, BF16), V((2,) + cshape, BF16), V(bshape, BF16), V(cshape, BF16),
        V(bshape, BF16), V(cshape, BF16), V(bshape, BF16), V(cshape, BF16),
        V((few,) + bshape, BF16), V((few,) + cshape, BF16),
        V((4, 8, C), F32), V((wide_count, 8, C), F32),
        V((C, kv_block), F32), V((C, kv_block), BF16), V(cshape, BF16),
        V((4, 8, C), F32), V(cshape, F32),
        D((2, 2, 2)), D((2, heads + 1)), D((2, heads + 1, few)), D((2, 3)), D((2, wide_count)), D((2, 3)),
        D((2, 4, heads + 1)),
    ]
    return pl.pallas_call(
        functools.partial(
            step_kernel, gd, wide_count, kv_rows, rest_rows, band, columns,
            (len(front_sems), 0, len(mid_refs)),
        ),
        out_shape=tuple(
            near(gd)(shape, kind)
            for shape, kind in (
                ((gd, 4, tokens, depth), BF16),
                ((gd * tok, kv_block), BF16),
                ((4,) + cshape, BF16),
                ((4, C, kv_block), BF16),
                ((gd, 8, C), F32),
                ((8, C), F32),
                (first.shape, F32),
                (first.shape, F32),
            )
        ),
        in_specs=[smem] * 3 + [hbm] * 6 + [vmem],
        out_specs=(vmem,) * 8,
        scratch_shapes=[
            V((band + 4, columns, C), BF16), V((band + 2, columns, C), BF16), V((4, rest_pad, C), BF16),
            V((4, tok, kv_block), BF16), V((gd, tok, kv_block), BF16), V((4, 16, C), F32),
            V((band + 4, columns, 3 * C), BF16), V((9 * C, C), BF16),
            *[V((band, columns, C), F32)] * 3, V((band, columns, C), BF16),
            V((band + 2, columns, 3 * C), BF16),
            *front_sems,
            V((4,) + bshape, BF16), V((4,) + cshape, BF16), V((8, C), F32), V((C, kv_block), BF16),
            *mid_refs,
            D((2, 2, few)),
            D((2,)),
            D((2, 2)),
        ],
        compiler_params=pltpu.CompilerParams(
            collective_id=1, has_side_effects=True, vmem_limit_bytes=(STEP_VMEM if gd <= 4 else 60) * 2**20
        ),
        name="step",
    )(noise_level, aug_level, crop_size, *map(far, (weights2, noisy, target, text, first, second)), mask)


STEP_VMEM = 40


AROWS = 2048


def adam_tiles(length):
    return pl.cdiv(length + 17 * C, AROWS * C)


def adam_kernel(
    gd, length, kv_rows, rest_rows, *refs,
):
    (
        texts, dkv, conv, t_all, small, scal, first, second, first_out, second_out, step_out,
        nat, rest, turned_dkv, edge, shift, carry,
    ) = refs
    s = pl.program_id(0)
    tok = dkv.shape[0] // gd
    n = lax.axis_index("narrow")
    start = lax.rem(lax.axis_index("wide"), gd) * length
    row0 = start // C
    lane0, row_off, row_shift, block0 = lax.rem(start, C), lax.rem(row0, AROWS), lax.rem(row0, 16), row0 // AROWS
    wrap = C - lane0
    kv_blocks = kv_rows // AROWS
    parts = dkv.shape[1] // C
    cols_tile = AROWS // parts

    def iotas(rows):
        shape = (rows, C)
        return lax.broadcasted_iota(jnp.int32, shape, 0), lax.broadcasted_iota(jnp.int32, shape, 1)

    def natural(tile):
        block = block0 + tile
        here = pl.multiple_of(tile * AROWS + 8, 8)

        @pl.when(block < kv_blocks)
        def _():
            at = pl.ds(pl.multiple_of(block * cols_tile, cols_tile), cols_tile)
            text = jnp.concatenate([texts[k, :, :, at].reshape(tok, cols_tile) for k in range(gd)], axis=0)
            grad = dot(text, turned_dkv[...], TN)
            for j in range(parts - 1):
                nat[pl.ds(here + j, cols_tile, stride=parts), :] = grad[:, j * C : (j + 1) * C]
            part = grad[:, (parts - 1) * C :]
            row, lane = iotas(cols_tile)
            before = jnp.where(row == 0, edge[0:1, :], pltpu.roll(part, 1, 0))
            nat[pl.ds(here - 1, cols_tile, stride=parts), :] = jnp.where(lane < wrap, before, part)
            edge[0:1, :] = part[cols_tile - 1 : cols_tile, :]

        @pl.when(block >= kv_blocks)
        def _():
            at = pl.multiple_of(jnp.minimum((block - kv_blocks) * AROWS, rest.shape[0] - 16 - AROWS), 8)
            row, lane = iotas(AROWS)
            both = jnp.where(lane >= lane0, rest[pl.ds(at + 8, AROWS), :], rest[pl.ds(at + 9, AROWS), :])
            nat[pl.ds(here, AROWS), :] = pltpu.roll(both, wrap, 1)

            @pl.when(block == kv_blocks)
            def _():
                row, lane = iotas(8)
                ahead = pltpu.roll(rest[8:16, :], wrap, 1)
                nat[pl.ds(here - 1, 1), :] = jnp.where(lane < wrap, edge[...], ahead)[0:1, :]

    def assemble():
        first_table, first_gain = 9 * C, 9 * C + 2 * LEVELS
        first_query = first_gain + 4
        first_out = first_query + C * HEADS
        quarter = conv.shape[1]
        width = dkv.shape[1]
        heads = width // HEAD
        for owner in range(4):
            lo, hi = owner * rest_rows, (owner + 1) * rest_rows

            @pl.when(n == owner)
            def _():
                for k in range(4):
                    a, b = max(lo, k * quarter), min(hi, (k + 1) * quarter)
                    if a < b:
                        assert (a, b) == (k * quarter, (k + 1) * quarter)
                        rest[8 + a - lo : 8 + b - lo, :] = conv[k].astype(F32)
                a, b = max(lo, first_query), min(hi, first_out)
                if a < b:
                    for h in range(HEADS):
                        c0 = max(0, -(-(a - first_query - h) // HEADS))
                        c1 = min(C, -(-(b - first_query - h) // HEADS))
                        cols = slice(h % heads * HEAD, h % heads * HEAD + HEAD)
                        c_lo, c_hi = c0 // 16 * 16, (c1 + 15) // 16 * 16
                        value = t_all[h // heads, c_lo:c_hi, cols].astype(F32)
                        start = first_query + c0 * HEADS + h - lo
                        rest[pl.ds(8 + start, c1 - c0, stride=HEADS), :] = value[c0 - c_lo : c1 - c_lo]
                for h in range(HEADS):
                    a, b = first_out + h * HEAD, first_out + (h + 1) * HEAD
                    if lo <= a and b <= hi:
                        cols = slice(h % heads * HEAD, h % heads * HEAD + HEAD)
                        rest[8 + a - lo : 8 + b - lo, :] = t_all[2 + h // heads, :, cols].astype(F32).T
                    else:
                        assert b <= lo or hi <= a
                if lo <= first_gain and first_gain + 4 <= hi:
                    total = small[0, 0:4]
                    for k in range(1, gd):
                        total = total + small[k, 0:4]
                    rest[8 + first_gain - lo : 8 + first_gain + 4 - lo, :] = total


        for k in range(gd):
            for level, shift_by in ((0, 0), (1, NOISE_LEVELS)):
                found = jnp.max(small[k, 7:8, level : level + 1]).astype(jnp.int32) + shift_by
                for half in range(2):
                    at_row = first_table + 2 * found + half - n * rest_rows

                    @pl.when((at_row >= 0) & (at_row < rest_rows))
                    def _():
                        rest[pl.ds(at_row + 8, 1), :] += small[k, 4 + half : 5 + half]

    @pl.when(s == 0)
    def _():
        edge[...] = jnp.zeros_like(edge)
        rest[...] = jnp.zeros_like(rest)
        carry[...] = jnp.zeros_like(carry)
        shift[...] = jnp.zeros_like(shift)
        row, lane = iotas(dkv.shape[0])
        moved = [
            pltpu.roll(dkv[:, j * C : (j + 1) * C].astype(F32), wrap, 1) for j in range(parts)
        ]
        for j in range(parts):
            turned_dkv[:, j * C : (j + 1) * C] = jnp.where(
                lane < wrap, moved[j], moved[(j + 1) % parts]
            ).astype(BF16)

        @pl.when(start + length > kv_rows * C)
        def _():
            assemble()

        natural(0)

    natural(s + 1)
    row, lane = iotas(AROWS)
    g = nat[pl.ds(s * AROWS + row_off + 8, AROWS), :] * scal[0:1]
    one = BETA_ONE * first.reshape(AROWS, C)[...] + (1.0 - BETA_ONE) * g
    two = BETA_TWO * second.reshape(AROWS, C)[...] + (1.0 - BETA_TWO) * g * g
    first_out.reshape(AROWS, C)[...] = one
    second_out.reshape(AROWS, C)[...] = two
    fixed_one = one * (scal[1:2] * (1.0 / (1.0 - BETA_ONE**STEP)))
    fixed_two = two * (1.0 / (1.0 - BETA_TWO**STEP))
    root = fixed_two * lax.rsqrt(fixed_two)
    step = fixed_one * pl.reciprocal(root + ADAM_EPS, approx=True)
    step = jnp.where((s * AROWS + row) * C + lane < length, step, 0.0)
    turned = pltpu.roll(step, lane0, 1)
    above = pltpu.roll(turned, 1, 0)
    above = jnp.where(row == 0, carry[0:1, :], above)
    carry[0:1, :] = turned[AROWS - 1 : AROWS, :]
    shift[pl.ds(row_shift, AROWS), :] = jnp.where(lane < lane0, above, turned)
    step_out[...] = shift[0:AROWS, :].astype(BF16)
    shift[0:16, :] = shift[AROWS : AROWS + 16, :]


def run_adam(texts, dkv, conv, t_all, small, scal, first, second, length, kv_rows, rest_rows):
    gd = texts.shape[0]
    tiles = adam_tiles(length)
    flat = pl.BlockSpec((1, AROWS * C), lambda s: (0, s))
    rest_pad = (pl.cdiv(rest_rows, AROWS) + 1) * AROWS + 16
    return pl.pallas_call(
        functools.partial(adam_kernel, gd, length, kv_rows, rest_rows),
        out_shape=(
            jax.ShapeDtypeStruct((1, length), F32),
            jax.ShapeDtypeStruct((1, length), F32),
            near(gd)((tiles * AROWS, C), BF16),
        ),
        grid=(tiles,),
        in_specs=[pl.BlockSpec(memory_space=pltpu.VMEM)] * 6 + [flat, flat],
        out_specs=[flat, flat, pl.BlockSpec((AROWS, C), lambda s: (s, 0))],
        scratch_shapes=[
            pltpu.VMEM(((tiles + 1) * AROWS + 16, C), F32),
            pltpu.VMEM((rest_pad, C), F32),
            pltpu.VMEM(dkv.shape, BF16),
            pltpu.VMEM((8, C), F32),
            pltpu.VMEM((AROWS + 16, C), F32),
            pltpu.VMEM((8, C), F32),
        ],
        compiler_params=pltpu.CompilerParams(vmem_limit_bytes=ADAM_VMEM),
        name="adam",
    )(*(hold(v, gd) for v in (texts, dkv, conv, t_all, small, scal, first, second)))


ADAM_VMEM = 24 * 2**20


def share_kernel(
    gd, rows, chunk, pad, l1, l2, u_ref, w_far, o_far, out_ref, w_near, o_near,
    recv_a, recv_b, part, in_sem, s_u, s_fo, s_fi, s_y, r_a, r_b, r_f, r_y,
):
    loads = [
        pltpu.make_async_copy(w_far, w_near.at[pl.ds(0, w_far.shape[0])], in_sem.at[1]),
        pltpu.make_async_copy(o_far, o_near.at[pl.ds(0, o_far.shape[0])], in_sem.at[2]),
    ]
    wide = lax.axis_index("wide")
    g = wide // gd
    spot = wide % gd
    chunks = rows // chunk
    is_outer = jnp.logical_or(g == 0, g == GROUPS - 1)
    is_inner = jnp.logical_not(is_outer)
    low = g < GROUPS // 2
    outer_id = jnp.where(low, g - 1, g + 1) * gd + spot
    mate_id = jnp.where(low, g + 1, g - 1) * gd + spot
    barrier = pltpu.get_barrier_semaphore()
    for k in range(1, gd):
        other = g * gd + lax.rem(spot + k, gd)
        pl.semaphore_signal(barrier, inc=1, device_id={"wide": other}, device_id_type=MESH)
    pl.semaphore_signal(barrier, inc=1, device_id={"wide": mate_id}, device_id_type=MESH)
    @pl.when(is_inner)
    def _():
        pl.semaphore_signal(barrier, inc=1, device_id={"wide": outer_id}, device_id_type=MESH)
        pl.semaphore_wait(barrier, gd + 1)
    @pl.when(is_outer)
    def _():
        pl.semaphore_wait(barrier, gd)

    def sl(c):
        return pl.ds(pl.multiple_of(c * chunk, chunk), chunk)
    def ol(c):
        return pl.ds(pl.multiple_of(pad + c * chunk, 16), chunk)
    def copy(src, dst, ss, rs, dev):
        return pltpu.make_async_remote_copy(src_ref=src, dst_ref=dst, send_sem=ss, recv_sem=rs,
                                            device_id={"wide": dev}, device_id_type=MESH)
    def send_a(c):
        return copy(u_ref.at[sl(c)], recv_a.at[sl(c)], s_u.at[c], r_a.at[c], mate_id)
    def send_b(c):
        return copy(part.at[sl(c)], recv_b.at[sl(c)], s_u.at[c], r_b.at[c], mate_id)
    def send_fo(c):
        return copy(out_ref.at[spot, ol(c)], out_ref.at[spot, ol(c)], s_fo.at[c], r_f.at[c], outer_id)
    def send_fi(c):
        return copy(out_ref.at[spot, ol(c)], out_ref.at[spot, ol(c)], s_fi.at[c], r_f.at[c], mate_id)
    def send_y(c, k):
        return copy(out_ref.at[spot, ol(c)], out_ref.at[spot, ol(c)], s_y.at[k - 1, c], r_y.at[k - 1, c],
                    g * gd + lax.rem(spot + k, gd))
    def wait_y(c, k):
        src = lax.rem(spot + gd - k, gd)
        copy(out_ref.at[src, ol(c)], out_ref.at[src, ol(c)], s_y.at[k - 1, c], r_y.at[k - 1, c], wide).wait_recv()
    def spread(c):
        for k in range(1, gd):
            send_y(c, k).start()
    def is_root(c):
        return lax.rem(c + g, 2) == 1

    @pl.when(is_outer)
    def _():
        @pl.loop(0, chunks)
        def _(c):
            send_a(c).start()
    for load in loads:
        load.start()
    for p in range(gd):
        out_ref[p, 0:pad] = jnp.zeros((pad, 128), jnp.bfloat16)
        out_ref[p, pad + rows : rows + 2 * pad] = jnp.zeros((pad, 128), jnp.bfloat16)

    @pl.when(is_outer)
    def _():
        @pl.loop(0, chunks)
        def _(c):
            send_fo(c).wait_recv()
            spread(c)
    @pl.when(is_inner)
    def _():
        @pl.loop(0, chunks + l2)
        def _(c):
            @pl.when(jnp.logical_and(c < chunks, jnp.logical_not(is_root(c))))
            def _():
                send_a(c).wait_recv()
                part[sl(c)] = (u_ref[sl(c)].astype(jnp.float32) + recv_a[sl(c)].astype(jnp.float32)).astype(jnp.bfloat16)
                send_b(c).start()
            d = c - l1
            @pl.when(jnp.logical_and(jnp.logical_and(d >= 0, d < chunks), is_root(d)))
            def _():
                send_a(d).wait_recv()
                send_b(d).wait_recv()
                out_ref[spot, ol(d)] = (u_ref[sl(d)].astype(jnp.float32) + recv_a[sl(d)].astype(jnp.float32) + recv_b[sl(d)].astype(jnp.float32)).astype(jnp.bfloat16)
                send_fo(d).start()
                send_fi(d).start()
                spread(d)
            e = c - l2
            @pl.when(jnp.logical_and(e >= 0, jnp.logical_not(is_root(e))))
            def _():
                send_fi(e).wait_recv()
                send_fo(e).start()
                spread(e)
    @pl.loop(0, chunks)
    def _(c):
        for k in range(1, gd):
            wait_y(c, k)
            send_y(c, k).wait_send()
        @pl.when(is_outer)
        def _():
            send_a(c).wait_send()
        @pl.when(is_inner)
        def _():
            send_fo(c).wait_send()
            @pl.when(is_root(c))
            def _():
                send_fi(c).wait_send()
            @pl.when(jnp.logical_not(is_root(c)))
            def _():
                send_b(c).wait_send()
    for load in loads:
        load.wait()


def share(u, weights2, outer2, gd, rows, chunk, pad, l1, l2):
    n = rows // chunk
    D = pltpu.SemaphoreType.DMA
    few = max(gd - 1, 1)
    held = pl.cdiv(weights2.shape[0], 256) * 256
    vmem, hbm = pl.BlockSpec(memory_space=pltpu.VMEM), pl.BlockSpec(memory_space=pltpu.HBM)
    return pl.pallas_call(
        functools.partial(share_kernel, gd, rows, chunk, pad, l1, l2),
        out_shape=(near(gd)((gd, rows + 2 * pad, C), BF16),) + (near(gd)((held, C), F32),) * 2,
        in_specs=[vmem, hbm, hbm],
        out_specs=(vmem,) * 3,
        scratch_shapes=[pltpu.VMEM((rows, C), BF16)] * 3
        + [
            D((3,)), D((n,)), D((n,)), D((n,)), D((few, n)),
            D((n,)), D((n,)), D((n,)), D((few, n)),
        ],
        compiler_params=pltpu.CompilerParams(
            collective_id=9, has_side_effects=True, vmem_limit_bytes=SHARE_VMEM
        ),
        name="share",
    )(hold(u, gd), far(weights2), far(outer2))


SHARE_VMEM = 32 * 2**20


def final_kernel(bases, pad, block, weights, outer, pieces, scal, new_weights, momentum, loss, count, held, sem):
    rows = new_weights.shape[0]
    total = pieces.shape[1]
    steps = pl.cdiv(rows, block)

    def writes(b, slot, size):
        here = pl.ds(b * block, size)
        return [
            pltpu.make_async_copy(held.at[slot, k, pl.ds(0, size)], out.at[here], sem.at[slot, k])
            for k, out in enumerate((new_weights, momentum))
        ]

    for b in range(steps):
        slot = b % 3
        size = min(block, rows - b * block)
        if b >= 3:
            for copy in writes(b - 3, slot, block):
                copy.wait()
        averaged = jnp.zeros((block, C), F32)
        for p, base in enumerate(bases):
            at = min(max(b * block - base + pad, 0), total - block)
            averaged = averaged + pieces[p, at : at + block, :].astype(F32)
        w = weights[b * block : (b + 1) * block, :]
        averaged = averaged + (INNER_RATE * DECAY_RATE) * w
        moved = OUTER_MOMENTUM * outer[b * block : (b + 1) * block, :] + averaged
        held[slot, 1] = moved
        held[slot, 0] = w - OUTER_RATE * (averaged + OUTER_MOMENTUM * moved)
        for copy in writes(b, slot, size):
            copy.start()
    loss[0] = jnp.max(scal[2:3])
    count[0] = jnp.max(scal[3:4])
    for b in range(max(steps - 3, 0), steps):
        for copy in writes(b, b % 3, min(block, rows - b * block)):
            copy.wait()


def run_final(rows, weights2, outer2, pieces, scal, bases, pad):
    hbm, smem = pl.BlockSpec(memory_space=pltpu.HBM), pl.BlockSpec(memory_space=pltpu.SMEM)
    block = weights2.shape[0] // 16
    assert block % 16 == 0 and block <= pad
    return pl.pallas_call(
        functools.partial(final_kernel, bases, pad, block),
        out_shape=(jax.ShapeDtypeStruct((rows, C), F32),) * 2 + (jax.ShapeDtypeStruct((1,), F32),) * 2,
        in_specs=[pl.BlockSpec(memory_space=pltpu.VMEM)] * 4,
        out_specs=(hbm, hbm, smem, smem),
        scratch_shapes=[pltpu.VMEM((3, 2, block, C), F32), pltpu.SemaphoreType.DMA((3, 2))],
        compiler_params=pltpu.CompilerParams(vmem_limit_bytes=12 * 2**20),
        name="final",
    )(*(hold(v, len(bases)) for v in (weights2, outer2, pieces, scal)))


def per_device(
    weights, first_moment, second_moment, outer_momentum, noisy_input, target,
    text_tokens, text_mask, noise_level, aug_level, crop_size,
):
    length = first_moment.shape[1]
    wide_count = lax.axis_size("wide")
    gd = wide_count // GROUPS
    weights2 = weights.reshape(-1, C)
    outer2 = outer_momentum.reshape(-1, C)

    texts, dkv, conv_all, t_all, small_all, scal, first, second = run_step(
        gd, wide_count, noise_level, aug_level, crop_size, weights2, noisy_input, target, text_tokens,
        first_moment, second_moment, text_mask,
    )
    kv_rows = TEXT_D * dkv.shape[1] // C
    rest_rows = weights2.shape[0] - kv_rows
    moment_one, moment_two, step = run_adam(
        texts, dkv, conv_all, t_all, small_all, scal, first, second, length, kv_rows, rest_rows
    )
    chunk = 160
    rows = pl.cdiv(length // C + 18, chunk) * chunk
    pad = 1120
    pieces, w_near, o_near = share(step, weights2, outer2, gd, rows, chunk, pad, 3, 6)
    bases = [p * length // C // 16 * 16 for p in range(gd)]
    new_weights, momentum_out, loss, count = run_final(
        weights2.shape[0], w_near, o_near, pieces, scal, bases, pad
    )
    return (
        new_weights.reshape(-1), momentum_out.reshape(-1), moment_one, moment_two,
        loss, count,
    )


def solution(mesh):
    placed = (
        P("narrow"),
        P("narrow", "wide"),
        P("narrow", "wide"),
        P("narrow"),
        P("wide", "narrow", None, None),
        P("wide", "narrow", None, None),
        P("wide", "narrow", None),
        P("wide", "narrow"),
        P("wide"),
        P("wide"),
        P("wide"),
    )
    return jax.shard_map(
        per_device,
        mesh=mesh,
        in_specs=placed,
        out_specs=(P("narrow"), P("narrow"), P("narrow", "wide"), P("narrow", "wide"), P(), P()),
        check_vma=False,
    )
```

```python
import functools
import math

import jax
import jax.numpy as jnp
from jax import lax
from jax.experimental import pallas as pl
from jax.experimental.pallas import tpu as pltpu
from jax.sharding import PartitionSpec as P

MESH = pl.DeviceIdType.MESH
C = 128
NORM_GROUPS = 32
HEADS = 8
HEAD = 128
TEXT_D = 4096
H = 128
W = 128
NOISE_LEVELS = 1000
AUG_LEVELS = 24
LEVELS = NOISE_LEVELS + AUG_LEVELS
GROUPS = 4
STEP = 8


EPS_NORM = 1e-05
CLIP_NORM = 0.002
BETA_ONE = 0.9
BETA_TWO = 0.99
INNER_RATE = 0.01
DECAY_RATE = 0.01
ADAM_EPS = 1e-08
OUTER_RATE = 0.7
OUTER_MOMENTUM = 0.9

TN = (((0,), (0,)), ((), ()))
F32 = jnp.float32
BF16 = jnp.bfloat16
LOG2E = 1.4426950408889634
LN2 = 0.6931471805599453
NT = (((1,), (1,)), ((), ()))
TILE = 8
TILE3 = 8


def dot(a, b, dims=(((1,), (0,)), ((), ()))):
    return lax.dot_general(a, b, dims, preferred_element_type=F32)


def two_parts(value):
    top = value.astype(BF16)
    return top, (value - top.astype(F32)).astype(BF16)


def shifted(value, by, keep):
    return jnp.where(keep, pltpu.roll(value, by, 0), 0.0)


CTILE = 16


def vectors(small, height, columns):
    total = small[0] + small[1] + small[2] + small[3]
    lane_group = lax.broadcasted_iota(jnp.int32, (C, C), 0) // (C // NORM_GROUPS)
    same = (lane_group == lax.broadcasted_iota(jnp.int32, (C, C), 1) // (C // NORM_GROUPS)).astype(F32)
    stats = jnp.dot(total[0:8], same, precision=lax.Precision.HIGHEST, preferred_element_type=F32)
    count = height * columns * C // NORM_GROUPS
    mean = stats[0:1] * (1.0 / count)
    spread = lax.rsqrt(stats[1:2] * (1.0 / count) - mean * mean + EPS_NORM)
    film_scale, film_shift = 1.0 + total[2:3], total[3:4]
    gains = total[8:12]
    gain = gains[0:1] * film_scale
    offset = gains[1:2] * film_scale + film_shift
    slope = spread * gain
    return mean, spread, slope, offset - mean * slope, film_scale, gains


def edges(columns):
    place = lax.broadcasted_iota(jnp.int32, (columns, C), 0)
    return place > 0, place < columns - 1


def activate(band, columns, height, noisy, small, conv_w, act3, wt3):
    row0 = lax.axis_index("narrow") * band
    mean, spread, slope, base, film_scale, gains = vectors(small, height, columns)
    not_first, not_last = edges(columns)

    @pl.loop(0, band + 4)
    def _(r):
        scaled = noisy[r].astype(F32) * slope + base
        value = scaled * jax.nn.sigmoid(scaled)
        row = row0 + r - 2
        value = jnp.where(jnp.logical_and(row >= 0, row < height), value, 0.0)
        value = value.astype(BF16).astype(F32)
        act3[r, :, 0:C] = shifted(value, 1, not_first).astype(BF16)
        act3[r, :, C : 2 * C] = value.astype(BF16)
        act3[r, :, 2 * C : 3 * C] = shifted(value, columns - 1, not_last).astype(BF16)

    for tap in range(9):
        rows = slice(tap * C, (tap + 1) * C)
        wt3[rows, :] = conv_w[rows, :].astype(F32).T.astype(BF16)


def convolve_tiles(first, last, band, columns, height, noisy, small, conv_w, act3, conv_s, xhat_s, rs_s, low_s):
    gains = vectors(small, height, columns)[5]
    pix = CTILE * columns

    @pl.loop(first, last)
    def _(t):
        q = t * CTILE
        conv = noisy[pl.ds(q + 2, CTILE)].astype(F32).reshape(pix, C)
        for dy in range(3):
            window = act3[pl.ds(q + 1 + dy, CTILE)].reshape(pix, 3 * C)
            conv = conv + dot(window, conv_w[dy * 3 * C : (dy + 1) * 3 * C, :])
        centered = conv - jnp.mean(conv, axis=1, keepdims=True)
        rs = lax.rsqrt(jnp.mean(centered * centered, axis=1, keepdims=True) + EPS_NORM)
        xhat = centered * rs
        here = pl.ds(q, CTILE)
        conv_s[here] = conv.reshape(CTILE, columns, C)
        xhat_s[here] = xhat.reshape(CTILE, columns, C)
        rs_s[here] = jnp.broadcast_to(rs, (pix, C)).reshape(CTILE, columns, C)
        low_s[here] = (xhat * gains[2:3] + gains[3:4]).astype(BF16).reshape(CTILE, columns, C)


def main_body(
    start_near, start_far, edge_send, edge_wait, band, columns, height, heads,
    rest_rows, crop_size, noise_level, aug_level, noisy, target, small, rest, keyval,
    blocks, dconv_w, packet, right,
    act3, wt3, conv_s, xhat_s, rs_s, low_s, diff3,
    m_cat, m_cat_t, n_cat, n_cat_t, conv_t, probs, dscore, y_t, z_t, sums,
    stage, query, out_w,
):
    tok, kv_block = keyval.shape[1:]
    width = heads * HEAD
    per_block = kv_block // HEAD
    narrow = lax.axis_index("narrow")
    row0 = narrow * band
    crop = crop_size[0]
    pix = TILE * columns
    first_query = 9 * C + 2 * LEVELS + 4
    first_out = first_query + C * heads

    def take(first, count, place):
        while count:
            owner, local = divmod(first, rest_rows)
            use = min(count, rest_rows - local)
            a = local // 16 * 16
            b = (local + use + 15) // 16 * 16
            stage[0 : b - a, :] = rest[owner, a:b, :].astype(F32)
            place(stage[local - a : local - a + use, :], use)
            first, count = first + use, count - use

    def filler(ref):
        at = [0]

        def place(value, use):
            ref[at[0] : at[0] + use, :] = value
            at[0] += use

        return place

    take(first_query, C * heads, filler(query))
    take(first_out, width, filler(out_w))
    mean, spread, slope, base, film_scale, gains = vectors(small, height, columns)
    ln_gain = gains[2:3]
    quarter = tok // 4
    masks = [small[owner, 4:5, 0:quarter] for owner in range(4)]
    ok = (jnp.concatenate(masks, axis=1) > 0.0) | (lax.broadcasted_iota(jnp.int32, (1, tok), 1) == 0)
    factor = LOG2E / math.sqrt(HEAD)
    for head in range(heads):
        cols = slice(head * HEAD, (head + 1) * HEAD)
        tcols = slice(head * tok, (head + 1) * tok)
        block, at = head // per_block, head % per_block * HEAD
        query_head = query[pl.ds(head, C, stride=heads), :].astype(BF16)
        out_head = out_w[cols, :].astype(BF16)
        m_head = dot(query_head, keyval[block, :, at : at + HEAD], NT) * factor

        @pl.when(narrow == block)
        def _():
            right[:, at : at + HEAD] = query_head

        @pl.when(narrow == block + heads // per_block)
        def _():
            right[:, at : at + HEAD] = out_w[cols, :].T.astype(BF16)

        top, rest = two_parts(m_head)
        m_cat[:C, tcols] = top
        m_cat[C:, tcols] = rest
        top, rest = two_parts(m_head.T)
        m_cat_t[tcols, :C] = top
        m_cat_t[tcols, C:] = rest
        n_head = dot(keyval[block + heads // per_block, :, at : at + HEAD], out_head)
        top, rest = two_parts(n_head)
        n_cat[tcols, :C] = top
        n_cat[tcols, C:] = rest
        top, rest = two_parts(n_head.T)
        n_cat_t[:C, tcols] = top
        n_cat_t[C:, tcols] = rest
    y_t[...] = jnp.zeros_like(y_t)
    z_t[...] = jnp.zeros_like(z_t)
    conv_t[...] = jnp.zeros_like(conv_t)
    sums[...] = jnp.zeros_like(sums)
    not_first, not_last = edges(columns)
    pix_row = lax.broadcasted_iota(jnp.int32, (pix, C), 0) // columns
    pix_col = lax.broadcasted_iota(jnp.int32, (pix, C), 0) % columns
    tiles = band // TILE

    @pl.loop(0, tiles)
    def _(t):
        q = jnp.where(t == 0, 0, jnp.where(t == 1, tiles - 1, t - 1)) * TILE
        here = pl.ds(q, TILE)
        conv = conv_s[here].reshape(pix, C)
        low = low_s[here].reshape(pix, C)
        low2 = jnp.concatenate([low, low], axis=1)
        for head in range(heads):
            tcols = slice(head * tok, (head + 1) * tok)
            if head % 2 == 0:
                scores = dot(low2, m_cat[:, head * tok : (head + 2) * tok])
            score = scores[:, head % 2 * tok : (head % 2 + 1) * tok]
            score = jnp.where(ok, score, -1e30)
            e = jnp.exp2(score - jnp.max(score, axis=1, keepdims=True))
            p = e * (1.0 / jnp.sum(e, axis=1, keepdims=True))
            probs[:, tcols] = p.astype(BF16)
        mixed = dot(probs[...], n_cat[...])
        output = conv + mixed[:, :C] + mixed[:, C:]
        valid = (row0 + q + pix_row < crop) & (pix_col < crop)
        err = jnp.where(valid, output - target[pl.ds(q + 1, TILE)].astype(F32).reshape(pix, C), 0.0)
        sums[4:5, :] += jnp.sum(err * err, axis=0, keepdims=True)
        dout = 2.0 * err
        dout_low = dout.astype(BF16)
        dout2 = jnp.concatenate([dout_low, dout_low], axis=1)
        for head in range(heads):
            tcols = slice(head * tok, (head + 1) * tok)
            if head % 2 == 0:
                dprobs = dot(dout2, n_cat_t[:, head * tok : (head + 2) * tok])
            dprob = dprobs[:, head % 2 * tok : (head % 2 + 1) * tok]
            p = probs[:, tcols].astype(F32)
            pd = p * dprob
            ds = pd - p * jnp.sum(pd, axis=1, keepdims=True)
            dscore[:, tcols] = ds.astype(BF16)
        dlay2 = dot(dscore[...], m_cat_t[...])
        dlay = (dlay2[:, :C] + dlay2[:, C:]) * LN2
        xhat = xhat_s[here].reshape(pix, C)
        rs = rs_s[here].reshape(pix, C)
        sums[2:3, :] += jnp.sum(dlay * xhat, axis=0, keepdims=True)
        sums[3:4, :] += jnp.sum(dlay, axis=0, keepdims=True)
        dxh = dlay * ln_gain
        dconv = dout + rs * (
            dxh
            - jnp.mean(dxh, axis=1, keepdims=True)
            - xhat * jnp.mean(dxh * xhat, axis=1, keepdims=True)
        )
        dout_t = dout.T.astype(BF16)
        lay_t = low.astype(F32).T.astype(BF16)
        y_t[...] += dot(dout_t, probs[...])
        z_t[...] += dot(lay_t, dscore[...])
        dconv_t = dconv.T.astype(BF16)
        for dy in range(3):
            window = act3[pl.ds(q + 1 + dy, TILE)].reshape(pix, 3 * C)
            conv_t[:, dy * 3 * C : (dy + 1) * 3 * C] += dot(dconv_t, window)
        for k in range(TILE):
            one = dconv[k * columns : (k + 1) * columns]
            diff3[q + 1 + k, :, 0:C] = shifted(one, columns - 1, not_last).astype(BF16)
            diff3[q + 1 + k, :, C : 2 * C] = one.astype(BF16)
            diff3[q + 1 + k, :, 2 * C : 3 * C] = shifted(one, 1, not_first).astype(BF16)

        for order in range(2):
            @pl.when(t == order)
            def _():
                edge_send(order)

    def back(t):
        r = t * TILE3
        grad = jnp.zeros((TILE3 * columns, C), F32)
        for dy in range(3):
            window = diff3[pl.ds(r + 2 - dy, TILE3)].reshape(TILE3 * columns, 3 * C)
            grad = grad + dot(window, wt3[dy * 3 * C : (dy + 1) * 3 * C, :])
        x = noisy[pl.ds(r + 2, TILE3)].astype(F32).reshape(TILE3 * columns, C)
        scaled = x * slope + base
        sig = jax.nn.sigmoid(scaled)
        ds = grad * (sig * (1.0 + scaled * (1.0 - sig)))
        sums[0:1, :] += jnp.sum(ds, axis=0, keepdims=True)
        sums[1:2, :] += jnp.sum(ds * ((x - mean) * spread), axis=0, keepdims=True)

    share_rows = dconv_w.shape[1]
    full = conv_t[...].T
    for owner in range(4):
        dconv_w[owner] = full[owner * share_rows : (owner + 1) * share_rows].astype(BF16)
        part = z_t if owner < 2 else y_t
        at = owner % 2 * per_block * tok
        blocks[owner] = part[:, at : at + per_block * tok].astype(BF16)
    start_near()
    edge_wait()
    halves = 1
    pl.loop(0, halves)(back)
    start_far()
    pl.loop(halves, band // TILE3)(back)
    a, b = sums[0:1], sums[1:2]
    packet[0:1] = film_scale * b
    packet[1:2] = film_scale * a
    packet[2:4] = sums[2:4]
    packet[4:5] = gains[0:1] * b + gains[1:2] * a
    packet[5:6] = a
    packet[6:7] = sums[4:5]
    lane = lax.broadcasted_iota(jnp.int32, (1, C), 1)
    facts = jnp.zeros((1, C), F32)
    for k, fact in enumerate((noise_level[0], aug_level[0], crop)):
        facts = jnp.where(lane == k, fact.astype(F32), facts)
    packet[7:8] = jnp.where(row0 == 0, facts, 0.0)


def cross_ids():
    n = lax.axis_index("narrow")
    mate = n + 1 - 2 * lax.rem(n, 2)
    across = lax.rem(n + 2, 4)
    corner = lax.rem(mate + 2, 4)
    return n, mate, across, corner


def to_narrow(src, dst, send_sem, recv_sem, device):
    return pltpu.make_async_remote_copy(
        src_ref=src, dst_ref=dst, send_sem=send_sem, recv_sem=recv_sem,
        device_id={"narrow": device}, device_id_type=MESH,
    )


class Gather:
    def __init__(self, view, sems, ids):
        self.view, self.sems = view, sems
        self.n, self.mate, self.across, self.corner = ids

    def _copy(self, block, slot, device):
        ref = self.view(block)
        return to_narrow(ref, ref, self.sems.at[0, slot], self.sems.at[1, slot], device)

    def start(self):
        self._copy(self.n, 1, self.across).start()
        self._copy(self.n, 0, self.mate).start()

    def relay(self):
        self._copy(self.across, 1, self.across).wait_recv()
        self._copy(self.across, 2, self.mate).start()

    def wait(self):
        self._copy(self.mate, 0, self.mate).wait_recv()
        self._copy(self.corner, 2, self.mate).wait_recv()

    def drain(self):
        self._copy(self.n, 1, self.across).wait_send()
        self._copy(self.n, 0, self.mate).wait_send()
        self._copy(self.across, 2, self.mate).wait_send()


def rest_needs(rest_rows):
    first, last = 9 * C, 9 * C + 2 * LEVELS
    needs = []
    for owner in range(4):
        lo, hi = owner * rest_rows, (owner + 1) * rest_rows
        keep = [r for r in ((lo, min(hi, first)), (max(lo, last), hi)) if r[0] < r[1]]
        assert len(keep) <= 1
        if keep:
            a, b = keep[0][0] - lo, keep[0][1] - lo
            needs.append((a // 16 * 16, (b + 15) // 16 * 16))
        else:
            needs.append(None)
    return needs


KPARTS = 4
WPARTS = 8


def front_body(
    kv_rows, rest_rows, greet, to_group, early, noise_level, aug_level, weights, noisy, target, text, mask,
    noisy_ext, target_ext, text_all, rest_all, keyval, own_kv, small,
    wide_f32, wide_bf, rest_f32, acc,
    w_sem, in_sem, text_sem, rest_sem, kv_sem, small_sem, halo_sem,
):
    ids = cross_ids()
    n, mate, across, corner = ids
    band = noisy.shape[1]
    tokens, depth = text.shape[1:]
    in_text = pltpu.make_async_copy(text.at[0], text_all.at[n], in_sem.at[0])
    in_text.start()
    in_rest = pltpu.make_async_copy(
        weights.at[pl.ds(kv_rows, rest_rows)], rest_f32.at[pl.ds(0, rest_rows)], in_sem.at[1]
    )
    in_rest.start()
    in_noisy = pltpu.make_async_copy(noisy.at[0], noisy_ext.at[pl.ds(2, band)], in_sem.at[2])
    in_noisy.start()
    w_step = kv_rows // WPARTS
    in_w = [
        pltpu.make_async_copy(
            weights.at[pl.ds(k * w_step, w_step)], wide_f32.at[pl.ds(k * w_step, w_step)], w_sem.at[k]
        )
        for k in range(WPARTS)
    ]
    for copy in in_w:
        copy.start()
    in_target = pltpu.make_async_copy(target.at[0], target_ext.at[pl.ds(1, band)], in_sem.at[3])
    in_target.start()
    greet()

    k_step = depth // KPARTS
    texts = [
        Gather(
            lambda b, k=k: text_all.at[b, :, pl.ds(k * k_step, k_step)], text_sem.at[k], ids
        )
        for k in range(KPARTS)
    ]
    in_text.wait()
    for part in texts:
        part.start()

    in_rest.wait()
    rest_f32[rest_rows:] = jnp.zeros((rest_f32.shape[0] - rest_rows, C), F32)
    for k in range(2):
        row_sum = jnp.zeros((1, C), F32)
        for level in (noise_level[0], NOISE_LEVELS + aug_level[0]):
            row = 9 * C + 2 * level + k - n * rest_rows
            found = rest_f32[pl.ds(jnp.clip(row, 0, rest_rows - 1), 1), :]
            found = found.astype(BF16).astype(F32)
            row_sum = row_sum + jnp.where((row >= 0) & (row < rest_rows), found, 0.0)
        small[n, 2 + k : 3 + k, :] = row_sum
    small[n, 4:16, :] = jnp.zeros((12, C), F32)
    for owner in range(4):
        for k in range(4):
            row = 9 * C + 2 * LEVELS + k - owner * rest_rows
            if 0 <= row < rest_rows:
                @pl.when(n == owner)
                def _():
                    small[n, 8 + k : 9 + k, :] = rest_f32[row : row + 1, :].astype(BF16).astype(F32)
    small[n, 4:5, 0:tokens] = mask[...].astype(F32)
    in_noisy.wait()

    def add_row(r, sums):
        x = noisy_ext[r + 2].astype(F32)
        return (
            sums[0] + jnp.sum(x.reshape(-1, 8, C), axis=0),
            sums[1] + jnp.sum((x * x).reshape(-1, 8, C), axis=0),
        )

    zero = jnp.zeros((8, C), F32)
    one, two = lax.fori_loop(0, band, add_row, (zero, zero))
    small[n, 0:1, :] = jnp.sum(one, axis=0, keepdims=True)
    small[n, 1:2, :] = jnp.sum(two, axis=0, keepdims=True)
    others = (mate, across, corner)

    def small_copy(slot, block):
        return to_narrow(
            small.at[block], small.at[block], small_sem.at[0, slot], small_sem.at[1, slot], others[slot]
        )

    for slot in range(3):
        small_copy(slot, n).start()

    in_target.wait()
    up = jnp.maximum(n - 1, 0)
    down = jnp.minimum(n + 1, 3)
    noisy_up = to_narrow(
        noisy_ext.at[pl.ds(2, 2)], noisy_ext.at[pl.ds(band + 2, 2)], halo_sem.at[0, 0], halo_sem.at[1, 0], up
    )
    noisy_down = to_narrow(
        noisy_ext.at[pl.ds(band, 2)], noisy_ext.at[pl.ds(0, 2)], halo_sem.at[0, 1], halo_sem.at[1, 1], down
    )
    @pl.when(n > 0)
    def _():
        noisy_up.start()

    @pl.when(n < 3)
    def _():
        noisy_down.start()

    @pl.when(n == 0)
    def _():
        noisy_ext[0:2] = jnp.zeros((2,) + noisy_ext.shape[1:], BF16)

    @pl.when(n == 3)
    def _():
        noisy_ext[band + 2 : band + 4] = jnp.zeros((2,) + noisy_ext.shape[1:], BF16)

    needs = rest_needs(rest_rows)
    rest_all[n] = rest_f32[...].astype(BF16)

    def rest_copy(owner, slot, device):
        a, b = needs[owner]
        ref = rest_all.at[owner, pl.ds(a, b - a)]
        return to_narrow(ref, ref, rest_sem.at[0, slot, owner], rest_sem.at[1, slot, owner], device)

    for owner in range(4):
        if needs[owner] is not None:
            @pl.when(n == owner)
            def _():
                rest_copy(owner, 1, across).start()
                rest_copy(owner, 0, mate).start()

    parts = wide_bf.shape[1] // C
    rows = 256
    for k in range(WPARTS):
        in_w[k].wait()

        @pl.loop(k * w_step // parts // rows, (k + 1) * w_step // parts // rows)
        def _(i):
            for j in range(parts):
                wide_bf[pl.ds(pl.multiple_of(i * rows, rows), rows), j * C : (j + 1) * C] = wide_f32[
                    pl.ds(i * rows * parts + j, rows, stride=parts), :
                ].astype(BF16)

    acc[...] = jnp.zeros_like(acc)
    for k in range(KPARTS):
        texts[k].relay()
    for k in range(KPARTS):
        texts[k].wait()

        @pl.loop(0, k_step // 512)
        def _(i):
            at = pl.ds(pl.multiple_of(k * k_step + i * 512, 512), 512)
            acc[...] += dot(text_all[:, :, at].reshape(4 * tokens, 512), wide_bf[at, :])

    keyval[n] = acc[...].astype(BF16)
    own_kv[...] = acc[...].astype(BF16)
    keys = Gather(lambda b: keyval.at[b], kv_sem, ids)
    keys.start()
    to_group()


    def relay_rest(owner):
        if needs[owner] is not None:
            @pl.when(across == owner)
            def _():
                rest_copy(owner, 1, across).wait_recv()
                rest_copy(owner, 2, mate).start()

    def settle_rest(owner):
        if needs[owner] is not None:
            @pl.when(mate == owner)
            def _():
                rest_copy(owner, 0, mate).wait_recv()

            @pl.when(corner == owner)
            def _():
                rest_copy(owner, 2, mate).wait_recv()

            @pl.when(n == owner)
            def _():
                rest_copy(owner, 1, across).wait_send()
                rest_copy(owner, 0, mate).wait_send()

            @pl.when(across == owner)
            def _():
                rest_copy(owner, 2, mate).wait_send()

    relay_rest(0)
    for slot, block in ((0, mate), (1, across), (2, corner)):
        small_copy(slot, block).wait_recv()
        small_copy(slot, n).wait_send()

    @pl.when(n > 0)
    def _():
        noisy_down.wait_recv()
        noisy_up.wait_send()

    @pl.when(n < 3)
    def _():
        noisy_up.wait_recv()
        noisy_down.wait_send()

    settle_rest(0)
    early(0)
    for owner in range(1, 4):
        relay_rest(owner)
    keys.relay()
    early(1)
    for owner in range(1, 4):
        settle_rest(owner)
    keys.wait()
    keys.drain()
    for part in texts:
        part.drain()


def mid_stages(gd, height, columns, from_group, blocks, conv, packet, right, kvs, texts, *refs):
    (
        dkv_all, conv_all, t_all, small_all, scal,
        near_b, near_c, sum_b, sum_c, far_b, far_c, own_b, own_c, group_b, group_c,
        packets, wides, t_own, t_send, c_send, norms, conv_sum,
        near_sem, far_sem, group_sem, packet_sem, wide_sem, norm_sem, give_sem,
    ) = refs
    ids = cross_ids()
    n, mate, across, corner = ids
    others = (mate, across, corner)
    wide_count = wides.shape[0]
    wide = lax.axis_index("wide")
    group = wide // gd
    spot = lax.rem(wide, gd)
    tok, kv_block = kvs.shape[1:]
    heads = kv_block // HEAD
    depth = texts.shape[-1]
    scale = jnp.where(n < 2, 1.0 / math.sqrt(HEAD), 1.0)

    def lanes(h):
        return pl.ds(h * tok, tok)

    def near(slot, which):
        owner = corner if slot == 0 else mate
        src, dst = ((blocks, near_b), (conv, near_c))[which]
        return to_narrow(
            src.at[owner], dst.at[slot], near_sem.at[0, slot, which], near_sem.at[1, slot, which], mate
        )

    def far(h):
        if h < heads:
            src, dst = sum_b.at[:, lanes(h)], far_b.at[:, lanes(h)]
        else:
            src, dst = sum_c, far_c
        return to_narrow(src, dst, far_sem.at[0, h], far_sem.at[1, h], across)

    def group_copy(k, h):
        if h < heads:
            src, dst = own_b.at[:, lanes(h)], group_b.at[k - 1, :, lanes(h)]
        else:
            src, dst = own_c, group_c.at[k - 1]
        return pltpu.make_async_remote_copy(
            src_ref=src, dst_ref=dst,
            send_sem=group_sem.at[0, h, k - 1], recv_sem=group_sem.at[1, h, k - 1],
            device_id={"wide": group * gd + lax.rem(spot + k, gd)}, device_id_type=MESH,
        )

    def packet_copy(slot, block):
        return to_narrow(
            packets.at[block], packets.at[block],
            packet_sem.at[0, slot], packet_sem.at[1, slot], others[slot],
        )

    def wide_copy(k, block):
        return pltpu.make_async_remote_copy(
            src_ref=wides.at[block], dst_ref=wides.at[block],
            send_sem=wide_sem.at[0, k - 1], recv_sem=wide_sem.at[1, k - 1],
            device_id={"wide": lax.rem(wide + k, wide_count)}, device_id_type=MESH,
        )

    def start_near():
        for slot in range(2):
            for which in range(2):
                near(slot, which).start()

    def start_far():
        near(0, 0).wait_recv()
        sum_b[...] = (blocks[across].astype(F32) + near_b[0].astype(F32)).astype(BF16)
        for h in range(heads):
            far(h).start()
        near(0, 1).wait_recv()
        sum_c[...] = (conv[across].astype(F32) + near_c[0].astype(F32)).astype(BF16)
        far(heads).start()

    q_rows, q_from = 96, 80

    def give_head(src_n, h):
        src, dst = t_send.at[pl.ds(0, q_rows), lanes(h)], t_all.at[src_n, pl.ds(0, q_rows), lanes(h)]
        return to_narrow(src, dst, give_sem.at[0, 0, h], give_sem.at[1, src_n, h], 2)

    def give_tail(src_n, h):
        rows = pl.ds(q_from, C - q_from)
        src, dst = t_send.at[rows, lanes(h)], t_all.at[src_n, rows, lanes(h)]
        return to_narrow(src, dst, give_sem.at[0, 1, h], give_sem.at[1, src_n, h], 3)

    def give_values(h):
        src, dst = t_send.at[:, lanes(h)], t_all.at[2, :, lanes(h)]
        return to_narrow(src, dst, give_sem.at[0, 1, h], give_sem.at[1, 2, h], 3)

    def give_conv(src_n):
        return to_narrow(
            c_send, conv_all.at[src_n], give_sem.at[0, 2, 0], give_sem.at[1, src_n, heads], 0
        )

    def project(k, h, value):
        cols = slice(h * HEAD, (h + 1) * HEAD)
        dkv_all[k * tok : (k + 1) * tok, cols] = (dot(value, right[:, cols], TN) * scale).astype(BF16)
        term = dot(value, kvs[k, :, cols]) * scale
        t_own[:, cols] = term if k == 0 else t_own[:, cols] + term

    def finish(gram):
        packets[n] = packet[...]
        for slot in range(3):
            packet_copy(slot, n).start()
        near(1, 0).wait_recv()
        near(1, 1).wait_recv()
        for h in range(heads):
            far(h).wait_recv()
            at = slice(h * tok, (h + 1) * tok)
            own_b[:, at] = (
                blocks[n, :, at].astype(F32) + near_b[1, :, at].astype(F32) + far_b[:, at].astype(F32)
            ).astype(BF16)
            for k in range(1, gd):
                group_copy(k, h).start()
        for slot, block in enumerate(others):
            packet_copy(slot, block).wait_recv()
        wides[wide] = packets[0] + packets[1] + packets[2] + packets[3]

        @pl.loop(1, wide_count)
        def _(k):
            wide_copy(k, wide).start()

        far(heads).wait_recv()
        conv_sum[...] = conv[n].astype(F32) + near_c[1].astype(F32) + far_c[...].astype(F32)
        own_c[...] = conv_sum[...].astype(BF16)
        for k in range(1, gd):
            group_copy(k, heads).start()
        for h in range(heads):
            project(0, h, own_b[:, h * tok : (h + 1) * tok])
        from_group()
        def text_products(a, firsts):
            rows = slice(a * tok, (a + 1) * tok) if gd <= 4 else slice(0, tok)
            gram[rows, :] = jnp.zeros((tok, gd * tok), F32)

            @pl.loop(0, depth // 1024)
            def _(i):
                at = pl.ds(pl.multiple_of(i * 1024, 1024), 1024)
                left = texts[a, :, :, at].reshape(tok, 1024)
                for b in range(firsts, gd):
                    part = dot(left, texts[b, :, :, at].reshape(tok, 1024), NT)
                    gram[rows, b * tok : (b + 1) * tok] += part

        if gd <= 4:
            for a in range(gd):
                text_products(a, a)
        for h in range(heads):
            for k in range(1, gd):
                group_copy(k, h).wait_recv()
                project(k, h, group_b[k - 1, :, h * tok : (h + 1) * tok])
            at = slice(h * HEAD, (h + 1) * HEAD)
            t_send[:, at] = t_own[:, at].astype(BF16)
            for k in range(4):
                @pl.when(n == k)
                def _():
                    if k < 2:
                        give_head(k, h).start()
                        give_tail(k, h).start()
                    elif k == 2:
                        give_values(h).start()
                    else:
                        t_all[3, :, at] = t_send[:, at]
        for k in range(1, gd):
            group_copy(k, heads).wait_recv()
            conv_sum[...] += group_c[k - 1].astype(F32)
        c_send[...] = conv_sum[...].astype(BF16)
        for k in range(4):
            @pl.when(n == k)
            def _():
                if k > 0:
                    give_conv(k).start()
                else:
                    conv_all[0] = c_send[...]

        @pl.loop(1, wide_count)
        def _(k):
            wide_copy(k, lax.rem(wide + wide_count - k, wide_count)).wait_recv()

        sq = jnp.sum(t_own[...] * t_own[...]) + jnp.sum(conv_sum[...] * conv_sum[...])
        for a in range(gd):
            da = dkv_all[a * tok : (a + 1) * tok, :]
            if gd > 4:
                text_products(a, a)
            rows = slice(a * tok, (a + 1) * tok) if gd <= 4 else slice(0, tok)
            for b in range(a, gd):
                db = dkv_all[b * tok : (b + 1) * tok, :]
                top, low = two_parts(gram[rows, b * tok : (b + 1) * tok])
                part = jnp.sum(da.astype(F32) * (dot(top, db) + dot(low, db)))
                sq = sq + (part if a == b else 2.0 * part)
        gains = jnp.zeros((4, C), F32)
        shared = jnp.zeros((1, C), F32)
        for a in range(gd):
            mine = wides[group * gd + a]
            small_all[a] = mine
            gains = gains + mine[0:4]
            for b in range(gd):
                his = wides[group * gd + b]
                same = (mine[7:8, 0:1] == his[7:8, 0:1]).astype(F32) + (mine[7:8, 1:2] == his[7:8, 1:2]).astype(F32)
                shared = shared + same * (mine[4:5] * his[4:5] + mine[5:6] * his[5:6])
        shared_sq = jnp.sum(gains * gains) + jnp.sum(shared)
        norms[n] = jnp.full((8, C), sq + jnp.where(n == 0, shared_sq, 0.0), F32)

        def norm_copy(slot, block):
            return to_narrow(
                norms.at[block], norms.at[block], norm_sem.at[0, slot], norm_sem.at[1, slot], others[slot]
            )

        for slot in range(3):
            norm_copy(slot, n).start()

        def tally(k, found):
            there = wides[k]
            crop = there[7:8, 2:3]
            pixels = jnp.minimum(crop, float(height)) * jnp.minimum(crop, float(columns))
            mine = jnp.where(k // gd == group, pixels, 0.0)
            return found[0] + pixels, found[1] + mine, found[2] + jnp.sum(there[6:7], axis=1, keepdims=True)

        none = jnp.zeros((1, 1), F32)
        total, own_count, loss = lax.fori_loop(0, wide_count, tally, (none, none, none))
        for slot, block in enumerate(others):
            norm_copy(slot, block).wait_recv()
        squares = norms[0, 0:1] + norms[1, 0:1] + norms[2, 0:1] + norms[3, 0:1]
        norm = jnp.sqrt(squares) / total
        scal[0:1] = jnp.minimum(1.0, CLIP_NORM / norm) / total
        scal[1:2] = jnp.broadcast_to(INNER_RATE * own_count / total, (1, C))
        scal[2:3] = jnp.broadcast_to(loss, (1, C))
        scal[3:4] = jnp.broadcast_to(total, (1, C))
        scal[4:8] = jnp.zeros((4, C), F32)

        for k in range(4):
            @pl.when(n == k)
            def _():
                for h in range(heads):
                    if k < 2:
                        give_head(k, h).wait_send()
                        give_tail(k, h).wait_send()
                    if k == 2:
                        give_values(h).wait_send()
                        give_head(0, h).wait_recv()
                        give_head(1, h).wait_recv()
                    if k == 3:
                        give_tail(0, h).wait_recv()
                        give_tail(1, h).wait_recv()
                        give_values(h).wait_recv()
                if k > 0:
                    give_conv(k).wait_send()
                else:
                    for j in range(1, 4):
                        give_conv(j).wait_recv()
        for slot in range(2):
            for which in range(2):
                near(slot, which).wait_send()
        for h in range(heads + 1):
            far(h).wait_send()
            for k in range(1, gd):
                group_copy(k, h).wait_send()
        for slot in range(3):
            packet_copy(slot, n).wait_send()
            norm_copy(slot, n).wait_send()

        @pl.loop(1, wide_count)
        def _(k):
            wide_copy(k, wide).wait_send()

    return start_near, start_far, finish


def step_kernel(gd, wide_count, kv_rows, rest_rows, band, columns, counts, *refs):
    refs = list(refs)
    noise_level, aug_level, crop_size, weights, noisy, target, text, first, second, mask = refs[:10]
    texts, dkv_all, conv_all, t_all, small_all, scal, first_near, second_near = refs[10:18]
    n_front, n_main, n_mid = counts
    at = 18
    (noisy_ext, target_ext, rest_all, keyval, kvs, small) = refs[at : at + 6]
    act3, wt3, conv_s, xhat_s, rs_s, low_s, diff3 = refs[at + 6 : at + 13]
    at += 13
    front_sems = refs[at : at + n_front]
    at += n_front
    (blocks, conv, packet, right) = refs[at : at + 4]
    at += 4
    mid_refs = refs[at : at + n_mid]
    at += n_mid
    group_text_sem, ahead_sem, edge_sem = refs[at : at + 3]
    ahead = [
        pltpu.make_async_copy(far, near, ahead_sem.at[k])
        for k, (far, near) in enumerate(((first, first_near), (second, second_near)))
    ]
    n, mate, across, corner = cross_ids()
    wide = lax.axis_index("wide")
    group, spot = wide // gd, lax.rem(wide, gd)
    tok, kv_block = kvs.shape[1:]
    depth = text.shape[2]
    barrier = pltpu.get_barrier_semaphore()
    for other in (mate, across, corner):
        pl.semaphore_signal(barrier, inc=1, device_id={"narrow": other}, device_id_type=MESH)

    @pl.loop(1, wide_count)
    def _(k):
        pl.semaphore_signal(
            barrier, inc=1, device_id={"wide": lax.rem(wide + k, wide_count)}, device_id_type=MESH
        )

    def greet():
        pl.semaphore_wait(barrier, 3 + wide_count - 1)

    def group_send(k, which):
        buf = (texts, kvs)[which]
        return pltpu.make_async_remote_copy(
            src_ref=buf.at[0], dst_ref=buf.at[k],
            send_sem=group_text_sem.at[0, which, k - 1], recv_sem=group_text_sem.at[1, which, k - 1],
            device_id={"wide": group * gd + lax.rem(spot + k, gd)}, device_id_type=MESH,
        )

    def to_group():
        for which in (1, 0):
            for k in range(1, gd):
                group_send(k, which).start()

    def from_group():
        for which in (1, 0):
            for k in range(1, gd):
                group_send(k, which).wait_recv()
                group_send(k, which).wait_send()

    def early(part):
        common = (band, columns, H, noisy_ext, small, rest_all.at[0], act3)
        tiles = band // CTILE
        if part == 0:
            activate(*common, wt3)
        bounds = (0, tiles // 2) if part == 0 else (tiles // 2, tiles)
        convolve_tiles(*bounds, *common, conv_s, xhat_s, rs_s, low_s)

    def front(wide_f32, wide_bf, rest_f32, acc):
        front_body(
            kv_rows, rest_rows, greet, to_group, early, noise_level, aug_level, weights, noisy, target, text, mask,
            noisy_ext, target_ext, texts.at[0], rest_all, keyval, kvs.at[0], small,
            wide_f32, wide_bf, rest_f32, acc, *front_sems,
        )

    V = pltpu.VMEM
    pl.run_scoped(
        front, V((kv_rows, C), F32), V((depth, kv_block), BF16), V((rest_all.shape[1], C), F32),
        V((tok, kv_block), F32),
    )
    for copy in ahead:
        copy.start()
    pix = TILE * columns

    start_near, start_far, finish = mid_stages(
        gd, H, W, from_group, blocks, conv, packet, right, kvs, texts,
        dkv_all, conv_all, t_all, small_all, scal, *mid_refs,
    )

    def edge(order):
        src, dst = (1, band + 1) if order == 0 else (band, 0)
        other = jnp.maximum(n - 1, 0) if order == 0 else jnp.minimum(n + 1, 3)
        return to_narrow(diff3.at[src], diff3.at[dst], edge_sem.at[0, order], edge_sem.at[1, order], other)

    def edge_send(order):
        @pl.when(n > 0 if order == 0 else n < 3)
        def _():
            edge(order).start()

    def edge_wait():
        @pl.when(n > 0)
        def _():
            edge(1).wait_recv()
            edge(0).wait_send()

        @pl.when(n < 3)
        def _():
            edge(0).wait_recv()
            edge(1).wait_send()

        @pl.when(n == 0)
        def _():
            diff3[0] = jnp.zeros(diff3.shape[1:], BF16)

        @pl.when(n == 3)
        def _():
            diff3[band + 1] = jnp.zeros(diff3.shape[1:], BF16)

    def main(*scratch):
        main_body(
            start_near, start_far, edge_send, edge_wait, band, columns, H, HEADS, rest_rows, crop_size, noise_level, aug_level,
            noisy_ext, target_ext, small, rest_all, keyval, blocks, conv, packet, right,
            act3, wt3, conv_s, xhat_s, rs_s, low_s, diff3, *scratch,
        )

    pl.run_scoped(
        main,
        V((2 * C, HEADS * tok), BF16),
        V((HEADS * tok, 2 * C), BF16),
        V((HEADS * tok, 2 * C), BF16),
        V((2 * C, HEADS * tok), BF16),
        V((C, 9 * C), F32),
        V((pix, HEADS * tok), BF16),
        V((pix, HEADS * tok), BF16),
        V((C, HEADS * tok), F32),
        V((C, HEADS * tok), F32),
        V((8, C), F32),
        V((rest_all.shape[1], C), F32),
        V((C * HEADS, C), F32),
        V((HEADS * HEAD, C), F32),
    )

    pl.run_scoped(finish, V((gd * tok if gd <= 4 else tok, gd * tok), F32))
    for copy in ahead:
        copy.wait()


def near(gd):
    return pltpu.VMEM if gd <= 4 else jax.ShapeDtypeStruct


def hold(value, gd):
    return pltpu.with_memory_space_constraint(value, pltpu.VMEM) if gd <= 4 else value


def far(value):
    return pltpu.with_memory_space_constraint(value, pltpu.HBM)


def run_step(
    gd, wide_count, noise_level, aug_level, crop_size, weights2, noisy, target, text, first, second, mask
):
    _, band, columns, _ = noisy.shape
    _, tokens, depth = text.shape
    tok = 4 * tokens
    kv_block = 2 * HEADS * HEAD // 4
    kv_rows = depth * kv_block // C
    rest_rows = weights2.shape[0] - kv_rows
    rest_pad = (rest_rows + 15) // 16 * 16
    assert 9 * C <= rest_rows and kv_block % HEAD == 0 and HEAD == C
    vmem = pl.BlockSpec(memory_space=pltpu.VMEM)
    smem = pl.BlockSpec(memory_space=pltpu.SMEM)
    hbm = pl.BlockSpec(memory_space=pltpu.HBM)
    D, V = pltpu.SemaphoreType.DMA, pltpu.VMEM
    few = max(gd - 1, 1)
    heads = kv_block // HEAD
    bshape, cshape = (C, kv_block // HEAD * tok), (9 * C // 4, C)
    front_sems = [D((WPARTS,)), D((4,)), D((KPARTS, 2, 3)), D((2, 3, 4)), D((2, 3)), D((2, 3)), D((2, 4))]
    mid_refs = [
        V((2,) + bshape, BF16), V((2,) + cshape, BF16), V(bshape, BF16), V(cshape, BF16),
        V(bshape, BF16), V(cshape, BF16), V(bshape, BF16), V(cshape, BF16),
        V((few,) + bshape, BF16), V((few,) + cshape, BF16),
        V((4, 8, C), F32), V((wide_count, 8, C), F32),
        V((C, kv_block), F32), V((C, kv_block), BF16), V(cshape, BF16),
        V((4, 8, C), F32), V(cshape, F32),
        D((2, 2, 2)), D((2, heads + 1)), D((2, heads + 1, few)), D((2, 3)), D((2, wide_count)), D((2, 3)),
        D((2, 4, heads + 1)),
    ]
    return pl.pallas_call(
        functools.partial(
            step_kernel, gd, wide_count, kv_rows, rest_rows, band, columns,
            (len(front_sems), 0, len(mid_refs)),
        ),
        out_shape=tuple(
            near(gd)(shape, kind)
            for shape, kind in (
                ((gd, 4, tokens, depth), BF16),
                ((gd * tok, kv_block), BF16),
                ((4,) + cshape, BF16),
                ((4, C, kv_block), BF16),
                ((gd, 8, C), F32),
                ((8, C), F32),
                (first.shape, F32),
                (first.shape, F32),
            )
        ),
        in_specs=[smem] * 3 + [hbm] * 6 + [vmem],
        out_specs=(vmem,) * 8,
        scratch_shapes=[
            V((band + 4, columns, C), BF16), V((band + 2, columns, C), BF16), V((4, rest_pad, C), BF16),
            V((4, tok, kv_block), BF16), V((gd, tok, kv_block), BF16), V((4, 16, C), F32),
            V((band + 4, columns, 3 * C), BF16), V((9 * C, C), BF16),
            *[V((band, columns, C), F32)] * 3, V((band, columns, C), BF16),
            V((band + 2, columns, 3 * C), BF16),
            *front_sems,
            V((4,) + bshape, BF16), V((4,) + cshape, BF16), V((8, C), F32), V((C, kv_block), BF16),
            *mid_refs,
            D((2, 2, few)),
            D((2,)),
            D((2, 2)),
        ],
        compiler_params=pltpu.CompilerParams(
            collective_id=1, has_side_effects=True, vmem_limit_bytes=(STEP_VMEM if gd <= 4 else 60) * 2**20
        ),
        name="step",
    )(noise_level, aug_level, crop_size, *map(far, (weights2, noisy, target, text, first, second)), mask)


STEP_VMEM = 40


AROWS = 2048


def adam_tiles(length):
    return pl.cdiv(length + 17 * C, AROWS * C)


def adam_kernel(
    gd, length, kv_rows, rest_rows, *refs,
):
    (
        texts, dkv, conv, t_all, small, scal, first, second, first_out, second_out, step_out,
        nat, rest, turned_dkv, edge, shift, carry,
    ) = refs
    s = pl.program_id(0)
    tok = dkv.shape[0] // gd
    n = lax.axis_index("narrow")
    start = lax.rem(lax.axis_index("wide"), gd) * length
    row0 = start // C
    lane0, row_off, row_shift, block0 = lax.rem(start, C), lax.rem(row0, AROWS), lax.rem(row0, 16), row0 // AROWS
    wrap = C - lane0
    kv_blocks = kv_rows // AROWS
    parts = dkv.shape[1] // C
    cols_tile = AROWS // parts

    def iotas(rows):
        shape = (rows, C)
        return lax.broadcasted_iota(jnp.int32, shape, 0), lax.broadcasted_iota(jnp.int32, shape, 1)

    def natural(tile):
        block = block0 + tile
        here = pl.multiple_of(tile * AROWS + 8, 8)

        @pl.when(block < kv_blocks)
        def _():
            at = pl.ds(pl.multiple_of(block * cols_tile, cols_tile), cols_tile)
            text = jnp.concatenate([texts[k, :, :, at].reshape(tok, cols_tile) for k in range(gd)], axis=0)
            grad = dot(text, turned_dkv[...], TN)
            for j in range(parts - 1):
                nat[pl.ds(here + j, cols_tile, stride=parts), :] = grad[:, j * C : (j + 1) * C]
            part = grad[:, (parts - 1) * C :]
            row, lane = iotas(cols_tile)
            before = jnp.where(row == 0, edge[0:1, :], pltpu.roll(part, 1, 0))
            nat[pl.ds(here - 1, cols_tile, stride=parts), :] = jnp.where(lane < wrap, before, part)
            edge[0:1, :] = part[cols_tile - 1 : cols_tile, :]

        @pl.when(block >= kv_blocks)
        def _():
            at = pl.multiple_of(jnp.minimum((block - kv_blocks) * AROWS, rest.shape[0] - 16 - AROWS), 8)
            row, lane = iotas(AROWS)
            both = jnp.where(lane >= lane0, rest[pl.ds(at + 8, AROWS), :], rest[pl.ds(at + 9, AROWS), :])
            nat[pl.ds(here, AROWS), :] = pltpu.roll(both, wrap, 1)

            @pl.when(block == kv_blocks)
            def _():
                row, lane = iotas(8)
                ahead = pltpu.roll(rest[8:16, :], wrap, 1)
                nat[pl.ds(here - 1, 1), :] = jnp.where(lane < wrap, edge[...], ahead)[0:1, :]

    def assemble():
        first_table, first_gain = 9 * C, 9 * C + 2 * LEVELS
        first_query = first_gain + 4
        first_out = first_query + C * HEADS
        quarter = conv.shape[1]
        width = dkv.shape[1]
        heads = width // HEAD
        for owner in range(4):
            lo, hi = owner * rest_rows, (owner + 1) * rest_rows

            @pl.when(n == owner)
            def _():
                for k in range(4):
                    a, b = max(lo, k * quarter), min(hi, (k + 1) * quarter)
                    if a < b:
                        assert (a, b) == (k * quarter, (k + 1) * quarter)
                        rest[8 + a - lo : 8 + b - lo, :] = conv[k].astype(F32)
                a, b = max(lo, first_query), min(hi, first_out)
                if a < b:
                    for h in range(HEADS):
                        c0 = max(0, -(-(a - first_query - h) // HEADS))
                        c1 = min(C, -(-(b - first_query - h) // HEADS))
                        cols = slice(h % heads * HEAD, h % heads * HEAD + HEAD)
                        c_lo, c_hi = c0 // 16 * 16, (c1 + 15) // 16 * 16
                        value = t_all[h // heads, c_lo:c_hi, cols].astype(F32)
                        start = first_query + c0 * HEADS + h - lo
                        rest[pl.ds(8 + start, c1 - c0, stride=HEADS), :] = value[c0 - c_lo : c1 - c_lo]
                for h in range(HEADS):
                    a, b = first_out + h * HEAD, first_out + (h + 1) * HEAD
                    if lo <= a and b <= hi:
                        cols = slice(h % heads * HEAD, h % heads * HEAD + HEAD)
                        rest[8 + a - lo : 8 + b - lo, :] = t_all[2 + h // heads, :, cols].astype(F32).T
                    else:
                        assert b <= lo or hi <= a
                if lo <= first_gain and first_gain + 4 <= hi:
                    total = small[0, 0:4]
                    for k in range(1, gd):
                        total = total + small[k, 0:4]
                    rest[8 + first_gain - lo : 8 + first_gain + 4 - lo, :] = total


        for k in range(gd):
            for level, shift_by in ((0, 0), (1, NOISE_LEVELS)):
                found = jnp.max(small[k, 7:8, level : level + 1]).astype(jnp.int32) + shift_by
                for half in range(2):
                    at_row = first_table + 2 * found + half - n * rest_rows

                    @pl.when((at_row >= 0) & (at_row < rest_rows))
                    def _():
                        rest[pl.ds(at_row + 8, 1), :] += small[k, 4 + half : 5 + half]

    @pl.when(s == 0)
    def _():
        edge[...] = jnp.zeros_like(edge)
        rest[...] = jnp.zeros_like(rest)
        carry[...] = jnp.zeros_like(carry)
        shift[...] = jnp.zeros_like(shift)
        row, lane = iotas(dkv.shape[0])
        moved = [
            pltpu.roll(dkv[:, j * C : (j + 1) * C].astype(F32), wrap, 1) for j in range(parts)
        ]
        for j in range(parts):
            turned_dkv[:, j * C : (j + 1) * C] = jnp.where(
                lane < wrap, moved[j], moved[(j + 1) % parts]
            ).astype(BF16)

        @pl.when(start + length > kv_rows * C)
        def _():
            assemble()

        natural(0)

    natural(s + 1)
    row, lane = iotas(AROWS)
    g = nat[pl.ds(s * AROWS + row_off + 8, AROWS), :] * scal[0:1]
    one = BETA_ONE * first.reshape(AROWS, C)[...] + (1.0 - BETA_ONE) * g
    two = BETA_TWO * second.reshape(AROWS, C)[...] + (1.0 - BETA_TWO) * g * g
    first_out.reshape(AROWS, C)[...] = one
    second_out.reshape(AROWS, C)[...] = two
    fixed_one = one * (scal[1:2] * (1.0 / (1.0 - BETA_ONE**STEP)))
    fixed_two = two * (1.0 / (1.0 - BETA_TWO**STEP))
    root = fixed_two * lax.rsqrt(fixed_two)
    step = fixed_one * pl.reciprocal(root + ADAM_EPS, approx=True)
    step = jnp.where((s * AROWS + row) * C + lane < length, step, 0.0)
    turned = pltpu.roll(step, lane0, 1)
    above = pltpu.roll(turned, 1, 0)
    above = jnp.where(row == 0, carry[0:1, :], above)
    carry[0:1, :] = turned[AROWS - 1 : AROWS, :]
    shift[pl.ds(row_shift, AROWS), :] = jnp.where(lane < lane0, above, turned)
    step_out[...] = shift[0:AROWS, :].astype(BF16)
    shift[0:16, :] = shift[AROWS : AROWS + 16, :]


def run_adam(texts, dkv, conv, t_all, small, scal, first, second, length, kv_rows, rest_rows):
    gd = texts.shape[0]
    tiles = adam_tiles(length)
    flat = pl.BlockSpec((1, AROWS * C), lambda s: (0, s))
    rest_pad = (pl.cdiv(rest_rows, AROWS) + 1) * AROWS + 16
    return pl.pallas_call(
        functools.partial(adam_kernel, gd, length, kv_rows, rest_rows),
        out_shape=(
            jax.ShapeDtypeStruct((1, length), F32),
            jax.ShapeDtypeStruct((1, length), F32),
            near(gd)((tiles * AROWS, C), BF16),
        ),
        grid=(tiles,),
        in_specs=[pl.BlockSpec(memory_space=pltpu.VMEM)] * 6 + [flat, flat],
        out_specs=[flat, flat, pl.BlockSpec((AROWS, C), lambda s: (s, 0))],
        scratch_shapes=[
            pltpu.VMEM(((tiles + 1) * AROWS + 16, C), F32),
            pltpu.VMEM((rest_pad, C), F32),
            pltpu.VMEM(dkv.shape, BF16),
            pltpu.VMEM((8, C), F32),
            pltpu.VMEM((AROWS + 16, C), F32),
            pltpu.VMEM((8, C), F32),
        ],
        compiler_params=pltpu.CompilerParams(vmem_limit_bytes=ADAM_VMEM),
        name="adam",
    )(*(hold(v, gd) for v in (texts, dkv, conv, t_all, small, scal, first, second)))


ADAM_VMEM = 24 * 2**20


def share_kernel(
    gd, rows, chunk, pad, l1, l2, u_ref, w_far, o_far, out_ref, w_near, o_near,
    recv_a, recv_b, part, in_sem, s_u, s_fo, s_fi, s_y, r_a, r_b, r_f, r_y,
):
    loads = [
        pltpu.make_async_copy(w_far, w_near.at[pl.ds(0, w_far.shape[0])], in_sem.at[1]),
        pltpu.make_async_copy(o_far, o_near.at[pl.ds(0, o_far.shape[0])], in_sem.at[2]),
    ]
    wide = lax.axis_index("wide")
    g = wide // gd
    spot = wide % gd
    chunks = rows // chunk
    is_outer = jnp.logical_or(g == 0, g == GROUPS - 1)
    is_inner = jnp.logical_not(is_outer)
    low = g < GROUPS // 2
    outer_id = jnp.where(low, g - 1, g + 1) * gd + spot
    mate_id = jnp.where(low, g + 1, g - 1) * gd + spot
    barrier = pltpu.get_barrier_semaphore()
    for k in range(1, gd):
        other = g * gd + lax.rem(spot + k, gd)
        pl.semaphore_signal(barrier, inc=1, device_id={"wide": other}, device_id_type=MESH)
    pl.semaphore_signal(barrier, inc=1, device_id={"wide": mate_id}, device_id_type=MESH)
    @pl.when(is_inner)
    def _():
        pl.semaphore_signal(barrier, inc=1, device_id={"wide": outer_id}, device_id_type=MESH)
        pl.semaphore_wait(barrier, gd + 1)
    @pl.when(is_outer)
    def _():
        pl.semaphore_wait(barrier, gd)

    def sl(c):
        return pl.ds(pl.multiple_of(c * chunk, chunk), chunk)
    def ol(c):
        return pl.ds(pl.multiple_of(pad + c * chunk, 16), chunk)
    def copy(src, dst, ss, rs, dev):
        return pltpu.make_async_remote_copy(src_ref=src, dst_ref=dst, send_sem=ss, recv_sem=rs,
                                            device_id={"wide": dev}, device_id_type=MESH)
    def send_a(c):
        return copy(u_ref.at[sl(c)], recv_a.at[sl(c)], s_u.at[c], r_a.at[c], mate_id)
    def send_b(c):
        return copy(part.at[sl(c)], recv_b.at[sl(c)], s_u.at[c], r_b.at[c], mate_id)
    def send_fo(c):
        return copy(out_ref.at[spot, ol(c)], out_ref.at[spot, ol(c)], s_fo.at[c], r_f.at[c], outer_id)
    def send_fi(c):
        return copy(out_ref.at[spot, ol(c)], out_ref.at[spot, ol(c)], s_fi.at[c], r_f.at[c], mate_id)
    def send_y(c, k):
        return copy(out_ref.at[spot, ol(c)], out_ref.at[spot, ol(c)], s_y.at[k - 1, c], r_y.at[k - 1, c],
                    g * gd + lax.rem(spot + k, gd))
    def wait_y(c, k):
        src = lax.rem(spot + gd - k, gd)
        copy(out_ref.at[src, ol(c)], out_ref.at[src, ol(c)], s_y.at[k - 1, c], r_y.at[k - 1, c], wide).wait_recv()
    def spread(c):
        for k in range(1, gd):
            send_y(c, k).start()
    def is_root(c):
        return lax.rem(c + g, 2) == 1

    @pl.when(is_outer)
    def _():
        @pl.loop(0, chunks)
        def _(c):
            send_a(c).start()
    for load in loads:
        load.start()
    for p in range(gd):
        out_ref[p, 0:pad] = jnp.zeros((pad, 128), jnp.bfloat16)
        out_ref[p, pad + rows : rows + 2 * pad] = jnp.zeros((pad, 128), jnp.bfloat16)

    @pl.when(is_outer)
    def _():
        @pl.loop(0, chunks)
        def _(c):
            send_fo(c).wait_recv()
            spread(c)
    @pl.when(is_inner)
    def _():
        @pl.loop(0, chunks + l2)
        def _(c):
            @pl.when(jnp.logical_and(c < chunks, jnp.logical_not(is_root(c))))
            def _():
                send_a(c).wait_recv()
                part[sl(c)] = (u_ref[sl(c)].astype(jnp.float32) + recv_a[sl(c)].astype(jnp.float32)).astype(jnp.bfloat16)
                send_b(c).start()
            d = c - l1
            @pl.when(jnp.logical_and(jnp.logical_and(d >= 0, d < chunks), is_root(d)))
            def _():
                send_a(d).wait_recv()
                send_b(d).wait_recv()
                out_ref[spot, ol(d)] = (u_ref[sl(d)].astype(jnp.float32) + recv_a[sl(d)].astype(jnp.float32) + recv_b[sl(d)].astype(jnp.float32)).astype(jnp.bfloat16)
                send_fo(d).start()
                send_fi(d).start()
                spread(d)
            e = c - l2
            @pl.when(jnp.logical_and(e >= 0, jnp.logical_not(is_root(e))))
            def _():
                send_fi(e).wait_recv()
                send_fo(e).start()
                spread(e)
    @pl.loop(0, chunks)
    def _(c):
        for k in range(1, gd):
            wait_y(c, k)
            send_y(c, k).wait_send()
        @pl.when(is_outer)
        def _():
            send_a(c).wait_send()
        @pl.when(is_inner)
        def _():
            send_fo(c).wait_send()
            @pl.when(is_root(c))
            def _():
                send_fi(c).wait_send()
            @pl.when(jnp.logical_not(is_root(c)))
            def _():
                send_b(c).wait_send()
    for load in loads:
        load.wait()


def share(u, weights2, outer2, gd, rows, chunk, pad, l1, l2):
    n = rows // chunk
    D = pltpu.SemaphoreType.DMA
    few = max(gd - 1, 1)
    held = pl.cdiv(weights2.shape[0], 256) * 256
    vmem, hbm = pl.BlockSpec(memory_space=pltpu.VMEM), pl.BlockSpec(memory_space=pltpu.HBM)
    return pl.pallas_call(
        functools.partial(share_kernel, gd, rows, chunk, pad, l1, l2),
        out_shape=(near(gd)((gd, rows + 2 * pad, C), BF16),) + (near(gd)((held, C), F32),) * 2,
        in_specs=[vmem, hbm, hbm],
        out_specs=(vmem,) * 3,
        scratch_shapes=[pltpu.VMEM((rows, C), BF16)] * 3
        + [
            D((3,)), D((n,)), D((n,)), D((n,)), D((few, n)),
            D((n,)), D((n,)), D((n,)), D((few, n)),
        ],
        compiler_params=pltpu.CompilerParams(
            collective_id=9, has_side_effects=True, vmem_limit_bytes=SHARE_VMEM
        ),
        name="share",
    )(hold(u, gd), far(weights2), far(outer2))


SHARE_VMEM = 32 * 2**20


def final_kernel(bases, pad, block, weights, outer, pieces, scal, new_weights, momentum, loss, count, held, sem):
    rows = new_weights.shape[0]
    total = pieces.shape[1]
    steps = pl.cdiv(rows, block)

    def writes(b, slot, size):
        here = pl.ds(b * block, size)
        return [
            pltpu.make_async_copy(held.at[slot, k, pl.ds(0, size)], out.at[here], sem.at[slot, k])
            for k, out in enumerate((new_weights, momentum))
        ]

    for b in range(steps):
        slot = b % 3
        size = min(block, rows - b * block)
        if b >= 3:
            for copy in writes(b - 3, slot, block):
                copy.wait()
        averaged = jnp.zeros((block, C), F32)
        for p, base in enumerate(bases):
            at = min(max(b * block - base + pad, 0), total - block)
            averaged = averaged + pieces[p, at : at + block, :].astype(F32)
        w = weights[b * block : (b + 1) * block, :]
        averaged = averaged + (INNER_RATE * DECAY_RATE) * w
        moved = OUTER_MOMENTUM * outer[b * block : (b + 1) * block, :] + averaged
        held[slot, 1] = moved
        held[slot, 0] = w - OUTER_RATE * (averaged + OUTER_MOMENTUM * moved)
        for copy in writes(b, slot, size):
            copy.start()
    loss[0] = jnp.max(scal[2:3])
    count[0] = jnp.max(scal[3:4])
    for b in range(max(steps - 3, 0), steps):
        for copy in writes(b, b % 3, min(block, rows - b * block)):
            copy.wait()


def run_final(rows, weights2, outer2, pieces, scal, bases, pad):
    hbm, smem = pl.BlockSpec(memory_space=pltpu.HBM), pl.BlockSpec(memory_space=pltpu.SMEM)
    block = weights2.shape[0] // 16
    assert block % 16 == 0 and block <= pad
    return pl.pallas_call(
        functools.partial(final_kernel, bases, pad, block),
        out_shape=(jax.ShapeDtypeStruct((rows, C), F32),) * 2 + (jax.ShapeDtypeStruct((1,), F32),) * 2,
        in_specs=[pl.BlockSpec(memory_space=pltpu.VMEM)] * 4,
        out_specs=(hbm, hbm, smem, smem),
        scratch_shapes=[pltpu.VMEM((3, 2, block, C), F32), pltpu.SemaphoreType.DMA((3, 2))],
        compiler_params=pltpu.CompilerParams(vmem_limit_bytes=12 * 2**20),
        name="final",
    )(*(hold(v, len(bases)) for v in (weights2, outer2, pieces, scal)))


def per_device(
    weights, first_moment, second_moment, outer_momentum, noisy_input, target,
    text_tokens, text_mask, noise_level, aug_level, crop_size,
):
    length = first_moment.shape[1]
    wide_count = lax.axis_size("wide")
    gd = wide_count // GROUPS
    weights2 = weights.reshape(-1, C)
    outer2 = outer_momentum.reshape(-1, C)

    texts, dkv, conv_all, t_all, small_all, scal, first, second = run_step(
        gd, wide_count, noise_level, aug_level, crop_size, weights2, noisy_input, target, text_tokens,
        first_moment, second_moment, text_mask,
    )
    kv_rows = TEXT_D * dkv.shape[1] // C
    rest_rows = weights2.shape[0] - kv_rows
    moment_one, moment_two, step = run_adam(
        texts, dkv, conv_all, t_all, small_all, scal, first, second, length, kv_rows, rest_rows
    )
    chunk = 160
    rows = pl.cdiv(length // C + 18, chunk) * chunk
    pad = 1120
    pieces, w_near, o_near = share(step, weights2, outer2, gd, rows, chunk, pad, 3, 6)
    bases = [p * length // C // 16 * 16 for p in range(gd)]
    new_weights, momentum_out, loss, count = run_final(
        weights2.shape[0], w_near, o_near, pieces, scal, bases, pad
    )
    return (
        new_weights.reshape(-1), momentum_out.reshape(-1), moment_one, moment_two,
        loss, count,
    )


def solution(mesh):
    placed = (
        P("narrow"),
        P("narrow", "wide"),
        P("narrow", "wide"),
        P("narrow"),
        P("wide", "narrow", None, None),
        P("wide", "narrow", None, None),
        P("wide", "narrow", None),
        P("wide", "narrow"),
        P("wide"),
        P("wide"),
        P("wide"),
    )
    return jax.shard_map(
        per_device,
        mesh=mesh,
        in_specs=placed,
        out_specs=(P("narrow"), P("narrow"), P("narrow", "wide"), P("narrow", "wide"), P(), P()),
        check_vma=False,
    )
```

```python
import functools
import math

import jax
import jax.numpy as jnp
from jax import lax
from jax.experimental import pallas as pl
from jax.experimental.pallas import tpu as pltpu
from jax.sharding import PartitionSpec as P

MESH = pl.DeviceIdType.MESH
C = 128
NORM_GROUPS = 32
HEADS = 8
HEAD = 128
TEXT_D = 4096
H = 128
W = 128
NOISE_LEVELS = 1000
AUG_LEVELS = 24
LEVELS = NOISE_LEVELS + AUG_LEVELS
GROUPS = 4
STEP = 8


EPS_NORM = 1e-05
CLIP_NORM = 0.002
BETA_ONE = 0.9
BETA_TWO = 0.99
INNER_RATE = 0.01
DECAY_RATE = 0.01
ADAM_EPS = 1e-08
OUTER_RATE = 0.7
OUTER_MOMENTUM = 0.9

TN = (((0,), (0,)), ((), ()))
F32 = jnp.float32
BF16 = jnp.bfloat16
LOG2E = 1.4426950408889634
LN2 = 0.6931471805599453
NT = (((1,), (1,)), ((), ()))
TILE = 8
TILE3 = 8


def dot(a, b, dims=(((1,), (0,)), ((), ()))):
    return lax.dot_general(a, b, dims, preferred_element_type=F32)


def two_parts(value):
    top = value.astype(BF16)
    return top, (value - top.astype(F32)).astype(BF16)


def shifted(value, by, keep):
    return jnp.where(keep, pltpu.roll(value, by, 0), 0.0)


CTILE = 16


def vectors(small, height, columns):
    total = small[0] + small[1] + small[2] + small[3]
    lane_group = lax.broadcasted_iota(jnp.int32, (C, C), 0) // (C // NORM_GROUPS)
    same = (lane_group == lax.broadcasted_iota(jnp.int32, (C, C), 1) // (C // NORM_GROUPS)).astype(F32)
    stats = jnp.dot(total[0:8], same, precision=lax.Precision.HIGHEST, preferred_element_type=F32)
    count = height * columns * C // NORM_GROUPS
    mean = stats[0:1] * (1.0 / count)
    spread = lax.rsqrt(stats[1:2] * (1.0 / count) - mean * mean + EPS_NORM)
    film_scale, film_shift = 1.0 + total[2:3], total[3:4]
    gains = total[8:12]
    gain = gains[0:1] * film_scale
    offset = gains[1:2] * film_scale + film_shift
    slope = spread * gain
    return mean, spread, slope, offset - mean * slope, film_scale, gains


def edges(columns):
    place = lax.broadcasted_iota(jnp.int32, (columns, C), 0)
    return place > 0, place < columns - 1


def activate(band, columns, height, noisy, small, conv_w, act3, wt3):
    row0 = lax.axis_index("narrow") * band
    mean, spread, slope, base, film_scale, gains = vectors(small, height, columns)
    not_first, not_last = edges(columns)

    @pl.loop(0, band + 4)
    def _(r):
        scaled = noisy[r].astype(F32) * slope + base
        value = scaled * jax.nn.sigmoid(scaled)
        row = row0 + r - 2
        value = jnp.where(jnp.logical_and(row >= 0, row < height), value, 0.0)
        value = value.astype(BF16).astype(F32)
        act3[r, :, 0:C] = shifted(value, 1, not_first).astype(BF16)
        act3[r, :, C : 2 * C] = value.astype(BF16)
        act3[r, :, 2 * C : 3 * C] = shifted(value, columns - 1, not_last).astype(BF16)

    for tap in range(9):
        rows = slice(tap * C, (tap + 1) * C)
        wt3[rows, :] = conv_w[rows, :].astype(F32).T.astype(BF16)


def convolve_tiles(first, last, band, columns, height, noisy, small, conv_w, act3, conv_s, xhat_s, rs_s, low_s):
    gains = vectors(small, height, columns)[5]
    pix = CTILE * columns

    @pl.loop(first, last)
    def _(t):
        q = t * CTILE
        conv = noisy[pl.ds(q + 2, CTILE)].astype(F32).reshape(pix, C)
        for dy in range(3):
            window = act3[pl.ds(q + 1 + dy, CTILE)].reshape(pix, 3 * C)
            conv = conv + dot(window, conv_w[dy * 3 * C : (dy + 1) * 3 * C, :])
        centered = conv - jnp.mean(conv, axis=1, keepdims=True)
        rs = lax.rsqrt(jnp.mean(centered * centered, axis=1, keepdims=True) + EPS_NORM)
        xhat = centered * rs
        here = pl.ds(q, CTILE)
        conv_s[here] = conv.reshape(CTILE, columns, C)
        xhat_s[here] = xhat.reshape(CTILE, columns, C)
        rs_s[here] = jnp.broadcast_to(rs, (pix, C)).reshape(CTILE, columns, C)
        low_s[here] = (xhat * gains[2:3] + gains[3:4]).astype(BF16).reshape(CTILE, columns, C)


def main_body(
    start_near, start_far, edge_send, edge_wait, band, columns, height, heads,
    rest_rows, crop_size, noise_level, aug_level, noisy, target, small, rest, keyval,
    blocks, dconv_w, packet, right,
    act3, wt3, conv_s, xhat_s, rs_s, low_s, diff3,
    m_cat, m_cat_t, n_cat, n_cat_t, conv_t, probs, dscore, y_t, z_t, sums,
    stage, query, out_w,
):
    tok, kv_block = keyval.shape[1:]
    width = heads * HEAD
    per_block = kv_block // HEAD
    narrow = lax.axis_index("narrow")
    row0 = narrow * band
    crop = crop_size[0]
    pix = TILE * columns
    first_query = 9 * C + 2 * LEVELS + 4
    first_out = first_query + C * heads

    def take(first, count, place):
        while count:
            owner, local = divmod(first, rest_rows)
            use = min(count, rest_rows - local)
            a = local // 16 * 16
            b = (local + use + 15) // 16 * 16
            stage[0 : b - a, :] = rest[owner, a:b, :].astype(F32)
            place(stage[local - a : local - a + use, :], use)
            first, count = first + use, count - use

    def filler(ref):
        at = [0]

        def place(value, use):
            ref[at[0] : at[0] + use, :] = value
            at[0] += use

        return place

    take(first_query, C * heads, filler(query))
    take(first_out, width, filler(out_w))
    mean, spread, slope, base, film_scale, gains = vectors(small, height, columns)
    ln_gain = gains[2:3]
    quarter = tok // 4
    masks = [small[owner, 4:5, 0:quarter] for owner in range(4)]
    ok = (jnp.concatenate(masks, axis=1) > 0.0) | (lax.broadcasted_iota(jnp.int32, (1, tok), 1) == 0)
    factor = LOG2E / math.sqrt(HEAD)
    for head in range(heads):
        cols = slice(head * HEAD, (head + 1) * HEAD)
        tcols = slice(head * tok, (head + 1) * tok)
        block, at = head // per_block, head % per_block * HEAD
        query_head = query[pl.ds(head, C, stride=heads), :].astype(BF16)
        out_head = out_w[cols, :].astype(BF16)
        m_head = dot(query_head, keyval[block, :, at : at + HEAD], NT) * factor

        @pl.when(narrow == block)
        def _():
            right[:, at : at + HEAD] = query_head

        @pl.when(narrow == block + heads // per_block)
        def _():
            right[:, at : at + HEAD] = out_w[cols, :].T.astype(BF16)

        top, rest = two_parts(m_head)
        m_cat[:C, tcols] = top
        m_cat[C:, tcols] = rest
        top, rest = two_parts(m_head.T)
        m_cat_t[tcols, :C] = top
        m_cat_t[tcols, C:] = rest
        n_head = dot(keyval[block + heads // per_block, :, at : at + HEAD], out_head)
        top, rest = two_parts(n_head)
        n_cat[tcols, :C] = top
        n_cat[tcols, C:] = rest
        top, rest = two_parts(n_head.T)
        n_cat_t[:C, tcols] = top
        n_cat_t[C:, tcols] = rest
    y_t[...] = jnp.zeros_like(y_t)
    z_t[...] = jnp.zeros_like(z_t)
    conv_t[...] = jnp.zeros_like(conv_t)
    sums[...] = jnp.zeros_like(sums)
    not_first, not_last = edges(columns)
    pix_row = lax.broadcasted_iota(jnp.int32, (pix, C), 0) // columns
    pix_col = lax.broadcasted_iota(jnp.int32, (pix, C), 0) % columns
    tiles = band // TILE

    @pl.loop(0, tiles)
    def _(t):
        q = jnp.where(t == 0, 0, jnp.where(t == 1, tiles - 1, t - 1)) * TILE
        here = pl.ds(q, TILE)
        conv = conv_s[here].reshape(pix, C)
        low = low_s[here].reshape(pix, C)
        low2 = jnp.concatenate([low, low], axis=1)
        for head in range(heads):
            tcols = slice(head * tok, (head + 1) * tok)
            if head % 2 == 0:
                scores = dot(low2, m_cat[:, head * tok : (head + 2) * tok])
            score = scores[:, head % 2 * tok : (head % 2 + 1) * tok]
            score = jnp.where(ok, score, -1e30)
            e = jnp.exp2(score - jnp.max(score, axis=1, keepdims=True))
            p = e * (1.0 / jnp.sum(e, axis=1, keepdims=True))
            probs[:, tcols] = p.astype(BF16)
        mixed = dot(probs[...], n_cat[...])
        output = conv + mixed[:, :C] + mixed[:, C:]
        valid = (row0 + q + pix_row < crop) & (pix_col < crop)
        err = jnp.where(valid, output - target[pl.ds(q + 1, TILE)].astype(F32).reshape(pix, C), 0.0)
        sums[4:5, :] += jnp.sum(err * err, axis=0, keepdims=True)
        dout = 2.0 * err
        dout_low = dout.astype(BF16)
        dout2 = jnp.concatenate([dout_low, dout_low], axis=1)
        for head in range(heads):
            tcols = slice(head * tok, (head + 1) * tok)
            if head % 2 == 0:
                dprobs = dot(dout2, n_cat_t[:, head * tok : (head + 2) * tok])
            dprob = dprobs[:, head % 2 * tok : (head % 2 + 1) * tok]
            p = probs[:, tcols].astype(F32)
            pd = p * dprob
            ds = pd - p * jnp.sum(pd, axis=1, keepdims=True)
            dscore[:, tcols] = ds.astype(BF16)
        dlay2 = dot(dscore[...], m_cat_t[...])
        dlay = (dlay2[:, :C] + dlay2[:, C:]) * LN2
        xhat = xhat_s[here].reshape(pix, C)
        rs = rs_s[here].reshape(pix, C)
        sums[2:3, :] += jnp.sum(dlay * xhat, axis=0, keepdims=True)
        sums[3:4, :] += jnp.sum(dlay, axis=0, keepdims=True)
        dxh = dlay * ln_gain
        dconv = dout + rs * (
            dxh
            - jnp.mean(dxh, axis=1, keepdims=True)
            - xhat * jnp.mean(dxh * xhat, axis=1, keepdims=True)
        )
        dout_t = dout_low.T
        lay_t = low.T
        y_t[...] += dot(dout_t, probs[...])
        z_t[...] += dot(lay_t, dscore[...])
        dconv_t = dconv.astype(BF16).T
        for dy in range(3):
            window = act3[pl.ds(q + 1 + dy, TILE)].reshape(pix, 3 * C)
            conv_t[:, dy * 3 * C : (dy + 1) * 3 * C] += dot(dconv_t, window)
        for k in range(TILE):
            one = dconv[k * columns : (k + 1) * columns]
            diff3[q + 1 + k, :, 0:C] = shifted(one, columns - 1, not_last).astype(BF16)
            diff3[q + 1 + k, :, C : 2 * C] = one.astype(BF16)
            diff3[q + 1 + k, :, 2 * C : 3 * C] = shifted(one, 1, not_first).astype(BF16)

        for order in range(2):
            @pl.when(t == order)
            def _():
                edge_send(order)

    def back(t):
        r = t * TILE3
        grad = jnp.zeros((TILE3 * columns, C), F32)
        for dy in range(3):
            window = diff3[pl.ds(r + 2 - dy, TILE3)].reshape(TILE3 * columns, 3 * C)
            grad = grad + dot(window, wt3[dy * 3 * C : (dy + 1) * 3 * C, :])
        x = noisy[pl.ds(r + 2, TILE3)].astype(F32).reshape(TILE3 * columns, C)
        scaled = x * slope + base
        sig = jax.nn.sigmoid(scaled)
        ds = grad * (sig * (1.0 + scaled * (1.0 - sig)))
        sums[0:1, :] += jnp.sum(ds, axis=0, keepdims=True)
        sums[1:2, :] += jnp.sum(ds * ((x - mean) * spread), axis=0, keepdims=True)

    share_rows = dconv_w.shape[1]
    full = conv_t[...].T
    for owner in range(4):
        dconv_w[owner] = full[owner * share_rows : (owner + 1) * share_rows].astype(BF16)
        part = z_t if owner < 2 else y_t
        at = owner % 2 * per_block * tok
        blocks[owner] = part[:, at : at + per_block * tok].astype(BF16)
    start_near()
    edge_wait()
    halves = 1
    pl.loop(0, halves)(back)
    start_far()
    pl.loop(halves, band // TILE3)(back)
    a, b = sums[0:1], sums[1:2]
    packet[0:1] = film_scale * b
    packet[1:2] = film_scale * a
    packet[2:4] = sums[2:4]
    packet[4:5] = gains[0:1] * b + gains[1:2] * a
    packet[5:6] = a
    packet[6:7] = sums[4:5]
    lane = lax.broadcasted_iota(jnp.int32, (1, C), 1)
    facts = jnp.zeros((1, C), F32)
    for k, fact in enumerate((noise_level[0], aug_level[0], crop)):
        facts = jnp.where(lane == k, fact.astype(F32), facts)
    packet[7:8] = jnp.where(row0 == 0, facts, 0.0)


def cross_ids():
    n = lax.axis_index("narrow")
    mate = n + 1 - 2 * lax.rem(n, 2)
    across = lax.rem(n + 2, 4)
    corner = lax.rem(mate + 2, 4)
    return n, mate, across, corner


def to_narrow(src, dst, send_sem, recv_sem, device):
    return pltpu.make_async_remote_copy(
        src_ref=src, dst_ref=dst, send_sem=send_sem, recv_sem=recv_sem,
        device_id={"narrow": device}, device_id_type=MESH,
    )


class Gather:
    def __init__(self, view, sems, ids):
        self.view, self.sems = view, sems
        self.n, self.mate, self.across, self.corner = ids

    def _copy(self, block, slot, device):
        ref = self.view(block)
        return to_narrow(ref, ref, self.sems.at[0, slot], self.sems.at[1, slot], device)

    def start(self):
        self._copy(self.n, 1, self.across).start()
        self._copy(self.n, 0, self.mate).start()

    def relay(self):
        self._copy(self.across, 1, self.across).wait_recv()
        self._copy(self.across, 2, self.mate).start()

    def wait(self):
        self._copy(self.mate, 0, self.mate).wait_recv()
        self._copy(self.corner, 2, self.mate).wait_recv()

    def drain(self):
        self._copy(self.n, 1, self.across).wait_send()
        self._copy(self.n, 0, self.mate).wait_send()
        self._copy(self.across, 2, self.mate).wait_send()


def rest_needs(rest_rows):
    first, last = 9 * C, 9 * C + 2 * LEVELS
    needs = []
    for owner in range(4):
        lo, hi = owner * rest_rows, (owner + 1) * rest_rows
        keep = [r for r in ((lo, min(hi, first)), (max(lo, last), hi)) if r[0] < r[1]]
        assert len(keep) <= 1
        if keep:
            a, b = keep[0][0] - lo, keep[0][1] - lo
            needs.append((a // 16 * 16, (b + 15) // 16 * 16))
        else:
            needs.append(None)
    return needs


KPARTS = 4
WPARTS = 8


def front_body(
    kv_rows, rest_rows, greet, to_group, early, noise_level, aug_level, weights, noisy, target, text, mask,
    noisy_ext, target_ext, text_all, rest_all, keyval, own_kv, small,
    wide_f32, wide_bf, rest_f32, acc,
    w_sem, in_sem, text_sem, rest_sem, kv_sem, small_sem, halo_sem,
):
    ids = cross_ids()
    n, mate, across, corner = ids
    band = noisy.shape[1]
    tokens, depth = text.shape[1:]
    in_text = pltpu.make_async_copy(text.at[0], text_all.at[n], in_sem.at[0])
    in_text.start()
    in_rest = pltpu.make_async_copy(
        weights.at[pl.ds(kv_rows, rest_rows)], rest_f32.at[pl.ds(0, rest_rows)], in_sem.at[1]
    )
    in_rest.start()
    in_noisy = pltpu.make_async_copy(noisy.at[0], noisy_ext.at[pl.ds(2, band)], in_sem.at[2])
    in_noisy.start()
    w_step = kv_rows // WPARTS
    in_w = [
        pltpu.make_async_copy(
            weights.at[pl.ds(k * w_step, w_step)], wide_f32.at[pl.ds(k * w_step, w_step)], w_sem.at[k]
        )
        for k in range(WPARTS)
    ]
    for copy in in_w:
        copy.start()
    in_target = pltpu.make_async_copy(target.at[0], target_ext.at[pl.ds(1, band)], in_sem.at[3])
    in_target.start()
    greet()

    k_step = depth // KPARTS
    texts = [
        Gather(
            lambda b, k=k: text_all.at[b, :, pl.ds(k * k_step, k_step)], text_sem.at[k], ids
        )
        for k in range(KPARTS)
    ]
    in_text.wait()
    for part in texts:
        part.start()

    in_rest.wait()
    rest_f32[rest_rows:] = jnp.zeros((rest_f32.shape[0] - rest_rows, C), F32)
    for k in range(2):
        row_sum = jnp.zeros((1, C), F32)
        for level in (noise_level[0], NOISE_LEVELS + aug_level[0]):
            row = 9 * C + 2 * level + k - n * rest_rows
            found = rest_f32[pl.ds(jnp.clip(row, 0, rest_rows - 1), 1), :]
            found = found.astype(BF16).astype(F32)
            row_sum = row_sum + jnp.where((row >= 0) & (row < rest_rows), found, 0.0)
        small[n, 2 + k : 3 + k, :] = row_sum
    small[n, 4:16, :] = jnp.zeros((12, C), F32)
    for owner in range(4):
        for k in range(4):
            row = 9 * C + 2 * LEVELS + k - owner * rest_rows
            if 0 <= row < rest_rows:
                @pl.when(n == owner)
                def _():
                    small[n, 8 + k : 9 + k, :] = rest_f32[row : row + 1, :].astype(BF16).astype(F32)
    small[n, 4:5, 0:tokens] = mask[...].astype(F32)
    in_noisy.wait()

    def add_row(r, sums):
        x = noisy_ext[r + 2].astype(F32)
        return (
            sums[0] + jnp.sum(x.reshape(-1, 8, C), axis=0),
            sums[1] + jnp.sum((x * x).reshape(-1, 8, C), axis=0),
        )

    zero = jnp.zeros((8, C), F32)
    one, two = lax.fori_loop(0, band, add_row, (zero, zero))
    small[n, 0:1, :] = jnp.sum(one, axis=0, keepdims=True)
    small[n, 1:2, :] = jnp.sum(two, axis=0, keepdims=True)
    others = (mate, across, corner)

    def small_copy(slot, block):
        return to_narrow(
            small.at[block], small.at[block], small_sem.at[0, slot], small_sem.at[1, slot], others[slot]
        )

    for slot in range(3):
        small_copy(slot, n).start()

    in_target.wait()
    up = jnp.maximum(n - 1, 0)
    down = jnp.minimum(n + 1, 3)
    noisy_up = to_narrow(
        noisy_ext.at[pl.ds(2, 2)], noisy_ext.at[pl.ds(band + 2, 2)], halo_sem.at[0, 0], halo_sem.at[1, 0], up
    )
    noisy_down = to_narrow(
        noisy_ext.at[pl.ds(band, 2)], noisy_ext.at[pl.ds(0, 2)], halo_sem.at[0, 1], halo_sem.at[1, 1], down
    )
    @pl.when(n > 0)
    def _():
        noisy_up.start()

    @pl.when(n < 3)
    def _():
        noisy_down.start()

    @pl.when(n == 0)
    def _():
        noisy_ext[0:2] = jnp.zeros((2,) + noisy_ext.shape[1:], BF16)

    @pl.when(n == 3)
    def _():
        noisy_ext[band + 2 : band + 4] = jnp.zeros((2,) + noisy_ext.shape[1:], BF16)

    needs = rest_needs(rest_rows)
    rest_all[n] = rest_f32[...].astype(BF16)

    def rest_copy(owner, slot, device):
        a, b = needs[owner]
        ref = rest_all.at[owner, pl.ds(a, b - a)]
        return to_narrow(ref, ref, rest_sem.at[0, slot, owner], rest_sem.at[1, slot, owner], device)

    for owner in range(4):
        if needs[owner] is not None:
            @pl.when(n == owner)
            def _():
                rest_copy(owner, 1, across).start()
                rest_copy(owner, 0, mate).start()

    parts = wide_bf.shape[1] // C
    rows = 256
    for k in range(WPARTS):
        in_w[k].wait()

        @pl.loop(k * w_step // parts // rows, (k + 1) * w_step // parts // rows)
        def _(i):
            for j in range(parts):
                wide_bf[pl.ds(pl.multiple_of(i * rows, rows), rows), j * C : (j + 1) * C] = wide_f32[
                    pl.ds(i * rows * parts + j, rows, stride=parts), :
                ].astype(BF16)

    acc[...] = jnp.zeros_like(acc)
    for k in range(KPARTS):
        texts[k].relay()
    for k in range(KPARTS):
        texts[k].wait()

        @pl.loop(0, k_step // 512)
        def _(i):
            at = pl.ds(pl.multiple_of(k * k_step + i * 512, 512), 512)
            acc[...] += dot(text_all[:, :, at].reshape(4 * tokens, 512), wide_bf[at, :])

    keyval[n] = acc[...].astype(BF16)
    own_kv[...] = acc[...].astype(BF16)
    keys = Gather(lambda b: keyval.at[b], kv_sem, ids)
    keys.start()
    to_group()


    def relay_rest(owner):
        if needs[owner] is not None:
            @pl.when(across == owner)
            def _():
                rest_copy(owner, 1, across).wait_recv()
                rest_copy(owner, 2, mate).start()

    def settle_rest(owner):
        if needs[owner] is not None:
            @pl.when(mate == owner)
            def _():
                rest_copy(owner, 0, mate).wait_recv()

            @pl.when(corner == owner)
            def _():
                rest_copy(owner, 2, mate).wait_recv()

            @pl.when(n == owner)
            def _():
                rest_copy(owner, 1, across).wait_send()
                rest_copy(owner, 0, mate).wait_send()

            @pl.when(across == owner)
            def _():
                rest_copy(owner, 2, mate).wait_send()

    relay_rest(0)
    for slot, block in ((0, mate), (1, across), (2, corner)):
        small_copy(slot, block).wait_recv()
        small_copy(slot, n).wait_send()

    @pl.when(n > 0)
    def _():
        noisy_down.wait_recv()
        noisy_up.wait_send()

    @pl.when(n < 3)
    def _():
        noisy_up.wait_recv()
        noisy_down.wait_send()

    settle_rest(0)
    early(0)
    for owner in range(1, 4):
        relay_rest(owner)
    keys.relay()
    early(1)
    for owner in range(1, 4):
        settle_rest(owner)
    keys.wait()
    keys.drain()
    for part in texts:
        part.drain()


def mid_stages(gd, height, columns, from_group, blocks, conv, packet, right, kvs, texts, *refs):
    (
        dkv_all, conv_all, t_all, small_all, scal,
        near_b, near_c, sum_b, sum_c, far_b, far_c, own_b, own_c, group_b, group_c,
        packets, wides, t_own, t_send, c_send, norms, conv_sum,
        near_sem, far_sem, group_sem, packet_sem, wide_sem, norm_sem, give_sem,
    ) = refs
    ids = cross_ids()
    n, mate, across, corner = ids
    others = (mate, across, corner)
    wide_count = wides.shape[0]
    wide = lax.axis_index("wide")
    group = wide // gd
    spot = lax.rem(wide, gd)
    tok, kv_block = kvs.shape[1:]
    heads = kv_block // HEAD
    depth = texts.shape[-1]
    scale = jnp.where(n < 2, 1.0 / math.sqrt(HEAD), 1.0)

    def lanes(h):
        return pl.ds(h * tok, tok)

    def near(slot, which):
        owner = corner if slot == 0 else mate
        src, dst = ((blocks, near_b), (conv, near_c))[which]
        return to_narrow(
            src.at[owner], dst.at[slot], near_sem.at[0, slot, which], near_sem.at[1, slot, which], mate
        )

    def far(h):
        if h < heads:
            src, dst = sum_b.at[:, lanes(h)], far_b.at[:, lanes(h)]
        else:
            src, dst = sum_c, far_c
        return to_narrow(src, dst, far_sem.at[0, h], far_sem.at[1, h], across)

    def group_copy(k, h):
        if h < heads:
            src, dst = own_b.at[:, lanes(h)], group_b.at[k - 1, :, lanes(h)]
        else:
            src, dst = own_c, group_c.at[k - 1]
        return pltpu.make_async_remote_copy(
            src_ref=src, dst_ref=dst,
            send_sem=group_sem.at[0, h, k - 1], recv_sem=group_sem.at[1, h, k - 1],
            device_id={"wide": group * gd + lax.rem(spot + k, gd)}, device_id_type=MESH,
        )

    def packet_copy(slot, block):
        return to_narrow(
            packets.at[block], packets.at[block],
            packet_sem.at[0, slot], packet_sem.at[1, slot], others[slot],
        )

    def wide_copy(k, block):
        return pltpu.make_async_remote_copy(
            src_ref=wides.at[block], dst_ref=wides.at[block],
            send_sem=wide_sem.at[0, k - 1], recv_sem=wide_sem.at[1, k - 1],
            device_id={"wide": lax.rem(wide + k, wide_count)}, device_id_type=MESH,
        )

    def start_near():
        for slot in range(2):
            for which in range(2):
                near(slot, which).start()

    def start_far():
        near(0, 0).wait_recv()
        sum_b[...] = (blocks[across].astype(F32) + near_b[0].astype(F32)).astype(BF16)
        for h in range(heads):
            far(h).start()
        near(0, 1).wait_recv()
        sum_c[...] = (conv[across].astype(F32) + near_c[0].astype(F32)).astype(BF16)
        far(heads).start()

    q_rows, q_from = 96, 80

    def give_head(src_n, h):
        src, dst = t_send.at[pl.ds(0, q_rows), lanes(h)], t_all.at[src_n, pl.ds(0, q_rows), lanes(h)]
        return to_narrow(src, dst, give_sem.at[0, 0, h], give_sem.at[1, src_n, h], 2)

    def give_tail(src_n, h):
        rows = pl.ds(q_from, C - q_from)
        src, dst = t_send.at[rows, lanes(h)], t_all.at[src_n, rows, lanes(h)]
        return to_narrow(src, dst, give_sem.at[0, 1, h], give_sem.at[1, src_n, h], 3)

    def give_values(h):
        src, dst = t_send.at[:, lanes(h)], t_all.at[2, :, lanes(h)]
        return to_narrow(src, dst, give_sem.at[0, 1, h], give_sem.at[1, 2, h], 3)

    def give_conv(src_n):
        return to_narrow(
            c_send, conv_all.at[src_n], give_sem.at[0, 2, 0], give_sem.at[1, src_n, heads], 0
        )

    def project(k, h, value):
        cols = slice(h * HEAD, (h + 1) * HEAD)
        dkv_all[k * tok : (k + 1) * tok, cols] = (dot(value, right[:, cols], TN) * scale).astype(BF16)
        term = dot(value, kvs[k, :, cols]) * scale
        t_own[:, cols] = term if k == 0 else t_own[:, cols] + term

    def finish(gram):
        packets[n] = packet[...]
        for slot in range(3):
            packet_copy(slot, n).start()
        near(1, 0).wait_recv()
        near(1, 1).wait_recv()
        for h in range(heads):
            far(h).wait_recv()
            at = slice(h * tok, (h + 1) * tok)
            own_b[:, at] = (
                blocks[n, :, at].astype(F32) + near_b[1, :, at].astype(F32) + far_b[:, at].astype(F32)
            ).astype(BF16)
            for k in range(1, gd):
                group_copy(k, h).start()
        for slot, block in enumerate(others):
            packet_copy(slot, block).wait_recv()
        wides[wide] = packets[0] + packets[1] + packets[2] + packets[3]

        @pl.loop(1, wide_count)
        def _(k):
            wide_copy(k, wide).start()

        far(heads).wait_recv()
        conv_sum[...] = conv[n].astype(F32) + near_c[1].astype(F32) + far_c[...].astype(F32)
        own_c[...] = conv_sum[...].astype(BF16)
        for k in range(1, gd):
            group_copy(k, heads).start()
        for h in range(heads):
            project(0, h, own_b[:, h * tok : (h + 1) * tok])
        from_group()
        def text_products(a, firsts):
            rows = slice(a * tok, (a + 1) * tok) if gd <= 4 else slice(0, tok)
            gram[rows, :] = jnp.zeros((tok, gd * tok), F32)

            @pl.loop(0, depth // 1024)
            def _(i):
                at = pl.ds(pl.multiple_of(i * 1024, 1024), 1024)
                left = texts[a, :, :, at].reshape(tok, 1024)
                for b in range(firsts, gd):
                    part = dot(left, texts[b, :, :, at].reshape(tok, 1024), NT)
                    gram[rows, b * tok : (b + 1) * tok] += part

        if gd <= 4:
            for a in range(gd):
                text_products(a, a)
        for h in range(heads):
            for k in range(1, gd):
                group_copy(k, h).wait_recv()
                project(k, h, group_b[k - 1, :, h * tok : (h + 1) * tok])
            at = slice(h * HEAD, (h + 1) * HEAD)
            t_send[:, at] = t_own[:, at].astype(BF16)
            for k in range(4):
                @pl.when(n == k)
                def _():
                    if k < 2:
                        give_head(k, h).start()
                        give_tail(k, h).start()
                    elif k == 2:
                        give_values(h).start()
                    else:
                        t_all[3, :, at] = t_send[:, at]
        for k in range(1, gd):
            group_copy(k, heads).wait_recv()
            conv_sum[...] += group_c[k - 1].astype(F32)
        c_send[...] = conv_sum[...].astype(BF16)
        for k in range(4):
            @pl.when(n == k)
            def _():
                if k > 0:
                    give_conv(k).start()
                else:
                    conv_all[0] = c_send[...]

        @pl.loop(1, wide_count)
        def _(k):
            wide_copy(k, lax.rem(wide + wide_count - k, wide_count)).wait_recv()

        sq = jnp.sum(t_own[...] * t_own[...]) + jnp.sum(conv_sum[...] * conv_sum[...])
        for a in range(gd):
            da = dkv_all[a * tok : (a + 1) * tok, :]
            if gd > 4:
                text_products(a, a)
            rows = slice(a * tok, (a + 1) * tok) if gd <= 4 else slice(0, tok)
            for b in range(a, gd):
                db = dkv_all[b * tok : (b + 1) * tok, :]
                top, low = two_parts(gram[rows, b * tok : (b + 1) * tok])
                part = jnp.sum(da.astype(F32) * (dot(top, db) + dot(low, db)))
                sq = sq + (part if a == b else 2.0 * part)
        gains = jnp.zeros((4, C), F32)
        shared = jnp.zeros((1, C), F32)
        for a in range(gd):
            mine = wides[group * gd + a]
            small_all[a] = mine
            gains = gains + mine[0:4]
            for b in range(gd):
                his = wides[group * gd + b]
                same = (mine[7:8, 0:1] == his[7:8, 0:1]).astype(F32) + (mine[7:8, 1:2] == his[7:8, 1:2]).astype(F32)
                shared = shared + same * (mine[4:5] * his[4:5] + mine[5:6] * his[5:6])
        shared_sq = jnp.sum(gains * gains) + jnp.sum(shared)
        norms[n] = jnp.full((8, C), sq + jnp.where(n == 0, shared_sq, 0.0), F32)

        def norm_copy(slot, block):
            return to_narrow(
                norms.at[block], norms.at[block], norm_sem.at[0, slot], norm_sem.at[1, slot], others[slot]
            )

        for slot in range(3):
            norm_copy(slot, n).start()

        def tally(k, found):
            there = wides[k]
            crop = there[7:8, 2:3]
            pixels = jnp.minimum(crop, float(height)) * jnp.minimum(crop, float(columns))
            mine = jnp.where(k // gd == group, pixels, 0.0)
            return found[0] + pixels, found[1] + mine, found[2] + jnp.sum(there[6:7], axis=1, keepdims=True)

        none = jnp.zeros((1, 1), F32)
        total, own_count, loss = lax.fori_loop(0, wide_count, tally, (none, none, none))
        for slot, block in enumerate(others):
            norm_copy(slot, block).wait_recv()
        squares = norms[0, 0:1] + norms[1, 0:1] + norms[2, 0:1] + norms[3, 0:1]
        norm = jnp.sqrt(squares) / total
        scal[0:1] = jnp.minimum(1.0, CLIP_NORM / norm) / total
        scal[1:2] = jnp.broadcast_to(INNER_RATE * own_count / total, (1, C))
        scal[2:3] = jnp.broadcast_to(loss, (1, C))
        scal[3:4] = jnp.broadcast_to(total, (1, C))
        scal[4:8] = jnp.zeros((4, C), F32)

        for k in range(4):
            @pl.when(n == k)
            def _():
                for h in range(heads):
                    if k < 2:
                        give_head(k, h).wait_send()
                        give_tail(k, h).wait_send()
                    if k == 2:
                        give_values(h).wait_send()
                        give_head(0, h).wait_recv()
                        give_head(1, h).wait_recv()
                    if k == 3:
                        give_tail(0, h).wait_recv()
                        give_tail(1, h).wait_recv()
                        give_values(h).wait_recv()
                if k > 0:
                    give_conv(k).wait_send()
                else:
                    for j in range(1, 4):
                        give_conv(j).wait_recv()
        for slot in range(2):
            for which in range(2):
                near(slot, which).wait_send()
        for h in range(heads + 1):
            far(h).wait_send()
            for k in range(1, gd):
                group_copy(k, h).wait_send()
        for slot in range(3):
            packet_copy(slot, n).wait_send()
            norm_copy(slot, n).wait_send()

        @pl.loop(1, wide_count)
        def _(k):
            wide_copy(k, wide).wait_send()

    return start_near, start_far, finish


def step_kernel(gd, wide_count, kv_rows, rest_rows, band, columns, counts, *refs):
    refs = list(refs)
    noise_level, aug_level, crop_size, weights, noisy, target, text, first, second, mask = refs[:10]
    texts, dkv_all, conv_all, t_all, small_all, scal, first_near, second_near = refs[10:18]
    n_front, n_main, n_mid = counts
    at = 18
    (noisy_ext, target_ext, rest_all, keyval, kvs, small) = refs[at : at + 6]
    act3, wt3, conv_s, xhat_s, rs_s, low_s, diff3 = refs[at + 6 : at + 13]
    at += 13
    front_sems = refs[at : at + n_front]
    at += n_front
    (blocks, conv, packet, right) = refs[at : at + 4]
    at += 4
    mid_refs = refs[at : at + n_mid]
    at += n_mid
    group_text_sem, ahead_sem, edge_sem = refs[at : at + 3]
    ahead = [
        pltpu.make_async_copy(far, near, ahead_sem.at[k])
        for k, (far, near) in enumerate(((first, first_near), (second, second_near)))
    ]
    n, mate, across, corner = cross_ids()
    wide = lax.axis_index("wide")
    group, spot = wide // gd, lax.rem(wide, gd)
    tok, kv_block = kvs.shape[1:]
    depth = text.shape[2]
    barrier = pltpu.get_barrier_semaphore()
    for other in (mate, across, corner):
        pl.semaphore_signal(barrier, inc=1, device_id={"narrow": other}, device_id_type=MESH)

    @pl.loop(1, wide_count)
    def _(k):
        pl.semaphore_signal(
            barrier, inc=1, device_id={"wide": lax.rem(wide + k, wide_count)}, device_id_type=MESH
        )

    def greet():
        pl.semaphore_wait(barrier, 3 + wide_count - 1)

    def group_send(k, which):
        buf = (texts, kvs)[which]
        return pltpu.make_async_remote_copy(
            src_ref=buf.at[0], dst_ref=buf.at[k],
            send_sem=group_text_sem.at[0, which, k - 1], recv_sem=group_text_sem.at[1, which, k - 1],
            device_id={"wide": group * gd + lax.rem(spot + k, gd)}, device_id_type=MESH,
        )

    def to_group():
        for which in (1, 0):
            for k in range(1, gd):
                group_send(k, which).start()

    def from_group():
        for which in (1, 0):
            for k in range(1, gd):
                group_send(k, which).wait_recv()
                group_send(k, which).wait_send()

    def early(part):
        common = (band, columns, H, noisy_ext, small, rest_all.at[0], act3)
        tiles = band // CTILE
        if part == 0:
            activate(*common, wt3)
        bounds = (0, tiles // 2) if part == 0 else (tiles // 2, tiles)
        convolve_tiles(*bounds, *common, conv_s, xhat_s, rs_s, low_s)

    def front(wide_f32, wide_bf, rest_f32, acc):
        front_body(
            kv_rows, rest_rows, greet, to_group, early, noise_level, aug_level, weights, noisy, target, text, mask,
            noisy_ext, target_ext, texts.at[0], rest_all, keyval, kvs.at[0], small,
            wide_f32, wide_bf, rest_f32, acc, *front_sems,
        )

    V = pltpu.VMEM
    pl.run_scoped(
        front, V((kv_rows, C), F32), V((depth, kv_block), BF16), V((rest_all.shape[1], C), F32),
        V((tok, kv_block), F32),
    )
    for copy in ahead:
        copy.start()
    pix = TILE * columns

    start_near, start_far, finish = mid_stages(
        gd, H, W, from_group, blocks, conv, packet, right, kvs, texts,
        dkv_all, conv_all, t_all, small_all, scal, *mid_refs,
    )

    def edge(order):
        src, dst = (1, band + 1) if order == 0 else (band, 0)
        other = jnp.maximum(n - 1, 0) if order == 0 else jnp.minimum(n + 1, 3)
        return to_narrow(diff3.at[src], diff3.at[dst], edge_sem.at[0, order], edge_sem.at[1, order], other)

    def edge_send(order):
        @pl.when(n > 0 if order == 0 else n < 3)
        def _():
            edge(order).start()

    def edge_wait():
        @pl.when(n > 0)
        def _():
            edge(1).wait_recv()
            edge(0).wait_send()

        @pl.when(n < 3)
        def _():
            edge(0).wait_recv()
            edge(1).wait_send()

        @pl.when(n == 0)
        def _():
            diff3[0] = jnp.zeros(diff3.shape[1:], BF16)

        @pl.when(n == 3)
        def _():
            diff3[band + 1] = jnp.zeros(diff3.shape[1:], BF16)

    def main(*scratch):
        main_body(
            start_near, start_far, edge_send, edge_wait, band, columns, H, HEADS, rest_rows, crop_size, noise_level, aug_level,
            noisy_ext, target_ext, small, rest_all, keyval, blocks, conv, packet, right,
            act3, wt3, conv_s, xhat_s, rs_s, low_s, diff3, *scratch,
        )

    pl.run_scoped(
        main,
        V((2 * C, HEADS * tok), BF16),
        V((HEADS * tok, 2 * C), BF16),
        V((HEADS * tok, 2 * C), BF16),
        V((2 * C, HEADS * tok), BF16),
        V((C, 9 * C), F32),
        V((pix, HEADS * tok), BF16),
        V((pix, HEADS * tok), BF16),
        V((C, HEADS * tok), F32),
        V((C, HEADS * tok), F32),
        V((8, C), F32),
        V((rest_all.shape[1], C), F32),
        V((C * HEADS, C), F32),
        V((HEADS * HEAD, C), F32),
    )

    pl.run_scoped(finish, V((gd * tok if gd <= 4 else tok, gd * tok), F32))
    for copy in ahead:
        copy.wait()


def near(gd):
    return pltpu.VMEM if gd <= 4 else jax.ShapeDtypeStruct


def hold(value, gd):
    return pltpu.with_memory_space_constraint(value, pltpu.VMEM) if gd <= 4 else value


def far(value):
    return pltpu.with_memory_space_constraint(value, pltpu.HBM)


def run_step(
    gd, wide_count, noise_level, aug_level, crop_size, weights2, noisy, target, text, first, second, mask
):
    _, band, columns, _ = noisy.shape
    _, tokens, depth = text.shape
    tok = 4 * tokens
    kv_block = 2 * HEADS * HEAD // 4
    kv_rows = depth * kv_block // C
    rest_rows = weights2.shape[0] - kv_rows
    rest_pad = (rest_rows + 15) // 16 * 16
    assert 9 * C <= rest_rows and kv_block % HEAD == 0 and HEAD == C
    vmem = pl.BlockSpec(memory_space=pltpu.VMEM)
    smem = pl.BlockSpec(memory_space=pltpu.SMEM)
    hbm = pl.BlockSpec(memory_space=pltpu.HBM)
    D, V = pltpu.SemaphoreType.DMA, pltpu.VMEM
    few = max(gd - 1, 1)
    heads = kv_block // HEAD
    bshape, cshape = (C, kv_block // HEAD * tok), (9 * C // 4, C)
    front_sems = [D((WPARTS,)), D((4,)), D((KPARTS, 2, 3)), D((2, 3, 4)), D((2, 3)), D((2, 3)), D((2, 4))]
    mid_refs = [
        V((2,) + bshape, BF16), V((2,) + cshape, BF16), V(bshape, BF16), V(cshape, BF16),
        V(bshape, BF16), V(cshape, BF16), V(bshape, BF16), V(cshape, BF16),
        V((few,) + bshape, BF16), V((few,) + cshape, BF16),
        V((4, 8, C), F32), V((wide_count, 8, C), F32),
        V((C, kv_block), F32), V((C, kv_block), BF16), V(cshape, BF16),
        V((4, 8, C), F32), V(cshape, F32),
        D((2, 2, 2)), D((2, heads + 1)), D((2, heads + 1, few)), D((2, 3)), D((2, wide_count)), D((2, 3)),
        D((2, 4, heads + 1)),
    ]
    return pl.pallas_call(
        functools.partial(
            step_kernel, gd, wide_count, kv_rows, rest_rows, band, columns,
            (len(front_sems), 0, len(mid_refs)),
        ),
        out_shape=tuple(
            near(gd)(shape, kind)
            for shape, kind in (
                ((gd, 4, tokens, depth), BF16),
                ((gd * tok, kv_block), BF16),
                ((4,) + cshape, BF16),
                ((4, C, kv_block), BF16),
                ((gd, 8, C), F32),
                ((8, C), F32),
                (first.shape, F32),
                (first.shape, F32),
            )
        ),
        in_specs=[smem] * 3 + [hbm] * 6 + [vmem],
        out_specs=(vmem,) * 8,
        scratch_shapes=[
            V((band + 4, columns, C), BF16), V((band + 2, columns, C), BF16), V((4, rest_pad, C), BF16),
            V((4, tok, kv_block), BF16), V((gd, tok, kv_block), BF16), V((4, 16, C), F32),
            V((band + 4, columns, 3 * C), BF16), V((9 * C, C), BF16),
            *[V((band, columns, C), F32)] * 3, V((band, columns, C), BF16),
            V((band + 2, columns, 3 * C), BF16),
            *front_sems,
            V((4,) + bshape, BF16), V((4,) + cshape, BF16), V((8, C), F32), V((C, kv_block), BF16),
            *mid_refs,
            D((2, 2, few)),
            D((2,)),
            D((2, 2)),
        ],
        compiler_params=pltpu.CompilerParams(
            collective_id=1, has_side_effects=True, vmem_limit_bytes=(STEP_VMEM if gd <= 4 else 60) * 2**20
        ),
        name="step",
    )(noise_level, aug_level, crop_size, *map(far, (weights2, noisy, target, text, first, second)), mask)


STEP_VMEM = 40


AROWS = 2048


def adam_tiles(length):
    return pl.cdiv(length + 17 * C, AROWS * C)


def adam_kernel(
    gd, length, kv_rows, rest_rows, *refs,
):
    (
        texts, dkv, conv, t_all, small, scal, first, second, first_out, second_out, step_out,
        nat, rest, turned_dkv, edge, shift, carry,
    ) = refs
    s = pl.program_id(0)
    tok = dkv.shape[0] // gd
    n = lax.axis_index("narrow")
    start = lax.rem(lax.axis_index("wide"), gd) * length
    row0 = start // C
    lane0, row_off, row_shift, block0 = lax.rem(start, C), lax.rem(row0, AROWS), lax.rem(row0, 16), row0 // AROWS
    wrap = C - lane0
    kv_blocks = kv_rows // AROWS
    parts = dkv.shape[1] // C
    cols_tile = AROWS // parts

    def iotas(rows):
        shape = (rows, C)
        return lax.broadcasted_iota(jnp.int32, shape, 0), lax.broadcasted_iota(jnp.int32, shape, 1)

    def natural(tile):
        block = block0 + tile
        here = pl.multiple_of(tile * AROWS + 8, 8)

        @pl.when(block < kv_blocks)
        def _():
            at = pl.ds(pl.multiple_of(block * cols_tile, cols_tile), cols_tile)
            text = jnp.concatenate([texts[k, :, :, at].reshape(tok, cols_tile) for k in range(gd)], axis=0)
            grad = dot(text, turned_dkv[...], TN)
            for j in range(parts - 1):
                nat[pl.ds(here + j, cols_tile, stride=parts), :] = grad[:, j * C : (j + 1) * C]
            part = grad[:, (parts - 1) * C :]
            row, lane = iotas(cols_tile)
            before = jnp.where(row == 0, edge[0:1, :], pltpu.roll(part, 1, 0))
            nat[pl.ds(here - 1, cols_tile, stride=parts), :] = jnp.where(lane < wrap, before, part)
            edge[0:1, :] = part[cols_tile - 1 : cols_tile, :]

        @pl.when(block >= kv_blocks)
        def _():
            at = pl.multiple_of(jnp.minimum((block - kv_blocks) * AROWS, rest.shape[0] - 16 - AROWS), 8)
            row, lane = iotas(AROWS)
            both = jnp.where(lane >= lane0, rest[pl.ds(at + 8, AROWS), :], rest[pl.ds(at + 9, AROWS), :])
            nat[pl.ds(here, AROWS), :] = pltpu.roll(both, wrap, 1)

            @pl.when(block == kv_blocks)
            def _():
                row, lane = iotas(8)
                ahead = pltpu.roll(rest[8:16, :], wrap, 1)
                nat[pl.ds(here - 1, 1), :] = jnp.where(lane < wrap, edge[...], ahead)[0:1, :]

    def assemble():
        first_table, first_gain = 9 * C, 9 * C + 2 * LEVELS
        first_query = first_gain + 4
        first_out = first_query + C * HEADS
        quarter = conv.shape[1]
        width = dkv.shape[1]
        heads = width // HEAD
        for owner in range(4):
            lo, hi = owner * rest_rows, (owner + 1) * rest_rows

            @pl.when(n == owner)
            def _():
                for k in range(4):
                    a, b = max(lo, k * quarter), min(hi, (k + 1) * quarter)
                    if a < b:
                        assert (a, b) == (k * quarter, (k + 1) * quarter)
                        rest[8 + a - lo : 8 + b - lo, :] = conv[k].astype(F32)
                a, b = max(lo, first_query), min(hi, first_out)
                if a < b:
                    for h in range(HEADS):
                        c0 = max(0, -(-(a - first_query - h) // HEADS))
                        c1 = min(C, -(-(b - first_query - h) // HEADS))
                        cols = slice(h % heads * HEAD, h % heads * HEAD + HEAD)
                        c_lo, c_hi = c0 // 16 * 16, (c1 + 15) // 16 * 16
                        value = t_all[h // heads, c_lo:c_hi, cols].astype(F32)
                        start = first_query + c0 * HEADS + h - lo
                        rest[pl.ds(8 + start, c1 - c0, stride=HEADS), :] = value[c0 - c_lo : c1 - c_lo]
                for h in range(HEADS):
                    a, b = first_out + h * HEAD, first_out + (h + 1) * HEAD
                    if lo <= a and b <= hi:
                        cols = slice(h % heads * HEAD, h % heads * HEAD + HEAD)
                        rest[8 + a - lo : 8 + b - lo, :] = t_all[2 + h // heads, :, cols].astype(F32).T
                    else:
                        assert b <= lo or hi <= a
                if lo <= first_gain and first_gain + 4 <= hi:
                    total = small[0, 0:4]
                    for k in range(1, gd):
                        total = total + small[k, 0:4]
                    rest[8 + first_gain - lo : 8 + first_gain + 4 - lo, :] = total


        for k in range(gd):
            for level, shift_by in ((0, 0), (1, NOISE_LEVELS)):
                found = jnp.max(small[k, 7:8, level : level + 1]).astype(jnp.int32) + shift_by
                for half in range(2):
                    at_row = first_table + 2 * found + half - n * rest_rows

                    @pl.when((at_row >= 0) & (at_row < rest_rows))
                    def _():
                        rest[pl.ds(at_row + 8, 1), :] += small[k, 4 + half : 5 + half]

    @pl.when(s == 0)
    def _():
        edge[...] = jnp.zeros_like(edge)
        rest[...] = jnp.zeros_like(rest)
        carry[...] = jnp.zeros_like(carry)
        shift[...] = jnp.zeros_like(shift)
        row, lane = iotas(dkv.shape[0])
        moved = [
            pltpu.roll(dkv[:, j * C : (j + 1) * C].astype(F32), wrap, 1) for j in range(parts)
        ]
        for j in range(parts):
            turned_dkv[:, j * C : (j + 1) * C] = jnp.where(
                lane < wrap, moved[j], moved[(j + 1) % parts]
            ).astype(BF16)

        @pl.when(start + length > kv_rows * C)
        def _():
            assemble()

        natural(0)

    natural(s + 1)
    row, lane = iotas(AROWS)
    g = nat[pl.ds(s * AROWS + row_off + 8, AROWS), :] * scal[0:1]
    one = BETA_ONE * first.reshape(AROWS, C)[...] + (1.0 - BETA_ONE) * g
    two = BETA_TWO * second.reshape(AROWS, C)[...] + (1.0 - BETA_TWO) * g * g
    first_out.reshape(AROWS, C)[...] = one
    second_out.reshape(AROWS, C)[...] = two
    fixed_one = one * (scal[1:2] * (1.0 / (1.0 - BETA_ONE**STEP)))
    fixed_two = two * (1.0 / (1.0 - BETA_TWO**STEP))
    root = fixed_two * lax.rsqrt(fixed_two)
    step = fixed_one * pl.reciprocal(root + ADAM_EPS, approx=True)
    step = jnp.where((s * AROWS + row) * C + lane < length, step, 0.0)
    turned = pltpu.roll(step, lane0, 1)
    above = pltpu.roll(turned, 1, 0)
    above = jnp.where(row == 0, carry[0:1, :], above)
    carry[0:1, :] = turned[AROWS - 1 : AROWS, :]
    shift[pl.ds(row_shift, AROWS), :] = jnp.where(lane < lane0, above, turned)
    step_out[...] = shift[0:AROWS, :].astype(BF16)
    shift[0:16, :] = shift[AROWS : AROWS + 16, :]


def run_adam(texts, dkv, conv, t_all, small, scal, first, second, length, kv_rows, rest_rows):
    gd = texts.shape[0]
    tiles = adam_tiles(length)
    flat = pl.BlockSpec((1, AROWS * C), lambda s: (0, s))
    rest_pad = (pl.cdiv(rest_rows, AROWS) + 1) * AROWS + 16
    return pl.pallas_call(
        functools.partial(adam_kernel, gd, length, kv_rows, rest_rows),
        out_shape=(
            jax.ShapeDtypeStruct((1, length), F32),
            jax.ShapeDtypeStruct((1, length), F32),
            near(gd)((tiles * AROWS, C), BF16),
        ),
        grid=(tiles,),
        in_specs=[pl.BlockSpec(memory_space=pltpu.VMEM)] * 6 + [flat, flat],
        out_specs=[flat, flat, pl.BlockSpec((AROWS, C), lambda s: (s, 0))],
        scratch_shapes=[
            pltpu.VMEM(((tiles + 1) * AROWS + 16, C), F32),
            pltpu.VMEM((rest_pad, C), F32),
            pltpu.VMEM(dkv.shape, BF16),
            pltpu.VMEM((8, C), F32),
            pltpu.VMEM((AROWS + 16, C), F32),
            pltpu.VMEM((8, C), F32),
        ],
        compiler_params=pltpu.CompilerParams(vmem_limit_bytes=ADAM_VMEM),
        name="adam",
    )(*(hold(v, gd) for v in (texts, dkv, conv, t_all, small, scal, first, second)))


ADAM_VMEM = 24 * 2**20


def share_kernel(
    gd, rows, chunk, pad, l1, l2, u_ref, w_far, o_far, out_ref, w_near, o_near,
    recv_a, recv_b, part, in_sem, s_u, s_fo, s_fi, s_y, r_a, r_b, r_f, r_y,
):
    loads = [
        pltpu.make_async_copy(w_far, w_near.at[pl.ds(0, w_far.shape[0])], in_sem.at[1]),
        pltpu.make_async_copy(o_far, o_near.at[pl.ds(0, o_far.shape[0])], in_sem.at[2]),
    ]
    wide = lax.axis_index("wide")
    g = wide // gd
    spot = wide % gd
    chunks = rows // chunk
    is_outer = jnp.logical_or(g == 0, g == GROUPS - 1)
    is_inner = jnp.logical_not(is_outer)
    low = g < GROUPS // 2
    outer_id = jnp.where(low, g - 1, g + 1) * gd + spot
    mate_id = jnp.where(low, g + 1, g - 1) * gd + spot
    barrier = pltpu.get_barrier_semaphore()
    for k in range(1, gd):
        other = g * gd + lax.rem(spot + k, gd)
        pl.semaphore_signal(barrier, inc=1, device_id={"wide": other}, device_id_type=MESH)
    pl.semaphore_signal(barrier, inc=1, device_id={"wide": mate_id}, device_id_type=MESH)
    @pl.when(is_inner)
    def _():
        pl.semaphore_signal(barrier, inc=1, device_id={"wide": outer_id}, device_id_type=MESH)
        pl.semaphore_wait(barrier, gd + 1)
    @pl.when(is_outer)
    def _():
        pl.semaphore_wait(barrier, gd)

    def sl(c):
        return pl.ds(pl.multiple_of(c * chunk, chunk), chunk)
    def ol(c):
        return pl.ds(pl.multiple_of(pad + c * chunk, 16), chunk)
    def copy(src, dst, ss, rs, dev):
        return pltpu.make_async_remote_copy(src_ref=src, dst_ref=dst, send_sem=ss, recv_sem=rs,
                                            device_id={"wide": dev}, device_id_type=MESH)
    def send_a(c):
        return copy(u_ref.at[sl(c)], recv_a.at[sl(c)], s_u.at[c], r_a.at[c], mate_id)
    def send_b(c):
        return copy(part.at[sl(c)], recv_b.at[sl(c)], s_u.at[c], r_b.at[c], mate_id)
    def send_fo(c):
        return copy(out_ref.at[spot, ol(c)], out_ref.at[spot, ol(c)], s_fo.at[c], r_f.at[c], outer_id)
    def send_fi(c):
        return copy(out_ref.at[spot, ol(c)], out_ref.at[spot, ol(c)], s_fi.at[c], r_f.at[c], mate_id)
    def send_y(c, k):
        return copy(out_ref.at[spot, ol(c)], out_ref.at[spot, ol(c)], s_y.at[k - 1, c], r_y.at[k - 1, c],
                    g * gd + lax.rem(spot + k, gd))
    def wait_y(c, k):
        src = lax.rem(spot + gd - k, gd)
        copy(out_ref.at[src, ol(c)], out_ref.at[src, ol(c)], s_y.at[k - 1, c], r_y.at[k - 1, c], wide).wait_recv()
    def spread(c):
        for k in range(1, gd):
            send_y(c, k).start()
    def is_root(c):
        return lax.rem(c + g, 2) == 1

    @pl.when(is_outer)
    def _():
        @pl.loop(0, chunks)
        def _(c):
            send_a(c).start()
    for load in loads:
        load.start()
    for p in range(gd):
        out_ref[p, 0:pad] = jnp.zeros((pad, 128), jnp.bfloat16)
        out_ref[p, pad + rows : rows + 2 * pad] = jnp.zeros((pad, 128), jnp.bfloat16)

    @pl.when(is_outer)
    def _():
        @pl.loop(0, chunks)
        def _(c):
            send_fo(c).wait_recv()
            spread(c)
    @pl.when(is_inner)
    def _():
        @pl.loop(0, chunks + l2)
        def _(c):
            @pl.when(jnp.logical_and(c < chunks, jnp.logical_not(is_root(c))))
            def _():
                send_a(c).wait_recv()
                part[sl(c)] = (u_ref[sl(c)].astype(jnp.float32) + recv_a[sl(c)].astype(jnp.float32)).astype(jnp.bfloat16)
                send_b(c).start()
            d = c - l1
            @pl.when(jnp.logical_and(jnp.logical_and(d >= 0, d < chunks), is_root(d)))
            def _():
                send_a(d).wait_recv()
                send_b(d).wait_recv()
                out_ref[spot, ol(d)] = (u_ref[sl(d)].astype(jnp.float32) + recv_a[sl(d)].astype(jnp.float32) + recv_b[sl(d)].astype(jnp.float32)).astype(jnp.bfloat16)
                send_fo(d).start()
                send_fi(d).start()
                spread(d)
            e = c - l2
            @pl.when(jnp.logical_and(e >= 0, jnp.logical_not(is_root(e))))
            def _():
                send_fi(e).wait_recv()
                send_fo(e).start()
                spread(e)
    @pl.loop(0, chunks)
    def _(c):
        for k in range(1, gd):
            wait_y(c, k)
            send_y(c, k).wait_send()
        @pl.when(is_outer)
        def _():
            send_a(c).wait_send()
        @pl.when(is_inner)
        def _():
            send_fo(c).wait_send()
            @pl.when(is_root(c))
            def _():
                send_fi(c).wait_send()
            @pl.when(jnp.logical_not(is_root(c)))
            def _():
                send_b(c).wait_send()
    for load in loads:
        load.wait()


def share(u, weights2, outer2, gd, rows, chunk, pad, l1, l2):
    n = rows // chunk
    D = pltpu.SemaphoreType.DMA
    few = max(gd - 1, 1)
    held = pl.cdiv(weights2.shape[0], 256) * 256
    vmem, hbm = pl.BlockSpec(memory_space=pltpu.VMEM), pl.BlockSpec(memory_space=pltpu.HBM)
    return pl.pallas_call(
        functools.partial(share_kernel, gd, rows, chunk, pad, l1, l2),
        out_shape=(near(gd)((gd, rows + 2 * pad, C), BF16),) + (near(gd)((held, C), F32),) * 2,
        in_specs=[vmem, hbm, hbm],
        out_specs=(vmem,) * 3,
        scratch_shapes=[pltpu.VMEM((rows, C), BF16)] * 3
        + [
            D((3,)), D((n,)), D((n,)), D((n,)), D((few, n)),
            D((n,)), D((n,)), D((n,)), D((few, n)),
        ],
        compiler_params=pltpu.CompilerParams(
            collective_id=9, has_side_effects=True, vmem_limit_bytes=SHARE_VMEM
        ),
        name="share",
    )(hold(u, gd), far(weights2), far(outer2))


SHARE_VMEM = 32 * 2**20


def final_kernel(bases, pad, block, weights, outer, pieces, scal, new_weights, momentum, loss, count, held, sem):
    rows = new_weights.shape[0]
    total = pieces.shape[1]
    steps = pl.cdiv(rows, block)

    def writes(b, slot, size):
        here = pl.ds(b * block, size)
        return [
            pltpu.make_async_copy(held.at[slot, k, pl.ds(0, size)], out.at[here], sem.at[slot, k])
            for k, out in enumerate((new_weights, momentum))
        ]

    for b in range(steps):
        slot = b % 3
        size = min(block, rows - b * block)
        if b >= 3:
            for copy in writes(b - 3, slot, block):
                copy.wait()
        averaged = jnp.zeros((block, C), F32)
        for p, base in enumerate(bases):
            at = min(max(b * block - base + pad, 0), total - block)
            averaged = averaged + pieces[p, at : at + block, :].astype(F32)
        w = weights[b * block : (b + 1) * block, :]
        averaged = averaged + (INNER_RATE * DECAY_RATE) * w
        moved = OUTER_MOMENTUM * outer[b * block : (b + 1) * block, :] + averaged
        held[slot, 1] = moved
        held[slot, 0] = w - OUTER_RATE * (averaged + OUTER_MOMENTUM * moved)
        for copy in writes(b, slot, size):
            copy.start()
    loss[0] = jnp.max(scal[2:3])
    count[0] = jnp.max(scal[3:4])
    for b in range(max(steps - 3, 0), steps):
        for copy in writes(b, b % 3, min(block, rows - b * block)):
            copy.wait()


def run_final(rows, weights2, outer2, pieces, scal, bases, pad):
    hbm, smem = pl.BlockSpec(memory_space=pltpu.HBM), pl.BlockSpec(memory_space=pltpu.SMEM)
    block = weights2.shape[0] // 16
    assert block % 16 == 0 and block <= pad
    return pl.pallas_call(
        functools.partial(final_kernel, bases, pad, block),
        out_shape=(jax.ShapeDtypeStruct((rows, C), F32),) * 2 + (jax.ShapeDtypeStruct((1,), F32),) * 2,
        in_specs=[pl.BlockSpec(memory_space=pltpu.VMEM)] * 4,
        out_specs=(hbm, hbm, smem, smem),
        scratch_shapes=[pltpu.VMEM((3, 2, block, C), F32), pltpu.SemaphoreType.DMA((3, 2))],
        compiler_params=pltpu.CompilerParams(vmem_limit_bytes=12 * 2**20),
        name="final",
    )(*(hold(v, len(bases)) for v in (weights2, outer2, pieces, scal)))


def per_device(
    weights, first_moment, second_moment, outer_momentum, noisy_input, target,
    text_tokens, text_mask, noise_level, aug_level, crop_size,
):
    length = first_moment.shape[1]
    wide_count = lax.axis_size("wide")
    gd = wide_count // GROUPS
    weights2 = weights.reshape(-1, C)
    outer2 = outer_momentum.reshape(-1, C)

    texts, dkv, conv_all, t_all, small_all, scal, first, second = run_step(
        gd, wide_count, noise_level, aug_level, crop_size, weights2, noisy_input, target, text_tokens,
        first_moment, second_moment, text_mask,
    )
    kv_rows = TEXT_D * dkv.shape[1] // C
    rest_rows = weights2.shape[0] - kv_rows
    moment_one, moment_two, step = run_adam(
        texts, dkv, conv_all, t_all, small_all, scal, first, second, length, kv_rows, rest_rows
    )
    chunk = 160
    rows = pl.cdiv(length // C + 18, chunk) * chunk
    pad = 1120
    pieces, w_near, o_near = share(step, weights2, outer2, gd, rows, chunk, pad, 3, 6)
    bases = [p * length // C // 16 * 16 for p in range(gd)]
    new_weights, momentum_out, loss, count = run_final(
        weights2.shape[0], w_near, o_near, pieces, scal, bases, pad
    )
    return (
        new_weights.reshape(-1), momentum_out.reshape(-1), moment_one, moment_two,
        loss, count,
    )


def solution(mesh):
    placed = (
        P("narrow"),
        P("narrow", "wide"),
        P("narrow", "wide"),
        P("narrow"),
        P("wide", "narrow", None, None),
        P("wide", "narrow", None, None),
        P("wide", "narrow", None),
        P("wide", "narrow"),
        P("wide"),
        P("wide"),
        P("wide"),
    )
    return jax.shard_map(
        per_device,
        mesh=mesh,
        in_specs=placed,
        out_specs=(P("narrow"), P("narrow"), P("narrow", "wide"), P("narrow", "wide"), P(), P()),
        check_vma=False,
    )
```
